256 devices in a mesh: row: 16 (over y_hi, x, core), col: 16 (over y_lo, z).
Axes of the slice: x: 4, y: 4 (y_hi: 2, y_lo: 2; y = y_hi * 2 + y_lo), z: 8, core: 2. Of those that a mesh axis runs over, the one named last changes fastest.
Arguments:
- features: bfloat16 [256, 256, 4, 128], P('row', 'col'), may hold values from -6 to 6
- conv_first: bfloat16 [3, 3, 128, 128], replicated, may hold values from -0.1875 to 0.1875
- conv_second: bfloat16 [3, 3, 128, 128], replicated, may hold values from -0.1875 to 0.1875
- coarse_conv: bfloat16 [3, 3, 128, 256], P(None, None, None, 'row'), may hold values from -0.1875 to 0.1875
- coarse_proj: bfloat16 [256, 128], P('row'), may hold values from -0.375 to 0.375
- cotangent: bfloat16 [256, 256, 4, 128], P('row', 'col'), may hold values from -6 to 6
Outputs:
- blended: bfloat16 [256, 256, 4, 128], P('row', 'col')
- feature_grad: bfloat16 [256, 256, 4, 128], P('row', 'col')
- first_grad: float32 [3, 3, 128, 128], replicated
- second_grad: float32 [3, 3, 128, 128], replicated
- coarse_conv_grad: float32 [3, 3, 128, 256], P(None, None, None, 'row')
- coarse_proj_grad: float32 [256, 128], P('row')
The draws below stay inside these ranges and needn't reach their ends.
All inputs are finite; a program needn't handle non-finite values.
Results may differ from the reference program's by a relative error of at most 0.015.
Values may be sent and summed in bfloat16 or wider, within the bound.
No kernel may reach another device: no remote copies, remote signals or barrier semaphores. Data moves between devices by JAX's collectives and lax.ppermute only.
A program may use at most 64 MiB of HBM per device.

```python
import jax
import jax.numpy as jnp

IMAGES = 4
FINE_CH = 128
COARSE_CH = 256
NH = 256
NW = 256


def shard_levels(key, shape, shards, least, high):
    def one(axis_at, parts):
        heights = jax.random.uniform(jax.random.fold_in(jax.random.fold_in(key, 6), axis_at), (parts,), jnp.float32, least / len(shards), high / len(shards))
        return jnp.repeat(jnp.exp(heights), shape[axis_at] // parts).reshape((-1,) + (1,) * (len(shape) - axis_at - 1))

    level = one(*shards[0])
    for cut in shards[1:]:
        level = level * one(*cut)
    return level


def normal_values(stream_key, shape, width, bound, split=(), dtype=jnp.bfloat16):
    level = shard_levels(stream_key, shape, split, -0.22, 0.18) if split else 1.0
    values = jax.random.normal(stream_key, shape, jnp.float32) * width * level
    return jnp.minimum(jnp.maximum(values, -bound), bound).astype(dtype)


def setup_inputs(seed: int = 0) -> dict:
    key_of = jax.random.split(jax.random.key(seed), 7)
    return {
        "features": normal_values(key_of[0], (NH, NW, IMAGES, FINE_CH), 1.0, 6.0, ((0, 16), (1, 16))),
        "conv_first": normal_values(key_of[1], (3, 3, FINE_CH, FINE_CH), (9 * FINE_CH) ** -0.5, 0.1875),
        "conv_second": normal_values(key_of[2], (3, 3, FINE_CH, FINE_CH), (9 * FINE_CH) ** -0.5, 0.1875),
        "coarse_conv": normal_values(key_of[3], (3, 3, FINE_CH, COARSE_CH), (9 * FINE_CH) ** -0.5, 0.1875, ((3, 16),)),
        "coarse_proj": normal_values(key_of[4], (COARSE_CH, FINE_CH), COARSE_CH ** -0.5, 0.375, ((0, 16),)),
        "cotangent": normal_values(key_of[5], (NH, NW, IMAGES, FINE_CH), 1.0, 6.0, ((0, 16), (1, 16))),
    }


def silu_slope(value):
    sigma = jax.nn.sigmoid(value)
    return sigma * (1.0 + value * (1.0 - sigma))

def padded_of(source):
    return jnp.pad(source.astype(jnp.float32), ((1, 1), (1, 1), (0, 0), (0, 0)))

def convolve(source, weight):
    padded = padded_of(source)
    height, breadth = (source.shape[0], source.shape[1])
    summed = jnp.zeros(source.shape[:3] + (weight.shape[3],), jnp.float32)
    for row_off in range(3):
        for col_off in range(3):
            summed = summed + jnp.einsum('hwbc,cd->hwbd', padded[row_off:row_off + height, col_off:col_off + breadth], weight[row_off, col_off].astype(jnp.float32))
    return summed

def transposed(source, weight):
    padded = padded_of(source)
    height, breadth = (source.shape[0], source.shape[1])
    summed = jnp.zeros(source.shape[:3] + (weight.shape[2],), jnp.float32)
    for row_off in range(3):
        for col_off in range(3):
            summed = summed + jnp.einsum('hwbd,cd->hwbc', padded[2 - row_off:2 - row_off + height, 2 - col_off:2 - col_off + breadth], weight[row_off, col_off].astype(jnp.float32))
    return summed

def weight_grad(source, grad):
    padded = padded_of(source)
    height, breadth = (source.shape[0], source.shape[1])
    pieces = []
    for row_off in range(3):
        for col_off in range(3):
            pieces.append(jnp.einsum('hwbc,hwbd->cd', padded[row_off:row_off + height, col_off:col_off + breadth], grad.astype(jnp.float32)))
    return jnp.stack(pieces).reshape((3, 3) + pieces[0].shape)

def block_sum(value):
    height, breadth, images, chans = value.shape
    return value.astype(jnp.float32).reshape(height // 2, 2, breadth // 2, 2, images, chans).sum(axis=(1, 3))

def enlarge(value):
    return jnp.repeat(jnp.repeat(value, 2, axis=0), 2, axis=1)

def reference(features, conv_first, conv_second, coarse_conv, coarse_proj, cotangent):
    fine_scale = 1.0 / (NH * NW * IMAGES) ** 0.5
    coarse_scale = 2.0 * fine_scale
    first_pre = convolve(features, conv_first)
    first_act = jax.nn.silu(first_pre).astype(jnp.bfloat16)
    second_pre = convolve(first_act, conv_second)
    second_act = jax.nn.silu(second_pre).astype(jnp.bfloat16)
    pooled_act = (0.25 * block_sum(second_act)).astype(jnp.bfloat16)
    coarse_pre = convolve(pooled_act, coarse_conv)
    coarse_act = jax.nn.silu(coarse_pre).astype(jnp.bfloat16)
    projected = jnp.einsum('hwbk,kc->hwbc', coarse_act.astype(jnp.float32), coarse_proj.astype(jnp.float32))
    blended = (second_act.astype(jnp.float32) + enlarge(projected)).astype(jnp.bfloat16)
    proj_in = block_sum(cotangent).astype(jnp.bfloat16)
    coarse_proj_grad = coarse_scale * jnp.einsum('hwbk,hwbc->kc', coarse_act.astype(jnp.float32), proj_in.astype(jnp.float32))
    act_grad = jnp.einsum('hwbc,kc->hwbk', proj_in.astype(jnp.float32), coarse_proj.astype(jnp.float32))
    coarse_pre_grad = (act_grad * silu_slope(coarse_pre)).astype(jnp.bfloat16)
    coarse_conv_grad = coarse_scale * weight_grad(pooled_act, coarse_pre_grad)
    pooled_grad = transposed(coarse_pre_grad, coarse_conv)
    second_in = cotangent.astype(jnp.float32) + 0.25 * enlarge(pooled_grad)
    second_pre_grad = (second_in * silu_slope(second_pre)).astype(jnp.bfloat16)
    second_grad = fine_scale * weight_grad(first_act, second_pre_grad)
    first_in = transposed(second_pre_grad, conv_second)
    first_pre_grad = (first_in * silu_slope(first_pre)).astype(jnp.bfloat16)
    first_grad = fine_scale * weight_grad(features, first_pre_grad)
    feature_grad = transposed(first_pre_grad, conv_first).astype(jnp.bfloat16)
    return (blended, feature_grad, first_grad, second_grad, coarse_conv_grad, coarse_proj_grad)
```

```python
import functools

import jax
import jax.numpy as jnp
from jax import lax
from jax.experimental import pallas as pl
from jax.experimental.pallas import tpu as pltpu
from jax.sharding import PartitionSpec as P

BF = jnp.bfloat16
F32 = jnp.float32
CH = 128
WIDE = 256
PARAMS = pltpu.CompilerParams(vmem_limit_bytes=48 * 1024 * 1024)


def dot_nn(a, b):
    return jnp.dot(a, b, preferred_element_type=F32)


def dot_nt(a, b):
    return lax.dot_general(a, b, (((1,), (1,)), ((), ())), preferred_element_type=F32)


def dot_tn(a, b):
    return lax.dot_general(a, b, (((0,), (0,)), ((), ())), preferred_element_type=F32)


def sigmoid(value):
    return 0.5 * jnp.tanh(0.5 * value) + 0.5


def slope_of(value):
    sigma = sigmoid(value)
    return sigma * (1.0 + value * (1.0 - sigma))


def rounded(value):
    return value.astype(BF).astype(F32)


def three(value):
    count = value.shape[0]
    left = pltpu.roll(value, 4, 0)
    right = pltpu.roll(value, count - 4, 0)
    return jnp.concatenate([left.astype(BF), value.astype(BF), right.astype(BF)], axis=1)


def taps(ref, start, rows, cols=None):
    parts = []
    for r in range(3):
        part = ref[pl.ds(start + r, rows)] if cols is None else ref[pl.ds(start + r, rows), cols[0] : cols[1], :]
        parts.append(part.reshape(part.shape[0] * part.shape[1], part.shape[2]))
    return jnp.concatenate(parts, axis=1)


def column_mask(first, width, limit):
    place = first + lax.broadcasted_iota(jnp.int32, (width, CH), 0) // 4
    return jnp.where((place >= 0) & (place < limit), 1.0, 0.0).astype(F32)


def row_ok(place, limit):
    return jnp.where((place >= 0) & (place < limit), 1.0, 0.0).astype(F32)


def masked(value, mask, first, limit):
    rows = []
    for k in range(value.shape[0]):
        rows.append((value[k] * (mask * row_ok(first + k, limit)))[None])
    return jnp.concatenate(rows, axis=0)


def pooled_pair(row):
    count = row.shape[0]
    low = (row + pltpu.roll(row, count - 4, 0)).reshape(count // 16, 2, 8, CH)
    high = (row + pltpu.roll(row, 4, 0)).reshape(count // 16, 2, 8, CH)
    first = lax.broadcasted_iota(jnp.int32, (count // 16, 8, CH), 1) < 4
    return jnp.where(first, low[:, 0], high[:, 1]).reshape(count // 2, CH)


def repeated(row):
    count = row.shape[0]
    first = lax.broadcasted_iota(jnp.int32, (count, CH), 0) % 8 < 4
    even = jnp.where(first, row, pltpu.roll(row, 4, 0)).reshape(count // 8, 1, 8, CH)
    odd = jnp.where(first, pltpu.roll(row, count - 4, 0), row).reshape(count // 8, 1, 8, CH)
    return jnp.concatenate([even, odd], axis=1).reshape(count * 2, CH)


def forward_kernel(meta, window, w1, w2, pool3, slope1, slope2, act, feat3o, act3o, feat3, act3, pre1, pre2, act2):
    top, left, height, breadth = (meta[0], meta[1], meta[2], meta[3])
    mask = column_mask(left - 8, 128, breadth)
    coarse_mask = column_mask(left // 2 - 4, 64, breadth // 2)

    @pl.loop(0, 8)
    def _(b):
        block = window[pl.ds(4 * b, 4)].reshape(512, CH).astype(F32)
        feat3[pl.ds(4 * b, 4)] = three(block).reshape(4, 128, 3 * CH)

    first_w = w1[...]

    @pl.loop(0, 6)
    def _(b):
        pre = dot_nn(taps(feat3, 5 * b, 5), first_w)
        pre1[pl.ds(5 * b, 5)] = pre.reshape(5, 128, CH)
        value = rounded(pre * sigmoid(pre)).reshape(5, 128, CH)
        value = masked(value, mask, top - 7 + 5 * b, height)
        act3[pl.ds(5 * b, 5)] = three(value.reshape(640, CH)).reshape(5, 128, 3 * CH)

    second_w = w2[...]

    @pl.loop(0, 7)
    def _(b):
        pre = dot_nn(taps(act3, 4 * b, 4), second_w)
        pre2[pl.ds(4 * b, 4)] = pre.reshape(4, 128, CH)
        value = (pre * sigmoid(pre)).astype(BF)
        act2[pl.ds(4 * b, 4)] = value.reshape(4, 128, CH)
        value = value.astype(F32).reshape(4, 128, CH)
        coarse = []
        for k in range(2):
            small = rounded(0.25 * pooled_pair(value[2 * k] + value[2 * k + 1]))
            coarse.append(small * (coarse_mask * row_ok(top // 2 - 3 + 2 * b + k, height // 2)))
        coarse = jnp.concatenate(coarse, axis=0)
        pool3[pl.ds(2 * b, 2)] = three(coarse).reshape(2, 64, 3 * CH)

    @pl.loop(0, 18)
    def _(k):
        slope1[k] = slope_of(pre1[k + 6, 16:112, :])
        feat3o[k] = feat3[k + 7, 32:96, :]
        act3o[k] = act3[k + 6, 32:96, :]

    @pl.loop(0, 20)
    def _(k):
        slope2[k] = slope_of(pre2[k + 4, 16:112, :])

    @pl.loop(0, 16)
    def _(k):
        act[k] = act2[k + 6, 32:96, :]


def fine_forward(meta, window, w1, w2):
    sds = jax.ShapeDtypeStruct
    vm = pl.BlockSpec(memory_space=pltpu.VMEM)
    return pl.pallas_call(
        forward_kernel,
        name="fine_forward",
        out_shape=(
            sds((14, 64, 384), BF),
            sds((18, 96, CH), F32),
            sds((20, 96, CH), F32),
            sds((16, 64, CH), BF),
            sds((18, 64, 384), BF),
            sds((18, 64, 384), BF),
        ),
        in_specs=[pl.BlockSpec(memory_space=pltpu.SMEM), vm, vm, vm],
        out_specs=[vm] * 6,
        scratch_shapes=[
            pltpu.VMEM((32, 128, 384), BF),
            pltpu.VMEM((30, 128, 384), BF),
            pltpu.VMEM((30, 128, CH), F32),
            pltpu.VMEM((28, 128, CH), F32),
            pltpu.VMEM((28, 128, CH), BF),
        ],
        compiler_params=PARAMS,
    )(meta, window, w1, w2)


def coarse_kernel(meta, pool3, cot, wg, proj, act, blended, grads, pooled_grad, wcat, wide3, projin):
    top, left, height, breadth = (meta[0], meta[1], meta[2], meta[3])
    for t in range(9):
        wcat[:, t * CH : (t + 1) * CH] = wg[:, t].reshape(WIDE, CH)
    proj_w = proj[...]

    @pl.loop(0, 12)
    def _(k):
        pair = cot[pl.ds(2 * k, 2)].astype(F32)
        projin[k] = pooled_pair(pair[0] + pair[1])

    proj_in = projin[...].reshape(576, CH)
    proj_in_bf = proj_in.astype(BF)
    pre = dot_nt(taps(pool3, 0, 12), wcat[...]).reshape(12, 64, WIDE)[:, 8:56].reshape(576, WIDE)
    sigma = sigmoid(pre)
    coarse_act = pre * sigma
    act_grad = dot_nt(proj_in_bf, proj_w)
    grad = rounded(act_grad * (sigma * (1.0 + pre * (1.0 - sigma)))).reshape(12, 48, WIDE)
    mask = column_mask(left // 2 - 2, 48, breadth // 2)
    mask = jnp.concatenate([mask, mask], axis=1)
    grad = masked(grad, mask, top // 2 - 2, height // 2)
    wide3[...] = three(grad.reshape(576, WIDE)).reshape(12, 48, 3 * WIDE)
    own_grad = grad[2:10, 8:40].reshape(256, WIDE).astype(BF)
    own_act = coarse_act.reshape(12, 48, WIDE)[2:10, 8:40].reshape(256, WIDE).astype(BF)
    own_in = proj_in.reshape(12, 48, CH)[2:10, 8:40].reshape(256, CH).astype(BF)
    for r in range(3):
        source = pool3[2 + r : 10 + r, 16:48, :].reshape(256, 3 * CH)
        part = dot_tn(own_grad, source).astype(BF)
        for s in range(3):
            t = 3 * r + s
            grads[:, 16 * t : 16 * t + 16, :] = part[:, s * CH : (s + 1) * CH].reshape(16, 16, CH)
    grads[:, 144:160, :] = dot_tn(own_act, own_in).astype(BF).reshape(16, 16, CH)
    total = None
    for r in range(3):
        lhs = wide3[r : r + 10].reshape(480, 3 * WIDE)
        rhs = jnp.concatenate([wg[:, 3 * (2 - r) + (2 - s)].reshape(WIDE, CH) for s in range(3)], axis=0)
        part = dot_nn(lhs, rhs)
        total = part if total is None else total + part
    pooled_grad[...] = total.reshape(10, 48, CH)
    projected = dot_nn(own_act, proj_w).reshape(8, 32, CH)
    for k in range(8):
        row = repeated(projected[k])
        for e in range(2):
            blended[2 * k + e] = (act[2 * k + e].astype(F32) + row).astype(BF)


def coarse_step(meta, pool3, cot, wg, proj, act):
    sds = jax.ShapeDtypeStruct
    vm = pl.BlockSpec(memory_space=pltpu.VMEM)
    return pl.pallas_call(
        coarse_kernel,
        name="coarse_step",
        out_shape=(sds((16, 64, CH), BF), sds((16, 160, CH), BF), sds((10, 48, CH), F32)),
        in_specs=[pl.BlockSpec(memory_space=pltpu.SMEM)] + [vm] * 5,
        out_specs=[vm] * 3,
        scratch_shapes=[
            pltpu.VMEM((WIDE, 9 * CH), BF),
            pltpu.VMEM((12, 48, 3 * WIDE), BF),
            pltpu.VMEM((12, 48, CH), F32),
        ],
        compiler_params=PARAMS,
    )(meta, pool3, cot, wg, proj, act)


def flipped(weight):
    return jnp.concatenate([weight[8 - t] for t in range(9)], axis=1)


def backward_kernel(meta, pooled_grad, cot, slope1, slope2, feat3, act3, w2, grads, first3, second3):
    top, left, height, breadth = (meta[0], meta[1], meta[2], meta[3])
    mask = column_mask(left - 4, 96, breadth)

    @pl.loop(0, 10)
    def _(k):
        wide = 0.25 * repeated(pooled_grad[k])
        rows = []
        for e in range(2):
            value = cot[2 * k + e + 2].astype(F32) + wide
            value = rounded(value * slope2[2 * k + e])
            rows.append(value * (mask * row_ok(top - 2 + 2 * k + e, height)))
        second3[pl.ds(2 * k, 2)] = three(jnp.concatenate(rows, axis=0)).reshape(2, 96, 3 * CH)

    def weight_grad(source, grad):
        return [dot_tn(source[r : r + 16].reshape(1024, 3 * CH), grad) for r in range(3)]

    def emit(base, parts):
        for r in range(3):
            grads[base + 384 * r : base + 384 * (r + 1), :] = parts[r].astype(BF)

    second_own = second3[2:18, 16:80, CH : 2 * CH].reshape(1024, CH)
    emit(1152, weight_grad(act3, second_own))
    back_w = flipped(w2)

    @pl.loop(0, 3)
    def _(b):
        value = dot_nt(taps(second3, 6 * b, 6), back_w).reshape(6, 96, CH)
        value = rounded(value * slope1[pl.ds(6 * b, 6)])
        value = masked(value, mask, top - 1 + 6 * b, height)
        out = three(value.reshape(576, CH)).reshape(6, 96, 3 * CH)
        first3[pl.ds(6 * b, 6)] = out[:, 16:80, :]

    first_own = first3[1:17, :, CH : 2 * CH].reshape(1024, CH)
    emit(0, weight_grad(feat3, first_own))


def fine_backward(meta, pooled_grad, cot, slope1, slope2, feat3, act3, w2):
    sds = jax.ShapeDtypeStruct
    vm = pl.BlockSpec(memory_space=pltpu.VMEM)
    return pl.pallas_call(
        backward_kernel,
        name="fine_backward",
        out_shape=(sds((2304, CH), BF), sds((18, 64, 384), BF)),
        in_specs=[pl.BlockSpec(memory_space=pltpu.SMEM)] + [vm] * 7,
        out_specs=[vm] * 2,
        scratch_shapes=[pltpu.VMEM((20, 96, 384), BF)],
        compiler_params=PARAMS,
    )(meta, pooled_grad, cot, slope1, slope2, feat3, act3, w2)


def feature_kernel(first3, w1, out):
    back_w = flipped(w1)

    @pl.loop(0, 2)
    def _(b):
        out[pl.ds(8 * b, 8)] = dot_nt(taps(first3, 8 * b, 8), back_w).astype(BF).reshape(8, 64, CH)


def feature_step(first3, w1):
    vm = pl.BlockSpec(memory_space=pltpu.VMEM)
    return pl.pallas_call(
        feature_kernel,
        name="feature_step",
        out_shape=jax.ShapeDtypeStruct((16, 64, CH), BF),
        in_specs=[vm] * 2,
        out_specs=vm,
        compiler_params=PARAMS,
    )(first3, w1)


def tile_compute(meta, window, cot, w1, w2, wg, proj):
    pool3, slope1, slope2, act, feat3, act3 = fine_forward(meta, window, w1.reshape(1152, CH), w2.reshape(1152, CH))
    blended, coarse_grads, pooled_grad = coarse_step(meta, pool3, cot, wg, proj, act)
    fine_grads, first3 = fine_backward(meta, pooled_grad, cot, slope1, slope2, feat3, act3, w2.reshape(9, CH, CH))
    feature_grad = feature_step(first3, w1.reshape(9, CH, CH))
    return blended, feature_grad, coarse_grads, fine_grads


def swap(value, axis, mask):
    count = lax.axis_size(axis)
    return lax.ppermute(value, axis, [(i, i ^ mask) for i in range(count)])


def shifted(value, axis, step):
    count = lax.axis_size(axis)
    pairs = [(i, i + step) for i in range(count) if 0 <= i + step < count]
    return lax.ppermute(value, axis, pairs)


def halo(features, cotangent):
    feat = features.reshape(16, 64, CH)
    cot = cotangent.reshape(16, 64, CH)

    def side(feat_part, cot_part):
        return jnp.concatenate([feat_part, cot_part], axis=1)

    right = shifted(side(feat[:, 32:], cot[:, 48:]), "col", 1)
    left = shifted(side(feat[:, :32], cot[:, :16]), "col", -1)
    feat = jnp.concatenate([right[:, :32], feat, left[:, :32]], axis=1)
    cot = jnp.concatenate([right[:, 32:], cot, left[:, 32:]], axis=1)

    def edge(feat_part, cot_part):
        return jnp.concatenate([feat_part, cot_part.reshape(3, 128, CH)], axis=0)

    down = shifted(edge(feat[8:], cot[12:]), "row", 1)
    up = shifted(edge(feat[:8], cot[:4]), "row", -1)
    feat = jnp.concatenate([down[:8], feat, up[:8]], axis=0)
    cot = jnp.concatenate([down[8:].reshape(4, 96, CH), cot, up[8:].reshape(4, 96, CH)], axis=0)
    return feat, cot


def gather_weights(coarse_conv, coarse_proj, me):
    own = jnp.concatenate(
        [coarse_conv.reshape(9, CH, 16).swapaxes(1, 2).reshape(144, CH), coarse_proj], axis=0
    )
    one = jnp.stack([own, swap(own, "row", 8)])
    two = jnp.stack([one] + [swap(one, "row", 2 * k) for k in range(1, 4)])
    whole = jnp.stack([two, swap(two, "row", 1)])
    return absolute(whole, me)


def absolute(value, me):
    rest = value.shape[3:]
    core, x, y = (me % 2, (me // 2) % 4, me // 8)
    value = jnp.where(core == 0, value, value[::-1])
    value = jnp.where(x % 2 == 0, value, value[:, jnp.array([1, 0, 3, 2])])
    value = jnp.where(x // 2 == 0, value, value[:, jnp.array([2, 3, 0, 1])])
    value = jnp.where(y == 0, value, value[:, :, ::-1])
    return value.transpose((2, 1, 0) + tuple(range(3, value.ndim))).reshape((16,) + rest)


def reduce_all(coarse_grads, fine_grads, me):
    core, x, y = (me % 2, (me // 2) % 4, me // 8)
    pick = functools.partial(lax.dynamic_index_in_dim, axis=0, keepdims=False)
    whole = jnp.concatenate([coarse_grads, fine_grads.reshape(16, 144, CH)], axis=1)
    whole = whole.reshape(2, 4, 2, 304, CH).transpose(2, 1, 0, 3, 4)
    got = swap(pick(whole, 1 - core), "row", 1)
    part = pick(whole, core).astype(F32) + got.astype(F32)
    got = [swap(pick(part, x ^ k).astype(BF), "row", 2 * k) for k in range(1, 4)]
    part = pick(part, x) + sum(g.astype(F32) for g in got)
    got = swap(pick(part, 1 - y).astype(BF), "row", 8)
    part = (pick(part, y) + got.astype(F32)).astype(BF)
    for base in (1, 4):
        got = [swap(part, "col", base * k) for k in range(1, 4)]
        a, b, c, d = (v.astype(F32) for v in [part] + got)
        total = (a + b) + (c + d)
        part = total.astype(BF)
    coarse = total[:160]
    own = part[160:]
    one = jnp.stack([own, swap(own, "row", 8)])
    two = jnp.stack([one] + [swap(one, "row", 2 * k) for k in range(1, 4)])
    fine = jnp.stack([two, swap(two, "row", 1)])
    return coarse, absolute(fine, me).reshape(2304, CH)


def local(features, conv_first, conv_second, coarse_conv, coarse_proj, cotangent):
    rows, cols = (lax.axis_size("row"), lax.axis_size("col"))
    height, breadth = (features.shape[0] * rows, features.shape[1] * cols)
    fine_scale = 1.0 / (height * breadth * features.shape[2]) ** 0.5
    coarse_scale = 2.0 * fine_scale
    me, mine = (lax.axis_index("row"), lax.axis_index("col"))
    meta = jnp.stack([me * 16, mine * 16, jnp.int32(height), jnp.int32(breadth)]).astype(jnp.int32)
    window, cot = halo(features, cotangent)
    slabs = gather_weights(coarse_conv, coarse_proj, me)
    wg = slabs[:, :144].reshape(16, 9, 16, CH)
    proj = slabs[:, 144:].reshape(WIDE, CH)
    blended, feature_grad, coarse_grads, fine_grads = tile_compute(meta, window, cot, conv_first, conv_second, wg, proj)
    coarse, fine = reduce_all(coarse_grads, fine_grads, me)
    fine = fine_scale * fine.astype(F32)
    coarse = coarse_scale * coarse
    shape = features.shape
    return (
        blended.reshape(shape),
        feature_grad.reshape(shape),
        fine[:1152].reshape(3, 3, CH, CH),
        fine[1152:].reshape(3, 3, CH, CH),
        coarse[:144].reshape(3, 3, 16, CH).swapaxes(2, 3),
        coarse[144:],
    )


def solution(mesh):
    in_specs = (
        P("row", "col", None, None),
        P(),
        P(),
        P(None, None, None, "row"),
        P("row", None),
        P("row", "col", None, None),
    )
    out_specs = (
        P("row", "col", None, None),
        P("row", "col", None, None),
        P(),
        P(),
        P(None, None, None, "row"),
        P("row", None),
    )
    return jax.shard_map(local, mesh=mesh, in_specs=in_specs, out_specs=out_specs, check_vma=False)
```

```python
import functools

import jax
import jax.numpy as jnp
from jax import lax
from jax.experimental import pallas as pl
from jax.experimental.pallas import tpu as pltpu
from jax.sharding import PartitionSpec as P

BF = jnp.bfloat16
F32 = jnp.float32
CH = 128
WIDE = 256
MIB = 1024 * 1024
VM = pl.BlockSpec(memory_space=pltpu.VMEM)
SM = pl.BlockSpec(memory_space=pltpu.SMEM)


def call(kernel, name, outs, ins, scratch=(), limit=16, flops=0, moved=0):
    shapes = tuple(jax.ShapeDtypeStruct(shape, dtype) for shape, dtype in outs)
    return pl.pallas_call(
        kernel,
        name=name,
        out_shape=shapes,
        in_specs=[SM if v.ndim == 1 else VM for v in ins],
        out_specs=tuple(VM for _ in outs),
        scratch_shapes=[pltpu.VMEM(shape, dtype) for shape, dtype in scratch],
        compiler_params=pltpu.CompilerParams(vmem_limit_bytes=limit * MIB),
        cost_estimate=pl.CostEstimate(flops=flops, bytes_accessed=moved, transcendentals=0),
    )(*ins)


def dot_nn(a, b):
    return jnp.dot(a, b, preferred_element_type=F32)


def dot_nt(a, b):
    return lax.dot_general(a, b, (((1,), (1,)), ((), ())), preferred_element_type=F32)


def dot_tn(a, b):
    return lax.dot_general(a, b, (((0,), (0,)), ((), ())), preferred_element_type=F32)


def sigmoid(value):
    return 0.5 * jnp.tanh(0.5 * value) + 0.5


def slope_of(value):
    sigma = sigmoid(value)
    return sigma * (1.0 + value * (1.0 - sigma))


def rounded(value):
    return value.astype(BF).astype(F32)


def three(value):
    count = value.shape[0]
    left = pltpu.roll(value, 4, 0)
    right = pltpu.roll(value, count - 4, 0)
    return jnp.concatenate([left.astype(BF), value.astype(BF), right.astype(BF)], axis=1)


def taps(ref, start, rows, cols=None):
    parts = []
    for r in range(3):
        part = ref[pl.ds(start + r, rows)] if cols is None else ref[pl.ds(start + r, rows), cols[0] : cols[1], :]
        parts.append(part.reshape(part.shape[0] * part.shape[1], part.shape[2]))
    return jnp.concatenate(parts, axis=1)


def column_mask(first, width, limit):
    place = first + lax.broadcasted_iota(jnp.int32, (width, CH), 0) // 4
    return jnp.where((place >= 0) & (place < limit), 1.0, 0.0).astype(F32)


def row_ok(place, limit):
    return jnp.where((place >= 0) & (place < limit), 1.0, 0.0).astype(F32)


def masked(value, mask, first, limit):
    rows = []
    for k in range(value.shape[0]):
        rows.append((value[k] * (mask * row_ok(first + k, limit)))[None])
    return jnp.concatenate(rows, axis=0)


def pooled_pair(row):
    count = row.shape[0]
    low = (row + pltpu.roll(row, count - 4, 0)).reshape(count // 16, 2, 8, CH)
    high = (row + pltpu.roll(row, 4, 0)).reshape(count // 16, 2, 8, CH)
    first = lax.broadcasted_iota(jnp.int32, (count // 16, 8, CH), 1) < 4
    return jnp.where(first, low[:, 0], high[:, 1]).reshape(count // 2, CH)


def repeated(row):
    count = row.shape[0]
    first = lax.broadcasted_iota(jnp.int32, (count, CH), 0) % 8 < 4
    even = jnp.where(first, row, pltpu.roll(row, 4, 0)).reshape(count // 8, 1, 8, CH)
    odd = jnp.where(first, pltpu.roll(row, count - 4, 0), row).reshape(count // 8, 1, 8, CH)
    return jnp.concatenate([even, odd], axis=1).reshape(count * 2, CH)


def pack_columns_kernel(feat, cot, conv, proj, right, left, weights):
    right[:, 0:32, :] = feat[:, 32:64, :]
    right[:, 32:48, :] = cot[:, 48:64, :]
    left[:, 0:32, :] = feat[:, 0:32, :]
    left[:, 32:48, :] = cot[:, 0:16, :]
    weights[0:144, :] = conv[...].reshape(144, CH)
    weights[144:160, :] = proj[...]


def pack_rows_kernel(feat, cot, before, after, own, other, down, up, weights):
    for out, first, second in ((down, 8, 12), (up, 0, 0)):
        out[0:8, 0:32, :] = before[first : first + 8, 0:32, :]
        out[0:8, 32:96, :] = feat[first : first + 8]
        out[0:8, 96:128, :] = after[first : first + 8, 0:32, :]
        out[8:12, 0:16, :] = before[second : second + 4, 32:48, :]
        out[8:12, 16:80, :] = cot[second : second + 4]
        out[8:12, 80:96, :] = after[second : second + 4, 32:48, :]
        out[8:12, 96:128, :] = jnp.zeros((4, 32, CH), BF)
    weights[0] = own[...]
    weights[1] = other[...]


def stack_kernel(*refs):
    out = refs[-1]
    for k, ref in enumerate(refs[:-1]):
        out[k] = ref[...]


def forward_kernel(
    meta, feat, before, after, above, below, w1, w2, pool3, slope1, slope2, act, feat3o, act3o, feat3, act3, pre1, pre2, act2
):
    top, left, height, breadth = (meta[0], meta[1], meta[2], meta[3])
    mask = column_mask(left - 8, 128, breadth)
    coarse_mask = column_mask(left // 2 - 4, 64, breadth // 2)

    @pl.loop(0, 4)
    def _(b):
        rows = pl.ds(4 * b, 4)
        middle = jnp.concatenate([before[rows, 0:32, :], feat[rows], after[rows, 0:32, :]], axis=1)
        feat3[pl.ds(4 * b + 8, 4)] = three(middle.reshape(512, CH).astype(F32)).reshape(4, 128, 3 * CH)

    @pl.loop(0, 2)
    def _(b):
        block = above[pl.ds(4 * b, 4)].reshape(512, CH).astype(F32)
        feat3[pl.ds(4 * b, 4)] = three(block).reshape(4, 128, 3 * CH)
        block = below[pl.ds(4 * b, 4)].reshape(512, CH).astype(F32)
        feat3[pl.ds(4 * b + 24, 4)] = three(block).reshape(4, 128, 3 * CH)

    first_w = w1[...]

    @pl.loop(0, 6)
    def _(b):
        pre = dot_nn(taps(feat3, 5 * b, 5), first_w)
        pre1[pl.ds(5 * b, 5)] = pre.reshape(5, 128, CH)
        value = rounded(pre * sigmoid(pre)).reshape(5, 128, CH)
        value = masked(value, mask, top - 7 + 5 * b, height)
        act3[pl.ds(5 * b, 5)] = three(value.reshape(640, CH)).reshape(5, 128, 3 * CH)

    second_w = w2[...]

    @pl.loop(0, 7)
    def _(b):
        pre = dot_nn(taps(act3, 4 * b, 4), second_w)
        pre2[pl.ds(4 * b, 4)] = pre.reshape(4, 128, CH)
        value = (pre * sigmoid(pre)).astype(BF)
        act2[pl.ds(4 * b, 4)] = value.reshape(4, 128, CH)
        value = value.astype(F32).reshape(4, 128, CH)
        coarse = []
        for k in range(2):
            small = rounded(0.25 * pooled_pair(value[2 * k] + value[2 * k + 1]))
            coarse.append(small * (coarse_mask * row_ok(top // 2 - 3 + 2 * b + k, height // 2)))
        coarse = jnp.concatenate(coarse, axis=0)
        pool3[pl.ds(2 * b, 2)] = three(coarse).reshape(2, 64, 3 * CH)

    @pl.loop(0, 18)
    def _(k):
        slope1[k] = slope_of(pre1[k + 6, 16:112, :])
        feat3o[k] = feat3[k + 7, 32:96, :]
        act3o[k] = act3[k + 6, 32:96, :]

    @pl.loop(0, 20)
    def _(k):
        slope2[k] = slope_of(pre2[k + 4, 16:112, :])

    @pl.loop(0, 16)
    def _(k):
        act[k] = act2[k + 6, 32:96, :]


def fine_forward(meta, feat, before, after, above, below, w1, w2):
    return call(
        forward_kernel,
        "fine_forward",
        (
            ((14, 64, 384), BF),
            ((18, 96, CH), F32),
            ((20, 96, CH), F32),
            ((16, 64, CH), BF),
            ((18, 64, 384), BF),
            ((18, 64, 384), BF),
        ),
        (meta, feat, before, after, above, below, w1, w2),
        (
            ((32, 128, 384), BF),
            ((30, 128, 384), BF),
            ((30, 128, CH), F32),
            ((28, 128, CH), F32),
            ((28, 128, CH), BF),
        ),
        limit=24,
        flops=4 * 10**9,
    )


def coarse_kernel(
    meta, pool3, cot, before, after, above, below, near0, near1, near2, near3, far, act,
    blended, keep, send, pooled_grad, wcat, projs, wide3, projin,
):
    top, left, height, breadth, me = (meta[0], meta[1], meta[2], meta[3], meta[4])
    core = me % 2
    near = (near0, near1, near2, near3)
    for rel in range(16):
        c, x, y = (rel % 2, (rel // 2) % 4, rel // 8)
        place = pl.ds(pl.multiple_of((me ^ rel) * 16, 16), 16)
        source = far.at[x, y] if c else near[x].at[y]
        for t in range(9):
            wcat[place, t * CH : (t + 1) * CH] = source[16 * t : 16 * t + 16, :]
        projs[place, :] = source[144:160, :]
    proj_w = projs[...]

    def pair_sum(a, b):
        return pooled_pair(a.astype(F32) + b.astype(F32))

    for k in range(2):
        projin[k] = pair_sum(above[8 + 2 * k, 0:96, :], above[9 + 2 * k, 0:96, :])
        projin[k + 10] = pair_sum(below[8 + 2 * k, 0:96, :], below[9 + 2 * k, 0:96, :])

    @pl.loop(0, 8)
    def _(k):
        rows = pl.ds(2 * k, 2)
        pair = jnp.concatenate([before[rows, 32:48, :], cot[rows], after[rows, 32:48, :]], axis=1)
        projin[k + 2] = pair_sum(pair[0], pair[1])

    proj_in = projin[...].reshape(576, CH)
    proj_in_bf = proj_in.astype(BF)
    pre = dot_nt(taps(pool3, 0, 12), wcat[...]).reshape(12, 64, WIDE)[:, 8:56].reshape(576, WIDE)
    sigma = sigmoid(pre)
    coarse_act = pre * sigma
    act_grad = dot_nt(proj_in_bf, proj_w)
    grad = rounded(act_grad * (sigma * (1.0 + pre * (1.0 - sigma)))).reshape(12, 48, WIDE)
    mask = column_mask(left // 2 - 2, 48, breadth // 2)
    mask = jnp.concatenate([mask, mask], axis=1)
    grad = masked(grad, mask, top // 2 - 2, height // 2)
    wide3[...] = three(grad.reshape(576, WIDE)).reshape(12, 48, 3 * WIDE)
    own_grad = grad[2:10, 8:40].reshape(256, WIDE).astype(BF)
    own_act = coarse_act.reshape(12, 48, WIDE)[2:10, 8:40].reshape(256, WIDE).astype(BF)
    own_in = proj_in.reshape(12, 48, CH)[2:10, 8:40].reshape(256, CH).astype(BF)

    def emit(first, last, value):
        value = value.reshape(8, 2, 16, CH)
        even, odd = (value[:, 0], value[:, 1])
        keep[:, first:last, :] = jnp.where(core == 0, even, odd).astype(BF)
        send[:, first:last, :] = jnp.where(core == 0, odd, even).astype(BF)

    for r in range(3):
        source = pool3[2 + r : 10 + r, 16:48, :].reshape(256, 3 * CH)
        part = dot_tn(own_grad, source)
        for s in range(3):
            t = 3 * r + s
            emit(16 * t, 16 * t + 16, part[:, s * CH : (s + 1) * CH])
    emit(144, 160, dot_tn(own_act, own_in))
    total = None
    for r in range(3):
        lhs = wide3[r : r + 10].reshape(480, 3 * WIDE)
        first = 3 * (2 - r)
        rhs = jnp.concatenate([wcat[:, (first + 2 - s) * CH : (first + 3 - s) * CH] for s in range(3)], axis=0)
        part = dot_nn(lhs, rhs)
        total = part if total is None else total + part
    pooled_grad[...] = total.reshape(10, 48, CH)
    projected = dot_nn(own_act, proj_w).reshape(8, 32, CH)
    for k in range(8):
        row = repeated(projected[k])
        for e in range(2):
            blended[2 * k + e] = (act[2 * k + e].astype(F32) + row).astype(BF)


def coarse_step(meta, pool3, cot, before, after, above, below, near, far, act):
    return call(
        coarse_kernel,
        "coarse_step",
        (((16, 64, CH), BF), ((8, 160, CH), BF), ((8, 160, CH), BF), ((10, 48, CH), F32)),
        (meta, pool3, cot, before, after, above, below) + tuple(near) + (far, act),
        (
            ((WIDE, 9 * CH), BF),
            ((WIDE, CH), BF),
            ((12, 48, 3 * WIDE), BF),
            ((12, 48, CH), F32),
        ),
        limit=20,
        flops=2 * 10**9,
    )


def flipped(weight):
    return jnp.concatenate([weight[8 - t] for t in range(9)], axis=1)


def backward_kernel(
    meta, pooled_grad, cot, before, after, above, below, slope1, slope2, feat3, act3, w2,
    keep, send, first3, second3, grads,
):
    top, left, height, breadth = (meta[0], meta[1], meta[2], meta[3])
    mask = column_mask(left - 4, 96, breadth)

    def second_rows(k, pair):
        wide = 0.25 * repeated(pooled_grad[k])
        rows = []
        for e in range(2):
            value = rounded((pair[e].astype(F32) + wide) * slope2[2 * k + e])
            rows.append(value * (mask * row_ok(top - 2 + 2 * k + e, height)))
        second3[pl.ds(2 * k, 2)] = three(jnp.concatenate(rows, axis=0)).reshape(2, 96, 3 * CH)

    second_rows(0, above[10:12, 0:96, :])
    second_rows(9, below[8:10, 0:96, :])

    @pl.loop(0, 8)
    def _(k):
        rows = pl.ds(2 * k, 2)
        second_rows(k + 1, jnp.concatenate([before[rows, 32:48, :], cot[rows], after[rows, 32:48, :]], axis=1))

    def weight_grad(source, grad):
        return [dot_tn(source[r : r + 16].reshape(1024, 3 * CH), grad) for r in range(3)]

    def emit(base, parts):
        for r in range(3):
            grads[base + 384 * r : base + 384 * (r + 1), :] = parts[r].astype(BF)

    second_own = second3[2:18, 16:80, CH : 2 * CH].reshape(1024, CH)
    emit(1152, weight_grad(act3, second_own))
    back_w = flipped(w2)

    @pl.loop(0, 3)
    def _(b):
        value = dot_nt(taps(second3, 6 * b, 6), back_w).reshape(6, 96, CH)
        value = rounded(value * slope1[pl.ds(6 * b, 6)])
        value = masked(value, mask, top - 1 + 6 * b, height)
        out = three(value.reshape(576, CH)).reshape(6, 96, 3 * CH)
        first3[pl.ds(6 * b, 6)] = out[:, 16:80, :]

    first_own = first3[1:17, :, CH : 2 * CH].reshape(1024, CH)
    emit(0, weight_grad(feat3, first_own))
    core = meta[4] % 2
    for k in range(8):
        keep[k] = grads[pl.ds(pl.multiple_of((2 * k + core) * 144, 16), 144), :]
        send[k] = grads[pl.ds(pl.multiple_of((2 * k + 1 - core) * 144, 16), 144), :]


def fine_backward(meta, pooled_grad, cot, before, after, above, below, slope1, slope2, feat3, act3, w2):
    return call(
        backward_kernel,
        "fine_backward",
        (((8, 144, CH), BF), ((8, 144, CH), BF), ((18, 64, 384), BF)),
        (meta, pooled_grad, cot, before, after, above, below, slope1, slope2, feat3, act3, w2),
        (((20, 96, 384), BF), ((2304, CH), BF)),
        limit=20,
        flops=2 * 10**9,
    )


def feature_kernel(first3, w1, out):
    back_w = flipped(w1)

    @pl.loop(0, 2)
    def _(b):
        out[pl.ds(8 * b, 8)] = dot_nt(taps(first3, 8 * b, 8), back_w).astype(BF).reshape(8, 64, CH)


def feature_step(first3, w1):
    return call(feature_kernel, "feature_step", (((16, 64, CH), BF),), (first3, w1), limit=12, flops=10**9)[0]


def scatter_core_kernel(meta, keep_c, keep_f, got_c, got_f, own, *sends):
    block = (meta[4] // 2) % 8
    for k in range(8):
        at = block ^ k
        coarse = keep_c[at].astype(F32) + got_c[at].astype(F32)
        fine = keep_f[at].astype(F32) + got_f[at].astype(F32)
        out = own if k == 0 else sends[k - 1]
        out[0:160, :] = coarse.astype(out.dtype)
        out[160:304, :] = fine.astype(out.dtype)


def scatter_row_kernel(meta, own, *refs):
    got, (mine, *sends), (total,) = (refs[:7], refs[7:11], refs[11:])
    value = own[...]
    for ref in got:
        value = value + ref[...].astype(F32)
    for k in range(3):
        total[k] = value[80 * k : 80 * k + 80]
    total[3, 0:64, :] = value[240:304]
    total[3, 64:80, :] = jnp.zeros((16, CH), F32)
    part = meta[5] % 4
    mine[...] = total[part]
    for k in range(1, 4):
        sends[k - 1][...] = total[part ^ k].astype(BF)


def sum_kernel(a, b, c, d, out):
    out[...] = ((a[...].astype(F32) + b[...].astype(F32)) + (c[...].astype(F32) + d[...].astype(F32))).astype(BF)


def column_kernel(scale, meta, a, b, c, d, conv, proj, fine, parts):
    for k, ref in enumerate((a, b, c, d)):
        parts[(meta[5] % 4) ^ k] = ref[...]
    for k in range(9):
        conv[k] = parts[k // 5, 16 * (k % 5) : 16 * (k % 5) + 16, :].astype(F32) * scale
    proj[...] = parts[1, 64:80, :].astype(F32) * scale
    fine[0:80, :] = parts[2]
    fine[80:144, :] = parts[3, 0:64, :]


def finish_kernel(scale, meta, mine, other, first, second):
    block, core = ((meta[4] // 2) % 8, meta[4] % 2)
    for at in range(8):
        out = first if at < 4 else second
        a = mine[block ^ at].astype(F32) * scale
        b = other[block ^ at].astype(F32) * scale
        out[2 * (at % 4)] = jnp.where(core == 0, a, b)
        out[2 * (at % 4) + 1] = jnp.where(core == 0, b, a)


def swap(value, axis, mask):
    count = lax.axis_size(axis)
    return lax.ppermute(value, axis, [(i, i ^ mask) for i in range(count)])


def shifted(value, axis, step):
    count = lax.axis_size(axis)
    pairs = [(i, i + step) for i in range(count) if 0 <= i + step < count]
    return lax.ppermute(value, axis, pairs)


def local(features, conv_first, conv_second, coarse_conv, coarse_proj, cotangent):
    rows, cols = (lax.axis_size("row"), lax.axis_size("col"))
    height, breadth = (features.shape[0] * rows, features.shape[1] * cols)
    fine_scale = 1.0 / (height * breadth * features.shape[2]) ** 0.5
    coarse_scale = 2.0 * fine_scale
    me, mine = (lax.axis_index("row"), lax.axis_index("col"))
    fixed = [jnp.int32(height), jnp.int32(breadth)]
    meta = jnp.stack([me * 16, mine * 16] + fixed + [me, mine]).astype(jnp.int32)
    feat = features.reshape(16, 64, CH)
    cot = cotangent.reshape(16, 64, CH)
    conv = coarse_conv.reshape(9, CH, 16).swapaxes(1, 2)
    slab = ((160, CH), BF)

    right, left, own = call(
        pack_columns_kernel, "pack_columns", (((16, 48, CH), BF), ((16, 48, CH), BF), slab), (feat, cot, conv, coarse_proj)
    )
    before = shifted(right, "col", 1)
    after = shifted(left, "col", -1)
    other = swap(own, "row", 8)
    down, up, near0 = call(
        pack_rows_kernel,
        "pack_rows",
        (((12, 128, CH), BF), ((12, 128, CH), BF), ((2, 160, CH), BF)),
        (feat, cot, before, after, own, other),
    )
    above = shifted(down, "row", 1)
    below = shifted(up, "row", -1)
    near = [near0] + [swap(near0, "row", 2 * k) for k in range(1, 4)]
    far = swap(call(stack_kernel, "stack_weights", (((4, 2, 160, CH), BF),), near)[0], "row", 1)

    halo = (before, after, above, below)
    w1, w2 = (conv_first.reshape(1152, CH), conv_second.reshape(1152, CH))
    pool3, slope1, slope2, act, feat3, act3 = fine_forward(meta, feat, *halo, w1, w2)
    blended, keep_c, send_c, pooled_grad = coarse_step(meta, pool3, cot, *halo, near, far, act)
    got_c = swap(send_c, "row", 1)
    keep_f, send_f, first3 = fine_backward(
        meta, pooled_grad, cot, *halo, slope1, slope2, feat3, act3, conv_second.reshape(9, CH, CH)
    )
    got_f = swap(send_f, "row", 1)
    feature_grad = feature_step(first3, conv_first.reshape(9, CH, CH))

    whole = (304, CH)
    total, *sends = call(
        scatter_core_kernel, "scatter_core", ((whole, F32),) + ((whole, BF),) * 7, (meta, keep_c, keep_f, got_c, got_f)
    )
    got = [swap(v, "row", 2 * (k + 1)) for k, v in enumerate(sends)]
    quarter = (80, CH)
    part, *sends = call(
        scatter_row_kernel,
        "scatter_row",
        ((quarter, F32),) + ((quarter, BF),) * 3,
        (meta, total, *got),
        (((4, 80, CH), F32),),
    )
    got = [swap(v, "col", k + 1) for k, v in enumerate(sends)]
    part = call(sum_kernel, "sum_four", ((quarter, BF),), (part, *got))[0]
    got = [swap(part, "col", 4 * k) for k in range(1, 4)]
    part = call(sum_kernel, "sum_four", ((quarter, BF),), (part, *got))[0]
    got = [swap(part, "col", k) for k in range(1, 4)]
    conv_grad, proj_grad, fine = call(
        functools.partial(column_kernel, coarse_scale),
        "gather_column",
        (((9, 16, CH), F32), ((16, CH), F32), ((144, CH), BF)),
        (meta, part, *got),
        (((4, 80, CH), BF),),
    )
    got = [swap(fine, "row", 2 * k) for k in range(1, 8)]
    fine = call(stack_kernel, "stack_grads", (((8, 144, CH), BF),), (fine, *got))[0]
    first, second = call(
        functools.partial(finish_kernel, fine_scale),
        "finish",
        (((8, 144, CH), F32), ((8, 144, CH), F32)),
        (meta, fine, swap(fine, "row", 1)),
    )
    shape = features.shape
    return (
        blended.reshape(shape),
        feature_grad.reshape(shape),
        first.reshape(3, 3, CH, CH),
        second.reshape(3, 3, CH, CH),
        conv_grad.reshape(3, 3, 16, CH).swapaxes(2, 3),
        proj_grad,
    )


def solution(mesh):
    in_specs = (
        P("row", "col", None, None),
        P(),
        P(),
        P(None, None, None, "row"),
        P("row", None),
        P("row", "col", None, None),
    )
    out_specs = (
        P("row", "col", None, None),
        P("row", "col", None, None),
        P(),
        P(),
        P(None, None, None, "row"),
        P("row", None),
    )
    return jax.shard_map(local, mesh=mesh, in_specs=in_specs, out_specs=out_specs, check_vma=False)
```

```python
import functools

import jax
import jax.numpy as jnp
from jax import lax
from jax.experimental import pallas as pl
from jax.experimental.pallas import tpu as pltpu
from jax.sharding import PartitionSpec as P

BF = jnp.bfloat16
F32 = jnp.float32
CH = 128
WIDE = 256
MIB = 1024 * 1024
VM = pl.BlockSpec(memory_space=pltpu.VMEM)
SM = pl.BlockSpec(memory_space=pltpu.SMEM)


def call(kernel, name, outs, ins, scratch=(), limit=16, flops=0, moved=0, far=False):
    shapes = tuple(jax.ShapeDtypeStruct(shape, dtype) for shape, dtype in outs)
    return pl.pallas_call(
        kernel,
        name=name,
        out_shape=shapes,
        in_specs=[pl.BlockSpec(memory_space=pl.ANY) if far else SM if v.ndim == 1 else VM for v in ins],
        out_specs=tuple(VM for _ in outs),
        scratch_shapes=[v if len(v) != 2 else pltpu.VMEM(*v) for v in scratch] if not far else list(scratch),
        compiler_params=pltpu.CompilerParams(vmem_limit_bytes=limit * MIB),
        cost_estimate=pl.CostEstimate(flops=flops, bytes_accessed=moved, transcendentals=0),
    )(*ins)


def dot_nn(a, b):
    return jnp.dot(a, b, preferred_element_type=F32)


def dot_nt(a, b):
    return lax.dot_general(a, b, (((1,), (1,)), ((), ())), preferred_element_type=F32)


def dot_tn(a, b):
    return lax.dot_general(a, b, (((0,), (0,)), ((), ())), preferred_element_type=F32)


def sigmoid(value):
    return 0.5 * jnp.tanh(0.5 * value) + 0.5


def slope_of(value):
    sigma = sigmoid(value)
    return sigma * (1.0 + value * (1.0 - sigma))


def rounded(value):
    return value.astype(BF).astype(F32)


def three(value):
    count = value.shape[0]
    left = pltpu.roll(value, 4, 0)
    right = pltpu.roll(value, count - 4, 0)
    return jnp.concatenate([left.astype(BF), value.astype(BF), right.astype(BF)], axis=1)


def taps(ref, start, rows, cols=None):
    parts = []
    for r in range(3):
        part = ref[pl.ds(start + r, rows)] if cols is None else ref[pl.ds(start + r, rows), cols[0] : cols[1], :]
        parts.append(part.reshape(part.shape[0] * part.shape[1], part.shape[2]))
    return jnp.concatenate(parts, axis=1)


def column_mask(first, width, limit):
    place = first + lax.broadcasted_iota(jnp.int32, (width, CH), 0) // 4
    return jnp.where((place >= 0) & (place < limit), 1.0, 0.0).astype(F32)


def row_ok(place, limit):
    return jnp.where((place >= 0) & (place < limit), 1.0, 0.0).astype(F32)


def masked(value, mask, first, limit):
    rows = []
    for k in range(value.shape[0]):
        rows.append((value[k] * (mask * row_ok(first + k, limit)))[None])
    return jnp.concatenate(rows, axis=0)


def pooled_pair(row):
    count = row.shape[0]
    low = (row + pltpu.roll(row, count - 4, 0)).reshape(count // 16, 2, 8, CH)
    high = (row + pltpu.roll(row, 4, 0)).reshape(count // 16, 2, 8, CH)
    first = lax.broadcasted_iota(jnp.int32, (count // 16, 8, CH), 1) < 4
    return jnp.where(first, low[:, 0], high[:, 1]).reshape(count // 2, CH)


def repeated(row):
    count = row.shape[0]
    first = lax.broadcasted_iota(jnp.int32, (count, CH), 0) % 8 < 4
    even = jnp.where(first, row, pltpu.roll(row, 4, 0)).reshape(count // 8, 1, 8, CH)
    odd = jnp.where(first, pltpu.roll(row, count - 4, 0), row).reshape(count // 8, 1, 8, CH)
    return jnp.concatenate([even, odd], axis=1).reshape(count * 2, CH)


def pack_columns_kernel(feat, cot, conv, proj, right, left, weights, done):
    pairs = [
        (feat.at[:, 32:64, :], right.at[:, 0:32, :]),
        (cot.at[:, 48:64, :], right.at[:, 32:48, :]),
        (feat.at[:, 0:32, :], left.at[:, 0:32, :]),
        (cot.at[:, 0:16, :], left.at[:, 32:48, :]),
        (proj, weights.at[144:160, :]),
    ] + [(conv.at[t], weights.at[16 * t : 16 * t + 16, :]) for t in range(9)]
    copies = [pltpu.make_async_copy(a, b, done.at[k]) for k, (a, b) in enumerate(pairs)]
    for copy in copies:
        copy.start()
    for copy in copies:
        copy.wait()


def pack_rows_kernel(feat, cot, before, after, down, up):
    for out, first, second in ((down, 8, 12), (up, 0, 0)):
        out[0:8, 0:32, :] = before[first : first + 8, 0:32, :]
        out[0:8, 32:96, :] = feat[first : first + 8]
        out[0:8, 96:128, :] = after[first : first + 8, 0:32, :]
        out[8:12, 0:16, :] = before[second : second + 4, 32:48, :]
        out[8:12, 16:80, :] = cot[second : second + 4]
        out[8:12, 80:96, :] = after[second : second + 4, 32:48, :]
        out[8:12, 96:128, :] = jnp.zeros((4, 32, CH), BF)


def stack_kernel(*refs):
    out = refs[-1]
    for k, ref in enumerate(refs[:-1]):
        out[k] = ref[...]


def first_kernel(meta, feat, before, after, above, below, w1, act3, slope1, feat3o, feat3, pre1):
    top, left, height, breadth = (meta[0], meta[1], meta[2], meta[3])
    mask = column_mask(left - 8, 128, breadth)

    @pl.loop(0, 4)
    def _(b):
        rows = pl.ds(4 * b, 4)
        middle = jnp.concatenate([before[rows, 0:32, :], feat[rows], after[rows, 0:32, :]], axis=1)
        feat3[pl.ds(4 * b + 8, 4)] = three(middle.reshape(512, CH).astype(F32)).reshape(4, 128, 3 * CH)

    @pl.loop(0, 2)
    def _(b):
        block = above[pl.ds(4 * b, 4)].reshape(512, CH).astype(F32)
        feat3[pl.ds(4 * b, 4)] = three(block).reshape(4, 128, 3 * CH)
        block = below[pl.ds(4 * b, 4)].reshape(512, CH).astype(F32)
        feat3[pl.ds(4 * b + 24, 4)] = three(block).reshape(4, 128, 3 * CH)

    first_w = w1[...]

    @pl.loop(0, 6)
    def _(b):
        pre = dot_nn(taps(feat3, 5 * b, 5), first_w)
        pre1[pl.ds(5 * b, 5)] = pre.reshape(5, 128, CH)
        value = rounded(pre * sigmoid(pre)).reshape(5, 128, CH)
        value = masked(value, mask, top - 7 + 5 * b, height)
        act3[pl.ds(5 * b, 5)] = three(value.reshape(640, CH)).reshape(5, 128, 3 * CH)

    @pl.loop(0, 18)
    def _(k):
        slope1[k] = slope_of(pre1[k + 6, 16:112, :])
        feat3o[k] = feat3[k + 7, 32:96, :]


def second_kernel(meta, act3, w2, pool3, slope2, act, act3o, pre2, act2):
    top, left, height, breadth = (meta[0], meta[1], meta[2], meta[3])
    coarse_mask = column_mask(left // 2 - 4, 64, breadth // 2)
    second_w = w2[...]

    @pl.loop(0, 7)
    def _(b):
        pre = dot_nn(taps(act3, 4 * b, 4), second_w)
        pre2[pl.ds(4 * b, 4)] = pre.reshape(4, 128, CH)
        value = (pre * sigmoid(pre)).astype(BF)
        act2[pl.ds(4 * b, 4)] = value.reshape(4, 128, CH)
        value = value.astype(F32).reshape(4, 128, CH)
        coarse = []
        for k in range(2):
            small = rounded(0.25 * pooled_pair(value[2 * k] + value[2 * k + 1]))
            coarse.append(small * (coarse_mask * row_ok(top // 2 - 3 + 2 * b + k, height // 2)))
        coarse = jnp.concatenate(coarse, axis=0)
        pool3[pl.ds(2 * b, 2)] = three(coarse).reshape(2, 64, 3 * CH)

    @pl.loop(0, 18)
    def _(k):
        act3o[k] = act3[k + 6, 32:96, :]

    @pl.loop(0, 20)
    def _(k):
        slope2[k] = slope_of(pre2[k + 4, 16:112, :])

    @pl.loop(0, 16)
    def _(k):
        act[k] = act2[k + 6, 32:96, :]


def first_step(meta, feat, before, after, above, below, w1):
    return call(
        first_kernel,
        "first_conv",
        (((30, 128, 384), BF), ((18, 96, CH), F32), ((18, 64, 384), BF)),
        (meta, feat, before, after, above, below, w1),
        (((32, 128, 384), BF), ((30, 128, CH), F32)),
        limit=20,
        flops=4 * 10**9,
    )


def second_step(meta, act3, w2):
    return call(
        second_kernel,
        "second_conv",
        (((14, 64, 384), BF), ((20, 96, CH), F32), ((16, 64, CH), BF), ((18, 64, 384), BF)),
        (meta, act3, w2),
        (((28, 128, CH), F32), ((28, 128, CH), BF)),
        limit=20,
        flops=4 * 10**9,
    )


def coarse_kernel(
    meta, pool3, cot, before, after, above, below, near0, near1, near2, near3, far, act,
    blended, keep, send, pooled_grad, wcat, projs, wide3, projin,
):
    top, left, height, breadth, me = (meta[0], meta[1], meta[2], meta[3], meta[4])
    core = me % 2
    near = (near0, near1, near2, near3)
    for rel in range(16):
        c, x, y = (rel % 2, (rel // 2) % 4, rel // 8)
        place = pl.ds(pl.multiple_of((me ^ rel) * 16, 16), 16)
        source = far.at[x, y] if c else near[x].at[y]
        for t in range(9):
            wcat[place, t * CH : (t + 1) * CH] = source[16 * t : 16 * t + 16, :]
        projs[place, :] = source[144:160, :]
    proj_w = projs[...]

    def pair_sum(a, b):
        return pooled_pair(a.astype(F32) + b.astype(F32))

    for k in range(2):
        projin[k] = pair_sum(above[8 + 2 * k, 0:96, :], above[9 + 2 * k, 0:96, :])
        projin[k + 10] = pair_sum(below[8 + 2 * k, 0:96, :], below[9 + 2 * k, 0:96, :])

    @pl.loop(0, 8)
    def _(k):
        rows = pl.ds(2 * k, 2)
        pair = jnp.concatenate([before[rows, 32:48, :], cot[rows], after[rows, 32:48, :]], axis=1)
        projin[k + 2] = pair_sum(pair[0], pair[1])

    proj_in = projin[...].reshape(576, CH)
    proj_in_bf = proj_in.astype(BF)
    pre = dot_nt(taps(pool3, 0, 12), wcat[...]).reshape(12, 64, WIDE)[:, 8:56].reshape(576, WIDE)
    sigma = sigmoid(pre)
    coarse_act = pre * sigma
    act_grad = dot_nt(proj_in_bf, proj_w)
    grad = rounded(act_grad * (sigma * (1.0 + pre * (1.0 - sigma)))).reshape(12, 48, WIDE)
    mask = column_mask(left // 2 - 2, 48, breadth // 2)
    mask = jnp.concatenate([mask, mask], axis=1)
    grad = masked(grad, mask, top // 2 - 2, height // 2)
    wide3[...] = three(grad.reshape(576, WIDE)).reshape(12, 48, 3 * WIDE)
    own_grad = grad[2:10, 8:40].reshape(256, WIDE).astype(BF)
    own_act = coarse_act.reshape(12, 48, WIDE)[2:10, 8:40].reshape(256, WIDE).astype(BF)
    own_in = proj_in.reshape(12, 48, CH)[2:10, 8:40].reshape(256, CH).astype(BF)

    def emit(first, last, value):
        value = value.reshape(8, 2, 16, CH)
        even, odd = (value[:, 0], value[:, 1])
        keep[:, first:last, :] = jnp.where(core == 0, even, odd).astype(BF)
        send[:, first:last, :] = jnp.where(core == 0, odd, even).astype(BF)

    for r in range(3):
        source = pool3[2 + r : 10 + r, 16:48, :].reshape(256, 3 * CH)
        part = dot_tn(own_grad, source)
        for s in range(3):
            t = 3 * r + s
            emit(16 * t, 16 * t + 16, part[:, s * CH : (s + 1) * CH])
    emit(144, 160, dot_tn(own_act, own_in))
    total = None
    for r in range(3):
        lhs = wide3[r : r + 10].reshape(480, 3 * WIDE)
        first = 3 * (2 - r)
        rhs = jnp.concatenate([wcat[:, (first + 2 - s) * CH : (first + 3 - s) * CH] for s in range(3)], axis=0)
        part = dot_nn(lhs, rhs)
        total = part if total is None else total + part
    pooled_grad[...] = total.reshape(10, 48, CH)
    projected = dot_nn(own_act, proj_w).reshape(8, 32, CH)
    for k in range(8):
        row = repeated(projected[k])
        for e in range(2):
            blended[2 * k + e] = (act[2 * k + e].astype(F32) + row).astype(BF)


def coarse_step(meta, pool3, cot, before, after, above, below, near, far, act):
    return call(
        coarse_kernel,
        "coarse_step",
        (((16, 64, CH), BF), ((8, 160, CH), BF), ((8, 160, CH), BF), ((10, 48, CH), F32)),
        (meta, pool3, cot, before, after, above, below) + tuple(near) + (far, act),
        (
            ((WIDE, 9 * CH), BF),
            ((WIDE, CH), BF),
            ((12, 48, 3 * WIDE), BF),
            ((12, 48, CH), F32),
        ),
        limit=20,
        flops=2 * 10**9,
    )


def flipped(weight):
    return jnp.concatenate([weight[8 - t] for t in range(9)], axis=1)


def backward_kernel(
    meta, pooled_grad, cot, before, after, above, below, slope1, slope2, feat3, act3, w2,
    keep, send, first3, second3, grads,
):
    top, left, height, breadth = (meta[0], meta[1], meta[2], meta[3])
    mask = column_mask(left - 4, 96, breadth)

    def second_rows(k, pair):
        wide = 0.25 * repeated(pooled_grad[k])
        rows = []
        for e in range(2):
            value = rounded((pair[e].astype(F32) + wide) * slope2[2 * k + e])
            rows.append(value * (mask * row_ok(top - 2 + 2 * k + e, height)))
        second3[pl.ds(2 * k, 2)] = three(jnp.concatenate(rows, axis=0)).reshape(2, 96, 3 * CH)

    second_rows(0, above[10:12, 0:96, :])
    second_rows(9, below[8:10, 0:96, :])

    @pl.loop(0, 8)
    def _(k):
        rows = pl.ds(2 * k, 2)
        second_rows(k + 1, jnp.concatenate([before[rows, 32:48, :], cot[rows], after[rows, 32:48, :]], axis=1))

    def weight_grad(source, grad):
        return [dot_tn(source[r : r + 16].reshape(1024, 3 * CH), grad) for r in range(3)]

    def emit(base, parts):
        for r in range(3):
            grads[base + 384 * r : base + 384 * (r + 1), :] = parts[r].astype(BF)

    second_own = second3[2:18, 16:80, CH : 2 * CH].reshape(1024, CH)
    emit(1152, weight_grad(act3, second_own))
    back_w = flipped(w2)

    @pl.loop(0, 3)
    def _(b):
        value = dot_nt(taps(second3, 6 * b, 6), back_w).reshape(6, 96, CH)
        value = rounded(value * slope1[pl.ds(6 * b, 6)])
        value = masked(value, mask, top - 1 + 6 * b, height)
        out = three(value.reshape(576, CH)).reshape(6, 96, 3 * CH)
        first3[pl.ds(6 * b, 6)] = out[:, 16:80, :]

    first_own = first3[1:17, :, CH : 2 * CH].reshape(1024, CH)
    emit(0, weight_grad(feat3, first_own))
    core = meta[4] % 2
    for k in range(8):
        keep[k] = grads[pl.ds(pl.multiple_of((2 * k + core) * 144, 16), 144), :]
        send[k] = grads[pl.ds(pl.multiple_of((2 * k + 1 - core) * 144, 16), 144), :]


def fine_backward(meta, pooled_grad, cot, before, after, above, below, slope1, slope2, feat3, act3, w2):
    return call(
        backward_kernel,
        "fine_backward",
        (((8, 144, CH), BF), ((8, 144, CH), BF), ((18, 64, 384), BF)),
        (meta, pooled_grad, cot, before, after, above, below, slope1, slope2, feat3, act3, w2),
        (((20, 96, 384), BF), ((2304, CH), BF)),
        limit=20,
        flops=2 * 10**9,
    )


def feature_kernel(first3, w1, out):
    back_w = flipped(w1)

    @pl.loop(0, 2)
    def _(b):
        out[pl.ds(8 * b, 8)] = dot_nt(taps(first3, 8 * b, 8), back_w).astype(BF).reshape(8, 64, CH)


def feature_step(first3, w1):
    return call(feature_kernel, "feature_step", (((16, 64, CH), BF),), (first3, w1), limit=12, flops=10**9)[0]


def scatter_core_kernel(keep_c, keep_f, got_c, got_f, out):
    for k in range(8):
        out[k, 0:160, :] = (keep_c[k].astype(F32) + got_c[k].astype(F32)).astype(BF)
        out[k, 160:304, :] = (keep_f[k].astype(F32) + got_f[k].astype(F32)).astype(BF)


def scatter_row_kernel(got, out, total):
    value = got[0].astype(F32)
    for k in range(1, 8):
        value = value + got[k].astype(F32)
    total[0:304, :] = value
    total[304:336, :] = jnp.zeros((32, CH), F32)
    for k in range(16):
        out[k] = total[20 * k : 20 * k + 32, :].astype(BF)


def scatter_column_kernel(got, out):
    value = got[0].astype(F32)
    for k in range(1, 16):
        value = value + got[k].astype(F32)
    value = value.astype(BF)
    for k in range(16):
        out[k] = value


def gather_column_kernel(scale, got, conv, proj, fine, total):
    for k in range(16):
        total[20 * k : 20 * k + 32, :] = got[k].astype(F32)
    for k in range(9):
        conv[k] = total[16 * k : 16 * k + 16, :] * scale
    proj[...] = total[144:160, :] * scale
    value = total[160:304, :].astype(BF)
    for k in range(8):
        fine[k] = value


def finish_kernel(scale, meta, mine, other, first, second):
    core = meta[4] % 2
    for at in range(8):
        out = first if at < 4 else second
        a = mine[at].astype(F32) * scale
        b = other[at].astype(F32) * scale
        out[2 * (at % 4)] = jnp.where(core == 0, a, b)
        out[2 * (at % 4) + 1] = jnp.where(core == 0, b, a)


def swap(value, axis, mask):
    count = lax.axis_size(axis)
    return lax.ppermute(value, axis, [(i, i ^ mask) for i in range(count)])


def shifted(value, axis, step):
    count = lax.axis_size(axis)
    pairs = [(i, i + step) for i in range(count) if 0 <= i + step < count]
    return lax.ppermute(value, axis, pairs)


def exchange_row(value):
    count = lax.axis_size("row")
    groups = [list(range(c, count, 2)) for c in range(2)]
    return lax.all_to_all(value, "row", 0, 0, axis_index_groups=groups, tiled=True)


def exchange_column(value):
    return lax.all_to_all(value, "col", 0, 0, tiled=True)


def after_all(value, *others):
    return lax.optimization_barrier((value,) + others)[0]


def local(features, conv_first, conv_second, coarse_conv, coarse_proj, cotangent):
    rows, cols = (lax.axis_size("row"), lax.axis_size("col"))
    height, breadth = (features.shape[0] * rows, features.shape[1] * cols)
    fine_scale = 1.0 / (height * breadth * features.shape[2]) ** 0.5
    coarse_scale = 2.0 * fine_scale
    me, mine = (lax.axis_index("row"), lax.axis_index("col"))
    fixed = [jnp.int32(height), jnp.int32(breadth)]
    meta = jnp.stack([me * 16, mine * 16] + fixed + [me, mine]).astype(jnp.int32)
    feat = features.reshape(16, 64, CH)
    cot = cotangent.reshape(16, 64, CH)
    conv = coarse_conv.reshape(9, CH, 16).swapaxes(1, 2)
    slab = ((160, CH), BF)

    right, left, own = call(
        pack_columns_kernel,
        "pack_columns",
        (((16, 48, CH), BF), ((16, 48, CH), BF), slab),
        (feat, cot, conv, coarse_proj),
        (pltpu.SemaphoreType.DMA((14,)),),
        far=True,
    )
    before = shifted(right, "col", 1)
    after = shifted(left, "col", -1)
    down, up = call(
        pack_rows_kernel, "pack_rows", (((12, 128, CH), BF), ((12, 128, CH), BF)), (feat, cot, before, after)
    )
    above = shifted(down, "row", 1)
    below = shifted(up, "row", -1)
    own = after_all(own, down)
    near0 = call(stack_kernel, "stack_two", (((2, 160, CH), BF),), (own, swap(own, "row", 8)))[0]
    near0 = after_all(near0, above, below)
    near = [near0] + [swap(near0, "row", 2 * k) for k in range(1, 4)]
    far = swap(call(stack_kernel, "stack_eight", (((4, 2, 160, CH), BF),), near)[0], "row", 1)

    halo = (before, after, above, below)
    w1, w2 = (conv_first.reshape(1152, CH), conv_second.reshape(1152, CH))
    act3w, slope1, feat3 = first_step(meta, feat, *halo, w1)
    pool3, slope2, act, act3 = second_step(meta, act3w, w2)
    blended, keep_c, send_c, pooled_grad = coarse_step(meta, pool3, cot, *halo, near, far, act)
    got_c = swap(send_c, "row", 1)
    keep_f, send_f, first3 = fine_backward(
        meta, pooled_grad, cot, *halo, slope1, slope2, feat3, act3, conv_second.reshape(9, CH, CH)
    )
    got_f = swap(send_f, "row", 1)
    feature_grad = feature_step(first3, conv_first.reshape(9, CH, CH))

    part = call(scatter_core_kernel, "scatter_core", (((8, 304, CH), BF),), (keep_c, keep_f, got_c, got_f))[0]
    part = call(
        scatter_row_kernel, "scatter_row", (((16, 32, CH), BF),), (exchange_row(part),), (((336, CH), F32),)
    )[0]
    part = call(scatter_column_kernel, "scatter_column", (((16, 32, CH), BF),), (exchange_column(part),))[0]
    conv_grad, proj_grad, fine = call(
        functools.partial(gather_column_kernel, coarse_scale),
        "gather_column",
        (((9, 16, CH), F32), ((16, CH), F32), ((8, 144, CH), BF)),
        (exchange_column(part),),
        (((336, CH), F32),),
    )
    fine = exchange_row(fine)
    first, second = call(
        functools.partial(finish_kernel, fine_scale),
        "finish",
        (((8, 144, CH), F32), ((8, 144, CH), F32)),
        (meta, fine, swap(fine, "row", 1)),
    )
    shape = features.shape
    return (
        blended.reshape(shape),
        feature_grad.reshape(shape),
        first.reshape(3, 3, CH, CH),
        second.reshape(3, 3, CH, CH),
        conv_grad.reshape(3, 3, 16, CH).swapaxes(2, 3),
        proj_grad,
    )


def solution(mesh):
    in_specs = (
        P("row", "col", None, None),
        P(),
        P(),
        P(None, None, None, "row"),
        P("row", None),
        P("row", "col", None, None),
    )
    out_specs = (
        P("row", "col", None, None),
        P("row", "col", None, None),
        P(),
        P(),
        P(None, None, None, "row"),
        P("row", None),
    )
    return jax.shard_map(local, mesh=mesh, in_specs=in_specs, out_specs=out_specs, check_vma=False)
```

```python
import functools

import jax
import jax.numpy as jnp
from jax import lax
from jax.experimental import pallas as pl
from jax.experimental.pallas import tpu as pltpu
from jax.sharding import PartitionSpec as P

BF = jnp.bfloat16
F32 = jnp.float32
CH = 128
WIDE = 256
MIB = 1024 * 1024
VM = pl.BlockSpec(memory_space=pltpu.VMEM)
SM = pl.BlockSpec(memory_space=pltpu.SMEM)
HBM = pl.BlockSpec(memory_space=pltpu.HBM)


def call(kernel, name, outs, ins, scratch=(), limit=16, flops=0, moved=0, far=()):
    ins = [pltpu.with_memory_space_constraint(v, pltpu.HBM) if k in far else v for k, v in enumerate(ins)]
    shapes = tuple(jax.ShapeDtypeStruct(shape, dtype) for shape, dtype in outs)
    return pl.pallas_call(
        kernel,
        name=name,
        out_shape=shapes,
        in_specs=[HBM if k in far else SM if v.ndim == 1 else VM for k, v in enumerate(ins)],
        out_specs=tuple(VM for _ in outs),
        scratch_shapes=[pltpu.VMEM(*v) if isinstance(v, tuple) else v for v in scratch],
        compiler_params=pltpu.CompilerParams(vmem_limit_bytes=limit * MIB),
        cost_estimate=pl.CostEstimate(flops=flops, bytes_accessed=moved, transcendentals=0),
    )(*ins)


def dot_nn(a, b):
    return jnp.dot(a, b, preferred_element_type=F32)


def dot_nt(a, b):
    return lax.dot_general(a, b, (((1,), (1,)), ((), ())), preferred_element_type=F32)


def dot_tn(a, b):
    return lax.dot_general(a, b, (((0,), (0,)), ((), ())), preferred_element_type=F32)


def sigmoid(value):
    return 0.5 * jnp.tanh(0.5 * value) + 0.5


def slope_of(value):
    sigma = sigmoid(value)
    return sigma * (1.0 + value * (1.0 - sigma))


def rounded(value):
    return value.astype(BF).astype(F32)


def three(value):
    count = value.shape[0]
    left = pltpu.roll(value, 4, 0)
    right = pltpu.roll(value, count - 4, 0)
    return jnp.concatenate([left.astype(BF), value.astype(BF), right.astype(BF)], axis=1)


def taps(ref, start, rows, cols=None):
    parts = []
    for r in range(3):
        part = ref[pl.ds(start + r, rows)] if cols is None else ref[pl.ds(start + r, rows), cols[0] : cols[1], :]
        parts.append(part.reshape(part.shape[0] * part.shape[1], part.shape[2]))
    return jnp.concatenate(parts, axis=1)


def column_mask(first, width, limit):
    place = first + lax.broadcasted_iota(jnp.int32, (width, CH), 0) // 4
    return jnp.where((place >= 0) & (place < limit), 1.0, 0.0).astype(F32)


def row_ok(place, limit):
    return jnp.where((place >= 0) & (place < limit), 1.0, 0.0).astype(F32)


def masked(value, mask, first, limit):
    rows = []
    for k in range(value.shape[0]):
        rows.append((value[k] * (mask * row_ok(first + k, limit)))[None])
    return jnp.concatenate(rows, axis=0)


def pooled_pair(row):
    count = row.shape[0]
    low = (row + pltpu.roll(row, count - 4, 0)).reshape(count // 16, 2, 8, CH)
    high = (row + pltpu.roll(row, 4, 0)).reshape(count // 16, 2, 8, CH)
    first = lax.broadcasted_iota(jnp.int32, (count // 16, 8, CH), 1) < 4
    return jnp.where(first, low[:, 0], high[:, 1]).reshape(count // 2, CH)


def repeated(row):
    count = row.shape[0]
    first = lax.broadcasted_iota(jnp.int32, (count, CH), 0) % 8 < 4
    even = jnp.where(first, row, pltpu.roll(row, 4, 0)).reshape(count // 8, 1, 8, CH)
    odd = jnp.where(first, pltpu.roll(row, count - 4, 0), row).reshape(count // 8, 1, 8, CH)
    return jnp.concatenate([even, odd], axis=1).reshape(count * 2, CH)


def aligned(start, size):
    return pl.ds(pl.multiple_of(start, 16), size)


def sides(meta, pair, other):
    even = meta[5] % 2 == 0
    return lax.select(even, other, pair), lax.select(even, pair, other)


def pack_columns_kernel(meta, feat, cot, conv, proj, pair, other, weights, done):
    odd = meta[5] % 2
    pairs = [
        (feat.at[:, aligned(32 - 32 * odd, 32), :], pair.at[:, 0:32, :]),
        (cot.at[:, aligned(48 - 48 * odd, 16), :], pair.at[:, 32:48, :]),
        (feat.at[:, aligned(32 * odd, 32), :], other.at[:, 0:32, :]),
        (cot.at[:, aligned(48 * odd, 16), :], other.at[:, 32:48, :]),
        (proj, weights.at[144:160, :]),
    ] + [(conv.at[t], weights.at[16 * t : 16 * t + 16, :]) for t in range(9)]
    copies = [pltpu.make_async_copy(a, b, done.at[k]) for k, (a, b) in enumerate(pairs)]
    for copy in copies:
        copy.start()
    for copy in copies:
        copy.wait()


def pack_rows_kernel(meta, feat, cot, pair, other, inner, outer, done):
    core = meta[4] % 2
    copies = []
    for k, (out, low) in enumerate(((inner, 1 - core), (outer, core))):
        pairs = (
            (feat.at[pl.ds(8 * low, 8)], out.at[0:8, 32:96, :]),
            (cot.at[pl.ds(12 * low, 4)], out.at[8:12, 16:80, :]),
        )
        copies += [pltpu.make_async_copy(a, b, done.at[2 * k + n]) for n, (a, b) in enumerate(pairs)]
    for copy in copies:
        copy.start()
    for out, low in ((inner, 1 - core), (outer, core)):
        for out_rows, first, inside, edge in (
            (slice(0, 8), 8 * low, slice(0, 32), slice(96, 128)),
            (slice(8, 12), 12 * low, slice(32, 48), slice(80, 96)),
        ):
            source = pl.ds(first, out_rows.stop - out_rows.start)
            before, after = sides(meta, pair[source, inside, :], other[source, inside, :])
            out[out_rows, 0 : inside.stop - inside.start, :] = before
            out[out_rows, edge, :] = after
        out[8:12, 96:128, :] = jnp.zeros((4, 32, CH), BF)
    for copy in copies:
        copy.wait()


def stack_kernel(*refs):
    out = refs[-1]
    for k, ref in enumerate(refs[:-1]):
        out[k] = ref[...]


def first_kernel(meta, feat_far, pair, other, inner, outer, w1_far, act3, slope1, feat3o, feat3, pre1, feat, w1, done):
    copies = [pltpu.make_async_copy(feat_far, feat, done.at[0]), pltpu.make_async_copy(w1_far, w1, done.at[1])]
    for copy in copies:
        copy.start()
    top, left, height, breadth = (meta[0], meta[1], meta[2], meta[3])
    mask = column_mask(left - 8, 128, breadth)

    below_at = 24 * (meta[4] % 2)

    @pl.loop(0, 2)
    def _(b):
        block = outer[pl.ds(4 * b, 4)].reshape(512, CH).astype(F32)
        feat3[pl.ds(4 * b + below_at, 4)] = three(block).reshape(4, 128, 3 * CH)
        block = inner[pl.ds(4 * b, 4)].reshape(512, CH).astype(F32)
        feat3[pl.ds(4 * b + 24 - below_at, 4)] = three(block).reshape(4, 128, 3 * CH)

    for copy in copies:
        copy.wait()

    @pl.loop(0, 4)
    def _(b):
        rows = pl.ds(4 * b, 4)
        before, after = sides(meta, pair[rows, 0:32, :], other[rows, 0:32, :])
        middle = jnp.concatenate([before, feat[rows], after], axis=1)
        feat3[pl.ds(4 * b + 8, 4)] = three(middle.reshape(512, CH).astype(F32)).reshape(4, 128, 3 * CH)

    first_w = w1[...]

    @pl.loop(0, 6)
    def _(b):
        pre = dot_nn(taps(feat3, 5 * b, 5), first_w)
        pre1[pl.ds(5 * b, 5)] = pre.reshape(5, 128, CH)
        value = rounded(pre * sigmoid(pre)).reshape(5, 128, CH)
        value = masked(value, mask, top - 7 + 5 * b, height)
        act3[pl.ds(5 * b, 5)] = three(value.reshape(640, CH)).reshape(5, 128, 3 * CH)

    @pl.loop(0, 18)
    def _(k):
        slope1[k] = slope_of(pre1[k + 6, 16:112, :])
        feat3o[k] = feat3[k + 7, 32:96, :]


def second_kernel(meta, act3, w2, pool3, slope2, act, act3o, pre2, act2):
    top, left, height, breadth = (meta[0], meta[1], meta[2], meta[3])
    coarse_mask = column_mask(left // 2 - 4, 64, breadth // 2)
    second_w = w2[...]

    @pl.loop(0, 7)
    def _(b):
        pre = dot_nn(taps(act3, 4 * b, 4), second_w)
        pre2[pl.ds(4 * b, 4)] = pre.reshape(4, 128, CH)
        value = (pre * sigmoid(pre)).astype(BF)
        act2[pl.ds(4 * b, 4)] = value.reshape(4, 128, CH)
        value = value.astype(F32).reshape(4, 128, CH)
        coarse = []
        for k in range(2):
            small = rounded(0.25 * pooled_pair(value[2 * k] + value[2 * k + 1]))
            coarse.append(small * (coarse_mask * row_ok(top // 2 - 3 + 2 * b + k, height // 2)))
        coarse = jnp.concatenate(coarse, axis=0)
        pool3[pl.ds(2 * b, 2)] = three(coarse).reshape(2, 64, 3 * CH)

    @pl.loop(0, 18)
    def _(k):
        act3o[k] = act3[k + 6, 32:96, :]

    @pl.loop(0, 20)
    def _(k):
        slope2[k] = slope_of(pre2[k + 4, 16:112, :])

    @pl.loop(0, 16)
    def _(k):
        act[k] = act2[k + 6, 32:96, :]


def first_step(meta, feat, halo, w1):
    return call(
        first_kernel,
        "first_conv",
        (((30, 128, 384), BF), ((18, 96, CH), F32), ((18, 64, 384), BF)),
        (meta, feat) + halo + (w1,),
        (
            ((32, 128, 384), BF),
            ((30, 128, CH), F32),
            ((16, 64, CH), BF),
            ((1152, CH), BF),
            pltpu.SemaphoreType.DMA((2,)),
        ),
        far=(1, 6),
        limit=20,
        flops=4 * 10**9,
    )


def second_step(meta, act3, w2):
    return call(
        second_kernel,
        "second_conv",
        (((14, 64, 384), BF), ((20, 96, CH), F32), ((16, 64, CH), BF), ((18, 64, 384), BF)),
        (meta, act3, w2),
        (((28, 128, CH), F32), ((28, 128, CH), BF)),
        limit=20,
        flops=4 * 10**9,
    )


def coarse_kernel(
    meta, pool3, cot, pair, other, inner, outer, near0, near1, near2, near3, far, act,
    blended, keep, send, pooled_grad, wcat, projs, wide3, projin,
):
    top, left, height, breadth, me = (meta[0], meta[1], meta[2], meta[3], meta[4])
    core = me % 2
    near = (near0, near1, near2, near3)
    for rel in range(16):
        c, x, y = (rel % 2, (rel // 2) % 4, rel // 8)
        place = pl.ds(pl.multiple_of((me ^ rel) * 16, 16), 16)
        source = far.at[x, y] if c else near[x].at[y]
        for t in range(9):
            wcat[place, t * CH : (t + 1) * CH] = source[16 * t : 16 * t + 16, :]
        projs[place, :] = source[144:160, :]
    proj_w = projs[...]

    def pair_sum(a, b):
        return pooled_pair(a.astype(F32) + b.astype(F32))

    below_at = 10 * core
    for k in range(2):
        projin[k + below_at] = pair_sum(outer[8 + 2 * k, 0:96, :], outer[9 + 2 * k, 0:96, :])
        projin[k + 10 - below_at] = pair_sum(inner[8 + 2 * k, 0:96, :], inner[9 + 2 * k, 0:96, :])

    @pl.loop(0, 8)
    def _(k):
        rows = pl.ds(2 * k, 2)
        before, after = sides(meta, pair[rows, 32:48, :], other[rows, 32:48, :])
        both = jnp.concatenate([before, cot[rows], after], axis=1)
        projin[k + 2] = pair_sum(both[0], both[1])

    proj_in = projin[...].reshape(576, CH)
    proj_in_bf = proj_in.astype(BF)
    pre = dot_nt(taps(pool3, 0, 12), wcat[...]).reshape(12, 64, WIDE)[:, 8:56].reshape(576, WIDE)
    sigma = sigmoid(pre)
    coarse_act = pre * sigma
    act_grad = dot_nt(proj_in_bf, proj_w)
    grad = rounded(act_grad * (sigma * (1.0 + pre * (1.0 - sigma)))).reshape(12, 48, WIDE)
    mask = column_mask(left // 2 - 2, 48, breadth // 2)
    mask = jnp.concatenate([mask, mask], axis=1)
    grad = masked(grad, mask, top // 2 - 2, height // 2)
    wide3[...] = three(grad.reshape(576, WIDE)).reshape(12, 48, 3 * WIDE)
    own_grad = grad[2:10, 8:40].reshape(256, WIDE).astype(BF)
    own_act = coarse_act.reshape(12, 48, WIDE)[2:10, 8:40].reshape(256, WIDE).astype(BF)
    own_in = proj_in.reshape(12, 48, CH)[2:10, 8:40].reshape(256, CH).astype(BF)

    def emit(first, last, value):
        value = value.reshape(8, 2, 16, CH)
        even, odd = (value[:, 0], value[:, 1])
        keep[:, first:last, :] = jnp.where(core == 0, even, odd).astype(BF)
        send[:, first:last, :] = jnp.where(core == 0, odd, even).astype(BF)

    for r in range(3):
        source = pool3[2 + r : 10 + r, 16:48, :].reshape(256, 3 * CH)
        part = dot_tn(own_grad, source)
        for s in range(3):
            t = 3 * r + s
            emit(16 * t, 16 * t + 16, part[:, s * CH : (s + 1) * CH])
    emit(144, 160, dot_tn(own_act, own_in))
    total = None
    for r in range(3):
        lhs = wide3[r : r + 10].reshape(480, 3 * WIDE)
        first = 3 * (2 - r)
        rhs = jnp.concatenate([wcat[:, (first + 2 - s) * CH : (first + 3 - s) * CH] for s in range(3)], axis=0)
        part = dot_nn(lhs, rhs)
        total = part if total is None else total + part
    pooled_grad[...] = total.reshape(10, 48, CH)
    projected = dot_nn(own_act, proj_w).reshape(8, 32, CH)
    for k in range(8):
        row = repeated(projected[k])
        for e in range(2):
            blended[2 * k + e] = (act[2 * k + e].astype(F32) + row).astype(BF)


def coarse_step(meta, pool3, cot, halo, near, far, act):
    return call(
        coarse_kernel,
        "coarse_step",
        (((16, 64, CH), BF), ((8, 160, CH), BF), ((8, 160, CH), BF), ((10, 48, CH), F32)),
        (meta, pool3, cot) + halo + tuple(near) + (far, act),
        (
            ((WIDE, 9 * CH), BF),
            ((WIDE, CH), BF),
            ((12, 48, 3 * WIDE), BF),
            ((12, 48, CH), F32),
        ),
        limit=20,
        flops=2 * 10**9,
    )


def flipped(weight):
    return jnp.concatenate([weight[8 - t] for t in range(9)], axis=1)


def backward_kernel(
    meta, pooled_grad, cot, pair, other, inner, outer, slope1, slope2, feat3, act3, w2,
    keep, send, first3, second3, grads,
):
    top, left, height, breadth = (meta[0], meta[1], meta[2], meta[3])
    mask = column_mask(left - 4, 96, breadth)

    def second_rows(k, both):
        wide = 0.25 * repeated(pooled_grad[k])
        rows = []
        for e in range(2):
            value = rounded((both[e].astype(F32) + wide) * slope2[2 * k + e])
            rows.append(value * (mask * row_ok(top - 2 + 2 * k + e, height)))
        second3[pl.ds(2 * k, 2)] = three(jnp.concatenate(rows, axis=0)).reshape(2, 96, 3 * CH)

    first_core = meta[4] % 2 == 0
    second_rows(0, lax.select(first_core, outer[10:12, 0:96, :], inner[10:12, 0:96, :]))
    second_rows(9, lax.select(first_core, inner[8:10, 0:96, :], outer[8:10, 0:96, :]))

    @pl.loop(0, 8)
    def _(k):
        rows = pl.ds(2 * k, 2)
        before, after = sides(meta, pair[rows, 32:48, :], other[rows, 32:48, :])
        second_rows(k + 1, jnp.concatenate([before, cot[rows], after], axis=1))

    def weight_grad(source, grad):
        return [dot_tn(source[r : r + 16].reshape(1024, 3 * CH), grad) for r in range(3)]

    def emit(base, parts):
        for r in range(3):
            grads[base + 384 * r : base + 384 * (r + 1), :] = parts[r].astype(BF)

    second_own = second3[2:18, 16:80, CH : 2 * CH].reshape(1024, CH)
    emit(1152, weight_grad(act3, second_own))
    back_w = flipped(w2)

    @pl.loop(0, 3)
    def _(b):
        value = dot_nt(taps(second3, 6 * b, 6), back_w).reshape(6, 96, CH)
        value = rounded(value * slope1[pl.ds(6 * b, 6)])
        value = masked(value, mask, top - 1 + 6 * b, height)
        out = three(value.reshape(576, CH)).reshape(6, 96, 3 * CH)
        first3[pl.ds(6 * b, 6)] = out[:, 16:80, :]

    first_own = first3[1:17, :, CH : 2 * CH].reshape(1024, CH)
    emit(0, weight_grad(feat3, first_own))
    core = meta[4] % 2
    for k in range(8):
        keep[k] = grads[pl.ds(pl.multiple_of((2 * k + core) * 144, 16), 144), :]
        send[k] = grads[pl.ds(pl.multiple_of((2 * k + 1 - core) * 144, 16), 144), :]


def fine_backward(meta, pooled_grad, cot, halo, slope1, slope2, feat3, act3, w2):
    return call(
        backward_kernel,
        "fine_backward",
        (((8, 144, CH), BF), ((8, 144, CH), BF), ((18, 64, 384), BF)),
        (meta, pooled_grad, cot) + halo + (slope1, slope2, feat3, act3, w2),
        (((20, 96, 384), BF), ((2304, CH), BF)),
        limit=20,
        flops=2 * 10**9,
    )


def feature_kernel(first3, w1, out):
    back_w = flipped(w1)

    @pl.loop(0, 2)
    def _(b):
        out[pl.ds(8 * b, 8)] = dot_nt(taps(first3, 8 * b, 8), back_w).astype(BF).reshape(8, 64, CH)


def feature_step(first3, w1):
    return call(feature_kernel, "feature_step", (((16, 64, CH), BF),), (first3, w1), limit=12, flops=10**9)[0]


def scatter_core_kernel(keep_c, keep_f, got_c, got_f, out):
    for k in range(8):
        out[k, 0:160, :] = (keep_c[k].astype(F32) + got_c[k].astype(F32)).astype(BF)
        out[k, 160:304, :] = (keep_f[k].astype(F32) + got_f[k].astype(F32)).astype(BF)


def scatter_row_kernel(got, out, total):
    value = got[0].astype(F32)
    for k in range(1, 8):
        value = value + got[k].astype(F32)
    total[0:304, :] = value
    total[304:336, :] = jnp.zeros((32, CH), F32)
    for k in range(16):
        out[k] = total[20 * k : 20 * k + 32, :].astype(BF)


def scatter_column_kernel(got, out):
    value = got[0].astype(F32)
    for k in range(1, 16):
        value = value + got[k].astype(F32)
    value = value.astype(BF)
    for k in range(16):
        out[k] = value


def gather_column_kernel(scale, got, conv, proj, fine, total):
    for k in range(16):
        total[20 * k : 20 * k + 32, :] = got[k].astype(F32)
    for k in range(9):
        conv[k] = total[16 * k : 16 * k + 16, :] * scale
    proj[...] = total[144:160, :] * scale
    value = total[160:304, :].astype(BF)
    for k in range(8):
        fine[k] = value


def finish_kernel(scale, meta, mine, other, first, second):
    core = meta[4] % 2
    for at in range(8):
        out = first if at < 4 else second
        a = mine[at].astype(F32) * scale
        b = other[at].astype(F32) * scale
        out[2 * (at % 4)] = jnp.where(core == 0, a, b)
        out[2 * (at % 4) + 1] = jnp.where(core == 0, b, a)


def swap(value, axis, mask):
    count = lax.axis_size(axis)
    return lax.ppermute(value, axis, [(i, i ^ mask) for i in range(count)])


def swap_outer(value, axis):
    count = lax.axis_size(axis)
    pairs = [(i, i + 1 if i % 2 else i - 1) for i in range(1, count - 1)]
    return lax.ppermute(value, axis, pairs)


def exchange_row(value):
    count = lax.axis_size("row")
    groups = [list(range(c, count, 2)) for c in range(2)]
    return lax.all_to_all(value, "row", 0, 0, axis_index_groups=groups, tiled=True)


def exchange_column(value):
    return lax.all_to_all(value, "col", 0, 0, tiled=True)


def after_all(value, *others):
    return lax.optimization_barrier((value,) + others)[0]


def local(features, conv_first, conv_second, coarse_conv, coarse_proj, cotangent):
    rows, cols = (lax.axis_size("row"), lax.axis_size("col"))
    height, breadth = (features.shape[0] * rows, features.shape[1] * cols)
    fine_scale = 1.0 / (height * breadth * features.shape[2]) ** 0.5
    coarse_scale = 2.0 * fine_scale
    me, mine = (lax.axis_index("row"), lax.axis_index("col"))
    fixed = [jnp.int32(height), jnp.int32(breadth)]
    meta = jnp.stack([me * 16, mine * 16] + fixed + [me, mine]).astype(jnp.int32)
    feat = features.reshape(16, 64, CH)
    cot = cotangent.reshape(16, 64, CH)
    conv = coarse_conv.reshape(9, CH, 16).swapaxes(1, 2)
    slab = ((160, CH), BF)

    side = ((16, 48, CH), BF)
    pair, other, own = call(
        pack_columns_kernel,
        "pack_columns",
        (side, side, slab),
        (meta, feat, cot, conv, coarse_proj),
        (pltpu.SemaphoreType.DMA((14,)),),
        far=(1, 2, 3, 4),
    )
    pair = swap(pair, "col", 1)
    other = swap_outer(other, "col")
    own_far = swap(own, "row", 8)
    edge = ((12, 128, CH), BF)
    inner, outer = call(
        pack_rows_kernel,
        "pack_rows",
        (edge, edge),
        (meta, feat, cot, pair, other),
        (pltpu.SemaphoreType.DMA((4,)),),
        far=(1, 2),
    )
    inner = swap(inner, "row", 1)
    outer = swap_outer(outer, "row")
    halo = (pair, other, inner, outer)
    w1, w2 = (conv_first.reshape(1152, CH), conv_second.reshape(1152, CH))
    act3w, slope1, feat3 = first_step(meta, feat, halo, w1)
    near0 = call(stack_kernel, "stack_two", (((2, 160, CH), BF),), (own, after_all(own_far, slope1)))[0]
    near = [near0] + [swap(near0, "row", 2 * k) for k in range(1, 4)]
    pool3, slope2, act, act3 = second_step(meta, act3w, w2)
    near = list(lax.optimization_barrier((slope2, *near)))[1:]
    far = swap(call(stack_kernel, "stack_eight", (((4, 2, 160, CH), BF),), near)[0], "row", 1)
    blended, keep_c, send_c, pooled_grad = coarse_step(meta, pool3, cot, halo, near, far, act)
    got_c = swap(send_c, "row", 1)
    keep_f, send_f, first3 = fine_backward(
        meta, pooled_grad, cot, halo, slope1, slope2, feat3, act3, conv_second.reshape(9, CH, CH)
    )
    got_f = swap(send_f, "row", 1)
    feature_grad = feature_step(first3, conv_first.reshape(9, CH, CH))

    got_f = after_all(got_f, feature_grad)
    part = call(scatter_core_kernel, "scatter_core", (((8, 304, CH), BF),), (keep_c, keep_f, got_c, got_f))[0]
    part = call(
        scatter_row_kernel, "scatter_row", (((16, 32, CH), BF),), (exchange_row(part),), (((336, CH), F32),)
    )[0]
    part = call(scatter_column_kernel, "scatter_column", (((16, 32, CH), BF),), (exchange_column(part),))[0]
    conv_grad, proj_grad, fine = call(
        functools.partial(gather_column_kernel, coarse_scale),
        "gather_column",
        (((9, 16, CH), F32), ((16, CH), F32), ((8, 144, CH), BF)),
        (exchange_column(part),),
        (((336, CH), F32),),
    )
    fine = exchange_row(fine)
    first, second = call(
        functools.partial(finish_kernel, fine_scale),
        "finish",
        (((8, 144, CH), F32), ((8, 144, CH), F32)),
        (meta, fine, swap(fine, "row", 1)),
    )
    shape = features.shape
    return (
        blended.reshape(shape),
        feature_grad.reshape(shape),
        first.reshape(3, 3, CH, CH),
        second.reshape(3, 3, CH, CH),
        conv_grad.reshape(3, 3, 16, CH).swapaxes(2, 3),
        proj_grad,
    )


def solution(mesh):
    in_specs = (
        P("row", "col", None, None),
        P(),
        P(),
        P(None, None, None, "row"),
        P("row", None),
        P("row", "col", None, None),
    )
    out_specs = (
        P("row", "col", None, None),
        P("row", "col", None, None),
        P(),
        P(),
        P(None, None, None, "row"),
        P("row", None),
    )
    return jax.shard_map(local, mesh=mesh, in_specs=in_specs, out_specs=out_specs, check_vma=False)
```

```python
import functools

import jax
import jax.numpy as jnp
from jax import lax
from jax.experimental import pallas as pl
from jax.experimental.pallas import tpu as pltpu
from jax.sharding import PartitionSpec as P

BF = jnp.bfloat16
F32 = jnp.float32
CH = 128
WIDE = 256
MIB = 1024 * 1024
VM = pl.BlockSpec(memory_space=pltpu.VMEM)
SM = pl.BlockSpec(memory_space=pltpu.SMEM)
HBM = pl.BlockSpec(memory_space=pltpu.HBM)


def call(kernel, name, outs, ins, scratch=(), limit=16, flops=0, moved=0, far=()):
    ins = [pltpu.with_memory_space_constraint(v, pltpu.HBM) if k in far else v for k, v in enumerate(ins)]
    shapes = tuple(jax.ShapeDtypeStruct(shape, dtype) for shape, dtype in outs)
    return pl.pallas_call(
        kernel,
        name=name,
        out_shape=shapes,
        in_specs=[HBM if k in far else SM if v.ndim == 1 else VM for k, v in enumerate(ins)],
        out_specs=tuple(VM for _ in outs),
        scratch_shapes=[pltpu.VMEM(*v) if isinstance(v, tuple) else v for v in scratch],
        compiler_params=pltpu.CompilerParams(vmem_limit_bytes=limit * MIB),
        cost_estimate=pl.CostEstimate(flops=flops, bytes_accessed=moved, transcendentals=0),
    )(*ins)


def dot_nn(a, b):
    return jnp.dot(a, b, preferred_element_type=F32)


def dot_nt(a, b):
    return lax.dot_general(a, b, (((1,), (1,)), ((), ())), preferred_element_type=F32)


def dot_tn(a, b):
    return lax.dot_general(a, b, (((0,), (0,)), ((), ())), preferred_element_type=F32)


def sigmoid(value):
    return 0.5 * jnp.tanh(0.5 * value) + 0.5


def slope_of(value):
    sigma = sigmoid(value)
    return sigma * (1.0 + value * (1.0 - sigma))


def rounded(value):
    return value.astype(BF).astype(F32)


def three(value):
    count = value.shape[0]
    left = pltpu.roll(value, 4, 0)
    right = pltpu.roll(value, count - 4, 0)
    return jnp.concatenate([left.astype(BF), value.astype(BF), right.astype(BF)], axis=1)


def taps(ref, start, rows, cols=None):
    parts = []
    for r in range(3):
        part = ref[pl.ds(start + r, rows)] if cols is None else ref[pl.ds(start + r, rows), cols[0] : cols[1], :]
        parts.append(part.reshape(part.shape[0] * part.shape[1], part.shape[2]))
    return jnp.concatenate(parts, axis=1)


def column_mask(first, width, limit):
    place = first + lax.broadcasted_iota(jnp.int32, (width, CH), 0) // 4
    return jnp.where((place >= 0) & (place < limit), 1.0, 0.0).astype(F32)


def row_ok(place, limit):
    return jnp.where((place >= 0) & (place < limit), 1.0, 0.0).astype(F32)


def masked(value, mask, first, limit):
    rows = []
    for k in range(value.shape[0]):
        rows.append((value[k] * (mask * row_ok(first + k, limit)))[None])
    return jnp.concatenate(rows, axis=0)


def pooled_pair(row):
    count = row.shape[0]
    low = (row + pltpu.roll(row, count - 4, 0)).reshape(count // 16, 2, 8, CH)
    high = (row + pltpu.roll(row, 4, 0)).reshape(count // 16, 2, 8, CH)
    first = lax.broadcasted_iota(jnp.int32, (count // 16, 8, CH), 1) < 4
    return jnp.where(first, low[:, 0], high[:, 1]).reshape(count // 2, CH)


def repeated(row):
    count = row.shape[0]
    first = lax.broadcasted_iota(jnp.int32, (count, CH), 0) % 8 < 4
    even = jnp.where(first, row, pltpu.roll(row, 4, 0)).reshape(count // 8, 1, 8, CH)
    odd = jnp.where(first, pltpu.roll(row, count - 4, 0), row).reshape(count // 8, 1, 8, CH)
    return jnp.concatenate([even, odd], axis=1).reshape(count * 2, CH)


def aligned(start, size):
    return pl.ds(pl.multiple_of(start, 16), size)


def sides(meta, pair, other):
    even = meta[5] % 2 == 0
    return lax.select(even, other, pair), lax.select(even, pair, other)


def pack_columns_kernel(meta, feat, cot, conv, proj, pair, other, weights, done):
    odd = meta[5] % 2
    pairs = [
        (feat.at[:, aligned(32 - 32 * odd, 32), :], pair.at[:, 0:32, :]),
        (cot.at[:, aligned(48 - 48 * odd, 16), :], pair.at[:, 32:48, :]),
        (feat.at[:, aligned(32 * odd, 32), :], other.at[:, 0:32, :]),
        (cot.at[:, aligned(48 * odd, 16), :], other.at[:, 32:48, :]),
        (proj, weights.at[144:160, :]),
    ] + [(conv.at[t], weights.at[16 * t : 16 * t + 16, :]) for t in range(9)]
    copies = [pltpu.make_async_copy(a, b, done.at[k]) for k, (a, b) in enumerate(pairs)]
    for copy in copies:
        copy.start()
    for copy in copies:
        copy.wait()


def pack_rows_kernel(meta, feat, cot, pair, other, inner, outer, done):
    core = meta[4] % 2
    copies = []
    for k, (out, low) in enumerate(((inner, 1 - core), (outer, core))):
        pairs = (
            (feat.at[pl.ds(8 * low, 8)], out.at[0:8, 32:96, :]),
            (cot.at[pl.ds(12 * low, 4)], out.at[8:12, 16:80, :]),
        )
        copies += [pltpu.make_async_copy(a, b, done.at[2 * k + n]) for n, (a, b) in enumerate(pairs)]
    for copy in copies:
        copy.start()
    for out, low in ((inner, 1 - core), (outer, core)):
        for out_rows, first, inside, edge in (
            (slice(0, 8), 8 * low, slice(0, 32), slice(96, 128)),
            (slice(8, 12), 12 * low, slice(32, 48), slice(80, 96)),
        ):
            source = pl.ds(first, out_rows.stop - out_rows.start)
            before, after = sides(meta, pair[source, inside, :], other[source, inside, :])
            out[out_rows, 0 : inside.stop - inside.start, :] = before
            out[out_rows, edge, :] = after
        out[8:12, 96:128, :] = jnp.zeros((4, 32, CH), BF)
    for copy in copies:
        copy.wait()


def stack_kernel(*refs):
    out = refs[-1]
    for k, ref in enumerate(refs[:-1]):
        out[k] = ref[...]


def first_kernel(meta, feat_far, pair, other, inner, outer, w1_far, act3, slope1, feat3o, feat3, pre1, feat, w1, done):
    copies = [pltpu.make_async_copy(feat_far, feat, done.at[0]), pltpu.make_async_copy(w1_far, w1, done.at[1])]
    for copy in copies:
        copy.start()
    top, left, height, breadth = (meta[0], meta[1], meta[2], meta[3])
    mask = column_mask(left - 8, 128, breadth)

    below_at = 24 * (meta[4] % 2)

    @pl.loop(0, 2)
    def _(b):
        block = outer[pl.ds(4 * b, 4)].reshape(512, CH).astype(F32)
        feat3[pl.ds(4 * b + below_at, 4)] = three(block).reshape(4, 128, 3 * CH)
        block = inner[pl.ds(4 * b, 4)].reshape(512, CH).astype(F32)
        feat3[pl.ds(4 * b + 24 - below_at, 4)] = three(block).reshape(4, 128, 3 * CH)

    for copy in copies:
        copy.wait()

    @pl.loop(0, 4)
    def _(b):
        rows = pl.ds(4 * b, 4)
        before, after = sides(meta, pair[rows, 0:32, :], other[rows, 0:32, :])
        middle = jnp.concatenate([before, feat[rows], after], axis=1)
        feat3[pl.ds(4 * b + 8, 4)] = three(middle.reshape(512, CH).astype(F32)).reshape(4, 128, 3 * CH)

    first_w = w1[...]

    @pl.loop(0, 6)
    def _(b):
        pre = dot_nn(taps(feat3, 5 * b, 5), first_w)
        pre1[pl.ds(5 * b, 5)] = pre.reshape(5, 128, CH)
        value = rounded(pre * sigmoid(pre)).reshape(5, 128, CH)
        value = masked(value, mask, top - 7 + 5 * b, height)
        act3[pl.ds(5 * b, 5)] = three(value.reshape(640, CH)).reshape(5, 128, 3 * CH)

    @pl.loop(0, 18)
    def _(k):
        slope1[k] = slope_of(pre1[k + 6, 16:112, :])
        feat3o[k] = feat3[k + 7, 32:96, :]


def second_kernel(meta, act3, w2, pool3, slope2, act, act3o, pre2, act2):
    top, left, height, breadth = (meta[0], meta[1], meta[2], meta[3])
    coarse_mask = column_mask(left // 2 - 4, 64, breadth // 2)
    second_w = w2[...]

    @pl.loop(0, 7)
    def _(b):
        pre = dot_nn(taps(act3, 4 * b, 4), second_w)
        pre2[pl.ds(4 * b, 4)] = pre.reshape(4, 128, CH)
        value = (pre * sigmoid(pre)).astype(BF)
        act2[pl.ds(4 * b, 4)] = value.reshape(4, 128, CH)
        value = value.astype(F32).reshape(4, 128, CH)
        coarse = []
        for k in range(2):
            small = rounded(0.25 * pooled_pair(value[2 * k] + value[2 * k + 1]))
            coarse.append(small * (coarse_mask * row_ok(top // 2 - 3 + 2 * b + k, height // 2)))
        coarse = jnp.concatenate(coarse, axis=0)
        pool3[pl.ds(2 * b, 2)] = three(coarse).reshape(2, 64, 3 * CH)

    @pl.loop(0, 18)
    def _(k):
        act3o[k] = act3[k + 6, 32:96, :]

    @pl.loop(0, 20)
    def _(k):
        slope2[k] = slope_of(pre2[k + 4, 16:112, :])

    @pl.loop(0, 16)
    def _(k):
        act[k] = act2[k + 6, 32:96, :]


def first_step(meta, feat, halo, w1):
    return call(
        first_kernel,
        "first_conv",
        (((30, 128, 384), BF), ((18, 96, CH), F32), ((18, 64, 384), BF)),
        (meta, feat) + halo + (w1,),
        (
            ((32, 128, 384), BF),
            ((30, 128, CH), F32),
            ((16, 64, CH), BF),
            ((1152, CH), BF),
            pltpu.SemaphoreType.DMA((2,)),
        ),
        far=(1, 6),
        limit=20,
        flops=4 * 10**9,
    )


def second_step(meta, act3, w2):
    return call(
        second_kernel,
        "second_conv",
        (((14, 64, 384), BF), ((20, 96, CH), F32), ((16, 64, CH), BF), ((18, 64, 384), BF)),
        (meta, act3, w2),
        (((28, 128, CH), F32), ((28, 128, CH), BF)),
        limit=20,
        flops=4 * 10**9,
    )


def coarse_kernel(
    meta, pool3, cot, pair, other, inner, outer, near0, near1, near2, near3, far, act,
    blended, keep, send, pooled_grad, wcat, projs, wide3, projin,
):
    top, left, height, breadth, me = (meta[0], meta[1], meta[2], meta[3], meta[4])
    core = me % 2
    near = (near0, near1, near2, near3)
    for rel in range(16):
        c, x, y = (rel % 2, (rel // 2) % 4, rel // 8)
        place = pl.ds(pl.multiple_of((me ^ rel) * 16, 16), 16)
        source = far.at[x, y] if c else near[x].at[y]
        for t in range(9):
            wcat[place, t * CH : (t + 1) * CH] = source[16 * t : 16 * t + 16, :]
        projs[place, :] = source[144:160, :]
    proj_w = projs[...]

    def pair_sum(a, b):
        return pooled_pair(a.astype(F32) + b.astype(F32))

    below_at = 10 * core
    for k in range(2):
        projin[k + below_at] = pair_sum(outer[8 + 2 * k, 0:96, :], outer[9 + 2 * k, 0:96, :])
        projin[k + 10 - below_at] = pair_sum(inner[8 + 2 * k, 0:96, :], inner[9 + 2 * k, 0:96, :])

    @pl.loop(0, 8)
    def _(k):
        rows = pl.ds(2 * k, 2)
        before, after = sides(meta, pair[rows, 32:48, :], other[rows, 32:48, :])
        both = jnp.concatenate([before, cot[rows], after], axis=1)
        projin[k + 2] = pair_sum(both[0], both[1])

    proj_in = projin[...].reshape(576, CH)
    proj_in_bf = proj_in.astype(BF)
    pre = dot_nt(taps(pool3, 0, 12), wcat[...]).reshape(12, 64, WIDE)[:, 8:56].reshape(576, WIDE)
    sigma = sigmoid(pre)
    coarse_act = pre * sigma
    act_grad = dot_nt(proj_in_bf, proj_w)
    grad = rounded(act_grad * (sigma * (1.0 + pre * (1.0 - sigma)))).reshape(12, 48, WIDE)
    mask = column_mask(left // 2 - 2, 48, breadth // 2)
    mask = jnp.concatenate([mask, mask], axis=1)
    grad = masked(grad, mask, top // 2 - 2, height // 2)
    wide3[...] = three(grad.reshape(576, WIDE)).reshape(12, 48, 3 * WIDE)
    own_grad = grad[2:10, 8:40].reshape(256, WIDE).astype(BF)
    own_act = coarse_act.reshape(12, 48, WIDE)[2:10, 8:40].reshape(256, WIDE).astype(BF)
    own_in = proj_in.reshape(12, 48, CH)[2:10, 8:40].reshape(256, CH).astype(BF)

    def emit(first, last, value):
        value = value.reshape(8, 2, 16, CH)
        even, odd = (value[:, 0], value[:, 1])
        keep[:, first:last, :] = jnp.where(core == 0, even, odd).astype(BF)
        send[:, first:last, :] = jnp.where(core == 0, odd, even).astype(BF)

    for r in range(3):
        source = pool3[2 + r : 10 + r, 16:48, :].reshape(256, 3 * CH)
        part = dot_tn(own_grad, source)
        for s in range(3):
            t = 3 * r + s
            emit(16 * t, 16 * t + 16, part[:, s * CH : (s + 1) * CH])
    emit(144, 160, dot_tn(own_act, own_in))
    total = None
    for r in range(3):
        lhs = wide3[r : r + 10].reshape(480, 3 * WIDE)
        first = 3 * (2 - r)
        rhs = jnp.concatenate([wcat[:, (first + 2 - s) * CH : (first + 3 - s) * CH] for s in range(3)], axis=0)
        part = dot_nn(lhs, rhs)
        total = part if total is None else total + part
    pooled_grad[...] = total.reshape(10, 48, CH)
    projected = dot_nn(own_act, proj_w).reshape(8, 32, CH)
    for k in range(8):
        row = repeated(projected[k])
        for e in range(2):
            blended[2 * k + e] = (act[2 * k + e].astype(F32) + row).astype(BF)


def coarse_step(meta, pool3, cot, halo, near, far, act):
    return call(
        coarse_kernel,
        "coarse_step",
        (((16, 64, CH), BF), ((8, 160, CH), BF), ((8, 160, CH), BF), ((10, 48, CH), F32)),
        (meta, pool3, cot) + halo + tuple(near) + (far, act),
        (
            ((WIDE, 9 * CH), BF),
            ((WIDE, CH), BF),
            ((12, 48, 3 * WIDE), BF),
            ((12, 48, CH), F32),
        ),
        limit=20,
        flops=2 * 10**9,
    )


def flipped(weight):
    return jnp.concatenate([weight[8 - t] for t in range(9)], axis=1)


def backward_kernel(
    meta, pooled_grad, cot, pair, other, inner, outer, slope1, slope2, feat3, act3, w2,
    keep, send, first3, second3, grads,
):
    top, left, height, breadth = (meta[0], meta[1], meta[2], meta[3])
    mask = column_mask(left - 4, 96, breadth)

    def second_rows(k, both):
        wide = 0.25 * repeated(pooled_grad[k])
        rows = []
        for e in range(2):
            value = rounded((both[e].astype(F32) + wide) * slope2[2 * k + e])
            rows.append(value * (mask * row_ok(top - 2 + 2 * k + e, height)))
        second3[pl.ds(2 * k, 2)] = three(jnp.concatenate(rows, axis=0)).reshape(2, 96, 3 * CH)

    first_core = meta[4] % 2 == 0
    second_rows(0, lax.select(first_core, outer[10:12, 0:96, :], inner[10:12, 0:96, :]))
    second_rows(9, lax.select(first_core, inner[8:10, 0:96, :], outer[8:10, 0:96, :]))

    @pl.loop(0, 8)
    def _(k):
        rows = pl.ds(2 * k, 2)
        before, after = sides(meta, pair[rows, 32:48, :], other[rows, 32:48, :])
        second_rows(k + 1, jnp.concatenate([before, cot[rows], after], axis=1))

    def weight_grad(source, grad):
        return [dot_tn(source[r : r + 16].reshape(1024, 3 * CH), grad) for r in range(3)]

    def emit(base, parts):
        for r in range(3):
            grads[base + 384 * r : base + 384 * (r + 1), :] = parts[r].astype(BF)

    second_own = second3[2:18, 16:80, CH : 2 * CH].reshape(1024, CH)
    emit(1152, weight_grad(act3, second_own))
    back_w = flipped(w2)

    @pl.loop(0, 3)
    def _(b):
        value = dot_nt(taps(second3, 6 * b, 6), back_w).reshape(6, 96, CH)
        value = rounded(value * slope1[pl.ds(6 * b, 6)])
        value = masked(value, mask, top - 1 + 6 * b, height)
        out = three(value.reshape(576, CH)).reshape(6, 96, 3 * CH)
        first3[pl.ds(6 * b, 6)] = out[:, 16:80, :]

    first_own = first3[1:17, :, CH : 2 * CH].reshape(1024, CH)
    emit(0, weight_grad(feat3, first_own))
    core = meta[4] % 2
    for k in range(8):
        keep[k] = grads[pl.ds(pl.multiple_of((2 * k + core) * 144, 16), 144), :]
        send[k] = grads[pl.ds(pl.multiple_of((2 * k + 1 - core) * 144, 16), 144), :]


def fine_backward(meta, pooled_grad, cot, halo, slope1, slope2, feat3, act3, w2):
    return call(
        backward_kernel,
        "fine_backward",
        (((8, 144, CH), BF), ((8, 144, CH), BF), ((18, 64, 384), BF)),
        (meta, pooled_grad, cot) + halo + (slope1, slope2, feat3, act3, w2),
        (((20, 96, 384), BF), ((2304, CH), BF)),
        limit=20,
        flops=2 * 10**9,
    )


def feature_kernel(first3, w1, out):
    back_w = flipped(w1)

    @pl.loop(0, 2)
    def _(b):
        out[pl.ds(8 * b, 8)] = dot_nt(taps(first3, 8 * b, 8), back_w).astype(BF).reshape(8, 64, CH)


def feature_step(first3, w1):
    return call(feature_kernel, "feature_step", (((16, 64, CH), BF),), (first3, w1), limit=12, flops=10**9)[0]


def scatter_core_kernel(keep_c, keep_f, got_c, got_f, out):
    for k in range(8):
        out[k, 0:160, :] = (keep_c[k].astype(F32) + got_c[k].astype(F32)).astype(BF)
        out[k, 160:304, :] = (keep_f[k].astype(F32) + got_f[k].astype(F32)).astype(BF)


def scatter_row_kernel(got, out, total):
    value = got[0].astype(F32)
    for k in range(1, 8):
        value = value + got[k].astype(F32)
    total[0:304, :] = value
    total[304:336, :] = jnp.zeros((32, CH), F32)
    for k in range(16):
        out[k] = total[20 * k : 20 * k + 32, :].astype(BF)


def scatter_column_kernel(got, out):
    value = got[0].astype(F32)
    for k in range(1, 16):
        value = value + got[k].astype(F32)
    value = value.astype(BF)
    for k in range(16):
        out[k] = value


def gather_column_kernel(scale, got, conv, proj, fine, total):
    for k in range(16):
        total[20 * k : 20 * k + 32, :] = got[k].astype(F32)
    for k in range(9):
        conv[k] = total[16 * k : 16 * k + 16, :] * scale
    proj[...] = total[144:160, :] * scale
    value = total[160:304, :].astype(BF)
    for k in range(8):
        fine[k] = value


def finish_kernel(scale, meta, mine, other, first, second):
    core = meta[4] % 2
    for at in range(8):
        out = first if at < 4 else second
        a = mine[at].astype(F32) * scale
        b = other[at].astype(F32) * scale
        out[2 * (at % 4)] = jnp.where(core == 0, a, b)
        out[2 * (at % 4) + 1] = jnp.where(core == 0, b, a)


def swap(value, axis, mask):
    count = lax.axis_size(axis)
    return lax.ppermute(value, axis, [(i, i ^ mask) for i in range(count)])


def swap_outer(value, axis):
    count = lax.axis_size(axis)
    pairs = [(i, i + 1 if i % 2 else i - 1) for i in range(1, count - 1)]
    return lax.ppermute(value, axis, pairs)


def exchange_row(value):
    count = lax.axis_size("row")
    groups = [list(range(c, count, 2)) for c in range(2)]
    return lax.all_to_all(value, "row", 0, 0, axis_index_groups=groups, tiled=True)


def exchange_column(value):
    return lax.all_to_all(value, "col", 0, 0, tiled=True)


def after_all(value, *others):
    return lax.optimization_barrier((value,) + others)[0]


def local(features, conv_first, conv_second, coarse_conv, coarse_proj, cotangent):
    rows, cols = (lax.axis_size("row"), lax.axis_size("col"))
    height, breadth = (features.shape[0] * rows, features.shape[1] * cols)
    fine_scale = 1.0 / (height * breadth * features.shape[2]) ** 0.5
    coarse_scale = 2.0 * fine_scale
    me, mine = (lax.axis_index("row"), lax.axis_index("col"))
    fixed = [jnp.int32(height), jnp.int32(breadth)]
    meta = jnp.stack([me * 16, mine * 16] + fixed + [me, mine]).astype(jnp.int32)
    feat = features.reshape(16, 64, CH)
    cot = cotangent.reshape(16, 64, CH)
    conv = coarse_conv.reshape(9, CH, 16).swapaxes(1, 2)
    slab = ((160, CH), BF)

    side = ((16, 48, CH), BF)
    pair, other, own = call(
        pack_columns_kernel,
        "pack_columns",
        (side, side, slab),
        (meta, feat, cot, conv, coarse_proj),
        (pltpu.SemaphoreType.DMA((14,)),),
        far=(1, 2, 3, 4),
    )
    pair = swap(pair, "col", 1)
    other = swap_outer(other, "col")
    own_far = swap(own, "row", 8)
    edge = ((12, 128, CH), BF)
    inner, outer = call(
        pack_rows_kernel,
        "pack_rows",
        (edge, edge),
        (meta, feat, cot, pair, other),
        (pltpu.SemaphoreType.DMA((4,)),),
        far=(1, 2),
    )
    near0 = call(stack_kernel, "stack_two", (((2, 160, CH), BF),), (own, own_far))[0]
    inner, outer, near0 = lax.optimization_barrier((inner, outer, near0))
    inner = swap(inner, "row", 1)
    outer = swap_outer(outer, "row")
    near = [near0] + [swap(near0, "row", 2 * k) for k in range(1, 4)]
    halo = (pair, other, inner, outer)
    w1, w2 = (conv_first.reshape(1152, CH), conv_second.reshape(1152, CH))
    act3w, slope1, feat3 = first_step(meta, feat, halo, w1)
    near = list(lax.optimization_barrier((slope1, *near)))[1:]
    far = swap(call(stack_kernel, "stack_eight", (((4, 2, 160, CH), BF),), near)[0], "row", 1)
    pool3, slope2, act, act3 = second_step(meta, act3w, w2)
    blended, keep_c, send_c, pooled_grad = coarse_step(meta, pool3, cot, halo, near, far, act)
    got_c = swap(send_c, "row", 1)
    keep_f, send_f, first3 = fine_backward(
        meta, pooled_grad, cot, halo, slope1, slope2, feat3, act3, conv_second.reshape(9, CH, CH)
    )
    got_f = swap(send_f, "row", 1)
    feature_grad = feature_step(first3, conv_first.reshape(9, CH, CH))

    got_f = after_all(got_f, feature_grad)
    part = call(scatter_core_kernel, "scatter_core", (((8, 304, CH), BF),), (keep_c, keep_f, got_c, got_f))[0]
    part = call(
        scatter_row_kernel, "scatter_row", (((16, 32, CH), BF),), (exchange_row(part),), (((336, CH), F32),)
    )[0]
    part = call(scatter_column_kernel, "scatter_column", (((16, 32, CH), BF),), (exchange_column(part),))[0]
    conv_grad, proj_grad, fine = call(
        functools.partial(gather_column_kernel, coarse_scale),
        "gather_column",
        (((9, 16, CH), F32), ((16, CH), F32), ((8, 144, CH), BF)),
        (exchange_column(part),),
        (((336, CH), F32),),
    )
    fine = exchange_row(fine)
    first, second = call(
        functools.partial(finish_kernel, fine_scale),
        "finish",
        (((8, 144, CH), F32), ((8, 144, CH), F32)),
        (meta, fine, swap(fine, "row", 1)),
    )
    shape = features.shape
    return (
        blended.reshape(shape),
        feature_grad.reshape(shape),
        first.reshape(3, 3, CH, CH),
        second.reshape(3, 3, CH, CH),
        conv_grad.reshape(3, 3, 16, CH).swapaxes(2, 3),
        proj_grad,
    )


def solution(mesh):
    in_specs = (
        P("row", "col", None, None),
        P(),
        P(),
        P(None, None, None, "row"),
        P("row", None),
        P("row", "col", None, None),
    )
    out_specs = (
        P("row", "col", None, None),
        P("row", "col", None, None),
        P(),
        P(),
        P(None, None, None, "row"),
        P("row", None),
    )
    return jax.shard_map(local, mesh=mesh, in_specs=in_specs, out_specs=out_specs, check_vma=False)
```

```python
import functools

import jax
import jax.numpy as jnp
from jax import lax
from jax.experimental import pallas as pl
from jax.experimental.pallas import tpu as pltpu
from jax.sharding import PartitionSpec as P

BF = jnp.bfloat16
F32 = jnp.float32
CH = 128
WIDE = 256
MIB = 1024 * 1024
VM = pl.BlockSpec(memory_space=pltpu.VMEM)
SM = pl.BlockSpec(memory_space=pltpu.SMEM)
HBM = pl.BlockSpec(memory_space=pltpu.HBM)


def call(kernel, name, outs, ins, scratch=(), limit=16, flops=0, moved=0, far=()):
    ins = [pltpu.with_memory_space_constraint(v, pltpu.HBM) if k in far else v for k, v in enumerate(ins)]
    shapes = tuple(jax.ShapeDtypeStruct(shape, dtype) for shape, dtype in outs)
    return pl.pallas_call(
        kernel,
        name=name,
        out_shape=shapes,
        in_specs=[HBM if k in far else SM if v.ndim == 1 else VM for k, v in enumerate(ins)],
        out_specs=tuple(VM for _ in outs),
        scratch_shapes=[pltpu.VMEM(*v) if isinstance(v, tuple) else v for v in scratch],
        compiler_params=pltpu.CompilerParams(vmem_limit_bytes=limit * MIB),
        cost_estimate=pl.CostEstimate(flops=flops, bytes_accessed=moved, transcendentals=0),
    )(*ins)


def dot_nn(a, b):
    return jnp.dot(a, b, preferred_element_type=F32)


def dot_nt(a, b):
    return lax.dot_general(a, b, (((1,), (1,)), ((), ())), preferred_element_type=F32)


def dot_tn(a, b):
    return lax.dot_general(a, b, (((0,), (0,)), ((), ())), preferred_element_type=F32)


def sigmoid(value):
    return 0.5 * jnp.tanh(0.5 * value) + 0.5


def slope_of(value):
    sigma = sigmoid(value)
    return sigma * (1.0 + value * (1.0 - sigma))


def rounded(value):
    return value.astype(BF).astype(F32)


def three(value):
    count = value.shape[0]
    left = pltpu.roll(value, 4, 0)
    right = pltpu.roll(value, count - 4, 0)
    return jnp.concatenate([left.astype(BF), value.astype(BF), right.astype(BF)], axis=1)


def paired(weight, axis):
    pad = jnp.zeros((3 * CH, CH) if axis == 0 else (CH, 3 * CH), BF)
    return jnp.concatenate(
        [jnp.concatenate([weight, pad], axis=axis), jnp.concatenate([pad, weight], axis=axis)], axis=1 - axis
    )


def four_rows(row, starts):
    parts = [jnp.concatenate([row(h + k) for h in starts], axis=0) for k in range(4)]
    return jnp.concatenate(parts, axis=1)


def split_rows(value, starts):
    size = value.shape[0] // len(starts)
    out = []
    for k in range(len(starts)):
        out += [value[k * size : (k + 1) * size, e * CH : (e + 1) * CH] for e in range(2)]
    return out


def weight_grad(source, grad):
    gap = jnp.zeros((64, CH), BF)
    parts = []
    for r in range(3):
        parts.append(jnp.concatenate([gap] * r + [grad.reshape(1024, CH)] + [gap] * (2 - r), axis=0))
    whole = dot_tn(source.reshape(1152, 3 * CH), jnp.concatenate(parts, axis=1))
    return [whole[:, r * CH : (r + 1) * CH] for r in range(3)]


def column_mask(first, width, limit):
    place = first + lax.broadcasted_iota(jnp.int32, (width, CH), 0) // 4
    return jnp.where((place >= 0) & (place < limit), 1.0, 0.0).astype(F32)


def row_ok(place, limit):
    return jnp.where((place >= 0) & (place < limit), 1.0, 0.0).astype(F32)


def masked(value, mask, first, limit):
    rows = []
    for k in range(value.shape[0]):
        rows.append((value[k] * (mask * row_ok(first + k, limit)))[None])
    return jnp.concatenate(rows, axis=0)


def pooled_pair(row):
    count = row.shape[0]
    low = (row + pltpu.roll(row, count - 4, 0)).reshape(count // 16, 2, 8, CH)
    high = (row + pltpu.roll(row, 4, 0)).reshape(count // 16, 2, 8, CH)
    first = lax.broadcasted_iota(jnp.int32, (count // 16, 8, CH), 1) < 4
    return jnp.where(first, low[:, 0], high[:, 1]).reshape(count // 2, CH)


def repeated(row):
    count = row.shape[0]
    first = lax.broadcasted_iota(jnp.int32, (count, CH), 0) % 8 < 4
    even = jnp.where(first, row, pltpu.roll(row, 4, 0)).reshape(count // 8, 1, 8, CH)
    odd = jnp.where(first, pltpu.roll(row, count - 4, 0), row).reshape(count // 8, 1, 8, CH)
    return jnp.concatenate([even, odd], axis=1).reshape(count * 2, CH)


def aligned(start, size):
    return pl.ds(pl.multiple_of(start, 16), size)


def sides(meta, pair, other):
    even = meta[5] % 2 == 0
    return lax.select(even, other, pair), lax.select(even, pair, other)


def pack_columns_kernel(meta, feat, cot, conv, proj, pair, other, weights, done):
    odd = meta[5] % 2
    pairs = [
        (feat.at[:, aligned(32 - 32 * odd, 32), :], pair.at[:, 0:32, :]),
        (cot.at[:, aligned(48 - 48 * odd, 16), :], pair.at[:, 32:48, :]),
        (feat.at[:, aligned(32 * odd, 32), :], other.at[:, 0:32, :]),
        (cot.at[:, aligned(48 * odd, 16), :], other.at[:, 32:48, :]),
        (proj, weights.at[144:160, :]),
    ] + [(conv.at[t], weights.at[16 * t : 16 * t + 16, :]) for t in range(9)]
    copies = [pltpu.make_async_copy(a, b, done.at[k]) for k, (a, b) in enumerate(pairs)]
    for copy in copies:
        copy.start()
    for copy in copies:
        copy.wait()


def pack_rows_kernel(meta, feat, cot, pair, other, inner, outer, inner_cot, outer_cot, done):
    core = meta[4] % 2
    jobs = []
    for low, first, second in ((1 - core, inner, inner_cot), (core, outer, outer_cot)):
        jobs.append((first, feat, pl.ds(8 * low, 8), 0, 32))
        jobs.append((second, cot, pl.ds(12 * low, 4), 32, 16))
    copies = []
    for k, (out, middle, rows, _, width) in enumerate(jobs):
        copies.append(pltpu.make_async_copy(middle.at[rows], out.at[:, width : width + 64, :], done.at[k]))
        copies[k].start()
    for out, _, rows, first, width in jobs:
        before, after = sides(meta, pair[rows, first : first + width, :], other[rows, first : first + width, :])
        out[:, 0:width, :] = before
        out[:, width + 64 :, :] = after
    for copy in copies:
        copy.wait()


def stack_kernel(*refs):
    out = refs[-1]
    for k, ref in enumerate(refs[:-1]):
        out[k] = ref[...]


def first_rows(meta, row, starts, weight):
    top, left, height, breadth = (meta[0], meta[1], meta[2], meta[3])
    mask = column_mask(left - 8, 128, breadth)
    pre = dot_nn(four_rows(row, [h - 1 for h in starts]), weight)
    out = {}
    for k, value in enumerate(split_rows(pre, starts)):
        h = starts[k // 2] + k % 2
        act = rounded(value * sigmoid(value)) * (mask * row_ok(top - 8 + h, height))
        out[h] = (value, three(act))
    return out


def second_rows(meta, row, starts, weight):
    top, left, height, breadth = (meta[0], meta[1], meta[2], meta[3])
    mask = column_mask(left // 2 - 4, 64, breadth // 2)
    rows = split_rows(dot_nn(four_rows(row, [h - 1 for h in starts]), weight), starts)
    out = {}
    for k, h in enumerate(starts):
        pre = rows[2 * k : 2 * k + 2]
        act = [(v * sigmoid(v)).astype(BF) for v in pre]
        small = rounded(0.25 * pooled_pair(act[0].astype(F32) + act[1].astype(F32)))
        small = small * (mask * row_ok(top // 2 - 4 + h // 2, height // 2))
        out[h] = (pre, act, three(small))
    return out


INNER_FIRST = [9, 11, 13, 15, 17, 19, 21]
INNER_SECOND = [10, 12, 14, 16, 18, 20]


def inner_kernel(
    meta, feat_far, pair, other, w1_far, w2_far,
    feat3, act3, slope1, pool3, slope2, act, weight1, weight2, feat, w1, w2, done,
):
    copies = [
        pltpu.make_async_copy(a, b, done.at[k]) for k, (a, b) in enumerate(((feat_far, feat), (w1_far, w1), (w2_far, w2)))
    ]
    for copy in copies:
        copy.start()
    for copy in copies:
        copy.wait()
    weight1[...] = paired(w1[...], 0)
    weight2[...] = paired(w2[...], 0)
    for k in range(16):
        before, after = sides(meta, pair[k, 0:32, :], other[k, 0:32, :])
        feat3[k] = three(jnp.concatenate([before, feat[k], after], axis=0).astype(F32))
    for h, (pre, wide) in first_rows(meta, lambda h: feat3[h - 8], INNER_FIRST, weight1[...]).items():
        act3[h - 9] = wide
        slope1[h - 9] = slope_of(pre[16:112])
    for h, (pre, value, small) in second_rows(meta, lambda h: act3[h - 9], INNER_SECOND, weight2[...]).items():
        pool3[h // 2 - 5] = small
        for e in range(2):
            slope2[h - 10 + e] = slope_of(pre[e][16:112])
            act[h - 10 + e] = value[e][32:96]


def outer_kernel(
    meta, inner, outer, feat3i, act3i, slope1i, pool3i, slope2i, acti, weight1, weight2,
    pool3, slope1, slope2, act, feat3o, act3o, feat3, act3,
):
    below_at = 24 * (meta[4] % 2)
    for k in range(8):
        feat3[k + below_at] = three(outer[k].astype(F32))
        feat3[k + 24 - below_at] = three(inner[k].astype(F32))
    feat3[8:24] = feat3i[...]
    for starts in ([1, 3, 5, 7], [23, 25, 27, 29]):
        for h, (pre, wide) in first_rows(meta, lambda h: feat3[h], starts, weight1[...]).items():
            act3[h - 1] = wide
            if 7 <= h <= 24:
                slope1[h - 7] = slope_of(pre[16:112])
    slope1[2:16] = slope1i[...]
    act3[8:22] = act3i[...]
    for starts in ([2, 4, 6, 8], [22, 24, 26, 28]):
        for h, (pre, value, small) in second_rows(meta, lambda h: act3[h - 1], starts, weight2[...]).items():
            pool3[h // 2 - 1] = small
            for e in range(2):
                if 6 <= h + e < 26:
                    slope2[h + e - 6] = slope_of(pre[e][16:112])
                if 8 <= h + e < 24:
                    act[h + e - 8] = value[e][32:96]
    pool3[4:10] = pool3i[...]
    slope2[4:16] = slope2i[...]
    act[2:14] = acti[...]
    feat3o[...] = feat3[7:25, 32:96, :]
    act3o[...] = act3[6:24, 32:96, :]


def inner_step(meta, feat, pair, other, w1, w2):
    return call(
        inner_kernel,
        "forward_inner",
        (
            ((16, 128, 384), BF),
            ((14, 128, 384), BF),
            ((14, 96, CH), F32),
            ((6, 64, 384), BF),
            ((12, 96, CH), F32),
            ((12, 64, CH), BF),
            ((1536, 256), BF),
            ((1536, 256), BF),
        ),
        (meta, feat, pair, other, w1, w2),
        (
            ((16, 64, CH), BF),
            ((1152, CH), BF),
            ((1152, CH), BF),
            pltpu.SemaphoreType.DMA((3,)),
        ),
        far=(1, 4, 5),
        limit=24,
        flops=0,
    )


def outer_step(meta, inner, outer, parts):
    return call(
        outer_kernel,
        "forward_outer",
        (
            ((14, 64, 384), BF),
            ((18, 96, CH), F32),
            ((20, 96, CH), F32),
            ((16, 64, CH), BF),
            ((18, 64, 384), BF),
            ((18, 64, 384), BF),
        ),
        (meta, inner, outer) + tuple(parts),
        (((32, 128, 384), BF), ((30, 128, 384), BF)),
        limit=24,
        flops=4 * 10**9,
    )


def coarse_kernel(
    meta, pool3, cot, pair, other, inner, outer, near0, near1, near2, near3, far, act,
    blended, keep, send, pooled_grad, wcat, projs, wide3, projin,
):
    top, left, height, breadth, me = (meta[0], meta[1], meta[2], meta[3], meta[4])
    core = me % 2
    near = (near0, near1, near2, near3)
    for rel in range(16):
        c, x, y = (rel % 2, (rel // 2) % 4, rel // 8)
        place = pl.ds(pl.multiple_of((me ^ rel) * 16, 16), 16)
        source = far.at[x, y] if c else near[x].at[y]
        for t in range(9):
            wcat[place, t * CH : (t + 1) * CH] = source[16 * t : 16 * t + 16, :]
        projs[place, :] = source[144:160, :]
    proj_w = projs[...]

    def pair_sum(a, b):
        return pooled_pair(a.astype(F32) + b.astype(F32))

    below_at = 10 * core
    for k in range(2):
        projin[k + below_at] = pair_sum(outer[2 * k], outer[2 * k + 1])
        projin[k + 10 - below_at] = pair_sum(inner[2 * k], inner[2 * k + 1])

    for k in range(8):
        rows = slice(2 * k, 2 * k + 2)
        before, after = sides(meta, pair[rows, 32:48, :], other[rows, 32:48, :])
        both = jnp.concatenate([before, cot[rows], after], axis=1)
        projin[k + 2] = pair_sum(both[0], both[1])

    proj_in = projin[...].reshape(576, CH)
    proj_in_bf = proj_in.astype(BF)
    lhs = jnp.concatenate([pool3[r : r + 12].reshape(768, 3 * CH) for r in range(3)], axis=1)
    pre = dot_nt(lhs, wcat[...]).reshape(12, 64, WIDE)[:, 8:56].reshape(576, WIDE)
    sigma = sigmoid(pre)
    coarse_act = pre * sigma
    act_grad = dot_nt(proj_in_bf, proj_w)
    grad = rounded(act_grad * (sigma * (1.0 + pre * (1.0 - sigma)))).reshape(12, 48, WIDE)
    mask = column_mask(left // 2 - 2, 48, breadth // 2)
    mask = jnp.concatenate([mask, mask], axis=1)
    grad = masked(grad, mask, top // 2 - 2, height // 2)
    wide3[...] = three(grad.reshape(576, WIDE)).reshape(12, 48, 3 * WIDE)
    own_grad = grad[2:10, 8:40].reshape(256, WIDE).astype(BF)
    own_act = coarse_act.reshape(12, 48, WIDE)[2:10, 8:40].reshape(256, WIDE).astype(BF)
    own_in = proj_in.reshape(12, 48, CH)[2:10, 8:40].reshape(256, CH).astype(BF)

    def emit(first, last, value):
        value = value.reshape(8, 2, 16, CH)
        even, odd = (value[:, 0], value[:, 1])
        keep[:, first:last, :] = jnp.where(core == 0, even, odd).astype(BF)
        send[:, first:last, :] = jnp.where(core == 0, odd, even).astype(BF)

    source = [pool3[2 + r : 10 + r, 16:48, :].reshape(256, 3 * CH) for r in range(3)]
    part = dot_tn(own_grad, jnp.concatenate(source, axis=1))
    for t in range(9):
        emit(16 * t, 16 * t + 16, part[:, t * CH : (t + 1) * CH])
    emit(144, 160, dot_tn(own_act, own_in))
    total = None
    for r in range(3):
        lhs = wide3[r : r + 10].reshape(480, 3 * WIDE)
        first = 3 * (2 - r)
        rhs = jnp.concatenate([wcat[:, (first + 2 - s) * CH : (first + 3 - s) * CH] for s in range(3)], axis=0)
        part = dot_nn(lhs, rhs)
        total = part if total is None else total + part
    pooled_grad[...] = total.reshape(10, 48, CH)
    projected = dot_nn(own_act, proj_w).reshape(8, 32, CH)
    for k in range(8):
        row = repeated(projected[k])
        for e in range(2):
            blended[2 * k + e] = (act[2 * k + e].astype(F32) + row).astype(BF)


def coarse_step(meta, pool3, cot, halo, near, far, act):
    return call(
        coarse_kernel,
        "coarse_step",
        (((16, 64, CH), BF), ((8, 160, CH), BF), ((8, 160, CH), BF), ((10, 48, CH), F32)),
        (meta, pool3, cot) + halo + tuple(near) + (far, act),
        (
            ((WIDE, 9 * CH), BF),
            ((WIDE, CH), BF),
            ((12, 48, 3 * WIDE), BF),
            ((12, 48, CH), F32),
        ),
        limit=20,
        flops=2 * 10**9,
    )


def flipped(weight):
    return jnp.concatenate([weight[8 - t] for t in range(9)], axis=1)


def backward_kernel(
    meta, pooled_grad, cot, pair, other, inner, outer, slope1, slope2, feat3, act3, w2,
    keep, send, first3, second3, grads,
):
    top, left, height, breadth = (meta[0], meta[1], meta[2], meta[3])
    mask = column_mask(left - 4, 96, breadth)

    def second_pair(k, both):
        wide = 0.25 * repeated(pooled_grad[k])
        for e in range(2):
            value = rounded((both[e].astype(F32) + wide) * slope2[2 * k + e])
            second3[2 * k + e] = three(value * (mask * row_ok(top - 2 + 2 * k + e, height)))

    first_core = meta[4] % 2 == 0
    second_pair(0, lax.select(first_core, outer[2:4], inner[2:4]))
    second_pair(9, lax.select(first_core, inner[0:2], outer[0:2]))
    for k in range(8):
        rows = slice(2 * k, 2 * k + 2)
        before, after = sides(meta, pair[rows, 32:48, :], other[rows, 32:48, :])
        second_pair(k + 1, jnp.concatenate([before, cot[rows], after], axis=1))

    def emit(base, parts):
        for r in range(3):
            grads[base + 384 * r : base + 384 * (r + 1), :] = parts[r].astype(BF)

    back_w = paired(flipped(w2), 1)
    for starts in ([0, 2, 4, 6], [8, 10, 12, 14, 16]):
        value = dot_nt(four_rows(lambda h: second3[h], starts), back_w)
        for k, row in enumerate(split_rows(value, starts)):
            h = starts[k // 2] + k % 2
            row = rounded(row * slope1[h]) * (mask * row_ok(top - 1 + h, height))
            first3[h] = three(row)[16:80]
    emit(1152, weight_grad(act3[...], second3[2:18, 16:80, CH : 2 * CH]))
    emit(0, weight_grad(feat3[...], first3[1:17, :, CH : 2 * CH]))
    core = meta[4] % 2
    for k in range(8):
        keep[k] = grads[pl.ds(pl.multiple_of((2 * k + core) * 144, 16), 144), :]
        send[k] = grads[pl.ds(pl.multiple_of((2 * k + 1 - core) * 144, 16), 144), :]


def fine_backward(meta, pooled_grad, cot, halo, slope1, slope2, feat3, act3, w2):
    return call(
        backward_kernel,
        "fine_backward",
        (((8, 144, CH), BF), ((8, 144, CH), BF), ((18, 64, 384), BF)),
        (meta, pooled_grad, cot) + halo + (slope1, slope2, feat3, act3, w2),
        (((20, 96, 384), BF), ((2304, CH), BF)),
        limit=20,
        flops=2 * 10**9,
    )


def feature_kernel(first3, w1, out):
    back_w = paired(flipped(w1), 1)
    for starts in ([0, 2, 4, 6], [8, 10, 12, 14]):
        value = dot_nt(four_rows(lambda h: first3[h], starts), back_w)
        for k, row in enumerate(split_rows(value, starts)):
            out[starts[0] + k] = row.astype(BF)


def feature_step(first3, w1):
    return call(feature_kernel, "feature_step", (((16, 64, CH), BF),), (first3, w1), limit=12, flops=10**9)[0]


def scatter_core_kernel(keep_c, keep_f, got_c, got_f, out):
    for k in range(8):
        out[k, 0:160, :] = (keep_c[k].astype(F32) + got_c[k].astype(F32)).astype(BF)
        out[k, 160:304, :] = (keep_f[k].astype(F32) + got_f[k].astype(F32)).astype(BF)


def scatter_row_kernel(got, out, total):
    value = got[0].astype(F32)
    for k in range(1, 8):
        value = value + got[k].astype(F32)
    total[0:304, :] = value
    total[304:336, :] = jnp.zeros((32, CH), F32)
    for k in range(16):
        out[k] = total[20 * k : 20 * k + 32, :].astype(BF)


def scatter_column_kernel(got, out):
    value = got[0].astype(F32)
    for k in range(1, 16):
        value = value + got[k].astype(F32)
    value = value.astype(BF)
    for k in range(16):
        out[k] = value


def gather_column_kernel(scale, got, conv, proj, fine, total):
    for k in range(16):
        total[20 * k : 20 * k + 32, :] = got[k].astype(F32)
    for k in range(9):
        conv[k] = total[16 * k : 16 * k + 16, :] * scale
    proj[...] = total[144:160, :] * scale
    value = total[160:304, :].astype(BF)
    for k in range(8):
        fine[k] = value


def finish_kernel(scale, meta, mine, other, first, second):
    core = meta[4] % 2
    for at in range(8):
        out = first if at < 4 else second
        a = mine[at].astype(F32) * scale
        b = other[at].astype(F32) * scale
        out[2 * (at % 4)] = jnp.where(core == 0, a, b)
        out[2 * (at % 4) + 1] = jnp.where(core == 0, b, a)


def swap(value, axis, mask):
    count = lax.axis_size(axis)
    return lax.ppermute(value, axis, [(i, i ^ mask) for i in range(count)])


def swap_outer(value, axis):
    count = lax.axis_size(axis)
    pairs = [(i, i + 1 if i % 2 else i - 1) for i in range(1, count - 1)]
    return lax.ppermute(value, axis, pairs)


def exchange_row(value):
    count = lax.axis_size("row")
    groups = [list(range(c, count, 2)) for c in range(2)]
    return lax.all_to_all(value, "row", 0, 0, axis_index_groups=groups, tiled=True)


def exchange_column(value):
    return lax.all_to_all(value, "col", 0, 0, tiled=True)


def after_all(value, *others):
    return lax.optimization_barrier((value,) + others)[0]


def local(features, conv_first, conv_second, coarse_conv, coarse_proj, cotangent):
    rows, cols = (lax.axis_size("row"), lax.axis_size("col"))
    height, breadth = (features.shape[0] * rows, features.shape[1] * cols)
    fine_scale = 1.0 / (height * breadth * features.shape[2]) ** 0.5
    coarse_scale = 2.0 * fine_scale
    me, mine = (lax.axis_index("row"), lax.axis_index("col"))
    fixed = [jnp.int32(height), jnp.int32(breadth)]
    meta = jnp.stack([me * 16, mine * 16] + fixed + [me, mine]).astype(jnp.int32)
    feat = features.reshape(16, 64, CH)
    cot = cotangent.reshape(16, 64, CH)
    conv = coarse_conv.reshape(9, CH, 16).swapaxes(1, 2)
    slab = ((160, CH), BF)

    side = ((16, 48, CH), BF)
    pair, other, own = call(
        pack_columns_kernel,
        "pack_columns",
        (side, side, slab),
        (meta, feat, cot, conv, coarse_proj),
        (pltpu.SemaphoreType.DMA((14,)),),
        far=(1, 2, 3, 4),
    )
    pair = swap(pair, "col", 1)
    other = swap_outer(other, "col")
    near0 = call(stack_kernel, "stack_two", (((2, 160, CH), BF),), (own, swap(own, "row", 8)))[0]
    edge, edge_cot = (((8, 128, CH), BF), ((4, 96, CH), BF))
    inner, outer, inner_cot, outer_cot = call(
        pack_rows_kernel,
        "pack_rows",
        (edge, edge, edge_cot, edge_cot),
        (meta, feat, cot, pair, other),
        (pltpu.SemaphoreType.DMA((4,)),),
        far=(1, 2),
    )
    inner, outer, near0 = lax.optimization_barrier((inner, outer, near0))
    inner = swap(inner, "row", 1)
    outer = swap_outer(outer, "row")
    w1, w2 = (conv_first.reshape(1152, CH), conv_second.reshape(1152, CH))
    pair_in = after_all(pair, near0)
    near = [near0] + [swap(near0, "row", 2 * k) for k in range(1, 4)]
    halo_cot = (pair, other, swap(inner_cot, "row", 1), swap_outer(outer_cot, "row"))
    parts = inner_step(meta, feat, pair_in, other, w1, w2)
    parts, near = lax.optimization_barrier((parts, near))
    far = swap(call(stack_kernel, "stack_eight", (((4, 2, 160, CH), BF),), near)[0], "row", 1)
    pool3, slope1, slope2, act, feat3, act3 = outer_step(meta, inner, outer, parts)
    blended, keep_c, send_c, pooled_grad = coarse_step(meta, pool3, cot, halo_cot, near, far, act)
    got_c = swap(send_c, "row", 1)
    keep_f, send_f, first3 = fine_backward(
        meta, pooled_grad, cot, halo_cot, slope1, slope2, feat3, act3, conv_second.reshape(9, CH, CH)
    )
    got_f = swap(send_f, "row", 1)
    feature_grad = feature_step(first3, conv_first.reshape(9, CH, CH))

    got_f = after_all(got_f, feature_grad)
    part = call(scatter_core_kernel, "scatter_core", (((8, 304, CH), BF),), (keep_c, keep_f, got_c, got_f))[0]
    part = call(
        scatter_row_kernel, "scatter_row", (((16, 32, CH), BF),), (exchange_row(part),), (((336, CH), F32),)
    )[0]
    part = call(scatter_column_kernel, "scatter_column", (((16, 32, CH), BF),), (exchange_column(part),))[0]
    conv_grad, proj_grad, fine = call(
        functools.partial(gather_column_kernel, coarse_scale),
        "gather_column",
        (((9, 16, CH), F32), ((16, CH), F32), ((8, 144, CH), BF)),
        (exchange_column(part),),
        (((336, CH), F32),),
    )
    fine = exchange_row(fine)
    first, second = call(
        functools.partial(finish_kernel, fine_scale),
        "finish",
        (((8, 144, CH), F32), ((8, 144, CH), F32)),
        (meta, fine, swap(fine, "row", 1)),
    )
    shape = features.shape
    return (
        blended.reshape(shape),
        feature_grad.reshape(shape),
        first.reshape(3, 3, CH, CH),
        second.reshape(3, 3, CH, CH),
        conv_grad.reshape(3, 3, 16, CH).swapaxes(2, 3),
        proj_grad,
    )


def solution(mesh):
    in_specs = (
        P("row", "col", None, None),
        P(),
        P(),
        P(None, None, None, "row"),
        P("row", None),
        P("row", "col", None, None),
    )
    out_specs = (
        P("row", "col", None, None),
        P("row", "col", None, None),
        P(),
        P(),
        P(None, None, None, "row"),
        P("row", None),
    )
    return jax.shard_map(local, mesh=mesh, in_specs=in_specs, out_specs=out_specs, check_vma=False)
```

```python
import functools

import jax
import jax.numpy as jnp
from jax import lax
from jax.experimental import pallas as pl
from jax.experimental.pallas import tpu as pltpu
from jax.sharding import PartitionSpec as P

BF = jnp.bfloat16
F32 = jnp.float32
CH = 128
WIDE = 256
MIB = 1024 * 1024
VM = pl.BlockSpec(memory_space=pltpu.VMEM)
SM = pl.BlockSpec(memory_space=pltpu.SMEM)
HBM = pl.BlockSpec(memory_space=pltpu.HBM)


def call(kernel, name, outs, ins, scratch=(), limit=16, flops=0, moved=0, far=()):
    ins = [pltpu.with_memory_space_constraint(v, pltpu.HBM) if k in far else v for k, v in enumerate(ins)]
    shapes = tuple(jax.ShapeDtypeStruct(shape, dtype) for shape, dtype in outs)
    return pl.pallas_call(
        kernel,
        name=name,
        out_shape=shapes,
        in_specs=[HBM if k in far else SM if v.ndim == 1 else VM for k, v in enumerate(ins)],
        out_specs=tuple(VM for _ in outs),
        scratch_shapes=[pltpu.VMEM(*v) if isinstance(v, tuple) else v for v in scratch],
        compiler_params=pltpu.CompilerParams(vmem_limit_bytes=limit * MIB),
        cost_estimate=pl.CostEstimate(flops=flops, bytes_accessed=moved, transcendentals=0),
    )(*ins)


def dot_nn(a, b):
    return jnp.dot(a, b, preferred_element_type=F32)


def dot_nt(a, b):
    return lax.dot_general(a, b, (((1,), (1,)), ((), ())), preferred_element_type=F32)


def dot_tn(a, b):
    return lax.dot_general(a, b, (((0,), (0,)), ((), ())), preferred_element_type=F32)


def sigmoid(value):
    return 0.5 * jnp.tanh(0.5 * value) + 0.5


def slope_of(value):
    sigma = sigmoid(value)
    return sigma * (1.0 + value * (1.0 - sigma))


def rounded(value):
    return value.astype(BF).astype(F32)


def three(value):
    count = value.shape[0]
    left = pltpu.roll(value, 4, 0)
    right = pltpu.roll(value, count - 4, 0)
    return jnp.concatenate([left.astype(BF), value.astype(BF), right.astype(BF)], axis=1)


def paired(weight, axis):
    pad = jnp.zeros((3 * CH, CH) if axis == 0 else (CH, 3 * CH), BF)
    return jnp.concatenate(
        [jnp.concatenate([weight, pad], axis=axis), jnp.concatenate([pad, weight], axis=axis)], axis=1 - axis
    )


def four_rows(row, starts):
    parts = [jnp.concatenate([row(h + k) for h in starts], axis=0) for k in range(4)]
    return jnp.concatenate(parts, axis=1)


def split_rows(value, starts):
    size = value.shape[0] // len(starts)
    out = []
    for k in range(len(starts)):
        out += [value[k * size : (k + 1) * size, e * CH : (e + 1) * CH] for e in range(2)]
    return out


def weight_grad(source, grad):
    gap = jnp.zeros((64, CH), BF)
    parts = []
    for r in range(3):
        parts.append(jnp.concatenate([gap] * r + [grad.reshape(1024, CH)] + [gap] * (2 - r), axis=0))
    whole = dot_tn(source.reshape(1152, 3 * CH), jnp.concatenate(parts, axis=1))
    return [whole[:, r * CH : (r + 1) * CH] for r in range(3)]


def column_mask(first, width, limit):
    place = first + lax.broadcasted_iota(jnp.int32, (width, CH), 0) // 4
    return jnp.where((place >= 0) & (place < limit), 1.0, 0.0).astype(F32)


def row_ok(place, limit):
    return jnp.where((place >= 0) & (place < limit), 1.0, 0.0).astype(F32)


def masked(value, mask, first, limit):
    rows = []
    for k in range(value.shape[0]):
        rows.append((value[k] * (mask * row_ok(first + k, limit)))[None])
    return jnp.concatenate(rows, axis=0)


def pooled_pair(row):
    count = row.shape[0]
    low = (row + pltpu.roll(row, count - 4, 0)).reshape(count // 16, 2, 8, CH)
    high = (row + pltpu.roll(row, 4, 0)).reshape(count // 16, 2, 8, CH)
    first = lax.broadcasted_iota(jnp.int32, (count // 16, 8, CH), 1) < 4
    return jnp.where(first, low[:, 0], high[:, 1]).reshape(count // 2, CH)


def repeated(row):
    count = row.shape[0]
    first = lax.broadcasted_iota(jnp.int32, (count, CH), 0) % 8 < 4
    even = jnp.where(first, row, pltpu.roll(row, 4, 0)).reshape(count // 8, 1, 8, CH)
    odd = jnp.where(first, pltpu.roll(row, count - 4, 0), row).reshape(count // 8, 1, 8, CH)
    return jnp.concatenate([even, odd], axis=1).reshape(count * 2, CH)


def aligned(start, size):
    return pl.ds(pl.multiple_of(start, 16), size)


def sides(meta, pair, other):
    even = meta[5] % 2 == 0
    return lax.select(even, other, pair), lax.select(even, pair, other)


def pack_columns_kernel(meta, feat, cot, conv, proj, pair, other, weights, done):
    odd = meta[5] % 2
    pairs = [
        (feat.at[:, aligned(32 - 32 * odd, 32), :], pair.at[:, 0:32, :]),
        (cot.at[:, aligned(48 - 48 * odd, 16), :], pair.at[:, 32:48, :]),
        (feat.at[:, aligned(32 * odd, 32), :], other.at[:, 0:32, :]),
        (cot.at[:, aligned(48 * odd, 16), :], other.at[:, 32:48, :]),
        (proj, weights.at[144:160, :]),
    ] + [(conv.at[t], weights.at[16 * t : 16 * t + 16, :]) for t in range(9)]
    copies = [pltpu.make_async_copy(a, b, done.at[k]) for k, (a, b) in enumerate(pairs)]
    for copy in copies:
        copy.start()
    for copy in copies:
        copy.wait()


EDGE = 8 * 128 + 4 * 96


def cot_edge(ref, first, count=1):
    value = ref[1024 + 96 * first : 1024 + 96 * (first + count), :]
    return value if count == 1 else value.reshape(count, 96, CH)


def pack_rows_kernel(meta, feat, cot, pair, other, inner, outer, done):
    core = meta[4] % 2
    jobs = []
    for low, out in ((1 - core, inner), (core, outer)):
        jobs += [(out, 128 * k, feat, 8 * low + k, 0, 32) for k in range(8)]
        jobs += [(out, 1024 + 96 * k, cot, 12 * low + k, 32, 16) for k in range(4)]
    copies = []
    for k, (out, base, middle, row, _, width) in enumerate(jobs):
        copies.append(pltpu.make_async_copy(middle.at[row], out.at[base + width : base + width + 64, :], done.at[k]))
        copies[k].start()
    for out, base, _, row, first, width in jobs:
        before, after = sides(meta, pair[row, first : first + width, :], other[row, first : first + width, :])
        out[base : base + width, :] = before
        out[base + width + 64 : base + 2 * width + 64, :] = after
    for copy in copies:
        copy.wait()


def stack_kernel(*refs):
    out = refs[-1]
    for k, ref in enumerate(refs[:-1]):
        out[k] = ref[...]


def first_rows(meta, row, starts, weight):
    top, left, height, breadth = (meta[0], meta[1], meta[2], meta[3])
    mask = column_mask(left - 8, 128, breadth)
    pre = dot_nn(four_rows(row, [h - 1 for h in starts]), weight)
    out = {}
    for k, value in enumerate(split_rows(pre, starts)):
        h = starts[k // 2] + k % 2
        act = rounded(value * sigmoid(value)) * (mask * row_ok(top - 8 + h, height))
        out[h] = (value, three(act))
    return out


def second_rows(meta, row, starts, weight):
    top, left, height, breadth = (meta[0], meta[1], meta[2], meta[3])
    mask = column_mask(left // 2 - 4, 64, breadth // 2)
    rows = split_rows(dot_nn(four_rows(row, [h - 1 for h in starts]), weight), starts)
    out = {}
    for k, h in enumerate(starts):
        pre = rows[2 * k : 2 * k + 2]
        act = [(v * sigmoid(v)).astype(BF) for v in pre]
        small = rounded(0.25 * pooled_pair(act[0].astype(F32) + act[1].astype(F32)))
        small = small * (mask * row_ok(top // 2 - 4 + h // 2, height // 2))
        out[h] = (pre, act, three(small))
    return out


INNER_FIRST = [9, 11, 13, 15, 17, 19, 21]
INNER_SECOND = [10, 12, 14, 16, 18, 20]


def inner_kernel(
    meta, feat_far, pair, other, w1_far, w2_far,
    feat3, act3, slope1, pool3, slope2, act, weight1, weight2, feat, w1, w2, done,
):
    copies = [
        pltpu.make_async_copy(a, b, done.at[k]) for k, (a, b) in enumerate(((feat_far, feat), (w1_far, w1), (w2_far, w2)))
    ]
    for copy in copies:
        copy.start()
    for copy in copies:
        copy.wait()
    weight1[...] = paired(w1[...], 0)
    weight2[...] = paired(w2[...], 0)
    for k in range(16):
        before, after = sides(meta, pair[k, 0:32, :], other[k, 0:32, :])
        feat3[k] = three(jnp.concatenate([before, feat[k], after], axis=0).astype(F32))
    for h, (pre, wide) in first_rows(meta, lambda h: feat3[h - 8], INNER_FIRST, weight1[...]).items():
        act3[h - 9] = wide
        slope1[h - 9] = slope_of(pre[16:112])
    for h, (pre, value, small) in second_rows(meta, lambda h: act3[h - 9], INNER_SECOND, weight2[...]).items():
        pool3[h // 2 - 5] = small
        for e in range(2):
            slope2[h - 10 + e] = slope_of(pre[e][16:112])
            act[h - 10 + e] = value[e][32:96]


def outer_kernel(
    meta, inner, outer, feat3i, act3i, slope1i, pool3i, slope2i, acti, weight1, weight2,
    pool3, slope1, slope2, act, feat3o, act3o, feat3, act3,
):
    below_at = 24 * (meta[4] % 2)
    for k in range(8):
        feat3[k + below_at] = three(outer[128 * k : 128 * k + 128, :].astype(F32))
        feat3[k + 24 - below_at] = three(inner[128 * k : 128 * k + 128, :].astype(F32))
    feat3[8:24] = feat3i[...]
    for starts in ([1, 3, 5, 7], [23, 25, 27, 29]):
        for h, (pre, wide) in first_rows(meta, lambda h: feat3[h], starts, weight1[...]).items():
            act3[h - 1] = wide
            if 7 <= h <= 24:
                slope1[h - 7] = slope_of(pre[16:112])
    slope1[2:16] = slope1i[...]
    act3[8:22] = act3i[...]
    for starts in ([2, 4, 6, 8], [22, 24, 26, 28]):
        for h, (pre, value, small) in second_rows(meta, lambda h: act3[h - 1], starts, weight2[...]).items():
            pool3[h // 2 - 1] = small
            for e in range(2):
                if 6 <= h + e < 26:
                    slope2[h + e - 6] = slope_of(pre[e][16:112])
                if 8 <= h + e < 24:
                    act[h + e - 8] = value[e][32:96]
    pool3[4:10] = pool3i[...]
    slope2[4:16] = slope2i[...]
    act[2:14] = acti[...]
    feat3o[...] = feat3[7:25, 32:96, :]
    act3o[...] = act3[6:24, 32:96, :]


def inner_step(meta, feat, pair, other, w1, w2):
    return call(
        inner_kernel,
        "forward_inner",
        (
            ((16, 128, 384), BF),
            ((14, 128, 384), BF),
            ((14, 96, CH), F32),
            ((6, 64, 384), BF),
            ((12, 96, CH), F32),
            ((12, 64, CH), BF),
            ((1536, 256), BF),
            ((1536, 256), BF),
        ),
        (meta, feat, pair, other, w1, w2),
        (
            ((16, 64, CH), BF),
            ((1152, CH), BF),
            ((1152, CH), BF),
            pltpu.SemaphoreType.DMA((3,)),
        ),
        far=(1, 4, 5),
        limit=24,
        flops=0,
    )


def outer_step(meta, inner, outer, parts):
    return call(
        outer_kernel,
        "forward_outer",
        (
            ((14, 64, 384), BF),
            ((18, 96, CH), F32),
            ((20, 96, CH), F32),
            ((16, 64, CH), BF),
            ((18, 64, 384), BF),
            ((18, 64, 384), BF),
        ),
        (meta, inner, outer) + tuple(parts),
        (((32, 128, 384), BF), ((30, 128, 384), BF)),
        limit=24,
        flops=4 * 10**9,
    )


def coarse_kernel(
    meta, pool3, cot, pair, other, inner, outer, near0, near1, near2, near3, far, act,
    blended, keep, send, pooled_grad, wcat, projs, wide3, projin,
):
    top, left, height, breadth, me = (meta[0], meta[1], meta[2], meta[3], meta[4])
    core = me % 2
    near = (near0, near1, near2, near3)
    for rel in range(16):
        c, x, y = (rel % 2, (rel // 2) % 4, rel // 8)
        place = pl.ds(pl.multiple_of((me ^ rel) * 16, 16), 16)
        source = far.at[x, y] if c else near[x].at[y]
        for t in range(9):
            wcat[place, t * CH : (t + 1) * CH] = source[16 * t : 16 * t + 16, :]
        projs[place, :] = source[144:160, :]
    proj_w = projs[...]

    def pair_sum(a, b):
        return pooled_pair(a.astype(F32) + b.astype(F32))

    below_at = 10 * core
    for k in range(2):
        projin[k + below_at] = pair_sum(cot_edge(outer, 2 * k), cot_edge(outer, 2 * k + 1))
        projin[k + 10 - below_at] = pair_sum(cot_edge(inner, 2 * k), cot_edge(inner, 2 * k + 1))

    for k in range(8):
        rows = slice(2 * k, 2 * k + 2)
        before, after = sides(meta, pair[rows, 32:48, :], other[rows, 32:48, :])
        both = jnp.concatenate([before, cot[rows], after], axis=1)
        projin[k + 2] = pair_sum(both[0], both[1])

    proj_in = projin[...].reshape(576, CH)
    proj_in_bf = proj_in.astype(BF)
    lhs = jnp.concatenate([pool3[r : r + 12].reshape(768, 3 * CH) for r in range(3)], axis=1)
    pre = dot_nt(lhs, wcat[...]).reshape(12, 64, WIDE)[:, 8:56].reshape(576, WIDE)
    sigma = sigmoid(pre)
    coarse_act = pre * sigma
    act_grad = dot_nt(proj_in_bf, proj_w)
    grad = rounded(act_grad * (sigma * (1.0 + pre * (1.0 - sigma)))).reshape(12, 48, WIDE)
    mask = column_mask(left // 2 - 2, 48, breadth // 2)
    mask = jnp.concatenate([mask, mask], axis=1)
    grad = masked(grad, mask, top // 2 - 2, height // 2)
    wide3[...] = three(grad.reshape(576, WIDE)).reshape(12, 48, 3 * WIDE)
    own_grad = grad[2:10, 8:40].reshape(256, WIDE).astype(BF)
    own_act = coarse_act.reshape(12, 48, WIDE)[2:10, 8:40].reshape(256, WIDE).astype(BF)
    own_in = proj_in.reshape(12, 48, CH)[2:10, 8:40].reshape(256, CH).astype(BF)

    def emit(first, last, value):
        value = value.reshape(8, 2, 16, CH)
        even, odd = (value[:, 0], value[:, 1])
        keep[:, first:last, :] = jnp.where(core == 0, even, odd).astype(BF)
        send[:, first:last, :] = jnp.where(core == 0, odd, even).astype(BF)

    source = [pool3[2 + r : 10 + r, 16:48, :].reshape(256, 3 * CH) for r in range(3)]
    part = dot_tn(own_grad, jnp.concatenate(source, axis=1))
    for t in range(9):
        emit(16 * t, 16 * t + 16, part[:, t * CH : (t + 1) * CH])
    emit(144, 160, dot_tn(own_act, own_in))
    total = None
    for r in range(3):
        lhs = wide3[r : r + 10].reshape(480, 3 * WIDE)
        first = 3 * (2 - r)
        rhs = jnp.concatenate([wcat[:, (first + 2 - s) * CH : (first + 3 - s) * CH] for s in range(3)], axis=0)
        part = dot_nn(lhs, rhs)
        total = part if total is None else total + part
    pooled_grad[...] = total.reshape(10, 48, CH)
    projected = dot_nn(own_act, proj_w).reshape(8, 32, CH)
    for k in range(8):
        row = repeated(projected[k])
        for e in range(2):
            blended[2 * k + e] = (act[2 * k + e].astype(F32) + row).astype(BF)


def coarse_step(meta, pool3, cot, halo, near, far, act):
    return call(
        coarse_kernel,
        "coarse_step",
        (((16, 64, CH), BF), ((8, 160, CH), BF), ((8, 160, CH), BF), ((10, 48, CH), F32)),
        (meta, pool3, cot) + halo + tuple(near) + (far, act),
        (
            ((WIDE, 9 * CH), BF),
            ((WIDE, CH), BF),
            ((12, 48, 3 * WIDE), BF),
            ((12, 48, CH), F32),
        ),
        limit=20,
        flops=2 * 10**9,
    )


def flipped(weight):
    return jnp.concatenate([weight[8 - t] for t in range(9)], axis=1)


def backward_kernel(
    meta, pooled_grad, cot, pair, other, inner, outer, slope1, slope2, feat3, act3, w2,
    keep, send, first3, second3, grads,
):
    top, left, height, breadth = (meta[0], meta[1], meta[2], meta[3])
    mask = column_mask(left - 4, 96, breadth)

    def second_pair(k, both):
        wide = 0.25 * repeated(pooled_grad[k])
        for e in range(2):
            value = rounded((both[e].astype(F32) + wide) * slope2[2 * k + e])
            second3[2 * k + e] = three(value * (mask * row_ok(top - 2 + 2 * k + e, height)))

    first_core = meta[4] % 2 == 0
    second_pair(0, lax.select(first_core, cot_edge(outer, 2, 2), cot_edge(inner, 2, 2)))
    second_pair(9, lax.select(first_core, cot_edge(inner, 0, 2), cot_edge(outer, 0, 2)))
    for k in range(8):
        rows = slice(2 * k, 2 * k + 2)
        before, after = sides(meta, pair[rows, 32:48, :], other[rows, 32:48, :])
        second_pair(k + 1, jnp.concatenate([before, cot[rows], after], axis=1))

    def emit(base, parts):
        for r in range(3):
            grads[base + 384 * r : base + 384 * (r + 1), :] = parts[r].astype(BF)

    back_w = paired(flipped(w2), 1)
    for starts in ([0, 2, 4, 6], [8, 10, 12, 14, 16]):
        value = dot_nt(four_rows(lambda h: second3[h], starts), back_w)
        for k, row in enumerate(split_rows(value, starts)):
            h = starts[k // 2] + k % 2
            row = rounded(row * slope1[h]) * (mask * row_ok(top - 1 + h, height))
            first3[h] = three(row)[16:80]
    emit(1152, weight_grad(act3[...], second3[2:18, 16:80, CH : 2 * CH]))
    emit(0, weight_grad(feat3[...], first3[1:17, :, CH : 2 * CH]))
    core = meta[4] % 2
    for k in range(8):
        keep[k] = grads[pl.ds(pl.multiple_of((2 * k + core) * 144, 16), 144), :]
        send[k] = grads[pl.ds(pl.multiple_of((2 * k + 1 - core) * 144, 16), 144), :]


def fine_backward(meta, pooled_grad, cot, halo, slope1, slope2, feat3, act3, w2):
    return call(
        backward_kernel,
        "fine_backward",
        (((8, 144, CH), BF), ((8, 144, CH), BF), ((18, 64, 384), BF)),
        (meta, pooled_grad, cot) + halo + (slope1, slope2, feat3, act3, w2),
        (((20, 96, 384), BF), ((2304, CH), BF)),
        limit=20,
        flops=2 * 10**9,
    )


def feature_kernel(first3, w1, out):
    back_w = paired(flipped(w1), 1)
    for starts in ([0, 2, 4, 6], [8, 10, 12, 14]):
        value = dot_nt(four_rows(lambda h: first3[h], starts), back_w)
        for k, row in enumerate(split_rows(value, starts)):
            out[starts[0] + k] = row.astype(BF)


def feature_step(first3, w1):
    return call(feature_kernel, "feature_step", (((16, 64, CH), BF),), (first3, w1), limit=12, flops=10**9)[0]


def scatter_core_kernel(keep_c, keep_f, got_c, got_f, out):
    for k in range(8):
        out[k, 0:160, :] = (keep_c[k].astype(F32) + got_c[k].astype(F32)).astype(BF)
        out[k, 160:304, :] = (keep_f[k].astype(F32) + got_f[k].astype(F32)).astype(BF)


def scatter_row_kernel(got, out, total):
    value = got[0].astype(F32)
    for k in range(1, 8):
        value = value + got[k].astype(F32)
    total[0:304, :] = value
    total[304:336, :] = jnp.zeros((32, CH), F32)
    for k in range(16):
        out[k] = total[20 * k : 20 * k + 32, :].astype(BF)


def scatter_column_kernel(got, out):
    value = got[0].astype(F32)
    for k in range(1, 16):
        value = value + got[k].astype(F32)
    value = value.astype(BF)
    for k in range(16):
        out[k] = value


def gather_column_kernel(scale, got, conv, proj, fine, total):
    for k in range(16):
        total[20 * k : 20 * k + 32, :] = got[k].astype(F32)
    for k in range(9):
        conv[k] = total[16 * k : 16 * k + 16, :] * scale
    proj[...] = total[144:160, :] * scale
    value = total[160:304, :].astype(BF)
    for k in range(8):
        fine[k] = value


def finish_kernel(scale, meta, mine, other, first, second):
    core = meta[4] % 2
    for at in range(8):
        out = first if at < 4 else second
        a = mine[at].astype(F32) * scale
        b = other[at].astype(F32) * scale
        out[2 * (at % 4)] = jnp.where(core == 0, a, b)
        out[2 * (at % 4) + 1] = jnp.where(core == 0, b, a)


def swap(value, axis, mask):
    count = lax.axis_size(axis)
    return lax.ppermute(value, axis, [(i, i ^ mask) for i in range(count)])


def swap_outer(value, axis):
    count = lax.axis_size(axis)
    pairs = [(i, i + 1 if i % 2 else i - 1) for i in range(1, count - 1)]
    return lax.ppermute(value, axis, pairs)


def exchange_row(value):
    count = lax.axis_size("row")
    groups = [list(range(c, count, 2)) for c in range(2)]
    return lax.all_to_all(value, "row", 0, 0, axis_index_groups=groups, tiled=True)


def exchange_column(value):
    return lax.all_to_all(value, "col", 0, 0, tiled=True)


def after_all(value, *others):
    return lax.optimization_barrier((value,) + others)[0]


def local(features, conv_first, conv_second, coarse_conv, coarse_proj, cotangent):
    rows, cols = (lax.axis_size("row"), lax.axis_size("col"))
    height, breadth = (features.shape[0] * rows, features.shape[1] * cols)
    fine_scale = 1.0 / (height * breadth * features.shape[2]) ** 0.5
    coarse_scale = 2.0 * fine_scale
    me, mine = (lax.axis_index("row"), lax.axis_index("col"))
    fixed = [jnp.int32(height), jnp.int32(breadth)]
    meta = jnp.stack([me * 16, mine * 16] + fixed + [me, mine]).astype(jnp.int32)
    feat = features.reshape(16, 64, CH)
    cot = cotangent.reshape(16, 64, CH)
    conv = coarse_conv.reshape(9, CH, 16).swapaxes(1, 2)
    slab = ((160, CH), BF)

    side = ((16, 48, CH), BF)
    pair, other, own = call(
        pack_columns_kernel,
        "pack_columns",
        (side, side, slab),
        (meta, feat, cot, conv, coarse_proj),
        (pltpu.SemaphoreType.DMA((14,)),),
        far=(1, 2, 3, 4),
    )
    pair = swap(pair, "col", 1)
    other = swap_outer(other, "col")
    near0 = call(stack_kernel, "stack_two", (((2, 160, CH), BF),), (own, swap(own, "row", 8)))[0]
    edge = ((EDGE, CH), BF)
    inner, outer = call(
        pack_rows_kernel,
        "pack_rows",
        (edge, edge),
        (meta, feat, cot, pair, other),
        (pltpu.SemaphoreType.DMA((24,)),),
        far=(1, 2),
    )
    inner, outer, near0 = lax.optimization_barrier((inner, outer, near0))
    inner = swap(inner, "row", 1)
    outer = swap_outer(outer, "row")
    w1, w2 = (conv_first.reshape(1152, CH), conv_second.reshape(1152, CH))
    pair_in = after_all(pair, near0)
    near = [near0] + [swap(near0, "row", 2 * k) for k in range(1, 4)]
    parts = inner_step(meta, feat, pair_in, other, w1, w2)
    parts, near = lax.optimization_barrier((parts, near))
    far = swap(call(stack_kernel, "stack_eight", (((4, 2, 160, CH), BF),), near)[0], "row", 1)
    pool3, slope1, slope2, act, feat3, act3 = outer_step(meta, inner, outer, parts)
    blended, keep_c, send_c, pooled_grad = coarse_step(meta, pool3, cot, (pair, other, inner, outer), near, far, act)
    got_c = swap(send_c, "row", 1)
    keep_f, send_f, first3 = fine_backward(
        meta, pooled_grad, cot, (pair, other, inner, outer), slope1, slope2, feat3, act3, conv_second.reshape(9, CH, CH)
    )
    got_f = swap(send_f, "row", 1)
    feature_grad = feature_step(first3, conv_first.reshape(9, CH, CH))

    got_f = after_all(got_f, feature_grad)
    part = call(scatter_core_kernel, "scatter_core", (((8, 304, CH), BF),), (keep_c, keep_f, got_c, got_f))[0]
    part = call(
        scatter_row_kernel, "scatter_row", (((16, 32, CH), BF),), (exchange_row(part),), (((336, CH), F32),)
    )[0]
    part = call(scatter_column_kernel, "scatter_column", (((16, 32, CH), BF),), (exchange_column(part),))[0]
    conv_grad, proj_grad, fine = call(
        functools.partial(gather_column_kernel, coarse_scale),
        "gather_column",
        (((9, 16, CH), F32), ((16, CH), F32), ((8, 144, CH), BF)),
        (exchange_column(part),),
        (((336, CH), F32),),
    )
    fine = exchange_row(fine)
    first, second = call(
        functools.partial(finish_kernel, fine_scale),
        "finish",
        (((8, 144, CH), F32), ((8, 144, CH), F32)),
        (meta, fine, swap(fine, "row", 1)),
    )
    shape = features.shape
    return (
        blended.reshape(shape),
        feature_grad.reshape(shape),
        first.reshape(3, 3, CH, CH),
        second.reshape(3, 3, CH, CH),
        conv_grad.reshape(3, 3, 16, CH).swapaxes(2, 3),
        proj_grad,
    )


def solution(mesh):
    in_specs = (
        P("row", "col", None, None),
        P(),
        P(),
        P(None, None, None, "row"),
        P("row", None),
        P("row", "col", None, None),
    )
    out_specs = (
        P("row", "col", None, None),
        P("row", "col", None, None),
        P(),
        P(),
        P(None, None, None, "row"),
        P("row", None),
    )
    return jax.shard_map(local, mesh=mesh, in_specs=in_specs, out_specs=out_specs, check_vma=False)
```

```python
import functools

import jax
import jax.numpy as jnp
from jax import lax
from jax.experimental import pallas as pl
from jax.experimental.pallas import tpu as pltpu
from jax.sharding import PartitionSpec as P

BF = jnp.bfloat16
F32 = jnp.float32
CH = 128
WIDE = 256
MIB = 1024 * 1024
VM = pl.BlockSpec(memory_space=pltpu.VMEM)
SM = pl.BlockSpec(memory_space=pltpu.SMEM)
HBM = pl.BlockSpec(memory_space=pltpu.HBM)


def call(kernel, name, outs, ins, scratch=(), limit=16, flops=0, moved=0, far=()):
    ins = [pltpu.with_memory_space_constraint(v, pltpu.HBM) if k in far else v for k, v in enumerate(ins)]
    shapes = tuple(jax.ShapeDtypeStruct(shape, dtype) for shape, dtype in outs)
    return pl.pallas_call(
        kernel,
        name=name,
        out_shape=shapes,
        in_specs=[HBM if k in far else SM if v.ndim == 1 else VM for k, v in enumerate(ins)],
        out_specs=tuple(VM for _ in outs),
        scratch_shapes=[pltpu.VMEM(*v) if isinstance(v, tuple) else v for v in scratch],
        compiler_params=pltpu.CompilerParams(vmem_limit_bytes=limit * MIB),
        cost_estimate=pl.CostEstimate(flops=flops, bytes_accessed=moved, transcendentals=0),
    )(*ins)


def dot_nn(a, b):
    return jnp.dot(a, b, preferred_element_type=F32)


def dot_nt(a, b):
    return lax.dot_general(a, b, (((1,), (1,)), ((), ())), preferred_element_type=F32)


def dot_tn(a, b):
    return lax.dot_general(a, b, (((0,), (0,)), ((), ())), preferred_element_type=F32)


def sigmoid(value):
    return 0.5 * jnp.tanh(0.5 * value) + 0.5


def slope_of(value):
    sigma = sigmoid(value)
    return sigma * (1.0 + value * (1.0 - sigma))


def rounded(value):
    return value.astype(BF).astype(F32)


def three(value):
    count = value.shape[0]
    left = pltpu.roll(value, 4, 0)
    right = pltpu.roll(value, count - 4, 0)
    return jnp.concatenate([left.astype(BF), value.astype(BF), right.astype(BF)], axis=1)


def paired(weight, axis):
    pad = jnp.zeros((3 * CH, CH) if axis == 0 else (CH, 3 * CH), BF)
    return jnp.concatenate(
        [jnp.concatenate([weight, pad], axis=axis), jnp.concatenate([pad, weight], axis=axis)], axis=1 - axis
    )


def flipped(weight):
    return jnp.concatenate([weight[(8 - t) * CH : (9 - t) * CH, :] for t in range(9)], axis=1)


def four_rows(row, starts):
    parts = [jnp.concatenate([row(h + k) for h in starts], axis=0) for k in range(4)]
    return jnp.concatenate(parts, axis=1)


def split_rows(value, starts):
    size = value.shape[0] // len(starts)
    out = []
    for k in range(len(starts)):
        out += [value[k * size : (k + 1) * size, e * CH : (e + 1) * CH] for e in range(2)]
    return out


def weight_grad(source, grad):
    gap = jnp.zeros((64, CH), BF)
    parts = []
    for r in range(3):
        parts.append(jnp.concatenate([gap] * r + [grad.reshape(1024, CH)] + [gap] * (2 - r), axis=0))
    whole = dot_tn(source.reshape(1152, 3 * CH), jnp.concatenate(parts, axis=1))
    return [whole[:, r * CH : (r + 1) * CH] for r in range(3)]


def column_mask(first, width, limit):
    place = first + lax.broadcasted_iota(jnp.int32, (width, CH), 0) // 4
    return jnp.where((place >= 0) & (place < limit), 1.0, 0.0).astype(F32)


def row_ok(place, limit):
    return jnp.where((place >= 0) & (place < limit), 1.0, 0.0).astype(F32)


def masked(value, mask, first, limit):
    rows = []
    for k in range(value.shape[0]):
        rows.append((value[k] * (mask * row_ok(first + k, limit)))[None])
    return jnp.concatenate(rows, axis=0)


def pooled_pair(row):
    count = row.shape[0]
    low = (row + pltpu.roll(row, count - 4, 0)).reshape(count // 16, 2, 8, CH)
    high = (row + pltpu.roll(row, 4, 0)).reshape(count // 16, 2, 8, CH)
    first = lax.broadcasted_iota(jnp.int32, (count // 16, 8, CH), 1) < 4
    return jnp.where(first, low[:, 0], high[:, 1]).reshape(count // 2, CH)


def repeated(row):
    count = row.shape[0]
    first = lax.broadcasted_iota(jnp.int32, (count, CH), 0) % 8 < 4
    even = jnp.where(first, row, pltpu.roll(row, 4, 0)).reshape(count // 8, 1, 8, CH)
    odd = jnp.where(first, pltpu.roll(row, count - 4, 0), row).reshape(count // 8, 1, 8, CH)
    return jnp.concatenate([even, odd], axis=1).reshape(count * 2, CH)


def aligned(start, size):
    return pl.ds(pl.multiple_of(start, 16), size)


def sides(meta, pair, other):
    even = meta[5] % 2 == 0
    return lax.select(even, other, pair), lax.select(even, pair, other)


def pack_columns_kernel(meta, feat, cot, conv, proj, pair, other, weights, done):
    odd = meta[5] % 2
    pairs = [
        (feat.at[:, aligned(32 - 32 * odd, 32), :], pair.at[:, 0:32, :]),
        (cot.at[:, aligned(48 - 48 * odd, 16), :], pair.at[:, 32:48, :]),
        (feat.at[:, aligned(32 * odd, 32), :], other.at[:, 0:32, :]),
        (cot.at[:, aligned(48 * odd, 16), :], other.at[:, 32:48, :]),
        (proj, weights.at[144:160, :]),
    ] + [(conv.at[t], weights.at[16 * t : 16 * t + 16, :]) for t in range(9)]
    copies = [pltpu.make_async_copy(a, b, done.at[k]) for k, (a, b) in enumerate(pairs)]
    for copy in copies:
        copy.start()
    for copy in copies:
        copy.wait()


EDGE = 8 * 128 + 4 * 96


def cot_edge(ref, first, count=1):
    value = ref[1024 + 96 * first : 1024 + 96 * (first + count), :]
    return value if count == 1 else value.reshape(count, 96, CH)


def prepare_kernel(feat_far, cot_far, w1_far, w2_far, feat, cot, weight1, weight2, back1, back2, w1, w2, done):
    pairs = ((w1_far, w1), (w2_far, w2), (feat_far, feat), (cot_far, cot))
    copies = [pltpu.make_async_copy(a, b, done.at[k]) for k, (a, b) in enumerate(pairs)]
    for copy in copies:
        copy.start()
    for k, (w, weight, back) in enumerate(((w1, weight1, back1), (w2, weight2, back2))):
        copies[k].wait()
        weight[...] = paired(w[...], 0)
        back[...] = paired(flipped(w), 1)
    for copy in copies[2:]:
        copy.wait()


def pack_rows_kernel(meta, feat, cot, pair, other, inner, outer):
    core = meta[4] % 2
    for low, out in ((1 - core, inner), (core, outer)):
        jobs = [(128 * k, feat, 8 * low + k, 0, 32) for k in range(8)]
        jobs += [(1024 + 96 * k, cot, 12 * low + k, 32, 16) for k in range(4)]
        for base, middle, row, first, width in jobs:
            before, after = sides(meta, pair[row, first : first + width, :], other[row, first : first + width, :])
            out[base : base + width, :] = before
            out[base + width : base + width + 64, :] = middle[row]
            out[base + width + 64 : base + 2 * width + 64, :] = after


def stack_kernel(*refs):
    out = refs[-1]
    for k, ref in enumerate(refs[:-1]):
        out[k] = ref[...]


def first_rows(meta, row, starts, weight):
    top, left, height, breadth = (meta[0], meta[1], meta[2], meta[3])
    mask = column_mask(left - 8, 128, breadth)
    pre = dot_nn(four_rows(row, [h - 1 for h in starts]), weight)
    out = {}
    for k, value in enumerate(split_rows(pre, starts)):
        h = starts[k // 2] + k % 2
        act = rounded(value * sigmoid(value)) * (mask * row_ok(top - 8 + h, height))
        out[h] = (value, three(act))
    return out


def second_rows(meta, row, starts, weight):
    top, left, height, breadth = (meta[0], meta[1], meta[2], meta[3])
    mask = column_mask(left // 2 - 4, 64, breadth // 2)
    rows = split_rows(dot_nn(four_rows(row, [h - 1 for h in starts]), weight), starts)
    out = {}
    for k, h in enumerate(starts):
        pre = rows[2 * k : 2 * k + 2]
        act = [(v * sigmoid(v)).astype(BF) for v in pre]
        small = rounded(0.25 * pooled_pair(act[0].astype(F32) + act[1].astype(F32)))
        small = small * (mask * row_ok(top // 2 - 4 + h // 2, height // 2))
        out[h] = (pre, act, three(small))
    return out


INNER_FIRST = [9, 11, 13, 15, 17, 19, 21]
INNER_SECOND = [10, 12, 14, 16, 18, 20]


def inner_kernel(meta, feat, pair, other, weight1, weight2, feat3, act3, slope1, pool3, slope2, act):
    for k in range(16):
        before, after = sides(meta, pair[k, 0:32, :], other[k, 0:32, :])
        feat3[k] = three(jnp.concatenate([before, feat[k], after], axis=0).astype(F32))
    for h, (pre, wide) in first_rows(meta, lambda h: feat3[h - 8], INNER_FIRST, weight1[...]).items():
        act3[h - 9] = wide
        slope1[h - 9] = slope_of(pre[16:112])
    for h, (pre, value, small) in second_rows(meta, lambda h: act3[h - 9], INNER_SECOND, weight2[...]).items():
        pool3[h // 2 - 5] = small
        for e in range(2):
            slope2[h - 10 + e] = slope_of(pre[e][16:112])
            act[h - 10 + e] = value[e][32:96]


def outer_kernel(
    meta, inner, outer, feat3i, act3i, slope1i, pool3i, slope2i, acti, weight1, weight2,
    pool3, slope1, slope2, act, feat3o, act3o, feat3, act3,
):
    below_at = 24 * (meta[4] % 2)
    for k in range(8):
        feat3[k + below_at] = three(outer[128 * k : 128 * k + 128, :].astype(F32))
        feat3[k + 24 - below_at] = three(inner[128 * k : 128 * k + 128, :].astype(F32))
    feat3[8:24] = feat3i[...]
    for starts in ([1, 3, 5, 7], [23, 25, 27, 29]):
        for h, (pre, wide) in first_rows(meta, lambda h: feat3[h], starts, weight1[...]).items():
            act3[h - 1] = wide
            if 7 <= h <= 24:
                slope1[h - 7] = slope_of(pre[16:112])
    slope1[2:16] = slope1i[...]
    act3[8:22] = act3i[...]
    for starts in ([2, 4, 6, 8], [22, 24, 26, 28]):
        for h, (pre, value, small) in second_rows(meta, lambda h: act3[h - 1], starts, weight2[...]).items():
            pool3[h // 2 - 1] = small
            for e in range(2):
                if 6 <= h + e < 26:
                    slope2[h + e - 6] = slope_of(pre[e][16:112])
                if 8 <= h + e < 24:
                    act[h + e - 8] = value[e][32:96]
    pool3[4:10] = pool3i[...]
    slope2[4:16] = slope2i[...]
    act[2:14] = acti[...]
    feat3o[...] = feat3[7:25, 32:96, :]
    act3o[...] = act3[6:24, 32:96, :]


def inner_step(meta, feat, pair, other, weight1, weight2):
    return call(
        inner_kernel,
        "forward_inner",
        (
            ((16, 128, 384), BF),
            ((14, 128, 384), BF),
            ((14, 96, CH), F32),
            ((6, 64, 384), BF),
            ((12, 96, CH), F32),
            ((12, 64, CH), BF),
        ),
        (meta, feat, pair, other, weight1, weight2),
        limit=24,
        flops=0,
    )


def outer_step(meta, inner, outer, parts, weight1, weight2):
    return call(
        outer_kernel,
        "forward_outer",
        (
            ((14, 64, 384), BF),
            ((18, 96, CH), F32),
            ((20, 96, CH), F32),
            ((16, 64, CH), BF),
            ((18, 64, 384), BF),
            ((18, 64, 384), BF),
        ),
        (meta, inner, outer) + tuple(parts) + (weight1, weight2),
        (((32, 128, 384), BF), ((30, 128, 384), BF)),
        limit=24,
        flops=4 * 10**9,
    )


def coarse_kernel(
    meta, pool3, cot, pair, other, inner, outer, near0, near1, near2, near3, far,
    own, projs_out, keep, send, pooled_grad, wcat, projs, wide3, projin,
):
    top, left, height, breadth, me = (meta[0], meta[1], meta[2], meta[3], meta[4])
    core = me % 2
    near = (near0, near1, near2, near3)
    for rel in range(16):
        c, x, y = (rel % 2, (rel // 2) % 4, rel // 8)
        place = pl.ds(pl.multiple_of((me ^ rel) * 16, 16), 16)
        source = far.at[x, y] if c else near[x].at[y]
        for t in range(9):
            wcat[place, t * CH : (t + 1) * CH] = source[16 * t : 16 * t + 16, :]
        projs[place, :] = source[144:160, :]
    proj_w = projs[...]

    def pair_sum(a, b):
        return pooled_pair(a.astype(F32) + b.astype(F32))

    below_at = 10 * core
    for k in range(2):
        projin[k + below_at] = pair_sum(cot_edge(outer, 2 * k), cot_edge(outer, 2 * k + 1))
        projin[k + 10 - below_at] = pair_sum(cot_edge(inner, 2 * k), cot_edge(inner, 2 * k + 1))

    for k in range(8):
        rows = slice(2 * k, 2 * k + 2)
        before, after = sides(meta, pair[rows, 32:48, :], other[rows, 32:48, :])
        both = jnp.concatenate([before, cot[rows], after], axis=1)
        projin[k + 2] = pair_sum(both[0], both[1])

    proj_in = projin[...].reshape(576, CH)
    proj_in_bf = proj_in.astype(BF)
    lhs = jnp.concatenate([pool3[r : r + 12].reshape(768, 3 * CH) for r in range(3)], axis=1)
    pre = dot_nt(lhs, wcat[...]).reshape(12, 64, WIDE)[:, 8:56].reshape(576, WIDE)
    sigma = sigmoid(pre)
    coarse_act = pre * sigma
    act_grad = dot_nt(proj_in_bf, proj_w)
    grad = rounded(act_grad * (sigma * (1.0 + pre * (1.0 - sigma)))).reshape(12, 48, WIDE)
    mask = column_mask(left // 2 - 2, 48, breadth // 2)
    mask = jnp.concatenate([mask, mask], axis=1)
    grad = masked(grad, mask, top // 2 - 2, height // 2)
    wide3[...] = three(grad.reshape(576, WIDE)).reshape(12, 48, 3 * WIDE)
    own_grad = grad[2:10, 8:40].reshape(256, WIDE).astype(BF)
    own_act = coarse_act.reshape(12, 48, WIDE)[2:10, 8:40].reshape(256, WIDE).astype(BF)
    own_in = proj_in.reshape(12, 48, CH)[2:10, 8:40].reshape(256, CH).astype(BF)

    def emit(first, last, value):
        value = value.reshape(8, 2, 16, CH)
        even, odd = (value[:, 0], value[:, 1])
        keep[:, first:last, :] = jnp.where(core == 0, even, odd).astype(BF)
        send[:, first:last, :] = jnp.where(core == 0, odd, even).astype(BF)

    source = [pool3[2 + r : 10 + r, 16:48, :].reshape(256, 3 * CH) for r in range(3)]
    part = dot_tn(own_grad, jnp.concatenate(source, axis=1))
    for t in range(9):
        emit(16 * t, 16 * t + 16, part[:, t * CH : (t + 1) * CH])
    emit(144, 160, dot_tn(own_act, own_in))
    total = None
    for r in range(3):
        lhs = wide3[r : r + 10].reshape(480, 3 * WIDE)
        first = 3 * (2 - r)
        rhs = jnp.concatenate([wcat[:, (first + 2 - s) * CH : (first + 3 - s) * CH] for s in range(3)], axis=0)
        part = dot_nn(lhs, rhs)
        total = part if total is None else total + part
    pooled_grad[...] = total.reshape(10, 48, CH)
    own[...] = own_act
    projs_out[...] = proj_w


def blend_kernel(own, proj, act, blended):
    projected = dot_nn(own[...], proj[...]).reshape(8, 32, CH)
    for k in range(8):
        row = repeated(projected[k])
        for e in range(2):
            blended[2 * k + e] = (act[2 * k + e].astype(F32) + row).astype(BF)


def coarse_step(meta, pool3, cot, halo, near, far):
    return call(
        coarse_kernel,
        "coarse_step",
        (((256, WIDE), BF), ((WIDE, CH), BF), ((8, 160, CH), BF), ((8, 160, CH), BF), ((10, 48, CH), F32)),
        (meta, pool3, cot) + halo + tuple(near) + (far,),
        (
            ((WIDE, 9 * CH), BF),
            ((WIDE, CH), BF),
            ((12, 48, 3 * WIDE), BF),
            ((12, 48, CH), F32),
        ),
        limit=20,
        flops=2 * 10**9,
    )


def backward_kernel(
    meta, pooled_grad, cot, pair, other, inner, outer, slope1, slope2, feat3, act3, back_w,
    keep, send, first3, second3, grads,
):
    top, left, height, breadth = (meta[0], meta[1], meta[2], meta[3])
    mask = column_mask(left - 4, 96, breadth)

    def second_pair(k, both):
        wide = 0.25 * repeated(pooled_grad[k])
        for e in range(2):
            value = rounded((both[e].astype(F32) + wide) * slope2[2 * k + e])
            second3[2 * k + e] = three(value * (mask * row_ok(top - 2 + 2 * k + e, height)))

    first_core = meta[4] % 2 == 0
    second_pair(0, lax.select(first_core, cot_edge(outer, 2, 2), cot_edge(inner, 2, 2)))
    second_pair(9, lax.select(first_core, cot_edge(inner, 0, 2), cot_edge(outer, 0, 2)))
    for k in range(8):
        rows = slice(2 * k, 2 * k + 2)
        before, after = sides(meta, pair[rows, 32:48, :], other[rows, 32:48, :])
        second_pair(k + 1, jnp.concatenate([before, cot[rows], after], axis=1))

    def emit(base, parts):
        for r in range(3):
            grads[base + 384 * r : base + 384 * (r + 1), :] = parts[r].astype(BF)

    for starts in ([0, 2, 4, 6], [8, 10, 12, 14, 16]):
        value = dot_nt(four_rows(lambda h: second3[h], starts), back_w[...])
        for k, row in enumerate(split_rows(value, starts)):
            h = starts[k // 2] + k % 2
            row = rounded(row * slope1[h]) * (mask * row_ok(top - 1 + h, height))
            first3[h] = three(row)[16:80]
    emit(1152, weight_grad(act3[...], second3[2:18, 16:80, CH : 2 * CH]))
    emit(0, weight_grad(feat3[...], first3[1:17, :, CH : 2 * CH]))
    core = meta[4] % 2
    for k in range(8):
        keep[k] = grads[pl.ds(pl.multiple_of((2 * k + core) * 144, 16), 144), :]
        send[k] = grads[pl.ds(pl.multiple_of((2 * k + 1 - core) * 144, 16), 144), :]


def fine_backward(meta, pooled_grad, cot, halo, slope1, slope2, feat3, act3, back_w):
    return call(
        backward_kernel,
        "fine_backward",
        (((8, 144, CH), BF), ((8, 144, CH), BF), ((18, 64, 384), BF)),
        (meta, pooled_grad, cot) + halo + (slope1, slope2, feat3, act3, back_w),
        (((20, 96, 384), BF), ((2304, CH), BF)),
        limit=20,
        flops=2 * 10**9,
    )


def feature_kernel(first3, back_w, out):
    for starts in ([0, 2, 4, 6], [8, 10, 12, 14]):
        value = dot_nt(four_rows(lambda h: first3[h], starts), back_w[...])
        for k, row in enumerate(split_rows(value, starts)):
            out[starts[0] + k] = row.astype(BF)


def feature_step(first3, back_w):
    return call(feature_kernel, "feature_step", (((16, 64, CH), BF),), (first3, back_w), limit=12, flops=10**9)[0]


def scatter_core_kernel(keep_c, keep_f, got_c, got_f, out):
    for k in range(8):
        out[k, 0:160, :] = (keep_c[k].astype(F32) + got_c[k].astype(F32)).astype(BF)
        out[k, 160:304, :] = (keep_f[k].astype(F32) + got_f[k].astype(F32)).astype(BF)


def scatter_row_kernel(got, out, total):
    value = got[0].astype(F32)
    for k in range(1, 8):
        value = value + got[k].astype(F32)
    total[0:304, :] = value
    total[304:336, :] = jnp.zeros((32, CH), F32)
    for k in range(16):
        out[k] = total[20 * k : 20 * k + 32, :].astype(BF)


def scatter_column_kernel(got, out):
    value = got[0].astype(F32)
    for k in range(1, 16):
        value = value + got[k].astype(F32)
    value = value.astype(BF)
    for k in range(16):
        out[k] = value


def gather_column_kernel(scale, got, conv, proj, fine, total):
    for k in range(16):
        total[20 * k : 20 * k + 32, :] = got[k].astype(F32)
    for k in range(9):
        conv[k] = total[16 * k : 16 * k + 16, :] * scale
    proj[...] = total[144:160, :] * scale
    value = total[160:304, :].astype(BF)
    for k in range(8):
        fine[k] = value


def finish_kernel(scale, meta, mine, other, first, second):
    core = meta[4] % 2
    for at in range(8):
        out = first if at < 4 else second
        a = mine[at].astype(F32) * scale
        b = other[at].astype(F32) * scale
        out[2 * (at % 4)] = jnp.where(core == 0, a, b)
        out[2 * (at % 4) + 1] = jnp.where(core == 0, b, a)


def swap(value, axis, mask):
    count = lax.axis_size(axis)
    return lax.ppermute(value, axis, [(i, i ^ mask) for i in range(count)])


def swap_outer(value, axis):
    count = lax.axis_size(axis)
    pairs = [(i, i + 1 if i % 2 else i - 1) for i in range(1, count - 1)]
    return lax.ppermute(value, axis, pairs)


def exchange_row(value):
    count = lax.axis_size("row")
    groups = [list(range(c, count, 2)) for c in range(2)]
    return lax.all_to_all(value, "row", 0, 0, axis_index_groups=groups, tiled=True)


def exchange_column(value):
    return lax.all_to_all(value, "col", 0, 0, tiled=True)


def after_all(value, *others):
    return lax.optimization_barrier((value,) + others)[0]


def local(features, conv_first, conv_second, coarse_conv, coarse_proj, cotangent):
    rows, cols = (lax.axis_size("row"), lax.axis_size("col"))
    height, breadth = (features.shape[0] * rows, features.shape[1] * cols)
    fine_scale = 1.0 / (height * breadth * features.shape[2]) ** 0.5
    coarse_scale = 2.0 * fine_scale
    me, mine = (lax.axis_index("row"), lax.axis_index("col"))
    fixed = [jnp.int32(height), jnp.int32(breadth)]
    meta = jnp.stack([me * 16, mine * 16] + fixed + [me, mine]).astype(jnp.int32)
    feat = features.reshape(16, 64, CH)
    cot = cotangent.reshape(16, 64, CH)
    conv = coarse_conv.reshape(9, CH, 16).swapaxes(1, 2)
    slab = ((160, CH), BF)

    side = ((16, 48, CH), BF)
    pair, other, own = call(
        pack_columns_kernel,
        "pack_columns",
        (side, side, slab),
        (meta, feat, cot, conv, coarse_proj),
        (pltpu.SemaphoreType.DMA((14,)),),
        far=(1, 2, 3, 4),
    )
    w1, w2 = (conv_first.reshape(1152, CH), conv_second.reshape(1152, CH))
    big, wide = (((16, 64, CH), BF), ((1536, 256), BF))
    feat_in, cot_in, weight1, weight2, back1, back2 = call(
        prepare_kernel,
        "prepare",
        (big, big, wide, wide, ((256, 1536), BF), ((256, 1536), BF)),
        (after_all(feat, own), cot, w1, w2),
        (((1152, CH), BF), ((1152, CH), BF), pltpu.SemaphoreType.DMA((4,))),
        far=(0, 1, 2, 3),
        flops=4 * 10**9,
    )
    pair = swap(pair, "col", 1)
    other = swap_outer(other, "col")
    near0 = call(stack_kernel, "stack_two", (((2, 160, CH), BF),), (own, swap(own, "row", 8)))[0]
    inner, outer = call(
        pack_rows_kernel, "pack_rows", (((EDGE, CH), BF),) * 2, (meta, feat_in, cot_in, pair, other)
    )
    inner, outer, near0 = lax.optimization_barrier((inner, outer, near0))
    inner = swap(inner, "row", 1)
    outer = swap_outer(outer, "row")
    pair_in = after_all(pair, near0)
    near = [near0] + [swap(near0, "row", 2 * k) for k in range(1, 4)]
    parts = inner_step(meta, feat_in, pair_in, other, weight1, weight2)
    parts, near = lax.optimization_barrier((parts, near))
    far = swap(call(stack_kernel, "stack_eight", (((4, 2, 160, CH), BF),), near)[0], "row", 1)
    pool3, slope1, slope2, act, feat3, act3 = outer_step(meta, inner, outer, parts, weight1, weight2)
    halo = (pair, other, inner, outer)
    own_act, proj, keep_c, send_c, pooled_grad = coarse_step(meta, pool3, cot_in, halo, near, far)
    got_c = swap(send_c, "row", 1)
    keep_f, send_f, first3 = fine_backward(
        meta, pooled_grad, cot_in, halo, slope1, slope2, feat3, act3, back2
    )
    got_f = swap(send_f, "row", 1)
    feature_grad = feature_step(first3, back1)

    got_f = after_all(got_f, feature_grad)
    part = call(scatter_core_kernel, "scatter_core", (((8, 304, CH), BF),), (keep_c, keep_f, got_c, got_f))[0]
    part = call(
        scatter_row_kernel, "scatter_row", (((16, 32, CH), BF),), (exchange_row(part),), (((336, CH), F32),)
    )[0]
    part = call(scatter_column_kernel, "scatter_column", (((16, 32, CH), BF),), (exchange_column(part),))[0]
    conv_grad, proj_grad, fine = call(
        functools.partial(gather_column_kernel, coarse_scale),
        "gather_column",
        (((9, 16, CH), F32), ((16, CH), F32), ((8, 144, CH), BF)),
        (exchange_column(part),),
        (((336, CH), F32),),
    )
    fine = exchange_row(fine)
    blended = call(blend_kernel, "blend", (((16, 64, CH), BF),), (after_all(own_act, fine), proj, act), flops=10**9)[0]
    other = after_all(swap(fine, "row", 1), blended)
    first, second = call(
        functools.partial(finish_kernel, fine_scale),
        "finish",
        (((8, 144, CH), F32), ((8, 144, CH), F32)),
        (meta, fine, other),
    )
    shape = features.shape
    return (
        blended.reshape(shape),
        feature_grad.reshape(shape),
        first.reshape(3, 3, CH, CH),
        second.reshape(3, 3, CH, CH),
        conv_grad.reshape(3, 3, 16, CH).swapaxes(2, 3),
        proj_grad,
    )


def solution(mesh):
    in_specs = (
        P("row", "col", None, None),
        P(),
        P(),
        P(None, None, None, "row"),
        P("row", None),
        P("row", "col", None, None),
    )
    out_specs = (
        P("row", "col", None, None),
        P("row", "col", None, None),
        P(),
        P(),
        P(None, None, None, "row"),
        P("row", None),
    )
    return jax.shard_map(local, mesh=mesh, in_specs=in_specs, out_specs=out_specs, check_vma=False)
```

```python
import functools

import jax
import jax.numpy as jnp
from jax import lax
from jax.experimental import pallas as pl
from jax.experimental.pallas import tpu as pltpu
from jax.sharding import PartitionSpec as P

BF = jnp.bfloat16
F32 = jnp.float32
CH = 128
WIDE = 256
MIB = 1024 * 1024
VM = pl.BlockSpec(memory_space=pltpu.VMEM)
SM = pl.BlockSpec(memory_space=pltpu.SMEM)
HBM = pl.BlockSpec(memory_space=pltpu.HBM)


def call(kernel, name, outs, ins, scratch=(), limit=16, flops=0, moved=0, far=()):
    ins = [pltpu.with_memory_space_constraint(v, pltpu.HBM) if k in far else v for k, v in enumerate(ins)]
    shapes = tuple(jax.ShapeDtypeStruct(shape, dtype) for shape, dtype in outs)
    return pl.pallas_call(
        kernel,
        name=name,
        out_shape=shapes,
        in_specs=[HBM if k in far else SM if v.ndim == 1 else VM for k, v in enumerate(ins)],
        out_specs=tuple(VM for _ in outs),
        scratch_shapes=[pltpu.VMEM(*v) if isinstance(v, tuple) else v for v in scratch],
        compiler_params=pltpu.CompilerParams(vmem_limit_bytes=limit * MIB),
        cost_estimate=pl.CostEstimate(flops=flops, bytes_accessed=moved, transcendentals=0),
    )(*ins)


def dot_nn(a, b):
    return jnp.dot(a, b, preferred_element_type=F32)


def dot_nt(a, b):
    return lax.dot_general(a, b, (((1,), (1,)), ((), ())), preferred_element_type=F32)


def dot_tn(a, b):
    return lax.dot_general(a, b, (((0,), (0,)), ((), ())), preferred_element_type=F32)


def sigmoid(value):
    return 0.5 * jnp.tanh(0.5 * value) + 0.5


def slope_of(value):
    sigma = sigmoid(value)
    return sigma * (1.0 + value * (1.0 - sigma))


def rounded(value):
    return value.astype(BF).astype(F32)


def three(value):
    count = value.shape[0]
    left = pltpu.roll(value, 4, 0)
    right = pltpu.roll(value, count - 4, 0)
    return jnp.concatenate([left.astype(BF), value.astype(BF), right.astype(BF)], axis=1)


def paired(weight, axis):
    pad = jnp.zeros((3 * CH, CH) if axis == 0 else (CH, 3 * CH), BF)
    return jnp.concatenate(
        [jnp.concatenate([weight, pad], axis=axis), jnp.concatenate([pad, weight], axis=axis)], axis=1 - axis
    )


def flipped(weight):
    return jnp.concatenate([weight[(8 - t) * CH : (9 - t) * CH, :] for t in range(9)], axis=1)


def four_rows(row, starts):
    parts = [jnp.concatenate([row(h + k) for h in starts], axis=0) for k in range(4)]
    return jnp.concatenate(parts, axis=1)


def split_rows(value, starts):
    size = value.shape[0] // len(starts)
    out = []
    for k in range(len(starts)):
        out += [value[k * size : (k + 1) * size, e * CH : (e + 1) * CH] for e in range(2)]
    return out


def weight_grad(source, grad):
    gap = jnp.zeros((64, CH), BF)
    parts = []
    for r in range(3):
        parts.append(jnp.concatenate([gap] * r + [grad.reshape(1024, CH)] + [gap] * (2 - r), axis=0))
    whole = dot_tn(source.reshape(1152, 3 * CH), jnp.concatenate(parts, axis=1))
    return [whole[:, r * CH : (r + 1) * CH] for r in range(3)]


def column_mask(first, width, limit):
    place = first + lax.broadcasted_iota(jnp.int32, (width, CH), 0) // 4
    return jnp.where((place >= 0) & (place < limit), 1.0, 0.0).astype(F32)


def row_ok(place, limit):
    return jnp.where((place >= 0) & (place < limit), 1.0, 0.0).astype(F32)


def masked(value, mask, first, limit):
    rows = []
    for k in range(value.shape[0]):
        rows.append((value[k] * (mask * row_ok(first + k, limit)))[None])
    return jnp.concatenate(rows, axis=0)


def pooled_pair(row):
    count = row.shape[0]
    low = (row + pltpu.roll(row, count - 4, 0)).reshape(count // 16, 2, 8, CH)
    high = (row + pltpu.roll(row, 4, 0)).reshape(count // 16, 2, 8, CH)
    first = lax.broadcasted_iota(jnp.int32, (count // 16, 8, CH), 1) < 4
    return jnp.where(first, low[:, 0], high[:, 1]).reshape(count // 2, CH)


def repeated(row):
    count = row.shape[0]
    first = lax.broadcasted_iota(jnp.int32, (count, CH), 0) % 8 < 4
    even = jnp.where(first, row, pltpu.roll(row, 4, 0)).reshape(count // 8, 1, 8, CH)
    odd = jnp.where(first, pltpu.roll(row, count - 4, 0), row).reshape(count // 8, 1, 8, CH)
    return jnp.concatenate([even, odd], axis=1).reshape(count * 2, CH)


def aligned(start, size):
    return pl.ds(pl.multiple_of(start, 16), size)


def sides(meta, pair, other):
    even = meta[5] % 2 == 0
    return lax.select(even, other, pair), lax.select(even, pair, other)


def pack_columns_kernel(meta, feat, cot, conv, proj, pair, other, weights, done):
    odd = meta[5] % 2
    pairs = [
        (feat.at[:, aligned(32 - 32 * odd, 32), :], pair.at[:, 0:32, :]),
        (cot.at[:, aligned(48 - 48 * odd, 16), :], pair.at[:, 32:48, :]),
        (feat.at[:, aligned(32 * odd, 32), :], other.at[:, 0:32, :]),
        (cot.at[:, aligned(48 * odd, 16), :], other.at[:, 32:48, :]),
        (proj, weights.at[144:160, :]),
    ] + [(conv.at[t], weights.at[16 * t : 16 * t + 16, :]) for t in range(9)]
    copies = [pltpu.make_async_copy(a, b, done.at[k]) for k, (a, b) in enumerate(pairs)]
    for copy in copies:
        copy.start()
    for copy in copies:
        copy.wait()


EDGE = 8 * 128 + 4 * 96


def cot_edge(ref, first, count=1):
    value = ref[1024 + 96 * first : 1024 + 96 * (first + count), :]
    return value if count == 1 else value.reshape(count, 96, CH)


def bring_kernel(feat_far, cot_far, feat, cot, done):
    copies = [
        pltpu.make_async_copy(a, b, done.at[k]) for k, (a, b) in enumerate(((feat_far, feat), (cot_far, cot)))
    ]
    for copy in copies:
        copy.start()
    for copy in copies:
        copy.wait()


def weights_kernel(w1_far, w2_far, weight1, weight2, back1, back2, w1, w2, done):
    copies = [pltpu.make_async_copy(a, b, done.at[k]) for k, (a, b) in enumerate(((w1_far, w1), (w2_far, w2)))]
    for copy in copies:
        copy.start()
    for copy, w, weight, back in zip(copies, (w1, w2), (weight1, weight2), (back1, back2)):
        copy.wait()
        weight[...] = paired(w[...], 0)
        back[...] = paired(flipped(w), 1)


def pack_rows_kernel(meta, feat, cot, pair, other, own, far, inner, outer, both):
    core = meta[4] % 2
    for low, out in ((1 - core, inner), (core, outer)):
        jobs = [(128 * k, feat, 8 * low + k, 0, 32) for k in range(8)]
        jobs += [(1024 + 96 * k, cot, 12 * low + k, 32, 16) for k in range(4)]
        for base, middle, row, first, width in jobs:
            before, after = sides(meta, pair[row, first : first + width, :], other[row, first : first + width, :])
            out[base : base + width, :] = before
            out[base + width : base + width + 64, :] = middle[row]
            out[base + width + 64 : base + 2 * width + 64, :] = after
    both[0] = own[...]
    both[1] = far[...]


def stack_kernel(*refs):
    out = refs[-1]
    for k, ref in enumerate(refs[:-1]):
        out[k] = ref[...]


def first_rows(meta, row, starts, weight):
    top, left, height, breadth = (meta[0], meta[1], meta[2], meta[3])
    mask = column_mask(left - 8, 128, breadth)
    pre = dot_nn(four_rows(row, [h - 1 for h in starts]), weight)
    out = {}
    for k, value in enumerate(split_rows(pre, starts)):
        h = starts[k // 2] + k % 2
        act = rounded(value * sigmoid(value)) * (mask * row_ok(top - 8 + h, height))
        out[h] = (value, three(act))
    return out


def second_rows(meta, row, starts, weight):
    top, left, height, breadth = (meta[0], meta[1], meta[2], meta[3])
    mask = column_mask(left // 2 - 4, 64, breadth // 2)
    rows = split_rows(dot_nn(four_rows(row, [h - 1 for h in starts]), weight), starts)
    out = {}
    for k, h in enumerate(starts):
        pre = rows[2 * k : 2 * k + 2]
        act = [(v * sigmoid(v)).astype(BF) for v in pre]
        small = rounded(0.25 * pooled_pair(act[0].astype(F32) + act[1].astype(F32)))
        small = small * (mask * row_ok(top // 2 - 4 + h // 2, height // 2))
        out[h] = (pre, act, three(small))
    return out


INNER_FIRST = [9, 11, 13, 15, 17, 19, 21]
INNER_SECOND = [10, 12, 14, 16, 18, 20]


def inner_kernel(meta, feat, pair, other, weight1, weight2, feat3, act3, slope1, pool3, slope2, act):
    for k in range(16):
        before, after = sides(meta, pair[k, 0:32, :], other[k, 0:32, :])
        feat3[k] = three(jnp.concatenate([before, feat[k], after], axis=0).astype(F32))
    for h, (pre, wide) in first_rows(meta, lambda h: feat3[h - 8], INNER_FIRST, weight1[...]).items():
        act3[h - 9] = wide
        slope1[h - 9] = slope_of(pre[16:112])
    for h, (pre, value, small) in second_rows(meta, lambda h: act3[h - 9], INNER_SECOND, weight2[...]).items():
        pool3[h // 2 - 5] = small
        for e in range(2):
            slope2[h - 10 + e] = slope_of(pre[e][16:112])
            act[h - 10 + e] = value[e][32:96]


def outer_kernel(
    meta, inner, outer, feat3i, act3i, slope1i, pool3i, slope2i, acti, weight1, weight2,
    pool3, slope1, slope2, act, feat3o, act3o, feat3, act3,
):
    below_at = 24 * (meta[4] % 2)
    for k in range(8):
        feat3[k + below_at] = three(outer[128 * k : 128 * k + 128, :].astype(F32))
        feat3[k + 24 - below_at] = three(inner[128 * k : 128 * k + 128, :].astype(F32))
    feat3[8:24] = feat3i[...]
    for starts in ([1, 3, 5, 7], [23, 25, 27, 29]):
        for h, (pre, wide) in first_rows(meta, lambda h: feat3[h], starts, weight1[...]).items():
            act3[h - 1] = wide
            if 7 <= h <= 24:
                slope1[h - 7] = slope_of(pre[16:112])
    slope1[2:16] = slope1i[...]
    act3[8:22] = act3i[...]
    for starts in ([2, 4, 6, 8], [22, 24, 26, 28]):
        for h, (pre, value, small) in second_rows(meta, lambda h: act3[h - 1], starts, weight2[...]).items():
            pool3[h // 2 - 1] = small
            for e in range(2):
                if 6 <= h + e < 26:
                    slope2[h + e - 6] = slope_of(pre[e][16:112])
                if 8 <= h + e < 24:
                    act[h + e - 8] = value[e][32:96]
    pool3[4:10] = pool3i[...]
    slope2[4:16] = slope2i[...]
    act[2:14] = acti[...]
    feat3o[...] = feat3[7:25, 32:96, :]
    act3o[...] = act3[6:24, 32:96, :]


def inner_step(meta, feat, pair, other, weight1, weight2):
    return call(
        inner_kernel,
        "forward_inner",
        (
            ((16, 128, 384), BF),
            ((14, 128, 384), BF),
            ((14, 96, CH), F32),
            ((6, 64, 384), BF),
            ((12, 96, CH), F32),
            ((12, 64, CH), BF),
        ),
        (meta, feat, pair, other, weight1, weight2),
        limit=24,
        flops=0,
    )


def outer_step(meta, inner, outer, parts, weight1, weight2):
    return call(
        outer_kernel,
        "forward_outer",
        (
            ((14, 64, 384), BF),
            ((18, 96, CH), F32),
            ((20, 96, CH), F32),
            ((16, 64, CH), BF),
            ((18, 64, 384), BF),
            ((18, 64, 384), BF),
        ),
        (meta, inner, outer) + tuple(parts) + (weight1, weight2),
        (((32, 128, 384), BF), ((30, 128, 384), BF)),
        limit=24,
        flops=4 * 10**9,
    )


def coarse_kernel(
    meta, pool3, cot, pair, other, inner, outer, near0, near1, near2, near3, far,
    own, projs_out, keep, send, pooled_grad, wcat, projs, wide3, projin,
):
    top, left, height, breadth, me = (meta[0], meta[1], meta[2], meta[3], meta[4])
    core = me % 2
    near = (near0, near1, near2, near3)
    for rel in range(16):
        c, x, y = (rel % 2, (rel // 2) % 4, rel // 8)
        place = pl.ds(pl.multiple_of((me ^ rel) * 16, 16), 16)
        source = far.at[x, y] if c else near[x].at[y]
        for t in range(9):
            wcat[place, t * CH : (t + 1) * CH] = source[16 * t : 16 * t + 16, :]
        projs[place, :] = source[144:160, :]
    proj_w = projs[...]

    def pair_sum(a, b):
        return pooled_pair(a.astype(F32) + b.astype(F32))

    below_at = 10 * core
    for k in range(2):
        projin[k + below_at] = pair_sum(cot_edge(outer, 2 * k), cot_edge(outer, 2 * k + 1))
        projin[k + 10 - below_at] = pair_sum(cot_edge(inner, 2 * k), cot_edge(inner, 2 * k + 1))

    for k in range(8):
        rows = slice(2 * k, 2 * k + 2)
        before, after = sides(meta, pair[rows, 32:48, :], other[rows, 32:48, :])
        both = jnp.concatenate([before, cot[rows], after], axis=1)
        projin[k + 2] = pair_sum(both[0], both[1])

    proj_in = projin[...].reshape(576, CH)
    proj_in_bf = proj_in.astype(BF)
    lhs = jnp.concatenate([pool3[r : r + 12].reshape(768, 3 * CH) for r in range(3)], axis=1)
    pre = dot_nt(lhs, wcat[...]).reshape(12, 64, WIDE)[:, 8:56].reshape(576, WIDE)
    sigma = sigmoid(pre)
    coarse_act = pre * sigma
    act_grad = dot_nt(proj_in_bf, proj_w)
    grad = rounded(act_grad * (sigma * (1.0 + pre * (1.0 - sigma)))).reshape(12, 48, WIDE)
    mask = column_mask(left // 2 - 2, 48, breadth // 2)
    mask = jnp.concatenate([mask, mask], axis=1)
    grad = masked(grad, mask, top // 2 - 2, height // 2)
    wide3[...] = three(grad.reshape(576, WIDE)).reshape(12, 48, 3 * WIDE)
    own_grad = grad[2:10, 8:40].reshape(256, WIDE).astype(BF)
    own_act = coarse_act.reshape(12, 48, WIDE)[2:10, 8:40].reshape(256, WIDE).astype(BF)
    own_in = proj_in.reshape(12, 48, CH)[2:10, 8:40].reshape(256, CH).astype(BF)

    def emit(first, last, value):
        value = value.reshape(8, 2, 16, CH)
        even, odd = (value[:, 0], value[:, 1])
        keep[:, first:last, :] = jnp.where(core == 0, even, odd).astype(BF)
        send[:, first:last, :] = jnp.where(core == 0, odd, even).astype(BF)

    source = [pool3[2 + r : 10 + r, 16:48, :].reshape(256, 3 * CH) for r in range(3)]
    part = dot_tn(own_grad, jnp.concatenate(source, axis=1))
    for t in range(9):
        emit(16 * t, 16 * t + 16, part[:, t * CH : (t + 1) * CH])
    emit(144, 160, dot_tn(own_act, own_in))
    total = None
    for r in range(3):
        lhs = wide3[r : r + 10].reshape(480, 3 * WIDE)
        first = 3 * (2 - r)
        rhs = jnp.concatenate([wcat[:, (first + 2 - s) * CH : (first + 3 - s) * CH] for s in range(3)], axis=0)
        part = dot_nn(lhs, rhs)
        total = part if total is None else total + part
    pooled_grad[...] = total.reshape(10, 48, CH)
    own[...] = own_act
    projs_out[...] = proj_w


def blend_kernel(own, proj, act, blended):
    projected = dot_nn(own[...], proj[...]).reshape(8, 32, CH)
    for k in range(8):
        row = repeated(projected[k])
        for e in range(2):
            blended[2 * k + e] = (act[2 * k + e].astype(F32) + row).astype(BF)


def coarse_step(meta, pool3, cot, halo, near, far):
    return call(
        coarse_kernel,
        "coarse_step",
        (((256, WIDE), BF), ((WIDE, CH), BF), ((8, 160, CH), BF), ((8, 160, CH), BF), ((10, 48, CH), F32)),
        (meta, pool3, cot) + halo + tuple(near) + (far,),
        (
            ((WIDE, 9 * CH), BF),
            ((WIDE, CH), BF),
            ((12, 48, 3 * WIDE), BF),
            ((12, 48, CH), F32),
        ),
        limit=20,
        flops=2 * 10**9,
    )


def backward_kernel(
    meta, pooled_grad, cot, pair, other, inner, outer, slope1, slope2, feat3, act3, back_w,
    keep, send, first3, second3, grads,
):
    top, left, height, breadth = (meta[0], meta[1], meta[2], meta[3])
    mask = column_mask(left - 4, 96, breadth)

    def second_pair(k, both):
        wide = 0.25 * repeated(pooled_grad[k])
        for e in range(2):
            value = rounded((both[e].astype(F32) + wide) * slope2[2 * k + e])
            second3[2 * k + e] = three(value * (mask * row_ok(top - 2 + 2 * k + e, height)))

    first_core = meta[4] % 2 == 0
    second_pair(0, lax.select(first_core, cot_edge(outer, 2, 2), cot_edge(inner, 2, 2)))
    second_pair(9, lax.select(first_core, cot_edge(inner, 0, 2), cot_edge(outer, 0, 2)))
    for k in range(8):
        rows = slice(2 * k, 2 * k + 2)
        before, after = sides(meta, pair[rows, 32:48, :], other[rows, 32:48, :])
        second_pair(k + 1, jnp.concatenate([before, cot[rows], after], axis=1))

    def emit(base, parts):
        for r in range(3):
            grads[base + 384 * r : base + 384 * (r + 1), :] = parts[r].astype(BF)

    for starts in ([0, 2, 4, 6], [8, 10, 12, 14, 16]):
        value = dot_nt(four_rows(lambda h: second3[h], starts), back_w[...])
        for k, row in enumerate(split_rows(value, starts)):
            h = starts[k // 2] + k % 2
            row = rounded(row * slope1[h]) * (mask * row_ok(top - 1 + h, height))
            first3[h] = three(row)[16:80]
    emit(1152, weight_grad(act3[...], second3[2:18, 16:80, CH : 2 * CH]))
    emit(0, weight_grad(feat3[...], first3[1:17, :, CH : 2 * CH]))
    core = meta[4] % 2
    for k in range(8):
        keep[k] = grads[pl.ds(pl.multiple_of((2 * k + core) * 144, 16), 144), :]
        send[k] = grads[pl.ds(pl.multiple_of((2 * k + 1 - core) * 144, 16), 144), :]


def fine_backward(meta, pooled_grad, cot, halo, slope1, slope2, feat3, act3, back_w):
    return call(
        backward_kernel,
        "fine_backward",
        (((8, 144, CH), BF), ((8, 144, CH), BF), ((18, 64, 384), BF)),
        (meta, pooled_grad, cot) + halo + (slope1, slope2, feat3, act3, back_w),
        (((20, 96, 384), BF), ((2304, CH), BF)),
        limit=20,
        flops=2 * 10**9,
    )


def feature_kernel(first3, back_w, out):
    for starts in ([0, 2, 4, 6], [8, 10, 12, 14]):
        value = dot_nt(four_rows(lambda h: first3[h], starts), back_w[...])
        for k, row in enumerate(split_rows(value, starts)):
            out[starts[0] + k] = row.astype(BF)


def feature_step(first3, back_w):
    return call(feature_kernel, "feature_step", (((16, 64, CH), BF),), (first3, back_w), limit=12, flops=10**9)[0]


def scatter_core_kernel(keep_c, keep_f, got_c, got_f, out):
    for k in range(8):
        out[k, 0:160, :] = (keep_c[k].astype(F32) + got_c[k].astype(F32)).astype(BF)
        out[k, 160:304, :] = (keep_f[k].astype(F32) + got_f[k].astype(F32)).astype(BF)


def scatter_row_kernel(got, out, total):
    value = got[0].astype(F32)
    for k in range(1, 8):
        value = value + got[k].astype(F32)
    total[0:304, :] = value
    total[304:336, :] = jnp.zeros((32, CH), F32)
    for k in range(16):
        out[k] = total[20 * k : 20 * k + 32, :].astype(BF)


def scatter_column_kernel(got, out):
    value = got[0].astype(F32)
    for k in range(1, 16):
        value = value + got[k].astype(F32)
    value = value.astype(BF)
    for k in range(16):
        out[k] = value


def gather_column_kernel(scale, got, conv, proj, fine, total):
    for k in range(16):
        total[20 * k : 20 * k + 32, :] = got[k].astype(F32)
    for k in range(9):
        conv[k] = total[16 * k : 16 * k + 16, :] * scale
    proj[...] = total[144:160, :] * scale
    value = total[160:304, :].astype(BF)
    for k in range(8):
        fine[k] = value


def finish_kernel(scale, meta, mine, other, first, second):
    core = meta[4] % 2
    for at in range(8):
        out = first if at < 4 else second
        a = mine[at].astype(F32) * scale
        b = other[at].astype(F32) * scale
        out[2 * (at % 4)] = jnp.where(core == 0, a, b)
        out[2 * (at % 4) + 1] = jnp.where(core == 0, b, a)


def swap(value, axis, mask):
    count = lax.axis_size(axis)
    return lax.ppermute(value, axis, [(i, i ^ mask) for i in range(count)])


def swap_outer(value, axis):
    count = lax.axis_size(axis)
    pairs = [(i, i + 1 if i % 2 else i - 1) for i in range(1, count - 1)]
    return lax.ppermute(value, axis, pairs)


def exchange_row(value):
    count = lax.axis_size("row")
    groups = [list(range(c, count, 2)) for c in range(2)]
    return lax.all_to_all(value, "row", 0, 0, axis_index_groups=groups, tiled=True)


def exchange_column(value):
    return lax.all_to_all(value, "col", 0, 0, tiled=True)


def after_all(value, *others):
    return lax.optimization_barrier((value,) + others)[0]


def local(features, conv_first, conv_second, coarse_conv, coarse_proj, cotangent):
    rows, cols = (lax.axis_size("row"), lax.axis_size("col"))
    height, breadth = (features.shape[0] * rows, features.shape[1] * cols)
    fine_scale = 1.0 / (height * breadth * features.shape[2]) ** 0.5
    coarse_scale = 2.0 * fine_scale
    me, mine = (lax.axis_index("row"), lax.axis_index("col"))
    fixed = [jnp.int32(height), jnp.int32(breadth)]
    meta = jnp.stack([me * 16, mine * 16] + fixed + [me, mine]).astype(jnp.int32)
    feat = features.reshape(16, 64, CH)
    cot = cotangent.reshape(16, 64, CH)
    conv = coarse_conv.reshape(9, CH, 16).swapaxes(1, 2)
    slab = ((160, CH), BF)

    side = ((16, 48, CH), BF)
    pair, other, own = call(
        pack_columns_kernel,
        "pack_columns",
        (side, side, slab),
        (meta, feat, cot, conv, coarse_proj),
        (pltpu.SemaphoreType.DMA((14,)),),
        far=(1, 2, 3, 4),
    )
    w1, w2 = (conv_first.reshape(1152, CH), conv_second.reshape(1152, CH))
    big, wide = (((16, 64, CH), BF), ((1536, 256), BF))
    feat_in, cot_in = call(
        bring_kernel,
        "bring",
        (big, big),
        (after_all(feat, own), cot),
        (pltpu.SemaphoreType.DMA((2,)),),
        far=(0, 1),
        flops=4 * 10**9,
    )
    own_far = swap(after_all(own, feat_in), "row", 8)
    weight1, weight2, back1, back2 = call(
        weights_kernel,
        "weights",
        (wide, wide, ((256, 1536), BF), ((256, 1536), BF)),
        (after_all(w1, feat_in), w2),
        (((1152, CH), BF), ((1152, CH), BF), pltpu.SemaphoreType.DMA((2,))),
        far=(0, 1),
        flops=4 * 10**9,
    )
    pair = swap(pair, "col", 1)
    other = swap_outer(other, "col")
    edge = ((EDGE, CH), BF)
    inner, outer, near0 = call(
        pack_rows_kernel,
        "pack_rows",
        (edge, edge, ((2, 160, CH), BF)),
        (meta, feat_in, cot_in, pair, after_all(other, weight1), own, own_far),
    )
    inner = swap(inner, "row", 1)
    outer = swap_outer(outer, "row")
    pair_in = after_all(pair, near0)
    near = [near0] + [swap(near0, "row", 2 * k) for k in range(1, 4)]
    parts = inner_step(meta, feat_in, pair_in, other, weight1, weight2)
    parts, near = lax.optimization_barrier((parts, near))
    far = swap(call(stack_kernel, "stack_eight", (((4, 2, 160, CH), BF),), near)[0], "row", 1)
    pool3, slope1, slope2, act, feat3, act3 = outer_step(meta, inner, outer, parts, weight1, weight2)
    halo = (pair, other, inner, outer)
    own_act, proj, keep_c, send_c, pooled_grad = coarse_step(meta, pool3, cot_in, halo, near, far)
    got_c = swap(send_c, "row", 1)
    keep_f, send_f, first3 = fine_backward(
        meta, pooled_grad, cot_in, halo, slope1, slope2, feat3, act3, back2
    )
    got_f = swap(send_f, "row", 1)
    feature_grad = feature_step(first3, back1)

    got_f = after_all(got_f, feature_grad)
    part = call(scatter_core_kernel, "scatter_core", (((8, 304, CH), BF),), (keep_c, keep_f, got_c, got_f))[0]
    part = call(
        scatter_row_kernel, "scatter_row", (((16, 32, CH), BF),), (exchange_row(part),), (((336, CH), F32),)
    )[0]
    part = call(scatter_column_kernel, "scatter_column", (((16, 32, CH), BF),), (exchange_column(part),))[0]
    conv_grad, proj_grad, fine = call(
        functools.partial(gather_column_kernel, coarse_scale),
        "gather_column",
        (((9, 16, CH), F32), ((16, CH), F32), ((8, 144, CH), BF)),
        (exchange_column(part),),
        (((336, CH), F32),),
    )
    fine = exchange_row(fine)
    blended = call(blend_kernel, "blend", (((16, 64, CH), BF),), (after_all(own_act, fine), proj, act), flops=10**9)[0]
    other = after_all(swap(fine, "row", 1), blended)
    first, second = call(
        functools.partial(finish_kernel, fine_scale),
        "finish",
        (((8, 144, CH), F32), ((8, 144, CH), F32)),
        (meta, fine, other),
    )
    shape = features.shape
    return (
        blended.reshape(shape),
        feature_grad.reshape(shape),
        first.reshape(3, 3, CH, CH),
        second.reshape(3, 3, CH, CH),
        conv_grad.reshape(3, 3, 16, CH).swapaxes(2, 3),
        proj_grad,
    )


def solution(mesh):
    in_specs = (
        P("row", "col", None, None),
        P(),
        P(),
        P(None, None, None, "row"),
        P("row", None),
        P("row", "col", None, None),
    )
    out_specs = (
        P("row", "col", None, None),
        P("row", "col", None, None),
        P(),
        P(),
        P(None, None, None, "row"),
        P("row", None),
    )
    return jax.shard_map(local, mesh=mesh, in_specs=in_specs, out_specs=out_specs, check_vma=False)
```

```python
import functools

import jax
import jax.numpy as jnp
from jax import lax
from jax.experimental import pallas as pl
from jax.experimental.pallas import tpu as pltpu
from jax.sharding import PartitionSpec as P

BF = jnp.bfloat16
F32 = jnp.float32
CH = 128
WIDE = 256
MIB = 1024 * 1024
VM = pl.BlockSpec(memory_space=pltpu.VMEM)
SM = pl.BlockSpec(memory_space=pltpu.SMEM)
HBM = pl.BlockSpec(memory_space=pltpu.HBM)


def call(kernel, name, outs, ins, scratch=(), limit=16, flops=0, moved=0, far=(), far_out=False):
    ins = [pltpu.with_memory_space_constraint(v, pltpu.HBM) if k in far else v for k, v in enumerate(ins)]
    shapes = tuple(jax.ShapeDtypeStruct(shape, dtype) for shape, dtype in outs)
    return pl.pallas_call(
        kernel,
        name=name,
        out_shape=shapes,
        in_specs=[HBM if k in far else SM if v.ndim == 1 else VM for k, v in enumerate(ins)],
        out_specs=tuple(HBM if far_out else VM for _ in outs),
        scratch_shapes=[pltpu.VMEM(*v) if isinstance(v, tuple) else v for v in scratch],
        compiler_params=pltpu.CompilerParams(vmem_limit_bytes=limit * MIB),
        cost_estimate=pl.CostEstimate(flops=flops, bytes_accessed=moved, transcendentals=0),
    )(*ins)


def dot_nn(a, b):
    return jnp.dot(a, b, preferred_element_type=F32)


def dot_nt(a, b):
    return lax.dot_general(a, b, (((1,), (1,)), ((), ())), preferred_element_type=F32)


def dot_tn(a, b):
    return lax.dot_general(a, b, (((0,), (0,)), ((), ())), preferred_element_type=F32)


def sigmoid(value):
    return 0.5 * jnp.tanh(0.5 * value) + 0.5


def slope_of(value):
    sigma = sigmoid(value)
    return sigma * (1.0 + value * (1.0 - sigma))


def rounded(value):
    return value.astype(BF).astype(F32)


def three(value):
    count = value.shape[0]
    left = pltpu.roll(value, 4, 0)
    right = pltpu.roll(value, count - 4, 0)
    return jnp.concatenate([left.astype(BF), value.astype(BF), right.astype(BF)], axis=1)


def paired(weight, axis):
    pad = jnp.zeros((3 * CH, CH) if axis == 0 else (CH, 3 * CH), BF)
    return jnp.concatenate(
        [jnp.concatenate([weight, pad], axis=axis), jnp.concatenate([pad, weight], axis=axis)], axis=1 - axis
    )


def flipped(weight):
    return jnp.concatenate([weight[(8 - t) * CH : (9 - t) * CH, :] for t in range(9)], axis=1)


def four_rows(row, starts):
    parts = [jnp.concatenate([row(h + k) for h in starts], axis=0) for k in range(4)]
    return jnp.concatenate(parts, axis=1)


def split_rows(value, starts):
    size = value.shape[0] // len(starts)
    out = []
    for k in range(len(starts)):
        out += [value[k * size : (k + 1) * size, e * CH : (e + 1) * CH] for e in range(2)]
    return out


def weight_grad(source, grad):
    gap = jnp.zeros((64, CH), BF)
    parts = []
    for r in range(3):
        parts.append(jnp.concatenate([gap] * r + [grad.reshape(1024, CH)] + [gap] * (2 - r), axis=0))
    whole = dot_tn(source.reshape(1152, 3 * CH), jnp.concatenate(parts, axis=1))
    return [whole[:, r * CH : (r + 1) * CH] for r in range(3)]


def column_mask(first, width, limit):
    place = first + lax.broadcasted_iota(jnp.int32, (width, CH), 0) // 4
    return jnp.where((place >= 0) & (place < limit), 1.0, 0.0).astype(F32)


def row_ok(place, limit):
    return jnp.where((place >= 0) & (place < limit), 1.0, 0.0).astype(F32)


def masked(value, mask, first, limit):
    rows = []
    for k in range(value.shape[0]):
        rows.append((value[k] * (mask * row_ok(first + k, limit)))[None])
    return jnp.concatenate(rows, axis=0)


def pooled_pair(row):
    count = row.shape[0]
    low = (row + pltpu.roll(row, count - 4, 0)).reshape(count // 16, 2, 8, CH)
    high = (row + pltpu.roll(row, 4, 0)).reshape(count // 16, 2, 8, CH)
    first = lax.broadcasted_iota(jnp.int32, (count // 16, 8, CH), 1) < 4
    return jnp.where(first, low[:, 0], high[:, 1]).reshape(count // 2, CH)


def repeated(row):
    count = row.shape[0]
    first = lax.broadcasted_iota(jnp.int32, (count, CH), 0) % 8 < 4
    even = jnp.where(first, row, pltpu.roll(row, 4, 0)).reshape(count // 8, 1, 8, CH)
    odd = jnp.where(first, pltpu.roll(row, count - 4, 0), row).reshape(count // 8, 1, 8, CH)
    return jnp.concatenate([even, odd], axis=1).reshape(count * 2, CH)


def aligned(start, size):
    return pl.ds(pl.multiple_of(start, 16), size)


def sides(meta, pair, other):
    even = meta[5] % 2 == 0
    return lax.select(even, other, pair), lax.select(even, pair, other)


def pack_columns_kernel(meta, feat, cot, pair, other, done):
    odd = meta[5] % 2
    pairs = [
        (feat.at[:, aligned(32 - 32 * odd, 32), :], pair.at[:, 0:32, :]),
        (cot.at[:, aligned(48 - 48 * odd, 16), :], pair.at[:, 32:48, :]),
        (feat.at[:, aligned(32 * odd, 32), :], other.at[:, 0:32, :]),
        (cot.at[:, aligned(48 * odd, 16), :], other.at[:, 32:48, :]),
    ]
    copies = [pltpu.make_async_copy(a, b, done.at[k]) for k, (a, b) in enumerate(pairs)]
    for copy in copies:
        copy.start()
    for copy in copies:
        copy.wait()


EDGE = 8 * 128 + 4 * 96


def cot_edge(ref, first, count=1):
    value = ref[1024 + 96 * first : 1024 + 96 * (first + count), :]
    return value if count == 1 else value.reshape(count, 96, CH)


def bring_kernel(feat_far, cot_far, conv, proj, feat, cot, weights, done):
    pairs = [(feat_far, feat), (cot_far, cot), (proj, weights.at[144:160, :])]
    pairs += [(conv.at[t], weights.at[16 * t : 16 * t + 16, :]) for t in range(9)]
    copies = [pltpu.make_async_copy(a, b, done.at[k]) for k, (a, b) in enumerate(pairs)]
    for copy in copies:
        copy.start()
    for copy in copies:
        copy.wait()


def weights_kernel(w1_far, w2_far, weight1, weight2, back1, back2, w1, w2, done):
    copies = [pltpu.make_async_copy(a, b, done.at[k]) for k, (a, b) in enumerate(((w1_far, w1), (w2_far, w2)))]
    for copy in copies:
        copy.start()
    for copy, w, weight, back in zip(copies, (w1, w2), (weight1, weight2), (back1, back2)):
        copy.wait()
        weight[...] = paired(w[...], 0)
        back[...] = paired(flipped(w), 1)


def pack_rows_kernel(meta, feat, cot, pair, other, own, far, inner, outer, both):
    core = meta[4] % 2
    for low, out in ((1 - core, inner), (core, outer)):
        jobs = [(128 * k, feat, 8 * low + k, 0, 32) for k in range(8)]
        jobs += [(1024 + 96 * k, cot, 12 * low + k, 32, 16) for k in range(4)]
        for base, middle, row, first, width in jobs:
            before, after = sides(meta, pair[row, first : first + width, :], other[row, first : first + width, :])
            out[base : base + width, :] = before
            out[base + width : base + width + 64, :] = middle[row]
            out[base + width + 64 : base + 2 * width + 64, :] = after
    both[0] = own[...]
    both[1] = far[...]


def stack_kernel(*refs):
    out = refs[-1]
    for k, ref in enumerate(refs[:-1]):
        out[k] = ref[...]


def first_rows(meta, row, starts, weight):
    top, left, height, breadth = (meta[0], meta[1], meta[2], meta[3])
    mask = column_mask(left - 8, 128, breadth)
    pre = dot_nn(four_rows(row, [h - 1 for h in starts]), weight)
    out = {}
    for k, value in enumerate(split_rows(pre, starts)):
        h = starts[k // 2] + k % 2
        act = rounded(value * sigmoid(value)) * (mask * row_ok(top - 8 + h, height))
        out[h] = (value, three(act))
    return out


def second_rows(meta, row, starts, weight):
    top, left, height, breadth = (meta[0], meta[1], meta[2], meta[3])
    mask = column_mask(left // 2 - 4, 64, breadth // 2)
    rows = split_rows(dot_nn(four_rows(row, [h - 1 for h in starts]), weight), starts)
    out = {}
    for k, h in enumerate(starts):
        pre = rows[2 * k : 2 * k + 2]
        act = [(v * sigmoid(v)).astype(BF) for v in pre]
        small = rounded(0.25 * pooled_pair(act[0].astype(F32) + act[1].astype(F32)))
        small = small * (mask * row_ok(top // 2 - 4 + h // 2, height // 2))
        out[h] = (pre, act, three(small))
    return out


INNER_FIRST = [9, 11, 13, 15, 17, 19, 21]
INNER_SECOND = [10, 12, 14, 16, 18, 20]


def inner_kernel(meta, feat, pair, other, weight1, weight2, feat3, act3, slope1, pool3, slope2, act):
    for k in range(16):
        before, after = sides(meta, pair[k, 0:32, :], other[k, 0:32, :])
        feat3[k] = three(jnp.concatenate([before, feat[k], after], axis=0).astype(F32))
    for h, (pre, wide) in first_rows(meta, lambda h: feat3[h - 8], INNER_FIRST, weight1[...]).items():
        act3[h - 9] = wide
        slope1[h - 9] = slope_of(pre[16:112])
    for h, (pre, value, small) in second_rows(meta, lambda h: act3[h - 9], INNER_SECOND, weight2[...]).items():
        pool3[h // 2 - 5] = small
        for e in range(2):
            slope2[h - 10 + e] = slope_of(pre[e][16:112])
            act[h - 10 + e] = value[e][32:96]


def outer_first_kernel(
    meta, inner, outer, feat3i, act3i, slope1i, weight1, act3, slope1, feat3o, act3o, feat3
):
    below_at = 24 * (meta[4] % 2)
    for k in range(8):
        feat3[k + below_at] = three(outer[128 * k : 128 * k + 128, :].astype(F32))
        feat3[k + 24 - below_at] = three(inner[128 * k : 128 * k + 128, :].astype(F32))
    feat3[8:24] = feat3i[...]
    for starts in ([1, 3, 5, 7], [23, 25, 27, 29]):
        for h, (pre, wide) in first_rows(meta, lambda h: feat3[h], starts, weight1[...]).items():
            act3[h - 1] = wide
            if 7 <= h <= 24:
                slope1[h - 7] = slope_of(pre[16:112])
    slope1[2:16] = slope1i[...]
    act3[8:22] = act3i[...]
    feat3o[...] = feat3[7:25, 32:96, :]
    act3o[...] = act3[6:24, 32:96, :]


def outer_second_kernel(meta, act3, pool3i, slope2i, acti, weight2, pool3, slope2, act):
    for starts in ([2, 4, 6, 8], [22, 24, 26, 28]):
        for h, (pre, value, small) in second_rows(meta, lambda h: act3[h - 1], starts, weight2[...]).items():
            pool3[h // 2 - 1] = small
            for e in range(2):
                if 6 <= h + e < 26:
                    slope2[h + e - 6] = slope_of(pre[e][16:112])
                if 8 <= h + e < 24:
                    act[h + e - 8] = value[e][32:96]
    pool3[4:10] = pool3i[...]
    slope2[4:16] = slope2i[...]
    act[2:14] = acti[...]


def inner_step(meta, feat, pair, other, weight1, weight2):
    return call(
        inner_kernel,
        "forward_inner",
        (
            ((16, 128, 384), BF),
            ((14, 128, 384), BF),
            ((14, 96, CH), F32),
            ((6, 64, 384), BF),
            ((12, 96, CH), F32),
            ((12, 64, CH), BF),
        ),
        (meta, feat, pair, other, weight1, weight2),
        limit=24,
        flops=0,
    )


def outer_first_step(meta, inner, outer, feat3, act3, slope1, weight1):
    return call(
        outer_first_kernel,
        "outer_first",
        (((30, 128, 384), BF), ((18, 96, CH), F32), ((18, 64, 384), BF), ((18, 64, 384), BF)),
        (meta, inner, outer, feat3, act3, slope1, weight1),
        (((32, 128, 384), BF),),
        limit=20,
        flops=2 * 10**9,
    )


def outer_second_step(meta, act3, pool3, slope2, act, weight2):
    return call(
        outer_second_kernel,
        "outer_second",
        (((14, 64, 384), BF), ((20, 96, CH), F32), ((16, 64, CH), BF)),
        (meta, act3, pool3, slope2, act, weight2),
        limit=16,
        flops=4 * 10**9,
    )


def coarse_kernel(
    meta, pool3, cot, pair, other, inner, outer, near0, near1, near2, near3, far,
    own, projs_out, keep, send, pooled_grad, wcat, projs, wide3, projin,
):
    top, left, height, breadth, me = (meta[0], meta[1], meta[2], meta[3], meta[4])
    core = me % 2
    near = (near0, near1, near2, near3)
    for rel in range(16):
        c, x, y = (rel % 2, (rel // 2) % 4, rel // 8)
        place = pl.ds(pl.multiple_of((me ^ rel) * 16, 16), 16)
        source = far.at[x, y] if c else near[x].at[y]
        for t in range(9):
            wcat[place, t * CH : (t + 1) * CH] = source[16 * t : 16 * t + 16, :]
        projs[place, :] = source[144:160, :]
    proj_w = projs[...]

    def pair_sum(a, b):
        return pooled_pair(a.astype(F32) + b.astype(F32))

    below_at = 10 * core
    for k in range(2):
        projin[k + below_at] = pair_sum(cot_edge(outer, 2 * k), cot_edge(outer, 2 * k + 1))
        projin[k + 10 - below_at] = pair_sum(cot_edge(inner, 2 * k), cot_edge(inner, 2 * k + 1))

    for k in range(8):
        rows = slice(2 * k, 2 * k + 2)
        before, after = sides(meta, pair[rows, 32:48, :], other[rows, 32:48, :])
        both = jnp.concatenate([before, cot[rows], after], axis=1)
        projin[k + 2] = pair_sum(both[0], both[1])

    proj_in = projin[...].reshape(576, CH)
    proj_in_bf = proj_in.astype(BF)
    lhs = jnp.concatenate([pool3[r : r + 12].reshape(768, 3 * CH) for r in range(3)], axis=1)
    pre = dot_nt(lhs, wcat[...]).reshape(12, 64, WIDE)[:, 8:56].reshape(576, WIDE)
    sigma = sigmoid(pre)
    coarse_act = pre * sigma
    act_grad = dot_nt(proj_in_bf, proj_w)
    grad = rounded(act_grad * (sigma * (1.0 + pre * (1.0 - sigma)))).reshape(12, 48, WIDE)
    mask = column_mask(left // 2 - 2, 48, breadth // 2)
    mask = jnp.concatenate([mask, mask], axis=1)
    grad = masked(grad, mask, top // 2 - 2, height // 2)
    wide3[...] = three(grad.reshape(576, WIDE)).reshape(12, 48, 3 * WIDE)
    own_grad = grad[2:10, 8:40].reshape(256, WIDE).astype(BF)
    own_act = coarse_act.reshape(12, 48, WIDE)[2:10, 8:40].reshape(256, WIDE).astype(BF)
    own_in = proj_in.reshape(12, 48, CH)[2:10, 8:40].reshape(256, CH).astype(BF)

    def emit(first, last, value):
        value = value.reshape(8, 2, 16, CH)
        even, odd = (value[:, 0], value[:, 1])
        keep[:, first:last, :] = jnp.where(core == 0, even, odd).astype(BF)
        send[:, first:last, :] = jnp.where(core == 0, odd, even).astype(BF)

    source = [pool3[2 + r : 10 + r, 16:48, :].reshape(256, 3 * CH) for r in range(3)]
    part = dot_tn(own_grad, jnp.concatenate(source, axis=1))
    for t in range(9):
        emit(16 * t, 16 * t + 16, part[:, t * CH : (t + 1) * CH])
    emit(144, 160, dot_tn(own_act, own_in))
    total = None
    for r in range(3):
        lhs = wide3[r : r + 10].reshape(480, 3 * WIDE)
        first = 3 * (2 - r)
        rhs = jnp.concatenate([wcat[:, (first + 2 - s) * CH : (first + 3 - s) * CH] for s in range(3)], axis=0)
        part = dot_nn(lhs, rhs)
        total = part if total is None else total + part
    pooled_grad[...] = total.reshape(10, 48, CH)
    own[...] = own_act
    projs_out[...] = proj_w


def blend_kernel(own, proj, act, blended):
    projected = dot_nn(own[...], proj[...]).reshape(8, 32, CH)
    for k in range(8):
        row = repeated(projected[k])
        for e in range(2):
            blended[2 * k + e] = (act[2 * k + e].astype(F32) + row).astype(BF)


def coarse_step(meta, pool3, cot, halo, near, far):
    return call(
        coarse_kernel,
        "coarse_step",
        (((256, WIDE), BF), ((WIDE, CH), BF), ((8, 160, CH), BF), ((8, 160, CH), BF), ((10, 48, CH), F32)),
        (meta, pool3, cot) + halo + tuple(near) + (far,),
        (
            ((WIDE, 9 * CH), BF),
            ((WIDE, CH), BF),
            ((12, 48, 3 * WIDE), BF),
            ((12, 48, CH), F32),
        ),
        limit=20,
        flops=2 * 10**9,
    )


def backward_kernel(
    meta, pooled_grad, cot, pair, other, inner, outer, slope1, slope2, feat3, act3, back_w,
    keep, send, first3, second3, grads,
):
    top, left, height, breadth = (meta[0], meta[1], meta[2], meta[3])
    mask = column_mask(left - 4, 96, breadth)

    def second_pair(k, both):
        wide = 0.25 * repeated(pooled_grad[k])
        for e in range(2):
            value = rounded((both[e].astype(F32) + wide) * slope2[2 * k + e])
            second3[2 * k + e] = three(value * (mask * row_ok(top - 2 + 2 * k + e, height)))

    first_core = meta[4] % 2 == 0
    second_pair(0, lax.select(first_core, cot_edge(outer, 2, 2), cot_edge(inner, 2, 2)))
    second_pair(9, lax.select(first_core, cot_edge(inner, 0, 2), cot_edge(outer, 0, 2)))
    for k in range(8):
        rows = slice(2 * k, 2 * k + 2)
        before, after = sides(meta, pair[rows, 32:48, :], other[rows, 32:48, :])
        second_pair(k + 1, jnp.concatenate([before, cot[rows], after], axis=1))

    def emit(base, parts):
        for r in range(3):
            grads[base + 384 * r : base + 384 * (r + 1), :] = parts[r].astype(BF)

    for starts in ([0, 2, 4, 6], [8, 10, 12, 14, 16]):
        value = dot_nt(four_rows(lambda h: second3[h], starts), back_w[...])
        for k, row in enumerate(split_rows(value, starts)):
            h = starts[k // 2] + k % 2
            row = rounded(row * slope1[h]) * (mask * row_ok(top - 1 + h, height))
            first3[h] = three(row)[16:80]
    emit(1152, weight_grad(act3[...], second3[2:18, 16:80, CH : 2 * CH]))
    emit(0, weight_grad(feat3[...], first3[1:17, :, CH : 2 * CH]))
    core = meta[4] % 2
    for k in range(8):
        keep[k] = grads[pl.ds(pl.multiple_of((2 * k + core) * 144, 16), 144), :]
        send[k] = grads[pl.ds(pl.multiple_of((2 * k + 1 - core) * 144, 16), 144), :]


def fine_backward(meta, pooled_grad, cot, halo, slope1, slope2, feat3, act3, back_w):
    return call(
        backward_kernel,
        "fine_backward",
        (((8, 144, CH), BF), ((8, 144, CH), BF), ((18, 64, 384), BF)),
        (meta, pooled_grad, cot) + halo + (slope1, slope2, feat3, act3, back_w),
        (((20, 96, 384), BF), ((2304, CH), BF)),
        limit=20,
        flops=2 * 10**9,
    )


def feature_kernel(first3, back_w, out):
    for starts in ([0, 2, 4, 6], [8, 10, 12, 14]):
        value = dot_nt(four_rows(lambda h: first3[h], starts), back_w[...])
        for k, row in enumerate(split_rows(value, starts)):
            out[starts[0] + k] = row.astype(BF)


def feature_step(first3, back_w):
    return call(feature_kernel, "feature_step", (((16, 64, CH), BF),), (first3, back_w), limit=12, flops=10**9)[0]


def scatter_core_kernel(keep_c, keep_f, got_c, got_f, out):
    for k in range(8):
        out[k, 0:160, :] = (keep_c[k].astype(F32) + got_c[k].astype(F32)).astype(BF)
        out[k, 160:304, :] = (keep_f[k].astype(F32) + got_f[k].astype(F32)).astype(BF)


def scatter_row_kernel(got, out, total):
    value = got[0].astype(F32)
    for k in range(1, 8):
        value = value + got[k].astype(F32)
    total[0:304, :] = value
    total[304:336, :] = jnp.zeros((32, CH), F32)
    for k in range(16):
        out[k] = total[20 * k : 20 * k + 32, :].astype(BF)


def scatter_column_kernel(got, out):
    value = got[0].astype(F32)
    for k in range(1, 16):
        value = value + got[k].astype(F32)
    value = value.astype(BF)
    for k in range(16):
        out[k] = value


def gather_column_kernel(scale, got, conv, proj, fine, total):
    for k in range(16):
        total[20 * k : 20 * k + 32, :] = got[k].astype(F32)
    for k in range(9):
        conv[k] = total[16 * k : 16 * k + 16, :] * scale
    proj[...] = total[144:160, :] * scale
    value = total[160:304, :].astype(BF)
    for k in range(8):
        fine[k] = value


def finish_kernel(scale, meta, mine, other, first, second, slabs, done):
    core = meta[4] % 2
    copies = []
    for at in range(8):
        out = first if at < 4 else second
        a = mine[at].astype(F32) * scale
        b = other[at].astype(F32) * scale
        slabs[2 * at] = jnp.where(core == 0, a, b)
        slabs[2 * at + 1] = jnp.where(core == 0, b, a)
        pair = slabs.at[2 * at : 2 * at + 2]
        copies.append(pltpu.make_async_copy(pair, out.at[2 * (at % 4) : 2 * (at % 4) + 2], done.at[at]))
        copies[at].start()
    for copy in copies:
        copy.wait()


def swap(value, axis, mask):
    count = lax.axis_size(axis)
    return lax.ppermute(value, axis, [(i, i ^ mask) for i in range(count)])


def swap_outer(value, axis):
    count = lax.axis_size(axis)
    pairs = [(i, i + 1 if i % 2 else i - 1) for i in range(1, count - 1)]
    return lax.ppermute(value, axis, pairs)


def exchange_row(value):
    count = lax.axis_size("row")
    groups = [list(range(c, count, 2)) for c in range(2)]
    return lax.all_to_all(value, "row", 0, 0, axis_index_groups=groups, tiled=True)


def exchange_column(value):
    return lax.all_to_all(value, "col", 0, 0, tiled=True)


def after_all(value, *others):
    return lax.optimization_barrier((value,) + others)[0]


def local(features, conv_first, conv_second, coarse_conv, coarse_proj, cotangent):
    rows, cols = (lax.axis_size("row"), lax.axis_size("col"))
    height, breadth = (features.shape[0] * rows, features.shape[1] * cols)
    fine_scale = 1.0 / (height * breadth * features.shape[2]) ** 0.5
    coarse_scale = 2.0 * fine_scale
    me, mine = (lax.axis_index("row"), lax.axis_index("col"))
    fixed = [jnp.int32(height), jnp.int32(breadth)]
    meta = jnp.stack([me * 16, mine * 16] + fixed + [me, mine]).astype(jnp.int32)
    feat = features.reshape(16, 64, CH)
    cot = cotangent.reshape(16, 64, CH)
    conv = coarse_conv.reshape(9, CH, 16).swapaxes(1, 2)
    slab = ((160, CH), BF)

    side = ((16, 48, CH), BF)
    pair, other = call(
        pack_columns_kernel,
        "pack_columns",
        (side, side),
        (meta, feat, cot),
        (pltpu.SemaphoreType.DMA((4,)),),
        far=(1, 2),
    )
    w1, w2 = (conv_first.reshape(1152, CH), conv_second.reshape(1152, CH))
    big, wide = (((16, 64, CH), BF), ((1536, 256), BF))
    feat_in, cot_in, own = call(
        bring_kernel,
        "bring",
        (big, big, slab),
        (after_all(feat, pair), cot, conv, coarse_proj),
        (pltpu.SemaphoreType.DMA((12,)),),
        far=(0, 1, 2, 3),
        flops=4 * 10**9,
    )
    own_far = swap(own, "row", 8)
    weight1, weight2, back1, back2 = call(
        weights_kernel,
        "weights",
        (wide, wide, ((256, 1536), BF), ((256, 1536), BF)),
        (after_all(w1, feat_in), w2),
        (((1152, CH), BF), ((1152, CH), BF), pltpu.SemaphoreType.DMA((2,))),
        far=(0, 1),
        flops=4 * 10**9,
    )
    pair = swap(pair, "col", 1)
    other = swap_outer(other, "col")
    edge = ((EDGE, CH), BF)
    inner, outer, near0 = call(
        pack_rows_kernel,
        "pack_rows",
        (edge, edge, ((2, 160, CH), BF)),
        (meta, feat_in, cot_in, pair, after_all(other, weight1), own, own_far),
    )
    inner = swap(inner, "row", 1)
    outer = swap_outer(outer, "row")
    pair_in = after_all(pair, near0)
    near = [near0] + [swap(near0, "row", 2 * k) for k in range(1, 4)]
    feat3, act3, slope1, pool3, slope2, act = inner_step(meta, feat_in, pair_in, other, weight1, weight2)
    act3, slope1, feat3, act3o = outer_first_step(meta, inner, outer, feat3, act3, slope1, weight1)
    near = list(lax.optimization_barrier((slope1, *near)))[1:]
    far = swap(call(stack_kernel, "stack_eight", (((4, 2, 160, CH), BF),), near)[0], "row", 1)
    pool3, slope2, act = outer_second_step(meta, act3, pool3, slope2, act, weight2)
    halo = (pair, other, inner, outer)
    own_act, proj, keep_c, send_c, pooled_grad = coarse_step(meta, pool3, cot_in, halo, near, far)
    got_c = swap(send_c, "row", 1)
    keep_f, send_f, first3 = fine_backward(
        meta, pooled_grad, cot_in, halo, slope1, slope2, feat3, act3o, back2
    )
    got_f = swap(send_f, "row", 1)
    feature_grad = feature_step(first3, back1)

    got_f = after_all(got_f, feature_grad)
    part = call(scatter_core_kernel, "scatter_core", (((8, 304, CH), BF),), (keep_c, keep_f, got_c, got_f))[0]
    part = call(
        scatter_row_kernel, "scatter_row", (((16, 32, CH), BF),), (exchange_row(part),), (((336, CH), F32),)
    )[0]
    part = call(scatter_column_kernel, "scatter_column", (((16, 32, CH), BF),), (exchange_column(part),))[0]
    conv_grad, proj_grad, fine = call(
        functools.partial(gather_column_kernel, coarse_scale),
        "gather_column",
        (((9, 16, CH), F32), ((16, CH), F32), ((8, 144, CH), BF)),
        (exchange_column(part),),
        (((336, CH), F32),),
    )
    fine = exchange_row(fine)
    blended = call(blend_kernel, "blend", (((16, 64, CH), BF),), (after_all(own_act, fine), proj, act), flops=10**9)[0]
    other = after_all(swap(fine, "row", 1), blended)
    first, second = call(
        functools.partial(finish_kernel, fine_scale),
        "finish",
        (((8, 144, CH), F32), ((8, 144, CH), F32)),
        (meta, fine, other),
        (((16, 144, CH), F32), pltpu.SemaphoreType.DMA((8,))),
        far_out=True,
    )
    shape = features.shape
    return (
        blended.reshape(shape),
        feature_grad.reshape(shape),
        first.reshape(3, 3, CH, CH),
        second.reshape(3, 3, CH, CH),
        conv_grad.reshape(3, 3, 16, CH).swapaxes(2, 3),
        proj_grad,
    )


def solution(mesh):
    in_specs = (
        P("row", "col", None, None),
        P(),
        P(),
        P(None, None, None, "row"),
        P("row", None),
        P("row", "col", None, None),
    )
    out_specs = (
        P("row", "col", None, None),
        P("row", "col", None, None),
        P(),
        P(),
        P(None, None, None, "row"),
        P("row", None),
    )
    return jax.shard_map(local, mesh=mesh, in_specs=in_specs, out_specs=out_specs, check_vma=False)
```

```python
import functools

import jax
import jax.numpy as jnp
from jax import lax
from jax.experimental import pallas as pl
from jax.experimental.pallas import tpu as pltpu
from jax.sharding import PartitionSpec as P

BF = jnp.bfloat16
F32 = jnp.float32
CH = 128
WIDE = 256
MIB = 1024 * 1024
VM = pl.BlockSpec(memory_space=pltpu.VMEM)
SM = pl.BlockSpec(memory_space=pltpu.SMEM)
HBM = pl.BlockSpec(memory_space=pltpu.HBM)


def call(kernel, name, outs, ins, scratch=(), limit=16, flops=0, moved=0, far=(), far_out=False):
    ins = [pltpu.with_memory_space_constraint(v, pltpu.HBM) if k in far else v for k, v in enumerate(ins)]
    shapes = tuple(jax.ShapeDtypeStruct(shape, dtype) for shape, dtype in outs)
    return pl.pallas_call(
        kernel,
        name=name,
        out_shape=shapes,
        in_specs=[HBM if k in far else SM if v.ndim == 1 else VM for k, v in enumerate(ins)],
        out_specs=tuple(HBM if far_out else VM for _ in outs),
        scratch_shapes=[pltpu.VMEM(*v) if isinstance(v, tuple) else v for v in scratch],
        compiler_params=pltpu.CompilerParams(vmem_limit_bytes=limit * MIB),
        cost_estimate=pl.CostEstimate(flops=flops, bytes_accessed=moved, transcendentals=0),
    )(*ins)


def dot_nn(a, b):
    return jnp.dot(a, b, preferred_element_type=F32)


def dot_nt(a, b):
    return lax.dot_general(a, b, (((1,), (1,)), ((), ())), preferred_element_type=F32)


def dot_tn(a, b):
    return lax.dot_general(a, b, (((0,), (0,)), ((), ())), preferred_element_type=F32)


def sigmoid(value):
    return 0.5 * jnp.tanh(0.5 * value) + 0.5


def slope_of(value):
    sigma = sigmoid(value)
    return sigma * (1.0 + value * (1.0 - sigma))


def rounded(value):
    return value.astype(BF).astype(F32)


def three(value):
    count = value.shape[0]
    left = pltpu.roll(value, 4, 0)
    right = pltpu.roll(value, count - 4, 0)
    return jnp.concatenate([left.astype(BF), value.astype(BF), right.astype(BF)], axis=1)


def paired(weight, axis):
    pad = jnp.zeros((3 * CH, CH) if axis == 0 else (CH, 3 * CH), BF)
    return jnp.concatenate(
        [jnp.concatenate([weight, pad], axis=axis), jnp.concatenate([pad, weight], axis=axis)], axis=1 - axis
    )


def flipped(weight):
    return jnp.concatenate([weight[(8 - t) * CH : (9 - t) * CH, :] for t in range(9)], axis=1)


def four_rows(row, starts):
    parts = [jnp.concatenate([row(h + k) for h in starts], axis=0) for k in range(4)]
    return jnp.concatenate(parts, axis=1)


def split_rows(value, starts):
    size = value.shape[0] // len(starts)
    out = []
    for k in range(len(starts)):
        out += [value[k * size : (k + 1) * size, e * CH : (e + 1) * CH] for e in range(2)]
    return out


def weight_grad(source, grad):
    gap = jnp.zeros((64, CH), BF)
    parts = []
    for r in range(3):
        parts.append(jnp.concatenate([gap] * r + [grad.reshape(1024, CH)] + [gap] * (2 - r), axis=0))
    whole = dot_tn(source.reshape(1152, 3 * CH), jnp.concatenate(parts, axis=1))
    return [whole[:, r * CH : (r + 1) * CH] for r in range(3)]


def column_mask(first, width, limit):
    place = first + lax.broadcasted_iota(jnp.int32, (width, CH), 0) // 4
    return jnp.where((place >= 0) & (place < limit), 1.0, 0.0).astype(F32)


def row_ok(place, limit):
    return jnp.where((place >= 0) & (place < limit), 1.0, 0.0).astype(F32)


def masked(value, mask, first, limit):
    rows = []
    for k in range(value.shape[0]):
        rows.append((value[k] * (mask * row_ok(first + k, limit)))[None])
    return jnp.concatenate(rows, axis=0)


def pooled_pair(row):
    count = row.shape[0]
    low = (row + pltpu.roll(row, count - 4, 0)).reshape(count // 16, 2, 8, CH)
    high = (row + pltpu.roll(row, 4, 0)).reshape(count // 16, 2, 8, CH)
    first = lax.broadcasted_iota(jnp.int32, (count // 16, 8, CH), 1) < 4
    return jnp.where(first, low[:, 0], high[:, 1]).reshape(count // 2, CH)


def repeated(row):
    count = row.shape[0]
    first = lax.broadcasted_iota(jnp.int32, (count, CH), 0) % 8 < 4
    even = jnp.where(first, row, pltpu.roll(row, 4, 0)).reshape(count // 8, 1, 8, CH)
    odd = jnp.where(first, pltpu.roll(row, count - 4, 0), row).reshape(count // 8, 1, 8, CH)
    return jnp.concatenate([even, odd], axis=1).reshape(count * 2, CH)


def aligned(start, size):
    return pl.ds(pl.multiple_of(start, 16), size)


def sides(meta, pair, other):
    even = meta[5] % 2 == 0
    return lax.select(even, other, pair), lax.select(even, pair, other)


def pack_columns_kernel(meta, feat, cot, pair, other, done):
    odd = meta[5] % 2
    pairs = [
        (feat.at[:, aligned(32 - 32 * odd, 32), :], pair.at[:, 0:32, :]),
        (cot.at[:, aligned(48 - 48 * odd, 16), :], pair.at[:, 32:48, :]),
        (feat.at[:, aligned(32 * odd, 32), :], other.at[:, 0:32, :]),
        (cot.at[:, aligned(48 * odd, 16), :], other.at[:, 32:48, :]),
    ]
    copies = [pltpu.make_async_copy(a, b, done.at[k]) for k, (a, b) in enumerate(pairs)]
    for copy in copies:
        copy.start()
    for copy in copies:
        copy.wait()


EDGE = 8 * 128 + 4 * 96


def cot_edge(ref, first, count=1):
    value = ref[1024 + 96 * first : 1024 + 96 * (first + count), :]
    return value if count == 1 else value.reshape(count, 96, CH)


def bring_kernel(feat_far, cot_far, conv, proj, feat, cot, weights, done):
    pairs = [(feat_far, feat), (cot_far, cot), (proj, weights.at[144:160, :])]
    pairs += [(conv.at[t], weights.at[16 * t : 16 * t + 16, :]) for t in range(9)]
    copies = [pltpu.make_async_copy(a, b, done.at[k]) for k, (a, b) in enumerate(pairs)]
    for copy in copies:
        copy.start()
    for copy in copies:
        copy.wait()


def weights_kernel(w1_far, w2_far, weight1, weight2, back1, back2, w1, w2, done):
    copies = [pltpu.make_async_copy(a, b, done.at[k]) for k, (a, b) in enumerate(((w1_far, w1), (w2_far, w2)))]
    for copy in copies:
        copy.start()
    for copy, w, weight, back in zip(copies, (w1, w2), (weight1, weight2), (back1, back2)):
        copy.wait()
        weight[...] = paired(w[...], 0)
        back[...] = paired(flipped(w), 1)


def pack_rows_kernel(meta, feat, cot, pair, other, own, far, inner, outer, both):
    core = meta[4] % 2
    for low, out in ((1 - core, inner), (core, outer)):
        jobs = [(128 * k, feat, 8 * low + k, 0, 32) for k in range(8)]
        jobs += [(1024 + 96 * k, cot, 12 * low + k, 32, 16) for k in range(4)]
        for base, middle, row, first, width in jobs:
            before, after = sides(meta, pair[row, first : first + width, :], other[row, first : first + width, :])
            out[base : base + width, :] = before
            out[base + width : base + width + 64, :] = middle[row]
            out[base + width + 64 : base + 2 * width + 64, :] = after
    both[0] = own[...]
    both[1] = far[...]


def stack_kernel(*refs):
    out = refs[-1]
    for k, ref in enumerate(refs[:-1]):
        out[k] = ref[...]


def first_rows(meta, row, starts, weight):
    top, left, height, breadth = (meta[0], meta[1], meta[2], meta[3])
    mask = column_mask(left - 8, 128, breadth)
    pre = dot_nn(four_rows(row, [h - 1 for h in starts]), weight)
    out = {}
    for k, value in enumerate(split_rows(pre, starts)):
        h = starts[k // 2] + k % 2
        act = rounded(value * sigmoid(value)) * (mask * row_ok(top - 8 + h, height))
        out[h] = (value, three(act))
    return out


def second_rows(meta, row, starts, weight):
    top, left, height, breadth = (meta[0], meta[1], meta[2], meta[3])
    mask = column_mask(left // 2 - 4, 64, breadth // 2)
    rows = split_rows(dot_nn(four_rows(row, [h - 1 for h in starts]), weight), starts)
    out = {}
    for k, h in enumerate(starts):
        pre = rows[2 * k : 2 * k + 2]
        act = [(v * sigmoid(v)).astype(BF) for v in pre]
        small = rounded(0.25 * pooled_pair(act[0].astype(F32) + act[1].astype(F32)))
        small = small * (mask * row_ok(top // 2 - 4 + h // 2, height // 2))
        out[h] = (pre, act, three(small))
    return out


INNER_FIRST = [9, 11, 13, 15, 17, 19, 21]
INNER_SECOND = [10, 12, 14, 16, 18, 20]


def inner_kernel(meta, feat, pair, other, weight1, weight2, feat3, act3, slope1, pool3, slope2, act):
    for k in range(16):
        before, after = sides(meta, pair[k, 0:32, :], other[k, 0:32, :])
        feat3[k] = three(jnp.concatenate([before, feat[k], after], axis=0).astype(F32))
    for h, (pre, wide) in first_rows(meta, lambda h: feat3[h - 8], INNER_FIRST, weight1[...]).items():
        act3[h - 9] = wide
        slope1[h - 9] = slope_of(pre[16:112])
    for h, (pre, value, small) in second_rows(meta, lambda h: act3[h - 9], INNER_SECOND, weight2[...]).items():
        pool3[h // 2 - 5] = small
        for e in range(2):
            slope2[h - 10 + e] = slope_of(pre[e][16:112])
            act[h - 10 + e] = value[e][32:96]


def outer_first_kernel(
    meta, inner, outer, feat3i, act3i, slope1i, weight1, act3, slope1, feat3o, act3o, feat3
):
    below_at = 24 * (meta[4] % 2)
    for k in range(8):
        feat3[k + below_at] = three(outer[128 * k : 128 * k + 128, :].astype(F32))
        feat3[k + 24 - below_at] = three(inner[128 * k : 128 * k + 128, :].astype(F32))
    feat3[8:24] = feat3i[...]
    for starts in ([1, 3, 5, 7], [23, 25, 27, 29]):
        for h, (pre, wide) in first_rows(meta, lambda h: feat3[h], starts, weight1[...]).items():
            act3[h - 1] = wide
            if 7 <= h <= 24:
                slope1[h - 7] = slope_of(pre[16:112])
    slope1[2:16] = slope1i[...]
    act3[8:22] = act3i[...]
    feat3o[...] = feat3[7:25, 32:96, :]
    act3o[...] = act3[6:24, 32:96, :]


def outer_second_kernel(meta, act3, pool3i, slope2i, acti, weight2, pool3, slope2, act):
    for starts in ([2, 4, 6, 8], [22, 24, 26, 28]):
        for h, (pre, value, small) in second_rows(meta, lambda h: act3[h - 1], starts, weight2[...]).items():
            pool3[h // 2 - 1] = small
            for e in range(2):
                if 6 <= h + e < 26:
                    slope2[h + e - 6] = slope_of(pre[e][16:112])
                if 8 <= h + e < 24:
                    act[h + e - 8] = value[e][32:96]
    pool3[4:10] = pool3i[...]
    slope2[4:16] = slope2i[...]
    act[2:14] = acti[...]


def inner_step(meta, feat, pair, other, weight1, weight2):
    return call(
        inner_kernel,
        "forward_inner",
        (
            ((16, 128, 384), BF),
            ((14, 128, 384), BF),
            ((14, 96, CH), F32),
            ((6, 64, 384), BF),
            ((12, 96, CH), F32),
            ((12, 64, CH), BF),
        ),
        (meta, feat, pair, other, weight1, weight2),
        limit=24,
        flops=0,
    )


def outer_first_step(meta, inner, outer, feat3, act3, slope1, weight1):
    return call(
        outer_first_kernel,
        "outer_first",
        (((30, 128, 384), BF), ((18, 96, CH), F32), ((18, 64, 384), BF), ((18, 64, 384), BF)),
        (meta, inner, outer, feat3, act3, slope1, weight1),
        (((32, 128, 384), BF),),
        limit=20,
        flops=2 * 10**9,
    )


def outer_second_step(meta, act3, pool3, slope2, act, weight2):
    return call(
        outer_second_kernel,
        "outer_second",
        (((14, 64, 384), BF), ((20, 96, CH), F32), ((16, 64, CH), BF)),
        (meta, act3, pool3, slope2, act, weight2),
        limit=16,
        flops=4 * 10**9,
    )


def coarse_kernel(
    meta, pool3, cot, pair, other, inner, outer, near0, near1, near2, near3, far,
    own, projs_out, keep, send, pooled_grad, wcat, projs, wide3, projin,
):
    top, left, height, breadth, me = (meta[0], meta[1], meta[2], meta[3], meta[4])
    core = me % 2
    near = (near0, near1, near2, near3)
    for rel in range(16):
        c, x, y = (rel % 2, (rel // 2) % 4, rel // 8)
        place = pl.ds(pl.multiple_of((me ^ rel) * 16, 16), 16)
        source = far.at[x, y] if c else near[x].at[y]
        for t in range(9):
            wcat[place, t * CH : (t + 1) * CH] = source[16 * t : 16 * t + 16, :]
        projs[place, :] = source[144:160, :]
    proj_w = projs[...]

    def pair_sum(a, b):
        return pooled_pair(a.astype(F32) + b.astype(F32))

    below_at = 10 * core
    for k in range(2):
        projin[k + below_at] = pair_sum(cot_edge(outer, 2 * k), cot_edge(outer, 2 * k + 1))
        projin[k + 10 - below_at] = pair_sum(cot_edge(inner, 2 * k), cot_edge(inner, 2 * k + 1))

    for k in range(8):
        rows = slice(2 * k, 2 * k + 2)
        before, after = sides(meta, pair[rows, 32:48, :], other[rows, 32:48, :])
        both = jnp.concatenate([before, cot[rows], after], axis=1)
        projin[k + 2] = pair_sum(both[0], both[1])

    proj_in = projin[...].reshape(576, CH)
    proj_in_bf = proj_in.astype(BF)
    lhs = jnp.concatenate([pool3[r : r + 12].reshape(768, 3 * CH) for r in range(3)], axis=1)
    pre = dot_nt(lhs, wcat[...]).reshape(12, 64, WIDE)[:, 8:56].reshape(576, WIDE)
    sigma = sigmoid(pre)
    coarse_act = pre * sigma
    act_grad = dot_nt(proj_in_bf, proj_w)
    grad = rounded(act_grad * (sigma * (1.0 + pre * (1.0 - sigma)))).reshape(12, 48, WIDE)
    mask = column_mask(left // 2 - 2, 48, breadth // 2)
    mask = jnp.concatenate([mask, mask], axis=1)
    grad = masked(grad, mask, top // 2 - 2, height // 2)
    wide3[...] = three(grad.reshape(576, WIDE)).reshape(12, 48, 3 * WIDE)
    own_grad = grad[2:10, 8:40].reshape(256, WIDE).astype(BF)
    own_act = coarse_act.reshape(12, 48, WIDE)[2:10, 8:40].reshape(256, WIDE).astype(BF)
    own_in = proj_in.reshape(12, 48, CH)[2:10, 8:40].reshape(256, CH).astype(BF)

    def emit(first, last, value):
        value = value.reshape(8, 2, 16, CH)
        even, odd = (value[:, 0], value[:, 1])
        keep[:, first:last, :] = jnp.where(core == 0, even, odd).astype(BF)
        send[:, first:last, :] = jnp.where(core == 0, odd, even).astype(BF)

    source = [pool3[2 + r : 10 + r, 16:48, :].reshape(256, 3 * CH) for r in range(3)]
    part = dot_tn(own_grad, jnp.concatenate(source, axis=1))
    for t in range(9):
        emit(16 * t, 16 * t + 16, part[:, t * CH : (t + 1) * CH])
    emit(144, 160, dot_tn(own_act, own_in))
    total = None
    for r in range(3):
        lhs = wide3[r : r + 10].reshape(480, 3 * WIDE)
        first = 3 * (2 - r)
        rhs = jnp.concatenate([wcat[:, (first + 2 - s) * CH : (first + 3 - s) * CH] for s in range(3)], axis=0)
        part = dot_nn(lhs, rhs)
        total = part if total is None else total + part
    pooled_grad[...] = total.reshape(10, 48, CH)
    own[...] = own_act
    projs_out[...] = proj_w


def blend_kernel(own, proj, act, blended):
    projected = dot_nn(own[...], proj[...]).reshape(8, 32, CH)
    for k in range(8):
        row = repeated(projected[k])
        for e in range(2):
            blended[2 * k + e] = (act[2 * k + e].astype(F32) + row).astype(BF)


def coarse_step(meta, pool3, cot, halo, near, far):
    return call(
        coarse_kernel,
        "coarse_step",
        (((256, WIDE), BF), ((WIDE, CH), BF), ((8, 160, CH), BF), ((8, 160, CH), BF), ((10, 48, CH), F32)),
        (meta, pool3, cot) + halo + tuple(near) + (far,),
        (
            ((WIDE, 9 * CH), BF),
            ((WIDE, CH), BF),
            ((12, 48, 3 * WIDE), BF),
            ((12, 48, CH), F32),
        ),
        limit=20,
        flops=2 * 10**9,
    )


def backward_kernel(
    meta, pooled_grad, cot, pair, other, inner, outer, slope1, slope2, feat3, act3, back_w,
    keep, send, first3, second3, grads,
):
    top, left, height, breadth = (meta[0], meta[1], meta[2], meta[3])
    mask = column_mask(left - 4, 96, breadth)

    def second_pair(k, both):
        wide = 0.25 * repeated(pooled_grad[k])
        for e in range(2):
            value = rounded((both[e].astype(F32) + wide) * slope2[2 * k + e])
            second3[2 * k + e] = three(value * (mask * row_ok(top - 2 + 2 * k + e, height)))

    first_core = meta[4] % 2 == 0
    second_pair(0, lax.select(first_core, cot_edge(outer, 2, 2), cot_edge(inner, 2, 2)))
    second_pair(9, lax.select(first_core, cot_edge(inner, 0, 2), cot_edge(outer, 0, 2)))
    for k in range(8):
        rows = slice(2 * k, 2 * k + 2)
        before, after = sides(meta, pair[rows, 32:48, :], other[rows, 32:48, :])
        second_pair(k + 1, jnp.concatenate([before, cot[rows], after], axis=1))

    def emit(base, parts):
        for r in range(3):
            grads[base + 384 * r : base + 384 * (r + 1), :] = parts[r].astype(BF)

    for starts in ([0, 2, 4, 6], [8, 10, 12, 14, 16]):
        value = dot_nt(four_rows(lambda h: second3[h], starts), back_w[...])
        for k, row in enumerate(split_rows(value, starts)):
            h = starts[k // 2] + k % 2
            row = rounded(row * slope1[h]) * (mask * row_ok(top - 1 + h, height))
            first3[h] = three(row)[16:80]
    emit(1152, weight_grad(act3[...], second3[2:18, 16:80, CH : 2 * CH]))
    emit(0, weight_grad(feat3[...], first3[1:17, :, CH : 2 * CH]))
    core = meta[4] % 2
    for k in range(8):
        keep[k] = grads[pl.ds(pl.multiple_of((2 * k + core) * 144, 16), 144), :]
        send[k] = grads[pl.ds(pl.multiple_of((2 * k + 1 - core) * 144, 16), 144), :]


def fine_backward(meta, pooled_grad, cot, halo, slope1, slope2, feat3, act3, back_w):
    return call(
        backward_kernel,
        "fine_backward",
        (((8, 144, CH), BF), ((8, 144, CH), BF), ((18, 64, 384), BF)),
        (meta, pooled_grad, cot) + halo + (slope1, slope2, feat3, act3, back_w),
        (((20, 96, 384), BF), ((2304, CH), BF)),
        limit=20,
        flops=2 * 10**9,
    )


def feature_kernel(first3, back_w, out):
    for starts in ([0, 2, 4, 6], [8, 10, 12, 14]):
        value = dot_nt(four_rows(lambda h: first3[h], starts), back_w[...])
        for k, row in enumerate(split_rows(value, starts)):
            out[starts[0] + k] = row.astype(BF)


def feature_step(first3, back_w):
    return call(feature_kernel, "feature_step", (((16, 64, CH), BF),), (first3, back_w), limit=12, flops=10**9)[0]


def scatter_core_kernel(keep_c, keep_f, got_c, got_f, out):
    for k in range(8):
        out[k, 0:160, :] = (keep_c[k].astype(F32) + got_c[k].astype(F32)).astype(BF)
        out[k, 160:304, :] = (keep_f[k].astype(F32) + got_f[k].astype(F32)).astype(BF)


def scatter_row_kernel(got, out, total):
    value = got[0].astype(F32)
    for k in range(1, 8):
        value = value + got[k].astype(F32)
    total[0:304, :] = value
    total[304:336, :] = jnp.zeros((32, CH), F32)
    for k in range(16):
        out[k] = total[20 * k : 20 * k + 32, :].astype(BF)


def scatter_column_kernel(got, out):
    value = got[0].astype(F32)
    for k in range(1, 16):
        value = value + got[k].astype(F32)
    value = value.astype(BF)
    for k in range(16):
        out[k] = value


def gather_column_kernel(scale, got, conv, proj, fine, total):
    for k in range(16):
        total[20 * k : 20 * k + 32, :] = got[k].astype(F32)
    for k in range(9):
        conv[k] = total[16 * k : 16 * k + 16, :] * scale
    proj[...] = total[144:160, :] * scale
    value = total[160:304, :].astype(BF)
    for k in range(8):
        fine[k] = value


def finish_kernel(scale, meta, mine, other, first, second, slabs, done):
    core = meta[4] % 2
    copies = []
    for at in range(8):
        out = first if at < 4 else second
        a = mine[at].astype(F32) * scale
        b = other[at].astype(F32) * scale
        slabs[2 * at] = jnp.where(core == 0, a, b)
        slabs[2 * at + 1] = jnp.where(core == 0, b, a)
        pair = slabs.at[2 * at : 2 * at + 2]
        copies.append(pltpu.make_async_copy(pair, out.at[2 * (at % 4) : 2 * (at % 4) + 2], done.at[at]))
        copies[at].start()
    for copy in copies:
        copy.wait()


def swap(value, axis, mask):
    count = lax.axis_size(axis)
    return lax.ppermute(value, axis, [(i, i ^ mask) for i in range(count)])


def swap_outer(value, axis):
    count = lax.axis_size(axis)
    pairs = [(i, i + 1 if i % 2 else i - 1) for i in range(1, count - 1)]
    return lax.ppermute(value, axis, pairs)


def exchange_row(value):
    count = lax.axis_size("row")
    groups = [list(range(c, count, 2)) for c in range(2)]
    return lax.all_to_all(value, "row", 0, 0, axis_index_groups=groups, tiled=True)


def exchange_column(value):
    return lax.all_to_all(value, "col", 0, 0, tiled=True)


def after_all(value, *others):
    return lax.optimization_barrier((value,) + others)[0]


def local(features, conv_first, conv_second, coarse_conv, coarse_proj, cotangent):
    rows, cols = (lax.axis_size("row"), lax.axis_size("col"))
    height, breadth = (features.shape[0] * rows, features.shape[1] * cols)
    fine_scale = 1.0 / (height * breadth * features.shape[2]) ** 0.5
    coarse_scale = 2.0 * fine_scale
    me, mine = (lax.axis_index("row"), lax.axis_index("col"))
    fixed = [jnp.int32(height), jnp.int32(breadth)]
    meta = jnp.stack([me * 16, mine * 16] + fixed + [me, mine]).astype(jnp.int32)
    feat = features.reshape(16, 64, CH)
    cot = cotangent.reshape(16, 64, CH)
    conv = coarse_conv.reshape(9, CH, 16).swapaxes(1, 2)
    slab = ((160, CH), BF)

    side = ((16, 48, CH), BF)
    pair, other = call(
        pack_columns_kernel,
        "pack_columns",
        (side, side),
        (meta, feat, cot),
        (pltpu.SemaphoreType.DMA((4,)),),
        far=(1, 2),
    )
    w1, w2 = (conv_first.reshape(1152, CH), conv_second.reshape(1152, CH))
    big, wide = (((16, 64, CH), BF), ((1536, 256), BF))
    feat_in, cot_in, own = call(
        bring_kernel,
        "bring",
        (big, big, slab),
        (after_all(feat, pair), cot, conv, coarse_proj),
        (pltpu.SemaphoreType.DMA((12,)),),
        far=(0, 1, 2, 3),
        flops=4 * 10**9,
    )
    own_far = swap(own, "row", 8)
    weight1, weight2, back1, back2 = call(
        weights_kernel,
        "weights",
        (wide, wide, ((256, 1536), BF), ((256, 1536), BF)),
        (after_all(w1, feat_in), w2),
        (((1152, CH), BF), ((1152, CH), BF), pltpu.SemaphoreType.DMA((2,))),
        far=(0, 1),
        flops=4 * 10**9,
    )
    pair = swap(pair, "col", 1)
    other = swap_outer(other, "col")
    edge = ((EDGE, CH), BF)
    inner, outer, near0 = call(
        pack_rows_kernel,
        "pack_rows",
        (edge, edge, ((2, 160, CH), BF)),
        (meta, feat_in, cot_in, pair, after_all(other, weight1), own, own_far),
    )
    inner = swap(inner, "row", 1)
    outer = swap_outer(outer, "row")
    feat3, act3, slope1, pool3, slope2, act = inner_step(meta, feat_in, pair, other, weight1, weight2)
    near0 = after_all(near0, slope1)
    near = [near0] + [swap(near0, "row", 2 * k) for k in range(1, 4)]
    act3, slope1, feat3, act3o = outer_first_step(meta, inner, outer, feat3, act3, slope1, weight1)
    near = list(lax.optimization_barrier((slope1, *near)))[1:]
    far = swap(call(stack_kernel, "stack_eight", (((4, 2, 160, CH), BF),), near)[0], "row", 1)
    pool3, slope2, act = outer_second_step(meta, act3, pool3, slope2, act, weight2)
    halo = (pair, other, inner, outer)
    own_act, proj, keep_c, send_c, pooled_grad = coarse_step(meta, pool3, cot_in, halo, near, far)
    got_c = swap(send_c, "row", 1)
    keep_f, send_f, first3 = fine_backward(
        meta, pooled_grad, cot_in, halo, slope1, slope2, feat3, act3o, back2
    )
    got_f = swap(send_f, "row", 1)
    feature_grad = feature_step(first3, back1)

    got_f = after_all(got_f, feature_grad)
    part = call(scatter_core_kernel, "scatter_core", (((8, 304, CH), BF),), (keep_c, keep_f, got_c, got_f))[0]
    part = call(
        scatter_row_kernel, "scatter_row", (((16, 32, CH), BF),), (exchange_row(part),), (((336, CH), F32),)
    )[0]
    part = call(scatter_column_kernel, "scatter_column", (((16, 32, CH), BF),), (exchange_column(part),))[0]
    conv_grad, proj_grad, fine = call(
        functools.partial(gather_column_kernel, coarse_scale),
        "gather_column",
        (((9, 16, CH), F32), ((16, CH), F32), ((8, 144, CH), BF)),
        (exchange_column(part),),
        (((336, CH), F32),),
    )
    fine = exchange_row(fine)
    blended = call(blend_kernel, "blend", (((16, 64, CH), BF),), (after_all(own_act, fine), proj, act), flops=10**9)[0]
    other = after_all(swap(fine, "row", 1), blended)
    first, second = call(
        functools.partial(finish_kernel, fine_scale),
        "finish",
        (((8, 144, CH), F32), ((8, 144, CH), F32)),
        (meta, fine, other),
        (((16, 144, CH), F32), pltpu.SemaphoreType.DMA((8,))),
        far_out=True,
    )
    shape = features.shape
    return (
        blended.reshape(shape),
        feature_grad.reshape(shape),
        first.reshape(3, 3, CH, CH),
        second.reshape(3, 3, CH, CH),
        conv_grad.reshape(3, 3, 16, CH).swapaxes(2, 3),
        proj_grad,
    )


def solution(mesh):
    in_specs = (
        P("row", "col", None, None),
        P(),
        P(),
        P(None, None, None, "row"),
        P("row", None),
        P("row", "col", None, None),
    )
    out_specs = (
        P("row", "col", None, None),
        P("row", "col", None, None),
        P(),
        P(),
        P(None, None, None, "row"),
        P("row", None),
    )
    return jax.shard_map(local, mesh=mesh, in_specs=in_specs, out_specs=out_specs, check_vma=False)
```

```python
import functools

import jax
import jax.numpy as jnp
from jax import lax
from jax.experimental import pallas as pl
from jax.experimental.pallas import tpu as pltpu
from jax.sharding import PartitionSpec as P

BF = jnp.bfloat16
F32 = jnp.float32
CH = 128
WIDE = 256
MIB = 1024 * 1024
VM = pl.BlockSpec(memory_space=pltpu.VMEM)
SM = pl.BlockSpec(memory_space=pltpu.SMEM)
HBM = pl.BlockSpec(memory_space=pltpu.HBM)


def call(kernel, name, outs, ins, scratch=(), limit=16, flops=0, moved=0, far=()):
    ins = [pltpu.with_memory_space_constraint(v, pltpu.HBM) if k in far else v for k, v in enumerate(ins)]
    shapes = tuple(jax.ShapeDtypeStruct(shape, dtype) for shape, dtype in outs)
    return pl.pallas_call(
        kernel,
        name=name,
        out_shape=shapes,
        in_specs=[HBM if k in far else SM if v.ndim == 1 else VM for k, v in enumerate(ins)],
        out_specs=tuple(VM for _ in outs),
        scratch_shapes=[pltpu.VMEM(*v) if isinstance(v, tuple) else v for v in scratch],
        compiler_params=pltpu.CompilerParams(vmem_limit_bytes=limit * MIB),
        cost_estimate=pl.CostEstimate(flops=flops, bytes_accessed=moved, transcendentals=0),
    )(*ins)


def dot_nn(a, b):
    return jnp.dot(a, b, preferred_element_type=F32)


def dot_nt(a, b):
    return lax.dot_general(a, b, (((1,), (1,)), ((), ())), preferred_element_type=F32)


def dot_tn(a, b):
    return lax.dot_general(a, b, (((0,), (0,)), ((), ())), preferred_element_type=F32)


def sigmoid(value):
    return 0.5 * jnp.tanh(0.5 * value) + 0.5


def slope_of(value):
    sigma = sigmoid(value)
    return sigma * (1.0 + value * (1.0 - sigma))


def rounded(value):
    return value.astype(BF).astype(F32)


def three(value):
    count = value.shape[0]
    left = pltpu.roll(value, 4, 0)
    right = pltpu.roll(value, count - 4, 0)
    return jnp.concatenate([left.astype(BF), value.astype(BF), right.astype(BF)], axis=1)


def paired(weight, axis):
    pad = jnp.zeros((3 * CH, CH) if axis == 0 else (CH, 3 * CH), BF)
    return jnp.concatenate(
        [jnp.concatenate([weight, pad], axis=axis), jnp.concatenate([pad, weight], axis=axis)], axis=1 - axis
    )


def flipped(weight):
    return jnp.concatenate([weight[(8 - t) * CH : (9 - t) * CH, :] for t in range(9)], axis=1)


def four_rows(row, starts):
    parts = [jnp.concatenate([row(h + k) for h in starts], axis=0) for k in range(4)]
    return jnp.concatenate(parts, axis=1)


def split_rows(value, starts):
    size = value.shape[0] // len(starts)
    out = []
    for k in range(len(starts)):
        out += [value[k * size : (k + 1) * size, e * CH : (e + 1) * CH] for e in range(2)]
    return out


def weight_grad(source, grad):
    gap = jnp.zeros((64, CH), BF)
    parts = []
    for r in range(3):
        parts.append(jnp.concatenate([gap] * r + [grad.reshape(1024, CH)] + [gap] * (2 - r), axis=0))
    whole = dot_tn(source.reshape(1152, 3 * CH), jnp.concatenate(parts, axis=1))
    return [whole[:, r * CH : (r + 1) * CH] for r in range(3)]


def column_mask(first, width, limit):
    place = first + lax.broadcasted_iota(jnp.int32, (width, CH), 0) // 4
    return jnp.where((place >= 0) & (place < limit), 1.0, 0.0).astype(F32)


def row_ok(place, limit):
    return jnp.where((place >= 0) & (place < limit), 1.0, 0.0).astype(F32)


def masked(value, mask, first, limit):
    rows = []
    for k in range(value.shape[0]):
        rows.append((value[k] * (mask * row_ok(first + k, limit)))[None])
    return jnp.concatenate(rows, axis=0)


def pooled_pair(row):
    count = row.shape[0]
    low = (row + pltpu.roll(row, count - 4, 0)).reshape(count // 16, 2, 8, CH)
    high = (row + pltpu.roll(row, 4, 0)).reshape(count // 16, 2, 8, CH)
    first = lax.broadcasted_iota(jnp.int32, (count // 16, 8, CH), 1) < 4
    return jnp.where(first, low[:, 0], high[:, 1]).reshape(count // 2, CH)


def repeated(row):
    count = row.shape[0]
    first = lax.broadcasted_iota(jnp.int32, (count, CH), 0) % 8 < 4
    even = jnp.where(first, row, pltpu.roll(row, 4, 0)).reshape(count // 8, 1, 8, CH)
    odd = jnp.where(first, pltpu.roll(row, count - 4, 0), row).reshape(count // 8, 1, 8, CH)
    return jnp.concatenate([even, odd], axis=1).reshape(count * 2, CH)


def aligned(start, size):
    return pl.ds(pl.multiple_of(start, 16), size)


def sides(meta, pair, other):
    even = meta[5] % 2 == 0
    return lax.select(even, other, pair), lax.select(even, pair, other)


def pack_columns_kernel(meta, feat, cot, pair, other, done):
    odd = meta[5] % 2
    pairs = [
        (feat.at[:, aligned(32 - 32 * odd, 32), :], pair.at[:, 0:32, :]),
        (cot.at[:, aligned(48 - 48 * odd, 16), :], pair.at[:, 32:48, :]),
        (feat.at[:, aligned(32 * odd, 32), :], other.at[:, 0:32, :]),
        (cot.at[:, aligned(48 * odd, 16), :], other.at[:, 32:48, :]),
    ]
    copies = [pltpu.make_async_copy(a, b, done.at[k]) for k, (a, b) in enumerate(pairs)]
    for copy in copies:
        copy.start()
    for copy in copies:
        copy.wait()


EDGE = 8 * 128 + 4 * 96


def cot_edge(ref, first, count=1):
    value = ref[1024 + 96 * first : 1024 + 96 * (first + count), :]
    return value if count == 1 else value.reshape(count, 96, CH)


def bring_kernel(feat_far, cot_far, conv, proj, feat, cot, weights, done):
    pairs = [(feat_far, feat), (cot_far, cot), (proj, weights.at[144:160, :])]
    pairs += [(conv.at[t], weights.at[16 * t : 16 * t + 16, :]) for t in range(9)]
    copies = [pltpu.make_async_copy(a, b, done.at[k]) for k, (a, b) in enumerate(pairs)]
    for copy in copies:
        copy.start()
    for copy in copies:
        copy.wait()


def weights_kernel(w1_far, w2_far, weight1, weight2, back1, back2, w1, w2, done):
    copies = [pltpu.make_async_copy(a, b, done.at[k]) for k, (a, b) in enumerate(((w1_far, w1), (w2_far, w2)))]
    for copy in copies:
        copy.start()
    for copy, w, weight, back in zip(copies, (w1, w2), (weight1, weight2), (back1, back2)):
        copy.wait()
        weight[...] = paired(w[...], 0)
        back[...] = paired(flipped(w), 1)


def pack_rows_kernel(meta, feat, cot, pair, other, own, far, inner, outer, both):
    core = meta[4] % 2
    for low, out in ((1 - core, inner), (core, outer)):
        jobs = [(128 * k, feat, 8 * low + k, 0, 32) for k in range(8)]
        jobs += [(1024 + 96 * k, cot, 12 * low + k, 32, 16) for k in range(4)]
        for base, middle, row, first, width in jobs:
            before, after = sides(meta, pair[row, first : first + width, :], other[row, first : first + width, :])
            out[base : base + width, :] = before
            out[base + width : base + width + 64, :] = middle[row]
            out[base + width + 64 : base + 2 * width + 64, :] = after
    both[0] = own[...]
    both[1] = far[...]


def stack_kernel(*refs):
    out = refs[-1]
    for k, ref in enumerate(refs[:-1]):
        out[k] = ref[...]


def first_rows(meta, row, starts, weight):
    top, left, height, breadth = (meta[0], meta[1], meta[2], meta[3])
    mask = column_mask(left - 8, 128, breadth)
    pre = dot_nn(four_rows(row, [h - 1 for h in starts]), weight)
    out = {}
    for k, value in enumerate(split_rows(pre, starts)):
        h = starts[k // 2] + k % 2
        act = rounded(value * sigmoid(value)) * (mask * row_ok(top - 8 + h, height))
        out[h] = (value, three(act))
    return out


def second_rows(meta, row, starts, weight):
    top, left, height, breadth = (meta[0], meta[1], meta[2], meta[3])
    mask = column_mask(left // 2 - 4, 64, breadth // 2)
    rows = split_rows(dot_nn(four_rows(row, [h - 1 for h in starts]), weight), starts)
    out = {}
    for k, h in enumerate(starts):
        pre = rows[2 * k : 2 * k + 2]
        act = [(v * sigmoid(v)).astype(BF) for v in pre]
        small = rounded(0.25 * pooled_pair(act[0].astype(F32) + act[1].astype(F32)))
        small = small * (mask * row_ok(top // 2 - 4 + h // 2, height // 2))
        out[h] = (pre, act, three(small))
    return out


INNER_FIRST = [9, 11, 13, 15, 17, 19, 21]
INNER_SECOND = [10, 12, 14, 16, 18, 20]


def inner_kernel(meta, feat, pair, other, weight1, weight2, feat3, act3, slope1, pool3, slope2, act):
    for k in range(16):
        before, after = sides(meta, pair[k, 0:32, :], other[k, 0:32, :])
        feat3[k] = three(jnp.concatenate([before, feat[k], after], axis=0).astype(F32))
    for h, (pre, wide) in first_rows(meta, lambda h: feat3[h - 8], INNER_FIRST, weight1[...]).items():
        act3[h - 9] = wide
        slope1[h - 9] = slope_of(pre[16:112])
    for h, (pre, value, small) in second_rows(meta, lambda h: act3[h - 9], INNER_SECOND, weight2[...]).items():
        pool3[h // 2 - 5] = small
        for e in range(2):
            slope2[h - 10 + e] = slope_of(pre[e][16:112])
            act[h - 10 + e] = value[e][32:96]


def outer_kernel(
    meta, inner, outer, feat3i, act3i, slope1i, pool3i, slope2i, acti, weight1, weight2,
    pool3, slope1, slope2, act, feat3o, act3o, feat3, act3,
):
    below_at = 24 * (meta[4] % 2)
    for k in range(8):
        feat3[k + below_at] = three(outer[128 * k : 128 * k + 128, :].astype(F32))
        feat3[k + 24 - below_at] = three(inner[128 * k : 128 * k + 128, :].astype(F32))
    feat3[8:24] = feat3i[...]
    for starts in ([1, 3, 5, 7], [23, 25, 27, 29]):
        for h, (pre, wide) in first_rows(meta, lambda h: feat3[h], starts, weight1[...]).items():
            act3[h - 1] = wide
            if 7 <= h <= 24:
                slope1[h - 7] = slope_of(pre[16:112])
    slope1[2:16] = slope1i[...]
    act3[8:22] = act3i[...]
    for starts in ([2, 4, 6, 8], [22, 24, 26, 28]):
        for h, (pre, value, small) in second_rows(meta, lambda h: act3[h - 1], starts, weight2[...]).items():
            pool3[h // 2 - 1] = small
            for e in range(2):
                if 6 <= h + e < 26:
                    slope2[h + e - 6] = slope_of(pre[e][16:112])
                if 8 <= h + e < 24:
                    act[h + e - 8] = value[e][32:96]
    pool3[4:10] = pool3i[...]
    slope2[4:16] = slope2i[...]
    act[2:14] = acti[...]
    feat3o[...] = feat3[7:25, 32:96, :]
    act3o[...] = act3[6:24, 32:96, :]


def inner_step(meta, feat, pair, other, weight1, weight2):
    return call(
        inner_kernel,
        "forward_inner",
        (
            ((16, 128, 384), BF),
            ((14, 128, 384), BF),
            ((14, 96, CH), F32),
            ((6, 64, 384), BF),
            ((12, 96, CH), F32),
            ((12, 64, CH), BF),
        ),
        (meta, feat, pair, other, weight1, weight2),
        limit=24,
        flops=0,
    )


def outer_step(meta, inner, outer, parts, weight1, weight2):
    return call(
        outer_kernel,
        "forward_outer",
        (
            ((14, 64, 384), BF),
            ((18, 96, CH), F32),
            ((20, 96, CH), F32),
            ((16, 64, CH), BF),
            ((18, 64, 384), BF),
            ((18, 64, 384), BF),
        ),
        (meta, inner, outer) + tuple(parts) + (weight1, weight2),
        (((32, 128, 384), BF), ((30, 128, 384), BF)),
        limit=24,
        flops=4 * 10**9,
    )


def coarse_kernel(
    meta, pool3, cot, pair, other, inner, outer, near0, near1, near2, near3, far,
    own, projs_out, keep, send, pooled_grad, wcat, projs, wide3, projin,
):
    top, left, height, breadth, me = (meta[0], meta[1], meta[2], meta[3], meta[4])
    core = me % 2
    near = (near0, near1, near2, near3)
    for rel in range(16):
        c, x, y = (rel % 2, (rel // 2) % 4, rel // 8)
        place = pl.ds(pl.multiple_of((me ^ rel) * 16, 16), 16)
        source = far.at[x, y] if c else near[x].at[y]
        for t in range(9):
            wcat[place, t * CH : (t + 1) * CH] = source[16 * t : 16 * t + 16, :]
        projs[place, :] = source[144:160, :]
    proj_w = projs[...]

    def pair_sum(a, b):
        return pooled_pair(a.astype(F32) + b.astype(F32))

    below_at = 10 * core
    for k in range(2):
        projin[k + below_at] = pair_sum(cot_edge(outer, 2 * k), cot_edge(outer, 2 * k + 1))
        projin[k + 10 - below_at] = pair_sum(cot_edge(inner, 2 * k), cot_edge(inner, 2 * k + 1))

    for k in range(8):
        rows = slice(2 * k, 2 * k + 2)
        before, after = sides(meta, pair[rows, 32:48, :], other[rows, 32:48, :])
        both = jnp.concatenate([before, cot[rows], after], axis=1)
        projin[k + 2] = pair_sum(both[0], both[1])

    proj_in = projin[...].reshape(576, CH)
    proj_in_bf = proj_in.astype(BF)
    lhs = jnp.concatenate([pool3[r : r + 12].reshape(768, 3 * CH) for r in range(3)], axis=1)
    pre = dot_nt(lhs, wcat[...]).reshape(12, 64, WIDE)[:, 8:56].reshape(576, WIDE)
    sigma = sigmoid(pre)
    coarse_act = pre * sigma
    act_grad = dot_nt(proj_in_bf, proj_w)
    grad = rounded(act_grad * (sigma * (1.0 + pre * (1.0 - sigma)))).reshape(12, 48, WIDE)
    mask = column_mask(left // 2 - 2, 48, breadth // 2)
    mask = jnp.concatenate([mask, mask], axis=1)
    grad = masked(grad, mask, top // 2 - 2, height // 2)
    wide3[...] = three(grad.reshape(576, WIDE)).reshape(12, 48, 3 * WIDE)
    own_grad = grad[2:10, 8:40].reshape(256, WIDE).astype(BF)
    own_act = coarse_act.reshape(12, 48, WIDE)[2:10, 8:40].reshape(256, WIDE).astype(BF)
    own_in = proj_in.reshape(12, 48, CH)[2:10, 8:40].reshape(256, CH).astype(BF)

    def emit(first, last, value):
        value = value.reshape(8, 2, 16, CH)
        even, odd = (value[:, 0], value[:, 1])
        keep[:, first:last, :] = jnp.where(core == 0, even, odd).astype(BF)
        send[:, first:last, :] = jnp.where(core == 0, odd, even).astype(BF)

    source = [pool3[2 + r : 10 + r, 16:48, :].reshape(256, 3 * CH) for r in range(3)]
    part = dot_tn(own_grad, jnp.concatenate(source, axis=1))
    for t in range(9):
        emit(16 * t, 16 * t + 16, part[:, t * CH : (t + 1) * CH])
    emit(144, 160, dot_tn(own_act, own_in))
    total = None
    for r in range(3):
        lhs = wide3[r : r + 10].reshape(480, 3 * WIDE)
        first = 3 * (2 - r)
        rhs = jnp.concatenate([wcat[:, (first + 2 - s) * CH : (first + 3 - s) * CH] for s in range(3)], axis=0)
        part = dot_nn(lhs, rhs)
        total = part if total is None else total + part
    pooled_grad[...] = total.reshape(10, 48, CH)
    own[...] = own_act
    projs_out[...] = proj_w


def blend_kernel(own, proj, act, blended):
    projected = dot_nn(own[...], proj[...]).reshape(8, 32, CH)
    for k in range(8):
        row = repeated(projected[k])
        for e in range(2):
            blended[2 * k + e] = (act[2 * k + e].astype(F32) + row).astype(BF)


def coarse_step(meta, pool3, cot, halo, near, far):
    return call(
        coarse_kernel,
        "coarse_step",
        (((256, WIDE), BF), ((WIDE, CH), BF), ((8, 160, CH), BF), ((8, 160, CH), BF), ((10, 48, CH), F32)),
        (meta, pool3, cot) + halo + tuple(near) + (far,),
        (
            ((WIDE, 9 * CH), BF),
            ((WIDE, CH), BF),
            ((12, 48, 3 * WIDE), BF),
            ((12, 48, CH), F32),
        ),
        limit=20,
        flops=2 * 10**9,
    )


def backward_kernel(
    meta, pooled_grad, cot, pair, other, inner, outer, slope1, slope2, feat3, act3, back_w,
    keep, send, first3, second3, grads,
):
    top, left, height, breadth = (meta[0], meta[1], meta[2], meta[3])
    mask = column_mask(left - 4, 96, breadth)

    def second_pair(k, both):
        wide = 0.25 * repeated(pooled_grad[k])
        for e in range(2):
            value = rounded((both[e].astype(F32) + wide) * slope2[2 * k + e])
            second3[2 * k + e] = three(value * (mask * row_ok(top - 2 + 2 * k + e, height)))

    first_core = meta[4] % 2 == 0
    second_pair(0, lax.select(first_core, cot_edge(outer, 2, 2), cot_edge(inner, 2, 2)))
    second_pair(9, lax.select(first_core, cot_edge(inner, 0, 2), cot_edge(outer, 0, 2)))
    for k in range(8):
        rows = slice(2 * k, 2 * k + 2)
        before, after = sides(meta, pair[rows, 32:48, :], other[rows, 32:48, :])
        second_pair(k + 1, jnp.concatenate([before, cot[rows], after], axis=1))

    def emit(base, parts):
        for r in range(3):
            grads[base + 384 * r : base + 384 * (r + 1), :] = parts[r].astype(BF)

    for starts in ([0, 2, 4, 6], [8, 10, 12, 14, 16]):
        value = dot_nt(four_rows(lambda h: second3[h], starts), back_w[...])
        for k, row in enumerate(split_rows(value, starts)):
            h = starts[k // 2] + k % 2
            row = rounded(row * slope1[h]) * (mask * row_ok(top - 1 + h, height))
            first3[h] = three(row)[16:80]
    emit(1152, weight_grad(act3[...], second3[2:18, 16:80, CH : 2 * CH]))
    emit(0, weight_grad(feat3[...], first3[1:17, :, CH : 2 * CH]))
    core = meta[4] % 2
    for k in range(8):
        keep[k] = grads[pl.ds(pl.multiple_of((2 * k + core) * 144, 16), 144), :]
        send[k] = grads[pl.ds(pl.multiple_of((2 * k + 1 - core) * 144, 16), 144), :]


def fine_backward(meta, pooled_grad, cot, halo, slope1, slope2, feat3, act3, back_w):
    return call(
        backward_kernel,
        "fine_backward",
        (((8, 144, CH), BF), ((8, 144, CH), BF), ((18, 64, 384), BF)),
        (meta, pooled_grad, cot) + halo + (slope1, slope2, feat3, act3, back_w),
        (((20, 96, 384), BF), ((2304, CH), BF)),
        limit=20,
        flops=2 * 10**9,
    )


def feature_kernel(first3, back_w, out):
    for starts in ([0, 2, 4, 6], [8, 10, 12, 14]):
        value = dot_nt(four_rows(lambda h: first3[h], starts), back_w[...])
        for k, row in enumerate(split_rows(value, starts)):
            out[starts[0] + k] = row.astype(BF)


def feature_step(first3, back_w):
    return call(feature_kernel, "feature_step", (((16, 64, CH), BF),), (first3, back_w), limit=12, flops=10**9)[0]


def scatter_core_kernel(keep_c, keep_f, got_c, got_f, out):
    for k in range(8):
        out[k, 0:160, :] = (keep_c[k].astype(F32) + got_c[k].astype(F32)).astype(BF)
        out[k, 160:304, :] = (keep_f[k].astype(F32) + got_f[k].astype(F32)).astype(BF)


def scatter_row_kernel(got, out, total):
    value = got[0].astype(F32)
    for k in range(1, 8):
        value = value + got[k].astype(F32)
    total[0:304, :] = value
    total[304:336, :] = jnp.zeros((32, CH), F32)
    for k in range(16):
        out[k] = total[20 * k : 20 * k + 24, :].astype(BF)


def scatter_column_kernel(got, out):
    value = got[0].astype(F32)
    for k in range(1, 16):
        value = value + got[k].astype(F32)
    value = value.astype(BF)
    for k in range(16):
        out[k] = value


def gather_column_kernel(scale, got, conv, proj, fine, total):
    for k in range(16):
        total[20 * k : 20 * k + 24, :] = got[k].astype(F32)
    for k in range(9):
        conv[k] = total[16 * k : 16 * k + 16, :] * scale
    proj[...] = total[144:160, :] * scale
    value = total[160:304, :].astype(BF)
    for k in range(8):
        fine[k] = value


def finish_kernel(scale, meta, mine, other, first, second):
    core = meta[4] % 2
    for at in range(8):
        out = first if at < 4 else second
        a = mine[at].astype(F32) * scale
        b = other[at].astype(F32) * scale
        out[2 * (at % 4)] = jnp.where(core == 0, a, b)
        out[2 * (at % 4) + 1] = jnp.where(core == 0, b, a)


def swap(value, axis, mask):
    count = lax.axis_size(axis)
    return lax.ppermute(value, axis, [(i, i ^ mask) for i in range(count)])


def swap_outer(value, axis):
    count = lax.axis_size(axis)
    pairs = [(i, i + 1 if i % 2 else i - 1) for i in range(1, count - 1)]
    return lax.ppermute(value, axis, pairs)


def exchange_row(value):
    count = lax.axis_size("row")
    groups = [list(range(c, count, 2)) for c in range(2)]
    return lax.all_to_all(value, "row", 0, 0, axis_index_groups=groups, tiled=True)


def exchange_column(value):
    return lax.all_to_all(value, "col", 0, 0, tiled=True)


def after_all(value, *others):
    return lax.optimization_barrier((value,) + others)[0]


def local(features, conv_first, conv_second, coarse_conv, coarse_proj, cotangent):
    rows, cols = (lax.axis_size("row"), lax.axis_size("col"))
    height, breadth = (features.shape[0] * rows, features.shape[1] * cols)
    fine_scale = 1.0 / (height * breadth * features.shape[2]) ** 0.5
    coarse_scale = 2.0 * fine_scale
    me, mine = (lax.axis_index("row"), lax.axis_index("col"))
    fixed = [jnp.int32(height), jnp.int32(breadth)]
    meta = jnp.stack([me * 16, mine * 16] + fixed + [me, mine]).astype(jnp.int32)
    feat = features.reshape(16, 64, CH)
    cot = cotangent.reshape(16, 64, CH)
    conv = coarse_conv.reshape(9, CH, 16).swapaxes(1, 2)
    slab = ((160, CH), BF)

    side = ((16, 48, CH), BF)
    pair, other = call(
        pack_columns_kernel,
        "pack_columns",
        (side, side),
        (meta, feat, cot),
        (pltpu.SemaphoreType.DMA((4,)),),
        far=(1, 2),
    )
    w1, w2 = (conv_first.reshape(1152, CH), conv_second.reshape(1152, CH))
    big, wide = (((16, 64, CH), BF), ((1536, 256), BF))
    feat_in, cot_in, own = call(
        bring_kernel,
        "bring",
        (big, big, slab),
        (after_all(feat, pair), cot, conv, coarse_proj),
        (pltpu.SemaphoreType.DMA((12,)),),
        far=(0, 1, 2, 3),
        flops=4 * 10**9,
    )
    own_far = swap(own, "row", 8)
    weight1, weight2, back1, back2 = call(
        weights_kernel,
        "weights",
        (wide, wide, ((256, 1536), BF), ((256, 1536), BF)),
        (after_all(w1, feat_in), w2),
        (((1152, CH), BF), ((1152, CH), BF), pltpu.SemaphoreType.DMA((2,))),
        far=(0, 1),
        flops=4 * 10**9,
    )
    pair = swap(pair, "col", 1)
    other = swap_outer(other, "col")
    edge = ((EDGE, CH), BF)
    inner, outer, near0 = call(
        pack_rows_kernel,
        "pack_rows",
        (edge, edge, ((2, 160, CH), BF)),
        (meta, feat_in, cot_in, pair, after_all(other, weight1), own, own_far),
    )
    outer = swap_outer(outer, "row")
    inner = swap(inner, "row", 1)
    pair_in = after_all(pair, near0)
    near = [near0] + [swap(near0, "row", 2 * k) for k in range(1, 4)]
    parts = inner_step(meta, feat_in, pair_in, other, weight1, weight2)
    parts, near = lax.optimization_barrier((parts, near))
    far = swap(call(stack_kernel, "stack_eight", (((4, 2, 160, CH), BF),), near)[0], "row", 1)
    pool3, slope1, slope2, act, feat3, act3 = outer_step(meta, inner, outer, parts, weight1, weight2)
    halo = (pair, other, inner, outer)
    own_act, proj, keep_c, send_c, pooled_grad = coarse_step(meta, pool3, cot_in, halo, near, far)
    got_c = swap(send_c, "row", 1)
    keep_f, send_f, first3 = fine_backward(
        meta, pooled_grad, cot_in, halo, slope1, slope2, feat3, act3, back2
    )
    got_f = swap(send_f, "row", 1)
    feature_grad = feature_step(first3, back1)

    got_f = after_all(got_f, feature_grad)
    part = call(scatter_core_kernel, "scatter_core", (((8, 304, CH), BF),), (keep_c, keep_f, got_c, got_f))[0]
    part = call(
        scatter_row_kernel, "scatter_row", (((16, 24, CH), BF),), (exchange_row(part),), (((336, CH), F32),)
    )[0]
    part = call(scatter_column_kernel, "scatter_column", (((16, 24, CH), BF),), (exchange_column(part),))[0]
    conv_grad, proj_grad, fine = call(
        functools.partial(gather_column_kernel, coarse_scale),
        "gather_column",
        (((9, 16, CH), F32), ((16, CH), F32), ((8, 144, CH), BF)),
        (exchange_column(part),),
        (((336, CH), F32),),
    )
    fine = exchange_row(fine)
    blended = call(blend_kernel, "blend", (((16, 64, CH), BF),), (after_all(own_act, fine), proj, act), flops=10**9)[0]
    other = after_all(swap(fine, "row", 1), blended)
    first, second = call(
        functools.partial(finish_kernel, fine_scale),
        "finish",
        (((8, 144, CH), F32), ((8, 144, CH), F32)),
        (meta, fine, other),
    )
    shape = features.shape
    return (
        blended.reshape(shape),
        feature_grad.reshape(shape),
        first.reshape(3, 3, CH, CH),
        second.reshape(3, 3, CH, CH),
        conv_grad.reshape(3, 3, 16, CH).swapaxes(2, 3),
        proj_grad,
    )


def solution(mesh):
    in_specs = (
        P("row", "col", None, None),
        P(),
        P(),
        P(None, None, None, "row"),
        P("row", None),
        P("row", "col", None, None),
    )
    out_specs = (
        P("row", "col", None, None),
        P("row", "col", None, None),
        P(),
        P(),
        P(None, None, None, "row"),
        P("row", None),
    )
    return jax.shard_map(local, mesh=mesh, in_specs=in_specs, out_specs=out_specs, check_vma=False)
```

```python
import functools

import jax
import jax.numpy as jnp
from jax import lax
from jax.experimental import pallas as pl
from jax.experimental.pallas import tpu as pltpu
from jax.sharding import PartitionSpec as P

BF = jnp.bfloat16
F32 = jnp.float32
CH = 128
WIDE = 256
MIB = 1024 * 1024
VM = pl.BlockSpec(memory_space=pltpu.VMEM)
SM = pl.BlockSpec(memory_space=pltpu.SMEM)
HBM = pl.BlockSpec(memory_space=pltpu.HBM)


def call(kernel, name, outs, ins, scratch=(), limit=16, flops=0, moved=0, far=()):
    ins = [pltpu.with_memory_space_constraint(v, pltpu.HBM) if k in far else v for k, v in enumerate(ins)]
    shapes = tuple(jax.ShapeDtypeStruct(shape, dtype) for shape, dtype in outs)
    return pl.pallas_call(
        kernel,
        name=name,
        out_shape=shapes,
        in_specs=[HBM if k in far else SM if v.ndim == 1 else VM for k, v in enumerate(ins)],
        out_specs=tuple(VM for _ in outs),
        scratch_shapes=[pltpu.VMEM(*v) if isinstance(v, tuple) else v for v in scratch],
        compiler_params=pltpu.CompilerParams(vmem_limit_bytes=limit * MIB),
        cost_estimate=pl.CostEstimate(flops=flops, bytes_accessed=moved, transcendentals=0),
    )(*ins)


def dot_nn(a, b):
    return jnp.dot(a, b, preferred_element_type=F32)


def dot_nt(a, b):
    return lax.dot_general(a, b, (((1,), (1,)), ((), ())), preferred_element_type=F32)


def dot_tn(a, b):
    return lax.dot_general(a, b, (((0,), (0,)), ((), ())), preferred_element_type=F32)


def sigmoid(value):
    return 0.5 * jnp.tanh(0.5 * value) + 0.5


def slope_of(value):
    sigma = sigmoid(value)
    return sigma * (1.0 + value * (1.0 - sigma))


def rounded(value):
    return value.astype(BF).astype(F32)


def three(value):
    count = value.shape[0]
    left = pltpu.roll(value, 4, 0)
    right = pltpu.roll(value, count - 4, 0)
    return jnp.concatenate([left.astype(BF), value.astype(BF), right.astype(BF)], axis=1)


def paired(weight, axis):
    pad = jnp.zeros((3 * CH, CH) if axis == 0 else (CH, 3 * CH), BF)
    return jnp.concatenate(
        [jnp.concatenate([weight, pad], axis=axis), jnp.concatenate([pad, weight], axis=axis)], axis=1 - axis
    )


def flipped(weight):
    return jnp.concatenate([weight[(8 - t) * CH : (9 - t) * CH, :] for t in range(9)], axis=1)


def four_rows(row, starts):
    parts = [jnp.concatenate([row(h + k) for h in starts], axis=0) for k in range(4)]
    return jnp.concatenate(parts, axis=1)


def split_rows(value, starts):
    size = value.shape[0] // len(starts)
    out = []
    for k in range(len(starts)):
        out += [value[k * size : (k + 1) * size, e * CH : (e + 1) * CH] for e in range(2)]
    return out


def weight_grad(source, grad):
    gap = jnp.zeros((64, CH), BF)
    parts = []
    for r in range(3):
        parts.append(jnp.concatenate([gap] * r + [grad.reshape(1024, CH)] + [gap] * (2 - r), axis=0))
    whole = dot_tn(source.reshape(1152, 3 * CH), jnp.concatenate(parts, axis=1))
    return [whole[:, r * CH : (r + 1) * CH] for r in range(3)]


def column_mask(first, width, limit):
    place = first + lax.broadcasted_iota(jnp.int32, (width, CH), 0) // 4
    return jnp.where((place >= 0) & (place < limit), 1.0, 0.0).astype(F32)


def row_ok(place, limit):
    return jnp.where((place >= 0) & (place < limit), 1.0, 0.0).astype(F32)


def masked(value, mask, first, limit):
    rows = []
    for k in range(value.shape[0]):
        rows.append((value[k] * (mask * row_ok(first + k, limit)))[None])
    return jnp.concatenate(rows, axis=0)


def pooled_pair(row):
    count = row.shape[0]
    low = (row + pltpu.roll(row, count - 4, 0)).reshape(count // 16, 2, 8, CH)
    high = (row + pltpu.roll(row, 4, 0)).reshape(count // 16, 2, 8, CH)
    first = lax.broadcasted_iota(jnp.int32, (count // 16, 8, CH), 1) < 4
    return jnp.where(first, low[:, 0], high[:, 1]).reshape(count // 2, CH)


def repeated(row):
    count = row.shape[0]
    first = lax.broadcasted_iota(jnp.int32, (count, CH), 0) % 8 < 4
    even = jnp.where(first, row, pltpu.roll(row, 4, 0)).reshape(count // 8, 1, 8, CH)
    odd = jnp.where(first, pltpu.roll(row, count - 4, 0), row).reshape(count // 8, 1, 8, CH)
    return jnp.concatenate([even, odd], axis=1).reshape(count * 2, CH)


def aligned(start, size):
    return pl.ds(pl.multiple_of(start, 16), size)


def sides(meta, pair, other):
    even = meta[5] % 2 == 0
    return lax.select(even, other, pair), lax.select(even, pair, other)


def pack_columns_kernel(meta, feat, cot, pair, other, done):
    odd = meta[5] % 2
    pairs = [
        (feat.at[:, aligned(32 - 32 * odd, 32), :], pair.at[:, 0:32, :]),
        (cot.at[:, aligned(48 - 48 * odd, 16), :], pair.at[:, 32:48, :]),
        (feat.at[:, aligned(32 * odd, 32), :], other.at[:, 0:32, :]),
        (cot.at[:, aligned(48 * odd, 16), :], other.at[:, 32:48, :]),
    ]
    copies = [pltpu.make_async_copy(a, b, done.at[k]) for k, (a, b) in enumerate(pairs)]
    for copy in copies:
        copy.start()
    for copy in copies:
        copy.wait()


EDGE = 8 * 128 + 4 * 96


def cot_edge(ref, first, count=1):
    value = ref[1024 + 96 * first : 1024 + 96 * (first + count), :]
    return value if count == 1 else value.reshape(count, 96, CH)


def bring_kernel(feat_far, cot_far, conv, proj, feat, cot, weights, done):
    pairs = [(feat_far, feat), (cot_far, cot), (proj, weights.at[144:160, :])]
    pairs += [(conv.at[t], weights.at[16 * t : 16 * t + 16, :]) for t in range(9)]
    copies = [pltpu.make_async_copy(a, b, done.at[k]) for k, (a, b) in enumerate(pairs)]
    for copy in copies:
        copy.start()
    for copy in copies:
        copy.wait()


def weights_kernel(w1_far, w2_far, weight1, weight2, back1, back2, w1, w2, done):
    copies = [pltpu.make_async_copy(a, b, done.at[k]) for k, (a, b) in enumerate(((w1_far, w1), (w2_far, w2)))]
    for copy in copies:
        copy.start()
    for copy, w, weight, back in zip(copies, (w1, w2), (weight1, weight2), (back1, back2)):
        copy.wait()
        weight[...] = paired(w[...], 0)
        back[...] = paired(flipped(w), 1)


def pack_rows_kernel(meta, feat, cot, pair, other, own, far, inner, outer, both):
    core = meta[4] % 2
    for low, out in ((1 - core, inner), (core, outer)):
        jobs = [(128 * k, feat, 8 * low + k, 0, 32) for k in range(8)]
        jobs += [(1024 + 96 * k, cot, 12 * low + k, 32, 16) for k in range(4)]
        for base, middle, row, first, width in jobs:
            before, after = sides(meta, pair[row, first : first + width, :], other[row, first : first + width, :])
            out[base : base + width, :] = before
            out[base + width : base + width + 64, :] = middle[row]
            out[base + width + 64 : base + 2 * width + 64, :] = after
    both[0] = own[...]
    both[1] = far[...]


def stack_kernel(*refs):
    out = refs[-1]
    for k, ref in enumerate(refs[:-1]):
        out[k] = ref[...]


def first_rows(meta, row, starts, weight):
    top, left, height, breadth = (meta[0], meta[1], meta[2], meta[3])
    mask = column_mask(left - 8, 128, breadth)
    pre = dot_nn(four_rows(row, [h - 1 for h in starts]), weight)
    out = {}
    for k, value in enumerate(split_rows(pre, starts)):
        h = starts[k // 2] + k % 2
        act = rounded(value * sigmoid(value)) * (mask * row_ok(top - 8 + h, height))
        out[h] = (value, three(act))
    return out


def second_rows(meta, row, starts, weight):
    top, left, height, breadth = (meta[0], meta[1], meta[2], meta[3])
    mask = column_mask(left // 2 - 4, 64, breadth // 2)
    rows = split_rows(dot_nn(four_rows(row, [h - 1 for h in starts]), weight), starts)
    out = {}
    for k, h in enumerate(starts):
        pre = rows[2 * k : 2 * k + 2]
        act = [(v * sigmoid(v)).astype(BF) for v in pre]
        small = rounded(0.25 * pooled_pair(act[0].astype(F32) + act[1].astype(F32)))
        small = small * (mask * row_ok(top // 2 - 4 + h // 2, height // 2))
        out[h] = (pre, act, three(small))
    return out


INNER_FIRST = [9, 11, 13, 15, 17, 19, 21]
INNER_SECOND = [10, 12, 14, 16, 18, 20]


def inner_kernel(meta, feat, pair, other, weight1, weight2, feat3, act3, slope1, pool3, slope2, act):
    for k in range(16):
        before, after = sides(meta, pair[k, 0:32, :], other[k, 0:32, :])
        feat3[k] = three(jnp.concatenate([before, feat[k], after], axis=0).astype(F32))
    for h, (pre, wide) in first_rows(meta, lambda h: feat3[h - 8], INNER_FIRST, weight1[...]).items():
        act3[h - 9] = wide
        slope1[h - 9] = slope_of(pre[16:112])
    for h, (pre, value, small) in second_rows(meta, lambda h: act3[h - 9], INNER_SECOND, weight2[...]).items():
        pool3[h // 2 - 5] = small
        for e in range(2):
            slope2[h - 10 + e] = slope_of(pre[e][16:112])
            act[h - 10 + e] = value[e][32:96]


def outer_kernel(
    meta, inner, outer, feat3i, act3i, slope1i, pool3i, slope2i, acti, weight1, weight2,
    pool3, slope1, slope2, act, feat3o, act3o, feat3, act3,
):
    below_at = 24 * (meta[4] % 2)
    for k in range(8):
        feat3[k + below_at] = three(outer[128 * k : 128 * k + 128, :].astype(F32))
        feat3[k + 24 - below_at] = three(inner[128 * k : 128 * k + 128, :].astype(F32))
    feat3[8:24] = feat3i[...]
    for starts in ([1, 3, 5, 7], [23, 25, 27, 29]):
        for h, (pre, wide) in first_rows(meta, lambda h: feat3[h], starts, weight1[...]).items():
            act3[h - 1] = wide
            if 7 <= h <= 24:
                slope1[h - 7] = slope_of(pre[16:112])
    slope1[2:16] = slope1i[...]
    act3[8:22] = act3i[...]
    for starts in ([2, 4, 6, 8], [22, 24, 26, 28]):
        for h, (pre, value, small) in second_rows(meta, lambda h: act3[h - 1], starts, weight2[...]).items():
            pool3[h // 2 - 1] = small
            for e in range(2):
                if 6 <= h + e < 26:
                    slope2[h + e - 6] = slope_of(pre[e][16:112])
                if 8 <= h + e < 24:
                    act[h + e - 8] = value[e][32:96]
    pool3[4:10] = pool3i[...]
    slope2[4:16] = slope2i[...]
    act[2:14] = acti[...]
    feat3o[...] = feat3[7:25, 32:96, :]
    act3o[...] = act3[6:24, 32:96, :]


def inner_step(meta, feat, pair, other, weight1, weight2):
    return call(
        inner_kernel,
        "forward_inner",
        (
            ((16, 128, 384), BF),
            ((14, 128, 384), BF),
            ((14, 96, CH), F32),
            ((6, 64, 384), BF),
            ((12, 96, CH), F32),
            ((12, 64, CH), BF),
        ),
        (meta, feat, pair, other, weight1, weight2),
        limit=24,
        flops=0,
    )


def outer_step(meta, inner, outer, parts, weight1, weight2):
    return call(
        outer_kernel,
        "forward_outer",
        (
            ((14, 64, 384), BF),
            ((18, 96, CH), F32),
            ((20, 96, CH), F32),
            ((16, 64, CH), BF),
            ((18, 64, 384), BF),
            ((18, 64, 384), BF),
        ),
        (meta, inner, outer) + tuple(parts) + (weight1, weight2),
        (((32, 128, 384), BF), ((30, 128, 384), BF)),
        limit=24,
        flops=4 * 10**9,
    )


def coarse_kernel(
    meta, pool3, cot, pair, other, inner, outer, near0, near1, near2, near3, far,
    own, projs_out, keep, send, pooled_grad, wcat, projs, wide3, projin,
):
    top, left, height, breadth, me = (meta[0], meta[1], meta[2], meta[3], meta[4])
    core = me % 2
    near = (near0, near1, near2, near3)
    for rel in range(16):
        c, x, y = (rel % 2, (rel // 2) % 4, rel // 8)
        place = pl.ds(pl.multiple_of((me ^ rel) * 16, 16), 16)
        source = far.at[x, y] if c else near[x].at[y]
        for t in range(9):
            wcat[place, t * CH : (t + 1) * CH] = source[16 * t : 16 * t + 16, :]
        projs[place, :] = source[144:160, :]
    proj_w = projs[...]

    def pair_sum(a, b):
        return pooled_pair(a.astype(F32) + b.astype(F32))

    below_at = 10 * core
    for k in range(2):
        projin[k + below_at] = pair_sum(cot_edge(outer, 2 * k), cot_edge(outer, 2 * k + 1))
        projin[k + 10 - below_at] = pair_sum(cot_edge(inner, 2 * k), cot_edge(inner, 2 * k + 1))

    for k in range(8):
        rows = slice(2 * k, 2 * k + 2)
        before, after = sides(meta, pair[rows, 32:48, :], other[rows, 32:48, :])
        both = jnp.concatenate([before, cot[rows], after], axis=1)
        projin[k + 2] = pair_sum(both[0], both[1])

    proj_in = projin[...].reshape(576, CH)
    proj_in_bf = proj_in.astype(BF)
    lhs = jnp.concatenate([pool3[r : r + 12].reshape(768, 3 * CH) for r in range(3)], axis=1)
    pre = dot_nt(lhs, wcat[...]).reshape(12, 64, WIDE)[:, 8:56].reshape(576, WIDE)
    sigma = sigmoid(pre)
    coarse_act = pre * sigma
    act_grad = dot_nt(proj_in_bf, proj_w)
    grad = rounded(act_grad * (sigma * (1.0 + pre * (1.0 - sigma)))).reshape(12, 48, WIDE)
    mask = column_mask(left // 2 - 2, 48, breadth // 2)
    mask = jnp.concatenate([mask, mask], axis=1)
    grad = masked(grad, mask, top // 2 - 2, height // 2)
    wide3[...] = three(grad.reshape(576, WIDE)).reshape(12, 48, 3 * WIDE)
    own_grad = grad[2:10, 8:40].reshape(256, WIDE).astype(BF)
    own_act = coarse_act.reshape(12, 48, WIDE)[2:10, 8:40].reshape(256, WIDE).astype(BF)
    own_in = proj_in.reshape(12, 48, CH)[2:10, 8:40].reshape(256, CH).astype(BF)

    def emit(first, last, value):
        value = value.reshape(8, 2, 16, CH)
        even, odd = (value[:, 0], value[:, 1])
        keep[:, first:last, :] = jnp.where(core == 0, even, odd).astype(BF)
        send[:, first:last, :] = jnp.where(core == 0, odd, even).astype(BF)

    source = [pool3[2 + r : 10 + r, 16:48, :].reshape(256, 3 * CH) for r in range(3)]
    part = dot_tn(own_grad, jnp.concatenate(source, axis=1))
    for t in range(9):
        emit(16 * t, 16 * t + 16, part[:, t * CH : (t + 1) * CH])
    emit(144, 160, dot_tn(own_act, own_in))
    total = None
    for r in range(3):
        lhs = wide3[r : r + 10].reshape(480, 3 * WIDE)
        first = 3 * (2 - r)
        rhs = jnp.concatenate([wcat[:, (first + 2 - s) * CH : (first + 3 - s) * CH] for s in range(3)], axis=0)
        part = dot_nn(lhs, rhs)
        total = part if total is None else total + part
    pooled_grad[...] = total.reshape(10, 48, CH)
    own[...] = own_act
    projs_out[...] = proj_w


def blend_kernel(own, proj, act, blended):
    projected = dot_nn(own[...], proj[...]).reshape(8, 32, CH)
    for k in range(8):
        row = repeated(projected[k])
        for e in range(2):
            blended[2 * k + e] = (act[2 * k + e].astype(F32) + row).astype(BF)


def coarse_step(meta, pool3, cot, halo, near, far):
    return call(
        coarse_kernel,
        "coarse_step",
        (((256, WIDE), BF), ((WIDE, CH), BF), ((8, 160, CH), BF), ((8, 160, CH), BF), ((10, 48, CH), F32)),
        (meta, pool3, cot) + halo + tuple(near) + (far,),
        (
            ((WIDE, 9 * CH), BF),
            ((WIDE, CH), BF),
            ((12, 48, 3 * WIDE), BF),
            ((12, 48, CH), F32),
        ),
        limit=20,
        flops=2 * 10**9,
    )


def backward_kernel(
    meta, pooled_grad, cot, pair, other, inner, outer, slope1, slope2, feat3, act3, back_w,
    keep, send, first3, second3, grads,
):
    top, left, height, breadth = (meta[0], meta[1], meta[2], meta[3])
    mask = column_mask(left - 4, 96, breadth)

    def second_pair(k, both):
        wide = 0.25 * repeated(pooled_grad[k])
        for e in range(2):
            value = rounded((both[e].astype(F32) + wide) * slope2[2 * k + e])
            second3[2 * k + e] = three(value * (mask * row_ok(top - 2 + 2 * k + e, height)))

    first_core = meta[4] % 2 == 0
    second_pair(0, lax.select(first_core, cot_edge(outer, 2, 2), cot_edge(inner, 2, 2)))
    second_pair(9, lax.select(first_core, cot_edge(inner, 0, 2), cot_edge(outer, 0, 2)))
    for k in range(8):
        rows = slice(2 * k, 2 * k + 2)
        before, after = sides(meta, pair[rows, 32:48, :], other[rows, 32:48, :])
        second_pair(k + 1, jnp.concatenate([before, cot[rows], after], axis=1))

    def emit(base, parts):
        for r in range(3):
            grads[base + 384 * r : base + 384 * (r + 1), :] = parts[r].astype(BF)

    for starts in ([0, 2, 4, 6], [8, 10, 12, 14, 16]):
        value = dot_nt(four_rows(lambda h: second3[h], starts), back_w[...])
        for k, row in enumerate(split_rows(value, starts)):
            h = starts[k // 2] + k % 2
            row = rounded(row * slope1[h]) * (mask * row_ok(top - 1 + h, height))
            first3[h] = three(row)[16:80]
    emit(1152, weight_grad(act3[...], second3[2:18, 16:80, CH : 2 * CH]))
    emit(0, weight_grad(feat3[...], first3[1:17, :, CH : 2 * CH]))
    core = meta[4] % 2
    for k in range(8):
        keep[k] = grads[pl.ds(pl.multiple_of((2 * k + core) * 144, 16), 144), :]
        send[k] = grads[pl.ds(pl.multiple_of((2 * k + 1 - core) * 144, 16), 144), :]


def fine_backward(meta, pooled_grad, cot, halo, slope1, slope2, feat3, act3, back_w):
    return call(
        backward_kernel,
        "fine_backward",
        (((8, 144, CH), BF), ((8, 144, CH), BF), ((18, 64, 384), BF)),
        (meta, pooled_grad, cot) + halo + (slope1, slope2, feat3, act3, back_w),
        (((20, 96, 384), BF), ((2304, CH), BF)),
        limit=20,
        flops=2 * 10**9,
    )


def feature_kernel(first3, back_w, out):
    for starts in ([0, 2, 4, 6], [8, 10, 12, 14]):
        value = dot_nt(four_rows(lambda h: first3[h], starts), back_w[...])
        for k, row in enumerate(split_rows(value, starts)):
            out[starts[0] + k] = row.astype(BF)


def feature_step(first3, back_w):
    return call(feature_kernel, "feature_step", (((16, 64, CH), BF),), (first3, back_w), limit=12, flops=10**9)[0]


def scatter_core_kernel(keep_c, keep_f, got_c, got_f, out):
    for k in range(8):
        coarse = keep_c[k].astype(F32) + got_c[k].astype(F32)
        fine = keep_f[k].astype(F32) + got_f[k].astype(F32)
        for j in range(2):
            out[2 * k + j, 0:80, :] = coarse[80 * j : 80 * j + 80].astype(BF)
            out[2 * k + j, 80:152, :] = fine[72 * j : 72 * j + 72].astype(BF)


def scatter_plane_kernel(got, out, total):
    value = got[0].astype(F32)
    for k in range(1, 16):
        value = value + got[k].astype(F32)
    total[0:152, :] = value
    total[152:160, :] = jnp.zeros((8, CH), F32)
    for k in range(8):
        out[k] = total[19 * k : 19 * k + 24, :].astype(BF)


def scatter_column_kernel(got, out):
    value = got[0].astype(F32)
    for k in range(1, 8):
        value = value + got[k].astype(F32)
    value = value.astype(BF)
    for k in range(16):
        out[k] = value


def gather_column_kernel(scale, got, conv, proj, fine, total):
    for j in range(2):
        for k in range(8):
            total[j, 19 * k : 19 * k + 24, :] = got[8 * j + k].astype(F32)
    for k in range(9):
        conv[k] = total[k // 5, 16 * (k % 5) : 16 * (k % 5) + 16, :] * scale
    proj[...] = total[1, 64:80, :] * scale
    value = jnp.concatenate([total[0, 80:152, :], total[1, 80:152, :]], axis=0).astype(BF)
    for k in range(8):
        fine[k] = value


def finish_kernel(scale, meta, mine, other, first, second):
    core = meta[4] % 2
    for at in range(8):
        out = first if at < 4 else second
        a = mine[at].astype(F32) * scale
        b = other[at].astype(F32) * scale
        out[2 * (at % 4)] = jnp.where(core == 0, a, b)
        out[2 * (at % 4) + 1] = jnp.where(core == 0, b, a)


def swap(value, axis, mask):
    count = lax.axis_size(axis)
    return lax.ppermute(value, axis, [(i, i ^ mask) for i in range(count)])


def swap_outer(value, axis):
    count = lax.axis_size(axis)
    pairs = [(i, i + 1 if i % 2 else i - 1) for i in range(1, count - 1)]
    return lax.ppermute(value, axis, pairs)


def exchange_row(value):
    count = lax.axis_size("row")
    groups = [list(range(c, count, 2)) for c in range(2)]
    return lax.all_to_all(value, "row", 0, 0, axis_index_groups=groups, tiled=True)


def exchange_plane(value):
    rows, cols = (lax.axis_size("row"), lax.axis_size("col"))
    groups = []
    for core in range(2):
        for z in range(cols // 2):
            groups.append([r * cols + c for r in range(core, rows, 2) for c in (z, z + cols // 2)])
    return lax.all_to_all(value, ("row", "col"), 0, 0, axis_index_groups=groups, tiled=True)


def exchange_depth(value):
    count = lax.axis_size("col")
    groups = [list(range(k, k + count // 2)) for k in (0, count // 2)]
    return lax.all_to_all(value, "col", 0, 0, axis_index_groups=groups, tiled=True)


def exchange_column(value):
    return lax.all_to_all(value, "col", 0, 0, tiled=True)


def after_all(value, *others):
    return lax.optimization_barrier((value,) + others)[0]


def local(features, conv_first, conv_second, coarse_conv, coarse_proj, cotangent):
    rows, cols = (lax.axis_size("row"), lax.axis_size("col"))
    height, breadth = (features.shape[0] * rows, features.shape[1] * cols)
    fine_scale = 1.0 / (height * breadth * features.shape[2]) ** 0.5
    coarse_scale = 2.0 * fine_scale
    me, mine = (lax.axis_index("row"), lax.axis_index("col"))
    fixed = [jnp.int32(height), jnp.int32(breadth)]
    meta = jnp.stack([me * 16, mine * 16] + fixed + [me, mine]).astype(jnp.int32)
    feat = features.reshape(16, 64, CH)
    cot = cotangent.reshape(16, 64, CH)
    conv = coarse_conv.reshape(9, CH, 16).swapaxes(1, 2)
    slab = ((160, CH), BF)

    side = ((16, 48, CH), BF)
    pair, other = call(
        pack_columns_kernel,
        "pack_columns",
        (side, side),
        (meta, feat, cot),
        (pltpu.SemaphoreType.DMA((4,)),),
        far=(1, 2),
    )
    w1, w2 = (conv_first.reshape(1152, CH), conv_second.reshape(1152, CH))
    big, wide = (((16, 64, CH), BF), ((1536, 256), BF))
    feat_in, cot_in, own = call(
        bring_kernel,
        "bring",
        (big, big, slab),
        (after_all(feat, pair), cot, conv, coarse_proj),
        (pltpu.SemaphoreType.DMA((12,)),),
        far=(0, 1, 2, 3),
        flops=4 * 10**9,
    )
    own_far = swap(own, "row", 8)
    weight1, weight2, back1, back2 = call(
        weights_kernel,
        "weights",
        (wide, wide, ((256, 1536), BF), ((256, 1536), BF)),
        (after_all(w1, feat_in), w2),
        (((1152, CH), BF), ((1152, CH), BF), pltpu.SemaphoreType.DMA((2,))),
        far=(0, 1),
        flops=4 * 10**9,
    )
    pair = swap(pair, "col", 1)
    other = swap_outer(other, "col")
    edge = ((EDGE, CH), BF)
    inner, outer, near0 = call(
        pack_rows_kernel,
        "pack_rows",
        (edge, edge, ((2, 160, CH), BF)),
        (meta, feat_in, cot_in, pair, after_all(other, weight1), own, own_far),
    )
    outer = swap_outer(outer, "row")
    inner = swap(inner, "row", 1)
    pair_in = after_all(pair, near0)
    near = [near0] + [swap(near0, "row", 2 * k) for k in range(1, 4)]
    parts = inner_step(meta, feat_in, pair_in, other, weight1, weight2)
    parts, near = lax.optimization_barrier((parts, near))
    far = swap(call(stack_kernel, "stack_eight", (((4, 2, 160, CH), BF),), near)[0], "row", 1)
    pool3, slope1, slope2, act, feat3, act3 = outer_step(meta, inner, outer, parts, weight1, weight2)
    halo = (pair, other, inner, outer)
    own_act, proj, keep_c, send_c, pooled_grad = coarse_step(meta, pool3, cot_in, halo, near, far)
    got_c = swap(send_c, "row", 1)
    keep_f, send_f, first3 = fine_backward(
        meta, pooled_grad, cot_in, halo, slope1, slope2, feat3, act3, back2
    )
    got_f = swap(send_f, "row", 1)
    feature_grad = feature_step(first3, back1)

    got_f = after_all(got_f, feature_grad)
    part = call(scatter_core_kernel, "scatter_core", (((16, 152, CH), BF),), (keep_c, keep_f, got_c, got_f))[0]
    part = call(
        scatter_plane_kernel, "scatter_plane", (((8, 24, CH), BF),), (exchange_plane(part),), (((160, CH), F32),)
    )[0]
    part = call(scatter_column_kernel, "scatter_column", (((16, 24, CH), BF),), (exchange_depth(part),))[0]
    conv_grad, proj_grad, fine = call(
        functools.partial(gather_column_kernel, coarse_scale),
        "gather_column",
        (((9, 16, CH), F32), ((16, CH), F32), ((8, 144, CH), BF)),
        (exchange_column(part),),
        (((2, 160, CH), F32),),
    )
    fine = exchange_row(fine)
    blended = call(blend_kernel, "blend", (((16, 64, CH), BF),), (after_all(own_act, fine), proj, act), flops=10**9)[0]
    other = after_all(swap(fine, "row", 1), blended)
    first, second = call(
        functools.partial(finish_kernel, fine_scale),
        "finish",
        (((8, 144, CH), F32), ((8, 144, CH), F32)),
        (meta, fine, other),
    )
    shape = features.shape
    return (
        blended.reshape(shape),
        feature_grad.reshape(shape),
        first.reshape(3, 3, CH, CH),
        second.reshape(3, 3, CH, CH),
        conv_grad.reshape(3, 3, 16, CH).swapaxes(2, 3),
        proj_grad,
    )


def solution(mesh):
    in_specs = (
        P("row", "col", None, None),
        P(),
        P(),
        P(None, None, None, "row"),
        P("row", None),
        P("row", "col", None, None),
    )
    out_specs = (
        P("row", "col", None, None),
        P("row", "col", None, None),
        P(),
        P(),
        P(None, None, None, "row"),
        P("row", None),
    )
    return jax.shard_map(local, mesh=mesh, in_specs=in_specs, out_specs=out_specs, check_vma=False)
```

```python
import functools

import jax
import jax.numpy as jnp
from jax import lax
from jax.experimental import pallas as pl
from jax.experimental.pallas import tpu as pltpu
from jax.sharding import PartitionSpec as P

BF = jnp.bfloat16
F32 = jnp.float32
CH = 128
WIDE = 256
MIB = 1024 * 1024
VM = pl.BlockSpec(memory_space=pltpu.VMEM)
SM = pl.BlockSpec(memory_space=pltpu.SMEM)
HBM = pl.BlockSpec(memory_space=pltpu.HBM)


def call(kernel, name, outs, ins, scratch=(), limit=16, flops=0, moved=0, far=()):
    ins = [pltpu.with_memory_space_constraint(v, pltpu.HBM) if k in far else v for k, v in enumerate(ins)]
    shapes = tuple(jax.ShapeDtypeStruct(shape, dtype) for shape, dtype in outs)
    return pl.pallas_call(
        kernel,
        name=name,
        out_shape=shapes,
        in_specs=[HBM if k in far else SM if v.ndim == 1 else VM for k, v in enumerate(ins)],
        out_specs=tuple(VM for _ in outs),
        scratch_shapes=[pltpu.VMEM(*v) if isinstance(v, tuple) else v for v in scratch],
        compiler_params=pltpu.CompilerParams(vmem_limit_bytes=limit * MIB),
        cost_estimate=pl.CostEstimate(flops=flops, bytes_accessed=moved, transcendentals=0),
    )(*ins)


def dot_nn(a, b):
    return jnp.dot(a, b, preferred_element_type=F32)


def dot_nt(a, b):
    return lax.dot_general(a, b, (((1,), (1,)), ((), ())), preferred_element_type=F32)


def dot_tn(a, b):
    return lax.dot_general(a, b, (((0,), (0,)), ((), ())), preferred_element_type=F32)


def sigmoid(value):
    return 0.5 * jnp.tanh(0.5 * value) + 0.5


def slope_of(value):
    sigma = sigmoid(value)
    return sigma * (1.0 + value * (1.0 - sigma))


def rounded(value):
    return value.astype(BF).astype(F32)


def three(value):
    count = value.shape[0]
    left = pltpu.roll(value, 4, 0)
    right = pltpu.roll(value, count - 4, 0)
    return jnp.concatenate([left.astype(BF), value.astype(BF), right.astype(BF)], axis=1)


def paired(weight, axis):
    pad = jnp.zeros((3 * CH, CH) if axis == 0 else (CH, 3 * CH), BF)
    return jnp.concatenate(
        [jnp.concatenate([weight, pad], axis=axis), jnp.concatenate([pad, weight], axis=axis)], axis=1 - axis
    )


def flipped(weight):
    return jnp.concatenate([weight[(8 - t) * CH : (9 - t) * CH, :] for t in range(9)], axis=1)


def four_rows(row, starts):
    parts = [jnp.concatenate([row(h + k) for h in starts], axis=0) for k in range(4)]
    return jnp.concatenate(parts, axis=1)


def split_rows(value, starts):
    size = value.shape[0] // len(starts)
    out = []
    for k in range(len(starts)):
        out += [value[k * size : (k + 1) * size, e * CH : (e + 1) * CH] for e in range(2)]
    return out


def weight_grad(source, grad):
    gap = jnp.zeros((64, CH), BF)
    parts = []
    for r in range(3):
        parts.append(jnp.concatenate([gap] * r + [grad.reshape(1024, CH)] + [gap] * (2 - r), axis=0))
    whole = dot_tn(source.reshape(1152, 3 * CH), jnp.concatenate(parts, axis=1))
    return [whole[:, r * CH : (r + 1) * CH] for r in range(3)]


def column_mask(first, width, limit):
    place = first + lax.broadcasted_iota(jnp.int32, (width, CH), 0) // 4
    return jnp.where((place >= 0) & (place < limit), 1.0, 0.0).astype(F32)


def row_ok(place, limit):
    return jnp.where((place >= 0) & (place < limit), 1.0, 0.0).astype(F32)


def masked(value, mask, first, limit):
    rows = []
    for k in range(value.shape[0]):
        rows.append((value[k] * (mask * row_ok(first + k, limit)))[None])
    return jnp.concatenate(rows, axis=0)


def pooled_pair(row):
    count = row.shape[0]
    low = (row + pltpu.roll(row, count - 4, 0)).reshape(count // 16, 2, 8, CH)
    high = (row + pltpu.roll(row, 4, 0)).reshape(count // 16, 2, 8, CH)
    first = lax.broadcasted_iota(jnp.int32, (count // 16, 8, CH), 1) < 4
    return jnp.where(first, low[:, 0], high[:, 1]).reshape(count // 2, CH)


def repeated(row):
    count = row.shape[0]
    first = lax.broadcasted_iota(jnp.int32, (count, CH), 0) % 8 < 4
    even = jnp.where(first, row, pltpu.roll(row, 4, 0)).reshape(count // 8, 1, 8, CH)
    odd = jnp.where(first, pltpu.roll(row, count - 4, 0), row).reshape(count // 8, 1, 8, CH)
    return jnp.concatenate([even, odd], axis=1).reshape(count * 2, CH)


def aligned(start, size):
    return pl.ds(pl.multiple_of(start, 16), size)


def sides(meta, pair, other):
    even = meta[5] % 2 == 0
    return lax.select(even, other, pair), lax.select(even, pair, other)


def pack_columns_kernel(meta, feat, cot, pair, other, done):
    odd = meta[5] % 2
    pairs = [
        (feat.at[:, aligned(32 - 32 * odd, 32), :], pair.at[:, 0:32, :]),
        (cot.at[:, aligned(48 - 48 * odd, 16), :], pair.at[:, 32:48, :]),
        (feat.at[:, aligned(32 * odd, 32), :], other.at[:, 0:32, :]),
        (cot.at[:, aligned(48 * odd, 16), :], other.at[:, 32:48, :]),
    ]
    copies = [pltpu.make_async_copy(a, b, done.at[k]) for k, (a, b) in enumerate(pairs)]
    for copy in copies:
        copy.start()
    for copy in copies:
        copy.wait()


EDGE = 8 * 128 + 4 * 96


def cot_edge(ref, first, count=1):
    value = ref[1024 + 96 * first : 1024 + 96 * (first + count), :]
    return value if count == 1 else value.reshape(count, 96, CH)


def bring_kernel(feat_far, cot_far, conv, proj, feat, cot, weights, done):
    pairs = [(feat_far, feat), (cot_far, cot), (proj, weights.at[144:160, :])]
    pairs += [(conv.at[t], weights.at[16 * t : 16 * t + 16, :]) for t in range(9)]
    copies = [pltpu.make_async_copy(a, b, done.at[k]) for k, (a, b) in enumerate(pairs)]
    for copy in copies:
        copy.start()
    for copy in copies:
        copy.wait()


def weights_kernel(w1_far, w2_far, weight1, weight2, back1, back2, w1, w2, done):
    copies = [pltpu.make_async_copy(a, b, done.at[k]) for k, (a, b) in enumerate(((w1_far, w1), (w2_far, w2)))]
    for copy in copies:
        copy.start()
    for copy, w, weight, back in zip(copies, (w1, w2), (weight1, weight2), (back1, back2)):
        copy.wait()
        weight[...] = paired(w[...], 0)
        back[...] = paired(flipped(w), 1)


def pack_rows_kernel(meta, feat, cot, pair, other, own, far, inner, outer, both):
    core = meta[4] % 2
    for low, out in ((1 - core, inner), (core, outer)):
        jobs = [(128 * k, feat, 8 * low + k, 0, 32) for k in range(8)]
        jobs += [(1024 + 96 * k, cot, 12 * low + k, 32, 16) for k in range(4)]
        for base, middle, row, first, width in jobs:
            before, after = sides(meta, pair[row, first : first + width, :], other[row, first : first + width, :])
            out[base : base + width, :] = before
            out[base + width : base + width + 64, :] = middle[row]
            out[base + width + 64 : base + 2 * width + 64, :] = after
    both[0] = own[...]
    both[1] = far[...]


def stack_kernel(*refs):
    out = refs[-1]
    for k, ref in enumerate(refs[:-1]):
        out[k] = ref[...]


def first_rows(meta, row, starts, weight):
    top, left, height, breadth = (meta[0], meta[1], meta[2], meta[3])
    mask = column_mask(left - 8, 128, breadth)
    pre = dot_nn(four_rows(row, [h - 1 for h in starts]), weight)
    out = {}
    for k, value in enumerate(split_rows(pre, starts)):
        h = starts[k // 2] + k % 2
        act = rounded(value * sigmoid(value)) * (mask * row_ok(top - 8 + h, height))
        out[h] = (value, three(act))
    return out


def second_rows(meta, row, starts, weight):
    top, left, height, breadth = (meta[0], meta[1], meta[2], meta[3])
    mask = column_mask(left // 2 - 4, 64, breadth // 2)
    rows = split_rows(dot_nn(four_rows(row, [h - 1 for h in starts]), weight), starts)
    out = {}
    for k, h in enumerate(starts):
        pre = rows[2 * k : 2 * k + 2]
        act = [(v * sigmoid(v)).astype(BF) for v in pre]
        small = rounded(0.25 * pooled_pair(act[0].astype(F32) + act[1].astype(F32)))
        small = small * (mask * row_ok(top // 2 - 4 + h // 2, height // 2))
        out[h] = (pre, act, three(small))
    return out


INNER_FIRST = [9, 11, 13, 15, 17, 19, 21]
INNER_SECOND = [10, 12, 14, 16, 18, 20]


def inner_kernel(meta, feat, pair, other, weight1, weight2, feat3, act3, slope1, pool3, slope2, act):
    for k in range(16):
        before, after = sides(meta, pair[k, 0:32, :], other[k, 0:32, :])
        feat3[k] = three(jnp.concatenate([before, feat[k], after], axis=0).astype(F32))
    for h, (pre, wide) in first_rows(meta, lambda h: feat3[h - 8], INNER_FIRST, weight1[...]).items():
        act3[h - 9] = wide
        slope1[h - 9] = slope_of(pre[16:112])
    for h, (pre, value, small) in second_rows(meta, lambda h: act3[h - 9], INNER_SECOND, weight2[...]).items():
        pool3[h // 2 - 5] = small
        for e in range(2):
            slope2[h - 10 + e] = slope_of(pre[e][16:112])
            act[h - 10 + e] = value[e][32:96]


def outer_kernel(
    meta, inner, outer, feat3i, act3i, slope1i, pool3i, slope2i, acti, weight1, weight2,
    pool3, slope1, slope2, act, feat3o, act3o, feat3, act3,
):
    below_at = 24 * (meta[4] % 2)
    for k in range(8):
        feat3[k + below_at] = three(outer[128 * k : 128 * k + 128, :].astype(F32))
        feat3[k + 24 - below_at] = three(inner[128 * k : 128 * k + 128, :].astype(F32))
    feat3[8:24] = feat3i[...]
    for starts in ([1, 3, 5, 7], [23, 25, 27, 29]):
        for h, (pre, wide) in first_rows(meta, lambda h: feat3[h], starts, weight1[...]).items():
            act3[h - 1] = wide
            if 7 <= h <= 24:
                slope1[h - 7] = slope_of(pre[16:112])
    slope1[2:16] = slope1i[...]
    act3[8:22] = act3i[...]
    for starts in ([2, 4, 6, 8], [22, 24, 26, 28]):
        for h, (pre, value, small) in second_rows(meta, lambda h: act3[h - 1], starts, weight2[...]).items():
            pool3[h // 2 - 1] = small
            for e in range(2):
                if 6 <= h + e < 26:
                    slope2[h + e - 6] = slope_of(pre[e][16:112])
                if 8 <= h + e < 24:
                    act[h + e - 8] = value[e][32:96]
    pool3[4:10] = pool3i[...]
    slope2[4:16] = slope2i[...]
    act[2:14] = acti[...]
    feat3o[...] = feat3[7:25, 32:96, :]
    act3o[...] = act3[6:24, 32:96, :]


def inner_step(meta, feat, pair, other, weight1, weight2):
    return call(
        inner_kernel,
        "forward_inner",
        (
            ((16, 128, 384), BF),
            ((14, 128, 384), BF),
            ((14, 96, CH), F32),
            ((6, 64, 384), BF),
            ((12, 96, CH), F32),
            ((12, 64, CH), BF),
        ),
        (meta, feat, pair, other, weight1, weight2),
        limit=24,
        flops=0,
    )


def outer_step(meta, inner, outer, parts, weight1, weight2):
    return call(
        outer_kernel,
        "forward_outer",
        (
            ((14, 64, 384), BF),
            ((18, 96, CH), F32),
            ((20, 96, CH), F32),
            ((16, 64, CH), BF),
            ((18, 64, 384), BF),
            ((18, 64, 384), BF),
        ),
        (meta, inner, outer) + tuple(parts) + (weight1, weight2),
        (((32, 128, 384), BF), ((30, 128, 384), BF)),
        limit=24,
        flops=4 * 10**9,
    )


def coarse_kernel(
    meta, pool3, cot, pair, other, inner, outer, near0, near1, near2, near3, far,
    own, projs_out, keep, send, pooled_grad, wcat, projs, wide3, projin,
):
    top, left, height, breadth, me = (meta[0], meta[1], meta[2], meta[3], meta[4])
    core = me % 2
    near = (near0, near1, near2, near3)
    for rel in range(16):
        c, x, y = (rel % 2, (rel // 2) % 4, rel // 8)
        place = pl.ds(pl.multiple_of((me ^ rel) * 16, 16), 16)
        source = far.at[x, y] if c else near[x].at[y]
        for t in range(9):
            wcat[place, t * CH : (t + 1) * CH] = source[16 * t : 16 * t + 16, :]
        projs[place, :] = source[144:160, :]
    proj_w = projs[...]

    def pair_sum(a, b):
        return pooled_pair(a.astype(F32) + b.astype(F32))

    below_at = 10 * core
    for k in range(2):
        projin[k + below_at] = pair_sum(cot_edge(outer, 2 * k), cot_edge(outer, 2 * k + 1))
        projin[k + 10 - below_at] = pair_sum(cot_edge(inner, 2 * k), cot_edge(inner, 2 * k + 1))

    for k in range(8):
        rows = slice(2 * k, 2 * k + 2)
        before, after = sides(meta, pair[rows, 32:48, :], other[rows, 32:48, :])
        both = jnp.concatenate([before, cot[rows], after], axis=1)
        projin[k + 2] = pair_sum(both[0], both[1])

    proj_in = projin[...].reshape(576, CH)
    proj_in_bf = proj_in.astype(BF)
    lhs = jnp.concatenate([pool3[r : r + 12].reshape(768, 3 * CH) for r in range(3)], axis=1)
    pre = dot_nt(lhs, wcat[...]).reshape(12, 64, WIDE)[:, 8:56].reshape(576, WIDE)
    sigma = sigmoid(pre)
    coarse_act = pre * sigma
    act_grad = dot_nt(proj_in_bf, proj_w)
    grad = rounded(act_grad * (sigma * (1.0 + pre * (1.0 - sigma)))).reshape(12, 48, WIDE)
    mask = column_mask(left // 2 - 2, 48, breadth // 2)
    mask = jnp.concatenate([mask, mask], axis=1)
    grad = masked(grad, mask, top // 2 - 2, height // 2)
    wide3[...] = three(grad.reshape(576, WIDE)).reshape(12, 48, 3 * WIDE)
    own_grad = grad[2:10, 8:40].reshape(256, WIDE).astype(BF)
    own_act = coarse_act.reshape(12, 48, WIDE)[2:10, 8:40].reshape(256, WIDE).astype(BF)
    own_in = proj_in.reshape(12, 48, CH)[2:10, 8:40].reshape(256, CH).astype(BF)

    def emit(first, last, value):
        value = value.reshape(8, 2, 16, CH)
        even, odd = (value[:, 0], value[:, 1])
        keep[:, first:last, :] = jnp.where(core == 0, even, odd).astype(BF)
        send[:, first:last, :] = jnp.where(core == 0, odd, even).astype(BF)

    source = [pool3[2 + r : 10 + r, 16:48, :].reshape(256, 3 * CH) for r in range(3)]
    part = dot_tn(own_grad, jnp.concatenate(source, axis=1))
    for t in range(9):
        emit(16 * t, 16 * t + 16, part[:, t * CH : (t + 1) * CH])
    emit(144, 160, dot_tn(own_act, own_in))
    total = None
    for r in range(3):
        lhs = wide3[r : r + 10].reshape(480, 3 * WIDE)
        first = 3 * (2 - r)
        rhs = jnp.concatenate([wcat[:, (first + 2 - s) * CH : (first + 3 - s) * CH] for s in range(3)], axis=0)
        part = dot_nn(lhs, rhs)
        total = part if total is None else total + part
    pooled_grad[...] = total.reshape(10, 48, CH)
    own[...] = own_act
    projs_out[...] = proj_w


def blend_kernel(scale, own, proj, act, coarse, blended, conv, proj_grad):
    for k in range(9):
        conv[k] = coarse[k // 5, 16 * (k % 5) : 16 * (k % 5) + 16, :].astype(F32) * scale
    proj_grad[...] = coarse[1, 64:80, :].astype(F32) * scale
    projected = dot_nn(own[...], proj[...]).reshape(8, 32, CH)
    for k in range(8):
        row = repeated(projected[k])
        for e in range(2):
            blended[2 * k + e] = (act[2 * k + e].astype(F32) + row).astype(BF)


def coarse_step(meta, pool3, cot, halo, near, far):
    return call(
        coarse_kernel,
        "coarse_step",
        (((256, WIDE), BF), ((WIDE, CH), BF), ((8, 160, CH), BF), ((8, 160, CH), BF), ((10, 48, CH), F32)),
        (meta, pool3, cot) + halo + tuple(near) + (far,),
        (
            ((WIDE, 9 * CH), BF),
            ((WIDE, CH), BF),
            ((12, 48, 3 * WIDE), BF),
            ((12, 48, CH), F32),
        ),
        limit=20,
        flops=2 * 10**9,
    )


def backward_kernel(
    meta, pooled_grad, cot, pair, other, inner, outer, slope1, slope2, feat3, act3, back_w,
    keep, send, first3, second3, grads,
):
    top, left, height, breadth = (meta[0], meta[1], meta[2], meta[3])
    mask = column_mask(left - 4, 96, breadth)

    def second_pair(k, both):
        wide = 0.25 * repeated(pooled_grad[k])
        for e in range(2):
            value = rounded((both[e].astype(F32) + wide) * slope2[2 * k + e])
            second3[2 * k + e] = three(value * (mask * row_ok(top - 2 + 2 * k + e, height)))

    first_core = meta[4] % 2 == 0
    second_pair(0, lax.select(first_core, cot_edge(outer, 2, 2), cot_edge(inner, 2, 2)))
    second_pair(9, lax.select(first_core, cot_edge(inner, 0, 2), cot_edge(outer, 0, 2)))
    for k in range(8):
        rows = slice(2 * k, 2 * k + 2)
        before, after = sides(meta, pair[rows, 32:48, :], other[rows, 32:48, :])
        second_pair(k + 1, jnp.concatenate([before, cot[rows], after], axis=1))

    def emit(base, parts):
        for r in range(3):
            grads[base + 384 * r : base + 384 * (r + 1), :] = parts[r].astype(BF)

    for starts in ([0, 2, 4, 6], [8, 10, 12, 14, 16]):
        value = dot_nt(four_rows(lambda h: second3[h], starts), back_w[...])
        for k, row in enumerate(split_rows(value, starts)):
            h = starts[k // 2] + k % 2
            row = rounded(row * slope1[h]) * (mask * row_ok(top - 1 + h, height))
            first3[h] = three(row)[16:80]
    emit(1152, weight_grad(act3[...], second3[2:18, 16:80, CH : 2 * CH]))
    emit(0, weight_grad(feat3[...], first3[1:17, :, CH : 2 * CH]))
    core = meta[4] % 2
    for k in range(8):
        keep[k] = grads[pl.ds(pl.multiple_of((2 * k + core) * 144, 16), 144), :]
        send[k] = grads[pl.ds(pl.multiple_of((2 * k + 1 - core) * 144, 16), 144), :]


def fine_backward(meta, pooled_grad, cot, halo, slope1, slope2, feat3, act3, back_w):
    return call(
        backward_kernel,
        "fine_backward",
        (((8, 144, CH), BF), ((8, 144, CH), BF), ((18, 64, 384), BF)),
        (meta, pooled_grad, cot) + halo + (slope1, slope2, feat3, act3, back_w),
        (((20, 96, 384), BF), ((2304, CH), BF)),
        limit=20,
        flops=2 * 10**9,
    )


def feature_kernel(first3, back_w, out):
    for starts in ([0, 2, 4, 6], [8, 10, 12, 14]):
        value = dot_nt(four_rows(lambda h: first3[h], starts), back_w[...])
        for k, row in enumerate(split_rows(value, starts)):
            out[starts[0] + k] = row.astype(BF)


def feature_step(first3, back_w):
    return call(feature_kernel, "feature_step", (((16, 64, CH), BF),), (first3, back_w), limit=12, flops=10**9)[0]


def scatter_core_kernel(keep_c, keep_f, got_c, got_f, out):
    for k in range(8):
        coarse = keep_c[k].astype(F32) + got_c[k].astype(F32)
        fine = keep_f[k].astype(F32) + got_f[k].astype(F32)
        for j in range(2):
            out[2 * k + j, 0:80, :] = coarse[80 * j : 80 * j + 80].astype(BF)
            out[2 * k + j, 80:152, :] = fine[72 * j : 72 * j + 72].astype(BF)


def scatter_plane_kernel(got, out, total):
    value = got[0].astype(F32)
    for k in range(1, 16):
        value = value + got[k].astype(F32)
    total[0:152, :] = value
    total[152:160, :] = jnp.zeros((8, CH), F32)
    for k in range(8):
        out[k] = total[19 * k : 19 * k + 24, :].astype(BF)


def scatter_column_kernel(got, out):
    value = got[0].astype(F32)
    for k in range(1, 8):
        value = value + got[k].astype(F32)
    value = value.astype(BF)
    for k in range(16):
        out[k] = value


def gather_column_kernel(meta, got, coarse, fine, total):
    for j in range(2):
        for k in range(8):
            total[j, 19 * k : 19 * k + 24, :] = got[8 * j + k].astype(F32)
    coarse[...] = total[:, 0:80, :].astype(BF)
    value = total[meta[5] // 8, 80:152, :].astype(BF)
    for k in range(16):
        fine[k] = value


def finish_kernel(scale, meta, mine, other, first, second):
    core = meta[4] % 2
    for at in range(8):
        out = first if at < 4 else second
        for j in range(2):
            rows = slice(72 * j, 72 * j + 72)
            a = mine[2 * at + j].astype(F32) * scale
            b = other[2 * at + j].astype(F32) * scale
            out[2 * (at % 4), rows, :] = jnp.where(core == 0, a, b)
            out[2 * (at % 4) + 1, rows, :] = jnp.where(core == 0, b, a)


def swap(value, axis, mask):
    count = lax.axis_size(axis)
    return lax.ppermute(value, axis, [(i, i ^ mask) for i in range(count)])


def swap_outer(value, axis):
    count = lax.axis_size(axis)
    pairs = [(i, i + 1 if i % 2 else i - 1) for i in range(1, count - 1)]
    return lax.ppermute(value, axis, pairs)


def exchange_plane(value):
    rows, cols = (lax.axis_size("row"), lax.axis_size("col"))
    groups = []
    for core in range(2):
        for z in range(cols // 2):
            groups.append([r * cols + c for r in range(core, rows, 2) for c in (z, z + cols // 2)])
    return lax.all_to_all(value, ("row", "col"), 0, 0, axis_index_groups=groups, tiled=True)


def exchange_depth(value):
    count = lax.axis_size("col")
    groups = [list(range(k, k + count // 2)) for k in (0, count // 2)]
    return lax.all_to_all(value, "col", 0, 0, axis_index_groups=groups, tiled=True)


def exchange_column(value):
    return lax.all_to_all(value, "col", 0, 0, tiled=True)


def after_all(value, *others):
    return lax.optimization_barrier((value,) + others)[0]


def local(features, conv_first, conv_second, coarse_conv, coarse_proj, cotangent):
    rows, cols = (lax.axis_size("row"), lax.axis_size("col"))
    height, breadth = (features.shape[0] * rows, features.shape[1] * cols)
    fine_scale = 1.0 / (height * breadth * features.shape[2]) ** 0.5
    coarse_scale = 2.0 * fine_scale
    me, mine = (lax.axis_index("row"), lax.axis_index("col"))
    fixed = [jnp.int32(height), jnp.int32(breadth)]
    meta = jnp.stack([me * 16, mine * 16] + fixed + [me, mine]).astype(jnp.int32)
    feat = features.reshape(16, 64, CH)
    cot = cotangent.reshape(16, 64, CH)
    conv = coarse_conv.reshape(9, CH, 16).swapaxes(1, 2)
    slab = ((160, CH), BF)

    side = ((16, 48, CH), BF)
    pair, other = call(
        pack_columns_kernel,
        "pack_columns",
        (side, side),
        (meta, feat, cot),
        (pltpu.SemaphoreType.DMA((4,)),),
        far=(1, 2),
    )
    w1, w2 = (conv_first.reshape(1152, CH), conv_second.reshape(1152, CH))
    big, wide = (((16, 64, CH), BF), ((1536, 256), BF))
    feat_in, cot_in, own = call(
        bring_kernel,
        "bring",
        (big, big, slab),
        (after_all(feat, pair), cot, conv, coarse_proj),
        (pltpu.SemaphoreType.DMA((12,)),),
        far=(0, 1, 2, 3),
        flops=4 * 10**9,
    )
    own_far = swap(own, "row", 8)
    weight1, weight2, back1, back2 = call(
        weights_kernel,
        "weights",
        (wide, wide, ((256, 1536), BF), ((256, 1536), BF)),
        (after_all(w1, feat_in), w2),
        (((1152, CH), BF), ((1152, CH), BF), pltpu.SemaphoreType.DMA((2,))),
        far=(0, 1),
        flops=4 * 10**9,
    )
    pair = swap(pair, "col", 1)
    other = swap_outer(other, "col")
    edge = ((EDGE, CH), BF)
    inner, outer, near0 = call(
        pack_rows_kernel,
        "pack_rows",
        (edge, edge, ((2, 160, CH), BF)),
        (meta, feat_in, cot_in, pair, after_all(other, weight1), own, own_far),
    )
    outer = swap_outer(outer, "row")
    inner = swap(inner, "row", 1)
    pair_in = after_all(pair, near0)
    near = [near0] + [swap(near0, "row", 2 * k) for k in range(1, 4)]
    parts = inner_step(meta, feat_in, pair_in, other, weight1, weight2)
    parts, near = lax.optimization_barrier((parts, near))
    far = swap(call(stack_kernel, "stack_eight", (((4, 2, 160, CH), BF),), near)[0], "row", 1)
    pool3, slope1, slope2, act, feat3, act3 = outer_step(meta, inner, outer, parts, weight1, weight2)
    halo = (pair, other, inner, outer)
    own_act, proj, keep_c, send_c, pooled_grad = coarse_step(meta, pool3, cot_in, halo, near, far)
    got_c = swap(send_c, "row", 1)
    keep_f, send_f, first3 = fine_backward(
        meta, pooled_grad, cot_in, halo, slope1, slope2, feat3, act3, back2
    )
    got_f = swap(send_f, "row", 1)
    feature_grad = feature_step(first3, back1)

    got_f = after_all(got_f, feature_grad)
    part = call(scatter_core_kernel, "scatter_core", (((16, 152, CH), BF),), (keep_c, keep_f, got_c, got_f))[0]
    part = call(
        scatter_plane_kernel, "scatter_plane", (((8, 24, CH), BF),), (exchange_plane(part),), (((160, CH), F32),)
    )[0]
    part = call(scatter_column_kernel, "scatter_column", (((16, 24, CH), BF),), (exchange_depth(part),))[0]
    coarse, fine = call(
        gather_column_kernel,
        "gather_column",
        (((2, 80, CH), BF), ((16, 72, CH), BF)),
        (meta, exchange_column(part)),
        (((2, 160, CH), F32),),
    )
    fine = exchange_plane(fine)
    blended, conv_grad, proj_grad = call(
        functools.partial(blend_kernel, coarse_scale),
        "blend",
        (((16, 64, CH), BF), ((9, 16, CH), F32), ((16, CH), F32)),
        (after_all(own_act, fine), proj, act, coarse),
        flops=10**9,
    )
    other = after_all(swap(fine, "row", 1), blended)
    first, second = call(
        functools.partial(finish_kernel, fine_scale),
        "finish",
        (((8, 144, CH), F32), ((8, 144, CH), F32)),
        (meta, fine, other),
    )
    shape = features.shape
    return (
        blended.reshape(shape),
        feature_grad.reshape(shape),
        first.reshape(3, 3, CH, CH),
        second.reshape(3, 3, CH, CH),
        conv_grad.reshape(3, 3, 16, CH).swapaxes(2, 3),
        proj_grad,
    )


def solution(mesh):
    in_specs = (
        P("row", "col", None, None),
        P(),
        P(),
        P(None, None, None, "row"),
        P("row", None),
        P("row", "col", None, None),
    )
    out_specs = (
        P("row", "col", None, None),
        P("row", "col", None, None),
        P(),
        P(),
        P(None, None, None, "row"),
        P("row", None),
    )
    return jax.shard_map(local, mesh=mesh, in_specs=in_specs, out_specs=out_specs, check_vma=False)
```

```python
import functools

import jax
import jax.numpy as jnp
from jax import lax
from jax.experimental import pallas as pl
from jax.experimental.pallas import tpu as pltpu
from jax.sharding import PartitionSpec as P

BF = jnp.bfloat16
F32 = jnp.float32
CH = 128
WIDE = 256
MIB = 1024 * 1024
VM = pl.BlockSpec(memory_space=pltpu.VMEM)
SM = pl.BlockSpec(memory_space=pltpu.SMEM)
HBM = pl.BlockSpec(memory_space=pltpu.HBM)


def call(kernel, name, outs, ins, scratch=(), limit=16, flops=0, moved=0, far=()):
    ins = [pltpu.with_memory_space_constraint(v, pltpu.HBM) if k in far else v for k, v in enumerate(ins)]
    shapes = tuple(jax.ShapeDtypeStruct(shape, dtype) for shape, dtype in outs)
    return pl.pallas_call(
        kernel,
        name=name,
        out_shape=shapes,
        in_specs=[HBM if k in far else SM if v.ndim == 1 else VM for k, v in enumerate(ins)],
        out_specs=tuple(VM for _ in outs),
        scratch_shapes=[pltpu.VMEM(*v) if isinstance(v, tuple) else v for v in scratch],
        compiler_params=pltpu.CompilerParams(vmem_limit_bytes=limit * MIB),
        cost_estimate=pl.CostEstimate(flops=flops, bytes_accessed=moved, transcendentals=0),
    )(*ins)


def dot_nn(a, b):
    return jnp.dot(a, b, preferred_element_type=F32)


def dot_nt(a, b):
    return lax.dot_general(a, b, (((1,), (1,)), ((), ())), preferred_element_type=F32)


def dot_tn(a, b):
    return lax.dot_general(a, b, (((0,), (0,)), ((), ())), preferred_element_type=F32)


def sigmoid(value):
    return 0.5 * jnp.tanh(0.5 * value) + 0.5


def slope_of(value):
    sigma = sigmoid(value)
    return sigma * (1.0 + value * (1.0 - sigma))


def rounded(value):
    return value.astype(BF).astype(F32)


def three(value):
    count = value.shape[0]
    left = pltpu.roll(value, 4, 0)
    right = pltpu.roll(value, count - 4, 0)
    return jnp.concatenate([left.astype(BF), value.astype(BF), right.astype(BF)], axis=1)


def paired(weight, axis):
    pad = jnp.zeros((3 * CH, CH) if axis == 0 else (CH, 3 * CH), BF)
    return jnp.concatenate(
        [jnp.concatenate([weight, pad], axis=axis), jnp.concatenate([pad, weight], axis=axis)], axis=1 - axis
    )


def flipped(weight):
    return jnp.concatenate([weight[(8 - t) * CH : (9 - t) * CH, :] for t in range(9)], axis=1)


def four_rows(row, starts):
    parts = [jnp.concatenate([row(h + k) for h in starts], axis=0) for k in range(4)]
    return jnp.concatenate(parts, axis=1)


def split_rows(value, starts):
    size = value.shape[0] // len(starts)
    out = []
    for k in range(len(starts)):
        out += [value[k * size : (k + 1) * size, e * CH : (e + 1) * CH] for e in range(2)]
    return out


def weight_grad(source, grad):
    gap = jnp.zeros((64, CH), BF)
    parts = []
    for r in range(3):
        parts.append(jnp.concatenate([gap] * r + [grad.reshape(1024, CH)] + [gap] * (2 - r), axis=0))
    whole = dot_tn(source.reshape(1152, 3 * CH), jnp.concatenate(parts, axis=1))
    return [whole[:, r * CH : (r + 1) * CH] for r in range(3)]


def column_mask(first, width, limit):
    place = first + lax.broadcasted_iota(jnp.int32, (width, CH), 0) // 4
    return jnp.where((place >= 0) & (place < limit), 1.0, 0.0).astype(F32)


def row_ok(place, limit):
    return jnp.where((place >= 0) & (place < limit), 1.0, 0.0).astype(F32)


def masked(value, mask, first, limit):
    rows = []
    for k in range(value.shape[0]):
        rows.append((value[k] * (mask * row_ok(first + k, limit)))[None])
    return jnp.concatenate(rows, axis=0)


def pooled_pair(row):
    count = row.shape[0]
    low = (row + pltpu.roll(row, count - 4, 0)).reshape(count // 16, 2, 8, CH)
    high = (row + pltpu.roll(row, 4, 0)).reshape(count // 16, 2, 8, CH)
    first = lax.broadcasted_iota(jnp.int32, (count // 16, 8, CH), 1) < 4
    return jnp.where(first, low[:, 0], high[:, 1]).reshape(count // 2, CH)


def repeated(row):
    count = row.shape[0]
    first = lax.broadcasted_iota(jnp.int32, (count, CH), 0) % 8 < 4
    even = jnp.where(first, row, pltpu.roll(row, 4, 0)).reshape(count // 8, 1, 8, CH)
    odd = jnp.where(first, pltpu.roll(row, count - 4, 0), row).reshape(count // 8, 1, 8, CH)
    return jnp.concatenate([even, odd], axis=1).reshape(count * 2, CH)


def aligned(start, size):
    return pl.ds(pl.multiple_of(start, 16), size)


def sides(meta, pair, other):
    even = meta[5] % 2 == 0
    return lax.select(even, other, pair), lax.select(even, pair, other)


def pack_columns_kernel(meta, feat, cot, pair, other, done):
    odd = meta[5] % 2
    pairs = [
        (feat.at[:, aligned(32 - 32 * odd, 32), :], pair.at[:, 0:32, :]),
        (cot.at[:, aligned(48 - 48 * odd, 16), :], pair.at[:, 32:48, :]),
        (feat.at[:, aligned(32 * odd, 32), :], other.at[:, 0:32, :]),
        (cot.at[:, aligned(48 * odd, 16), :], other.at[:, 32:48, :]),
    ]
    copies = [pltpu.make_async_copy(a, b, done.at[k]) for k, (a, b) in enumerate(pairs)]
    for copy in copies:
        copy.start()
    for copy in copies:
        copy.wait()


EDGE = 8 * 128 + 2 * 96 + 48


def cot_edge(ref):
    return ref[1024:1216, :].reshape(2, 96, CH)


def bring_kernel(feat_far, cot_far, conv, proj, feat, cot, weights, done):
    pairs = [(feat_far, feat), (cot_far, cot), (proj, weights.at[144:160, :])]
    pairs += [(conv.at[t], weights.at[16 * t : 16 * t + 16, :]) for t in range(9)]
    copies = [pltpu.make_async_copy(a, b, done.at[k]) for k, (a, b) in enumerate(pairs)]
    for copy in copies:
        copy.start()
    for copy in copies:
        copy.wait()


def weights_kernel(w1_far, w2_far, weight1, weight2, back1, back2, w1, w2, done):
    copies = [pltpu.make_async_copy(a, b, done.at[k]) for k, (a, b) in enumerate(((w1_far, w1), (w2_far, w2)))]
    for copy in copies:
        copy.start()
    for copy, w, weight, back in zip(copies, (w1, w2), (weight1, weight2), (back1, back2)):
        copy.wait()
        weight[...] = paired(w[...], 0)
        back[...] = paired(flipped(w), 1)


def pack_rows_kernel(meta, feat, cot, pair, other, own, far, inner, outer, both):
    core = meta[4] % 2

    def cot_row(row):
        before, after = sides(meta, pair[row, 32:48, :], other[row, 32:48, :])
        return jnp.concatenate([before, cot[row], after], axis=0)

    for low, out in ((1 - core, inner), (core, outer)):
        for k in range(8):
            row = 8 * low + k
            before, after = sides(meta, pair[row, 0:32, :], other[row, 0:32, :])
            out[128 * k : 128 * k + 32, :] = before
            out[128 * k + 32 : 128 * k + 96, :] = feat[row]
            out[128 * k + 96 : 128 * k + 128, :] = after
        for k in range(2):
            out[1024 + 96 * k : 1120 + 96 * k, :] = cot_row(14 * low + k)
        away = 2 + 10 * low
        both_rows = cot_row(away).astype(F32) + cot_row(away + 1).astype(F32)
        out[1216:1264, :] = pooled_pair(both_rows).astype(BF)
    both[0] = own[...]
    both[1] = far[...]


def stack_kernel(*refs):
    out = refs[-1]
    for k, ref in enumerate(refs[:-1]):
        out[k] = ref[...]


def first_rows(meta, row, starts, weight):
    top, left, height, breadth = (meta[0], meta[1], meta[2], meta[3])
    mask = column_mask(left - 8, 128, breadth)
    pre = dot_nn(four_rows(row, [h - 1 for h in starts]), weight)
    out = {}
    for k, value in enumerate(split_rows(pre, starts)):
        h = starts[k // 2] + k % 2
        act = rounded(value * sigmoid(value)) * (mask * row_ok(top - 8 + h, height))
        out[h] = (value, three(act))
    return out


def second_rows(meta, row, starts, weight):
    top, left, height, breadth = (meta[0], meta[1], meta[2], meta[3])
    mask = column_mask(left // 2 - 4, 64, breadth // 2)
    rows = split_rows(dot_nn(four_rows(row, [h - 1 for h in starts]), weight), starts)
    out = {}
    for k, h in enumerate(starts):
        pre = rows[2 * k : 2 * k + 2]
        act = [(v * sigmoid(v)).astype(BF) for v in pre]
        small = rounded(0.25 * pooled_pair(act[0].astype(F32) + act[1].astype(F32)))
        small = small * (mask * row_ok(top // 2 - 4 + h // 2, height // 2))
        out[h] = (pre, act, three(small))
    return out


INNER_FIRST = [9, 11, 13, 15, 17, 19, 21]
INNER_SECOND = [10, 12, 14, 16, 18, 20]


def inner_kernel(meta, feat, pair, other, weight1, weight2, feat3, act3, slope1, pool3, slope2, act):
    for k in range(16):
        before, after = sides(meta, pair[k, 0:32, :], other[k, 0:32, :])
        feat3[k] = three(jnp.concatenate([before, feat[k], after], axis=0).astype(F32))
    for h, (pre, wide) in first_rows(meta, lambda h: feat3[h - 8], INNER_FIRST, weight1[...]).items():
        act3[h - 9] = wide
        slope1[h - 9] = slope_of(pre[16:112])
    for h, (pre, value, small) in second_rows(meta, lambda h: act3[h - 9], INNER_SECOND, weight2[...]).items():
        pool3[h // 2 - 5] = small
        for e in range(2):
            slope2[h - 10 + e] = slope_of(pre[e][16:112])
            act[h - 10 + e] = value[e][32:96]


def outer_kernel(
    meta, inner, outer, feat3i, act3i, slope1i, pool3i, slope2i, acti, weight1, weight2,
    pool3, slope1, slope2, act, feat3o, act3o, feat3, act3,
):
    below_at = 8 * (meta[4] % 2)
    for k in range(8):
        feat3[k + below_at] = three(outer[128 * k : 128 * k + 128, :].astype(F32))
        feat3[k + 8 - below_at] = three(inner[128 * k : 128 * k + 128, :].astype(F32))

    def feat_row(h):
        return feat3i[h - 8] if 8 <= h < 24 else feat3[h if h < 8 else h - 16]

    def act_row(h):
        return act3i[h - 9] if 9 <= h < 23 else act3[h - 1 if h < 9 else h - 15]

    for starts in ([1, 3, 5, 7], [23, 25, 27, 29]):
        for h, (pre, wide) in first_rows(meta, feat_row, starts, weight1[...]).items():
            act3[h - 1 if h < 9 else h - 15] = wide
            if 7 <= h <= 24:
                slope1[h - 7] = slope_of(pre[16:112])
    slope1[2:16] = slope1i[...]
    for starts in ([2, 4, 6, 8], [22, 24, 26, 28]):
        for h, (pre, value, small) in second_rows(meta, act_row, starts, weight2[...]).items():
            pool3[h // 2 - 1] = small
            for e in range(2):
                if 6 <= h + e < 26:
                    slope2[h + e - 6] = slope_of(pre[e][16:112])
                if 8 <= h + e < 24:
                    act[h + e - 8] = value[e][32:96]
    pool3[4:10] = pool3i[...]
    slope2[4:16] = slope2i[...]
    act[2:14] = acti[...]
    for k in range(18):
        feat3o[k] = feat_row(k + 7)[32:96]
        act3o[k] = act_row(k + 7)[32:96]


def inner_step(meta, feat, pair, other, weight1, weight2):
    return call(
        inner_kernel,
        "forward_inner",
        (
            ((16, 128, 384), BF),
            ((14, 128, 384), BF),
            ((14, 96, CH), F32),
            ((6, 64, 384), BF),
            ((12, 96, CH), F32),
            ((12, 64, CH), BF),
        ),
        (meta, feat, pair, other, weight1, weight2),
        limit=24,
        flops=0,
    )


def outer_step(meta, inner, outer, parts, weight1, weight2):
    return call(
        outer_kernel,
        "forward_outer",
        (
            ((14, 64, 384), BF),
            ((18, 96, CH), F32),
            ((20, 96, CH), F32),
            ((16, 64, CH), BF),
            ((18, 64, 384), BF),
            ((18, 64, 384), BF),
        ),
        (meta, inner, outer) + tuple(parts) + (weight1, weight2),
        (((16, 128, 384), BF),) * 2,
        limit=24,
        flops=4 * 10**9,
    )


def coarse_kernel(
    meta, pool3, cot, pair, other, inner, outer, near0, near1, near2, near3, far,
    own, projs_out, keep, send, pooled_grad, wcat, projs, wide3, projin,
):
    top, left, height, breadth, me = (meta[0], meta[1], meta[2], meta[3], meta[4])
    core = me % 2
    near = (near0, near1, near2, near3)
    for rel in range(16):
        c, x, y = (rel % 2, (rel // 2) % 4, rel // 8)
        place = pl.ds(pl.multiple_of((me ^ rel) * 16, 16), 16)
        source = far.at[x, y] if c else near[x].at[y]
        for t in range(9):
            wcat[place, t * CH : (t + 1) * CH] = source[16 * t : 16 * t + 16, :]
        projs[place, :] = source[144:160, :]
    proj_w = projs[...]

    def pair_sum(a, b):
        return pooled_pair(a.astype(F32) + b.astype(F32))

    for ref, far_at, near_at in ((outer, 11 * core, 1 + 9 * core), (inner, 11 - 11 * core, 10 - 9 * core)):
        projin[far_at] = ref[1216:1264, :].astype(F32)
        near_rows = cot_edge(ref)
        projin[near_at] = pair_sum(near_rows[0], near_rows[1])

    for k in range(8):
        rows = slice(2 * k, 2 * k + 2)
        before, after = sides(meta, pair[rows, 32:48, :], other[rows, 32:48, :])
        both = jnp.concatenate([before, cot[rows], after], axis=1)
        projin[k + 2] = pair_sum(both[0], both[1])

    proj_in = projin[...].reshape(576, CH)
    proj_in_bf = proj_in.astype(BF)
    lhs = jnp.concatenate([pool3[r : r + 12].reshape(768, 3 * CH) for r in range(3)], axis=1)
    pre = dot_nt(lhs, wcat[...]).reshape(12, 64, WIDE)[:, 8:56].reshape(576, WIDE)
    sigma = sigmoid(pre)
    coarse_act = pre * sigma
    act_grad = dot_nt(proj_in_bf, proj_w)
    grad = rounded(act_grad * (sigma * (1.0 + pre * (1.0 - sigma)))).reshape(12, 48, WIDE)
    mask = column_mask(left // 2 - 2, 48, breadth // 2)
    mask = jnp.concatenate([mask, mask], axis=1)
    grad = masked(grad, mask, top // 2 - 2, height // 2)
    wide3[...] = three(grad.reshape(576, WIDE)).reshape(12, 48, 3 * WIDE)
    own_grad = grad[2:10, 8:40].reshape(256, WIDE).astype(BF)
    own_act = coarse_act.reshape(12, 48, WIDE)[2:10, 8:40].reshape(256, WIDE).astype(BF)
    own_in = proj_in.reshape(12, 48, CH)[2:10, 8:40].reshape(256, CH).astype(BF)

    def emit(first, last, value):
        value = value.reshape(8, 2, 16, CH)
        even, odd = (value[:, 0], value[:, 1])
        keep[:, first:last, :] = jnp.where(core == 0, even, odd).astype(BF)
        send[:, first:last, :] = jnp.where(core == 0, odd, even).astype(BF)

    source = [pool3[2 + r : 10 + r, 16:48, :].reshape(256, 3 * CH) for r in range(3)]
    part = dot_tn(own_grad, jnp.concatenate(source, axis=1))
    for t in range(9):
        emit(16 * t, 16 * t + 16, part[:, t * CH : (t + 1) * CH])
    emit(144, 160, dot_tn(own_act, own_in))
    total = None
    for r in range(3):
        lhs = wide3[r : r + 10].reshape(480, 3 * WIDE)
        first = 3 * (2 - r)
        rhs = jnp.concatenate([wcat[:, (first + 2 - s) * CH : (first + 3 - s) * CH] for s in range(3)], axis=0)
        part = dot_nn(lhs, rhs)
        total = part if total is None else total + part
    pooled_grad[...] = total.reshape(10, 48, CH)
    own[...] = own_act
    projs_out[...] = proj_w


def blend_kernel(scale, own, proj, act, coarse, blended, conv, proj_grad):
    for k in range(9):
        conv[k] = coarse[k // 5, 16 * (k % 5) : 16 * (k % 5) + 16, :].astype(F32) * scale
    proj_grad[...] = coarse[1, 64:80, :].astype(F32) * scale
    projected = dot_nn(own[...], proj[...]).reshape(8, 32, CH)
    for k in range(8):
        row = repeated(projected[k])
        for e in range(2):
            blended[2 * k + e] = (act[2 * k + e].astype(F32) + row).astype(BF)


def coarse_step(meta, pool3, cot, halo, near, far):
    return call(
        coarse_kernel,
        "coarse_step",
        (((256, WIDE), BF), ((WIDE, CH), BF), ((8, 160, CH), BF), ((8, 160, CH), BF), ((10, 48, CH), F32)),
        (meta, pool3, cot) + halo + tuple(near) + (far,),
        (
            ((WIDE, 9 * CH), BF),
            ((WIDE, CH), BF),
            ((12, 48, 3 * WIDE), BF),
            ((12, 48, CH), F32),
        ),
        limit=20,
        flops=2 * 10**9,
    )


def backward_kernel(
    meta, pooled_grad, cot, pair, other, inner, outer, slope1, slope2, feat3, act3, back_w,
    keep, send, first3, second3, grads,
):
    top, left, height, breadth = (meta[0], meta[1], meta[2], meta[3])
    mask = column_mask(left - 4, 96, breadth)

    def second_pair(k, both):
        wide = 0.25 * repeated(pooled_grad[k])
        for e in range(2):
            value = rounded((both[e].astype(F32) + wide) * slope2[2 * k + e])
            second3[2 * k + e] = three(value * (mask * row_ok(top - 2 + 2 * k + e, height)))

    first_core = meta[4] % 2 == 0
    second_pair(0, lax.select(first_core, cot_edge(outer), cot_edge(inner)))
    second_pair(9, lax.select(first_core, cot_edge(inner), cot_edge(outer)))
    for k in range(8):
        rows = slice(2 * k, 2 * k + 2)
        before, after = sides(meta, pair[rows, 32:48, :], other[rows, 32:48, :])
        second_pair(k + 1, jnp.concatenate([before, cot[rows], after], axis=1))

    def emit(base, parts):
        for r in range(3):
            grads[base + 384 * r : base + 384 * (r + 1), :] = parts[r].astype(BF)

    for starts in ([0, 2, 4, 6], [8, 10, 12, 14, 16]):
        value = dot_nt(four_rows(lambda h: second3[h], starts), back_w[...])
        for k, row in enumerate(split_rows(value, starts)):
            h = starts[k // 2] + k % 2
            row = rounded(row * slope1[h]) * (mask * row_ok(top - 1 + h, height))
            first3[h] = three(row)[16:80]
    emit(1152, weight_grad(act3[...], second3[2:18, 16:80, CH : 2 * CH]))
    emit(0, weight_grad(feat3[...], first3[1:17, :, CH : 2 * CH]))
    core = meta[4] % 2
    for k in range(8):
        keep[k] = grads[pl.ds(pl.multiple_of((2 * k + core) * 144, 16), 144), :]
        send[k] = grads[pl.ds(pl.multiple_of((2 * k + 1 - core) * 144, 16), 144), :]


def fine_backward(meta, pooled_grad, cot, halo, slope1, slope2, feat3, act3, back_w):
    return call(
        backward_kernel,
        "fine_backward",
        (((8, 144, CH), BF), ((8, 144, CH), BF), ((18, 64, 384), BF)),
        (meta, pooled_grad, cot) + halo + (slope1, slope2, feat3, act3, back_w),
        (((20, 96, 384), BF), ((2304, CH), BF)),
        limit=20,
        flops=2 * 10**9,
    )


def feature_kernel(first3, back_w, out):
    for starts in ([0, 2, 4, 6], [8, 10, 12, 14]):
        value = dot_nt(four_rows(lambda h: first3[h], starts), back_w[...])
        for k, row in enumerate(split_rows(value, starts)):
            out[starts[0] + k] = row.astype(BF)


def feature_step(first3, back_w):
    return call(feature_kernel, "feature_step", (((16, 64, CH), BF),), (first3, back_w), limit=12, flops=10**9)[0]


def scatter_core_kernel(keep_c, keep_f, got_c, got_f, out):
    for k in range(8):
        coarse = keep_c[k].astype(F32) + got_c[k].astype(F32)
        fine = keep_f[k].astype(F32) + got_f[k].astype(F32)
        for j in range(2):
            out[2 * k + j, 0:80, :] = coarse[80 * j : 80 * j + 80].astype(BF)
            out[2 * k + j, 80:152, :] = fine[72 * j : 72 * j + 72].astype(BF)


def scatter_plane_kernel(got, out, total):
    value = got[0].astype(F32)
    for k in range(1, 16):
        value = value + got[k].astype(F32)
    total[0:152, :] = value
    total[152:160, :] = jnp.zeros((8, CH), F32)
    for k in range(8):
        out[k] = total[19 * k : 19 * k + 24, :].astype(BF)


def scatter_column_kernel(got, out):
    value = got[0].astype(F32)
    for k in range(1, 8):
        value = value + got[k].astype(F32)
    value = value.astype(BF)
    for k in range(16):
        out[k] = value


def gather_column_kernel(meta, got, coarse, fine, total):
    for j in range(2):
        for k in range(8):
            total[j, 19 * k : 19 * k + 24, :] = got[8 * j + k].astype(F32)
    coarse[...] = total[:, 0:80, :].astype(BF)
    value = total[meta[5] // 8, 80:152, :].astype(BF)
    for k in range(16):
        fine[k] = value


def finish_kernel(scale, meta, mine, other, first, second):
    core = meta[4] % 2
    for at in range(8):
        out = first if at < 4 else second
        for j in range(2):
            rows = slice(72 * j, 72 * j + 72)
            a = mine[2 * at + j].astype(F32) * scale
            b = other[2 * at + j].astype(F32) * scale
            out[2 * (at % 4), rows, :] = jnp.where(core == 0, a, b)
            out[2 * (at % 4) + 1, rows, :] = jnp.where(core == 0, b, a)


def swap(value, axis, mask):
    count = lax.axis_size(axis)
    return lax.ppermute(value, axis, [(i, i ^ mask) for i in range(count)])


def swap_outer(value, axis):
    count = lax.axis_size(axis)
    pairs = [(i, i + 1 if i % 2 else i - 1) for i in range(1, count - 1)]
    return lax.ppermute(value, axis, pairs)


def exchange_plane(value):
    rows, cols = (lax.axis_size("row"), lax.axis_size("col"))
    groups = []
    for core in range(2):
        for z in range(cols // 2):
            groups.append([r * cols + c for r in range(core, rows, 2) for c in (z, z + cols // 2)])
    return lax.all_to_all(value, ("row", "col"), 0, 0, axis_index_groups=groups, tiled=True)


def exchange_depth(value):
    count = lax.axis_size("col")
    groups = [list(range(k, k + count // 2)) for k in (0, count // 2)]
    return lax.all_to_all(value, "col", 0, 0, axis_index_groups=groups, tiled=True)


def exchange_column(value):
    return lax.all_to_all(value, "col", 0, 0, tiled=True)


def after_all(value, *others):
    return lax.optimization_barrier((value,) + others)[0]


def local(features, conv_first, conv_second, coarse_conv, coarse_proj, cotangent):
    rows, cols = (lax.axis_size("row"), lax.axis_size("col"))
    height, breadth = (features.shape[0] * rows, features.shape[1] * cols)
    fine_scale = 1.0 / (height * breadth * features.shape[2]) ** 0.5
    coarse_scale = 2.0 * fine_scale
    me, mine = (lax.axis_index("row"), lax.axis_index("col"))
    fixed = [jnp.int32(height), jnp.int32(breadth)]
    meta = jnp.stack([me * 16, mine * 16] + fixed + [me, mine]).astype(jnp.int32)
    feat = features.reshape(16, 64, CH)
    cot = cotangent.reshape(16, 64, CH)
    conv = coarse_conv.reshape(9, CH, 16).swapaxes(1, 2)
    slab = ((160, CH), BF)

    side = ((16, 48, CH), BF)
    pair, other = call(
        pack_columns_kernel,
        "pack_columns",
        (side, side),
        (meta, feat, cot),
        (pltpu.SemaphoreType.DMA((4,)),),
        far=(1, 2),
    )
    w1, w2 = (conv_first.reshape(1152, CH), conv_second.reshape(1152, CH))
    big, wide = (((16, 64, CH), BF), ((1536, 256), BF))
    feat_in, cot_in, own = call(
        bring_kernel,
        "bring",
        (big, big, slab),
        (after_all(feat, pair), cot, conv, coarse_proj),
        (pltpu.SemaphoreType.DMA((12,)),),
        far=(0, 1, 2, 3),
        flops=4 * 10**9,
    )
    own_far = swap(own, "row", 8)
    weight1, weight2, back1, back2 = call(
        weights_kernel,
        "weights",
        (wide, wide, ((256, 1536), BF), ((256, 1536), BF)),
        (after_all(w1, feat_in), w2),
        (((1152, CH), BF), ((1152, CH), BF), pltpu.SemaphoreType.DMA((2,))),
        far=(0, 1),
        flops=4 * 10**9,
    )
    pair = swap(pair, "col", 1)
    other = swap_outer(other, "col")
    edge = ((EDGE, CH), BF)
    inner, outer, near0 = call(
        pack_rows_kernel,
        "pack_rows",
        (edge, edge, ((2, 160, CH), BF)),
        (meta, feat_in, cot_in, pair, after_all(other, weight1), own, own_far),
    )
    outer = swap_outer(outer, "row")
    inner = swap(inner, "row", 1)
    pair_in = after_all(pair, near0)
    near = [near0] + [swap(near0, "row", 2 * k) for k in range(1, 4)]
    parts = inner_step(meta, feat_in, pair_in, other, weight1, weight2)
    parts, near = lax.optimization_barrier((parts, near))
    far = swap(call(stack_kernel, "stack_eight", (((4, 2, 160, CH), BF),), near)[0], "row", 1)
    pool3, slope1, slope2, act, feat3, act3 = outer_step(meta, inner, outer, parts, weight1, weight2)
    halo = (pair, other, inner, outer)
    own_act, proj, keep_c, send_c, pooled_grad = coarse_step(meta, pool3, cot_in, halo, near, far)
    got_c = swap(send_c, "row", 1)
    keep_f, send_f, first3 = fine_backward(
        meta, pooled_grad, cot_in, halo, slope1, slope2, feat3, act3, back2
    )
    got_f = swap(send_f, "row", 1)
    feature_grad = feature_step(first3, back1)

    got_f = after_all(got_f, feature_grad)
    part = call(scatter_core_kernel, "scatter_core", (((16, 152, CH), BF),), (keep_c, keep_f, got_c, got_f))[0]
    part = call(
        scatter_plane_kernel, "scatter_plane", (((8, 24, CH), BF),), (exchange_plane(part),), (((160, CH), F32),)
    )[0]
    part = call(scatter_column_kernel, "scatter_column", (((16, 24, CH), BF),), (exchange_depth(part),))[0]
    coarse, fine = call(
        gather_column_kernel,
        "gather_column",
        (((2, 80, CH), BF), ((16, 72, CH), BF)),
        (meta, exchange_column(part)),
        (((2, 160, CH), F32),),
    )
    fine = exchange_plane(fine)
    blended, conv_grad, proj_grad = call(
        functools.partial(blend_kernel, coarse_scale),
        "blend",
        (((16, 64, CH), BF), ((9, 16, CH), F32), ((16, CH), F32)),
        (after_all(own_act, fine), proj, act, coarse),
        flops=10**9,
    )
    other = after_all(swap(fine, "row", 1), blended)
    first, second = call(
        functools.partial(finish_kernel, fine_scale),
        "finish",
        (((8, 144, CH), F32), ((8, 144, CH), F32)),
        (meta, fine, other),
    )
    shape = features.shape
    return (
        blended.reshape(shape),
        feature_grad.reshape(shape),
        first.reshape(3, 3, CH, CH),
        second.reshape(3, 3, CH, CH),
        conv_grad.reshape(3, 3, 16, CH).swapaxes(2, 3),
        proj_grad,
    )


def solution(mesh):
    in_specs = (
        P("row", "col", None, None),
        P(),
        P(),
        P(None, None, None, "row"),
        P("row", None),
        P("row", "col", None, None),
    )
    out_specs = (
        P("row", "col", None, None),
        P("row", "col", None, None),
        P(),
        P(),
        P(None, None, None, "row"),
        P("row", None),
    )
    return jax.shard_map(local, mesh=mesh, in_specs=in_specs, out_specs=out_specs, check_vma=False)
```

```python
import functools

import jax
import jax.numpy as jnp
from jax import lax
from jax.experimental import pallas as pl
from jax.experimental.pallas import tpu as pltpu
from jax.sharding import PartitionSpec as P

BF = jnp.bfloat16
F32 = jnp.float32
CH = 128
WIDE = 256
MIB = 1024 * 1024
VM = pl.BlockSpec(memory_space=pltpu.VMEM)
SM = pl.BlockSpec(memory_space=pltpu.SMEM)
HBM = pl.BlockSpec(memory_space=pltpu.HBM)


def call(kernel, name, outs, ins, scratch=(), limit=16, flops=0, moved=0, far=()):
    ins = [pltpu.with_memory_space_constraint(v, pltpu.HBM) if k in far else v for k, v in enumerate(ins)]
    shapes = tuple(jax.ShapeDtypeStruct(shape, dtype) for shape, dtype in outs)
    return pl.pallas_call(
        kernel,
        name=name,
        out_shape=shapes,
        in_specs=[HBM if k in far else SM if v.ndim == 1 else VM for k, v in enumerate(ins)],
        out_specs=tuple(VM for _ in outs),
        scratch_shapes=[pltpu.VMEM(*v) if isinstance(v, tuple) else v for v in scratch],
        compiler_params=pltpu.CompilerParams(vmem_limit_bytes=limit * MIB),
        cost_estimate=pl.CostEstimate(flops=flops, bytes_accessed=moved, transcendentals=0),
    )(*ins)


def dot_nn(a, b):
    return jnp.dot(a, b, preferred_element_type=F32)


def dot_nt(a, b):
    return lax.dot_general(a, b, (((1,), (1,)), ((), ())), preferred_element_type=F32)


def dot_tn(a, b):
    return lax.dot_general(a, b, (((0,), (0,)), ((), ())), preferred_element_type=F32)


def sigmoid(value):
    return 0.5 * jnp.tanh(0.5 * value) + 0.5


def slope_of(value):
    sigma = sigmoid(value)
    return sigma * (1.0 + value * (1.0 - sigma))


def rounded(value):
    return value.astype(BF).astype(F32)


def three(value):
    count = value.shape[0]
    left = pltpu.roll(value, 4, 0)
    right = pltpu.roll(value, count - 4, 0)
    return jnp.concatenate([left.astype(BF), value.astype(BF), right.astype(BF)], axis=1)


def paired(weight, axis):
    pad = jnp.zeros((3 * CH, CH) if axis == 0 else (CH, 3 * CH), BF)
    return jnp.concatenate(
        [jnp.concatenate([weight, pad], axis=axis), jnp.concatenate([pad, weight], axis=axis)], axis=1 - axis
    )


def flipped(weight):
    return jnp.concatenate([weight[(8 - t) * CH : (9 - t) * CH, :] for t in range(9)], axis=1)


def four_rows(row, starts):
    parts = [jnp.concatenate([row(h + k) for h in starts], axis=0) for k in range(4)]
    return jnp.concatenate(parts, axis=1)


def split_rows(value, starts):
    size = value.shape[0] // len(starts)
    out = []
    for k in range(len(starts)):
        out += [value[k * size : (k + 1) * size, e * CH : (e + 1) * CH] for e in range(2)]
    return out


def weight_grad(source, grad):
    gap = jnp.zeros((64, CH), BF)
    parts = []
    for r in range(3):
        parts.append(jnp.concatenate([gap] * r + [grad.reshape(1024, CH)] + [gap] * (2 - r), axis=0))
    whole = dot_tn(source.reshape(1152, 3 * CH), jnp.concatenate(parts, axis=1))
    return [whole[:, r * CH : (r + 1) * CH] for r in range(3)]


def column_mask(first, width, limit):
    place = first + lax.broadcasted_iota(jnp.int32, (width, CH), 0) // 4
    return jnp.where((place >= 0) & (place < limit), 1.0, 0.0).astype(F32)


def row_ok(place, limit):
    return jnp.where((place >= 0) & (place < limit), 1.0, 0.0).astype(F32)


def masked(value, mask, first, limit):
    rows = []
    for k in range(value.shape[0]):
        rows.append((value[k] * (mask * row_ok(first + k, limit)))[None])
    return jnp.concatenate(rows, axis=0)


def pooled_pair(row):
    count = row.shape[0]
    low = (row + pltpu.roll(row, count - 4, 0)).reshape(count // 16, 2, 8, CH)
    high = (row + pltpu.roll(row, 4, 0)).reshape(count // 16, 2, 8, CH)
    first = lax.broadcasted_iota(jnp.int32, (count // 16, 8, CH), 1) < 4
    return jnp.where(first, low[:, 0], high[:, 1]).reshape(count // 2, CH)


def repeated(row):
    count = row.shape[0]
    first = lax.broadcasted_iota(jnp.int32, (count, CH), 0) % 8 < 4
    even = jnp.where(first, row, pltpu.roll(row, 4, 0)).reshape(count // 8, 1, 8, CH)
    odd = jnp.where(first, pltpu.roll(row, count - 4, 0), row).reshape(count // 8, 1, 8, CH)
    return jnp.concatenate([even, odd], axis=1).reshape(count * 2, CH)


def aligned(start, size):
    return pl.ds(pl.multiple_of(start, 16), size)


def sides(meta, pair, other):
    even = meta[5] % 2 == 0
    return lax.select(even, other, pair), lax.select(even, pair, other)


def pack_columns_kernel(meta, feat, cot, conv, proj, pair, other, weights, done):
    odd = meta[5] % 2
    pairs = [
        (feat.at[:, aligned(32 - 32 * odd, 32), :], pair.at[:, 0:32, :]),
        (cot.at[:, aligned(48 - 48 * odd, 16), :], pair.at[:, 32:48, :]),
        (feat.at[:, aligned(32 * odd, 32), :], other.at[:, 0:32, :]),
        (cot.at[:, aligned(48 * odd, 16), :], other.at[:, 32:48, :]),
        (proj, weights.at[144:160, :]),
    ] + [(conv.at[t], weights.at[16 * t : 16 * t + 16, :]) for t in range(9)]
    copies = [pltpu.make_async_copy(a, b, done.at[k]) for k, (a, b) in enumerate(pairs)]
    for copy in copies:
        copy.start()
    for copy in copies:
        copy.wait()


EDGE = 8 * 128 + 2 * 96 + 48


def cot_edge(ref):
    return ref[1024:1216, :].reshape(2, 96, CH)


def copy_kernel(value, out):
    out[...] = value[...]


def bring_kernel(feat_far, cot_far, feat, cot, done):
    pairs = [(feat_far, feat), (cot_far, cot)]
    copies = [pltpu.make_async_copy(a, b, done.at[k]) for k, (a, b) in enumerate(pairs)]
    for copy in copies:
        copy.start()
    for copy in copies:
        copy.wait()


def weights_kernel(w1_far, w2_far, weight1, weight2, back1, back2, w1, w2, done):
    copies = [pltpu.make_async_copy(a, b, done.at[k]) for k, (a, b) in enumerate(((w1_far, w1), (w2_far, w2)))]
    for copy in copies:
        copy.start()
    for copy, w, weight, back in zip(copies, (w1, w2), (weight1, weight2), (back1, back2)):
        copy.wait()
        weight[...] = paired(w[...], 0)
        back[...] = paired(flipped(w), 1)


def pack_rows_kernel(meta, feat, cot, pair, other, own, far, inner, outer, both):
    core = meta[4] % 2

    def cot_row(row):
        before, after = sides(meta, pair[row, 32:48, :], other[row, 32:48, :])
        return jnp.concatenate([before, cot[row], after], axis=0)

    for low, out in ((1 - core, inner), (core, outer)):
        for k in range(8):
            row = 8 * low + k
            before, after = sides(meta, pair[row, 0:32, :], other[row, 0:32, :])
            out[128 * k : 128 * k + 32, :] = before
            out[128 * k + 32 : 128 * k + 96, :] = feat[row]
            out[128 * k + 96 : 128 * k + 128, :] = after
        for k in range(2):
            out[1024 + 96 * k : 1120 + 96 * k, :] = cot_row(14 * low + k)
        away = 2 + 10 * low
        both_rows = cot_row(away).astype(F32) + cot_row(away + 1).astype(F32)
        out[1216:1264, :] = pooled_pair(both_rows).astype(BF)
    both[0] = own[...]
    both[1] = far[...]


def stack_kernel(*refs):
    out = refs[-1]
    for k, ref in enumerate(refs[:-1]):
        out[k] = ref[...]


def first_rows(meta, row, starts, weight):
    top, left, height, breadth = (meta[0], meta[1], meta[2], meta[3])
    mask = column_mask(left - 8, 128, breadth)
    pre = dot_nn(four_rows(row, [h - 1 for h in starts]), weight)
    out = {}
    for k, value in enumerate(split_rows(pre, starts)):
        h = starts[k // 2] + k % 2
        act = rounded(value * sigmoid(value)) * (mask * row_ok(top - 8 + h, height))
        out[h] = (value, three(act))
    return out


def second_rows(meta, row, starts, weight):
    top, left, height, breadth = (meta[0], meta[1], meta[2], meta[3])
    mask = column_mask(left // 2 - 4, 64, breadth // 2)
    rows = split_rows(dot_nn(four_rows(row, [h - 1 for h in starts]), weight), starts)
    out = {}
    for k, h in enumerate(starts):
        pre = rows[2 * k : 2 * k + 2]
        act = [(v * sigmoid(v)).astype(BF) for v in pre]
        small = rounded(0.25 * pooled_pair(act[0].astype(F32) + act[1].astype(F32)))
        small = small * (mask * row_ok(top // 2 - 4 + h // 2, height // 2))
        out[h] = (pre, act, three(small))
    return out


INNER_FIRST = [9, 11, 13, 15, 17, 19, 21]
INNER_SECOND = [10, 12, 14, 16, 18, 20]


def inner_kernel(meta, feat, pair, other, weight1, weight2, feat3, act3, slope1, pool3, slope2, act):
    for k in range(16):
        before, after = sides(meta, pair[k, 0:32, :], other[k, 0:32, :])
        feat3[k] = three(jnp.concatenate([before, feat[k], after], axis=0).astype(F32))
    for h, (pre, wide) in first_rows(meta, lambda h: feat3[h - 8], INNER_FIRST, weight1[...]).items():
        act3[h - 9] = wide
        slope1[h - 9] = slope_of(pre[16:112])
    for h, (pre, value, small) in second_rows(meta, lambda h: act3[h - 9], INNER_SECOND, weight2[...]).items():
        pool3[h // 2 - 5] = small
        for e in range(2):
            slope2[h - 10 + e] = slope_of(pre[e][16:112])
            act[h - 10 + e] = value[e][32:96]


def outer_kernel(
    meta, inner, outer, feat3i, act3i, slope1i, pool3i, slope2i, acti, weight1, weight2,
    pool3, slope1, slope2, act, feat3o, act3o, feat3, act3,
):
    below_at = 8 * (meta[4] % 2)
    for k in range(8):
        feat3[k + below_at] = three(outer[128 * k : 128 * k + 128, :].astype(F32))
        feat3[k + 8 - below_at] = three(inner[128 * k : 128 * k + 128, :].astype(F32))

    def feat_row(h):
        return feat3i[h - 8] if 8 <= h < 24 else feat3[h if h < 8 else h - 16]

    def act_row(h):
        return act3i[h - 9] if 9 <= h < 23 else act3[h - 1 if h < 9 else h - 15]

    for starts in ([1, 3, 5, 7], [23, 25, 27, 29]):
        for h, (pre, wide) in first_rows(meta, feat_row, starts, weight1[...]).items():
            act3[h - 1 if h < 9 else h - 15] = wide
            if 7 <= h <= 24:
                slope1[h - 7] = slope_of(pre[16:112])
    slope1[2:16] = slope1i[...]
    for starts in ([2, 4, 6, 8], [22, 24, 26, 28]):
        for h, (pre, value, small) in second_rows(meta, act_row, starts, weight2[...]).items():
            pool3[h // 2 - 1] = small
            for e in range(2):
                if 6 <= h + e < 26:
                    slope2[h + e - 6] = slope_of(pre[e][16:112])
                if 8 <= h + e < 24:
                    act[h + e - 8] = value[e][32:96]
    pool3[4:10] = pool3i[...]
    slope2[4:16] = slope2i[...]
    act[2:14] = acti[...]
    for k in range(18):
        feat3o[k] = feat_row(k + 7)[32:96]
        act3o[k] = act_row(k + 7)[32:96]


def inner_step(meta, feat, pair, other, weight1, weight2):
    return call(
        inner_kernel,
        "forward_inner",
        (
            ((16, 128, 384), BF),
            ((14, 128, 384), BF),
            ((14, 96, CH), F32),
            ((6, 64, 384), BF),
            ((12, 96, CH), F32),
            ((12, 64, CH), BF),
        ),
        (meta, feat, pair, other, weight1, weight2),
        limit=24,
        flops=0,
    )


def outer_step(meta, inner, outer, parts, weight1, weight2):
    return call(
        outer_kernel,
        "forward_outer",
        (
            ((14, 64, 384), BF),
            ((18, 96, CH), F32),
            ((20, 96, CH), F32),
            ((16, 64, CH), BF),
            ((18, 64, 384), BF),
            ((18, 64, 384), BF),
        ),
        (meta, inner, outer) + tuple(parts) + (weight1, weight2),
        (((16, 128, 384), BF),) * 2,
        limit=24,
        flops=4 * 10**9,
    )


def coarse_kernel(
    meta, pool3, cot, pair, other, inner, outer, near0, near1, near2, near3, far,
    own, projs_out, keep, send, pooled_grad, wcat, projs, wide3, projin,
):
    top, left, height, breadth, me = (meta[0], meta[1], meta[2], meta[3], meta[4])
    core = me % 2
    near = (near0, near1, near2, near3)
    for rel in range(16):
        c, x, y = (rel % 2, (rel // 2) % 4, rel // 8)
        place = pl.ds(pl.multiple_of((me ^ rel) * 16, 16), 16)
        source = far.at[x, y] if c else near[x].at[y]
        for t in range(9):
            wcat[place, t * CH : (t + 1) * CH] = source[16 * t : 16 * t + 16, :]
        projs[place, :] = source[144:160, :]
    proj_w = projs[...]

    def pair_sum(a, b):
        return pooled_pair(a.astype(F32) + b.astype(F32))

    for ref, far_at, near_at in ((outer, 11 * core, 1 + 9 * core), (inner, 11 - 11 * core, 10 - 9 * core)):
        projin[far_at] = ref[1216:1264, :].astype(F32)
        near_rows = cot_edge(ref)
        projin[near_at] = pair_sum(near_rows[0], near_rows[1])

    for k in range(8):
        rows = slice(2 * k, 2 * k + 2)
        before, after = sides(meta, pair[rows, 32:48, :], other[rows, 32:48, :])
        both = jnp.concatenate([before, cot[rows], after], axis=1)
        projin[k + 2] = pair_sum(both[0], both[1])

    proj_in = projin[...].reshape(576, CH)
    proj_in_bf = proj_in.astype(BF)
    lhs = jnp.concatenate([pool3[r : r + 12].reshape(768, 3 * CH) for r in range(3)], axis=1)
    pre = dot_nt(lhs, wcat[...]).reshape(12, 64, WIDE)[:, 8:56].reshape(576, WIDE)
    sigma = sigmoid(pre)
    coarse_act = pre * sigma
    act_grad = dot_nt(proj_in_bf, proj_w)
    grad = rounded(act_grad * (sigma * (1.0 + pre * (1.0 - sigma)))).reshape(12, 48, WIDE)
    mask = column_mask(left // 2 - 2, 48, breadth // 2)
    mask = jnp.concatenate([mask, mask], axis=1)
    grad = masked(grad, mask, top // 2 - 2, height // 2)
    wide3[...] = three(grad.reshape(576, WIDE)).reshape(12, 48, 3 * WIDE)
    own_grad = grad[2:10, 8:40].reshape(256, WIDE).astype(BF)
    own_act = coarse_act.reshape(12, 48, WIDE)[2:10, 8:40].reshape(256, WIDE).astype(BF)
    own_in = proj_in.reshape(12, 48, CH)[2:10, 8:40].reshape(256, CH).astype(BF)

    def emit(first, last, value):
        value = value.reshape(8, 2, 16, CH)
        even, odd = (value[:, 0], value[:, 1])
        keep[:, first:last, :] = jnp.where(core == 0, even, odd).astype(BF)
        send[:, first:last, :] = jnp.where(core == 0, odd, even).astype(BF)

    source = [pool3[2 + r : 10 + r, 16:48, :].reshape(256, 3 * CH) for r in range(3)]
    part = dot_tn(own_grad, jnp.concatenate(source, axis=1))
    for t in range(9):
        emit(16 * t, 16 * t + 16, part[:, t * CH : (t + 1) * CH])
    emit(144, 160, dot_tn(own_act, own_in))
    total = None
    for r in range(3):
        lhs = wide3[r : r + 10].reshape(480, 3 * WIDE)
        first = 3 * (2 - r)
        rhs = jnp.concatenate([wcat[:, (first + 2 - s) * CH : (first + 3 - s) * CH] for s in range(3)], axis=0)
        part = dot_nn(lhs, rhs)
        total = part if total is None else total + part
    pooled_grad[...] = total.reshape(10, 48, CH)
    own[...] = own_act
    projs_out[...] = proj_w


def blend_kernel(scale, own, proj, act, coarse, blended, conv, proj_grad):
    for k in range(9):
        conv[k] = coarse[k // 5, 16 * (k % 5) : 16 * (k % 5) + 16, :].astype(F32) * scale
    proj_grad[...] = coarse[1, 64:80, :].astype(F32) * scale
    projected = dot_nn(own[...], proj[...]).reshape(8, 32, CH)
    for k in range(8):
        row = repeated(projected[k])
        for e in range(2):
            blended[2 * k + e] = (act[2 * k + e].astype(F32) + row).astype(BF)


def coarse_step(meta, pool3, cot, halo, near, far):
    return call(
        coarse_kernel,
        "coarse_step",
        (((256, WIDE), BF), ((WIDE, CH), BF), ((8, 160, CH), BF), ((8, 160, CH), BF), ((10, 48, CH), F32)),
        (meta, pool3, cot) + halo + tuple(near) + (far,),
        (
            ((WIDE, 9 * CH), BF),
            ((WIDE, CH), BF),
            ((12, 48, 3 * WIDE), BF),
            ((12, 48, CH), F32),
        ),
        limit=20,
        flops=2 * 10**9,
    )


def backward_kernel(
    meta, pooled_grad, cot, pair, other, inner, outer, slope1, slope2, feat3, act3, back_w,
    keep, send, first3, second3, grads,
):
    top, left, height, breadth = (meta[0], meta[1], meta[2], meta[3])
    mask = column_mask(left - 4, 96, breadth)

    def second_pair(k, both):
        wide = 0.25 * repeated(pooled_grad[k])
        for e in range(2):
            value = rounded((both[e].astype(F32) + wide) * slope2[2 * k + e])
            second3[2 * k + e] = three(value * (mask * row_ok(top - 2 + 2 * k + e, height)))

    first_core = meta[4] % 2 == 0
    second_pair(0, lax.select(first_core, cot_edge(outer), cot_edge(inner)))
    second_pair(9, lax.select(first_core, cot_edge(inner), cot_edge(outer)))
    for k in range(8):
        rows = slice(2 * k, 2 * k + 2)
        before, after = sides(meta, pair[rows, 32:48, :], other[rows, 32:48, :])
        second_pair(k + 1, jnp.concatenate([before, cot[rows], after], axis=1))

    def emit(base, parts):
        for r in range(3):
            grads[base + 384 * r : base + 384 * (r + 1), :] = parts[r].astype(BF)

    for starts in ([0, 2, 4, 6], [8, 10, 12, 14, 16]):
        value = dot_nt(four_rows(lambda h: second3[h], starts), back_w[...])
        for k, row in enumerate(split_rows(value, starts)):
            h = starts[k // 2] + k % 2
            row = rounded(row * slope1[h]) * (mask * row_ok(top - 1 + h, height))
            first3[h] = three(row)[16:80]
    emit(1152, weight_grad(act3[...], second3[2:18, 16:80, CH : 2 * CH]))
    emit(0, weight_grad(feat3[...], first3[1:17, :, CH : 2 * CH]))
    core = meta[4] % 2
    for k in range(8):
        keep[k] = grads[pl.ds(pl.multiple_of((2 * k + core) * 144, 16), 144), :]
        send[k] = grads[pl.ds(pl.multiple_of((2 * k + 1 - core) * 144, 16), 144), :]


def fine_backward(meta, pooled_grad, cot, halo, slope1, slope2, feat3, act3, back_w):
    return call(
        backward_kernel,
        "fine_backward",
        (((8, 144, CH), BF), ((8, 144, CH), BF), ((18, 64, 384), BF)),
        (meta, pooled_grad, cot) + halo + (slope1, slope2, feat3, act3, back_w),
        (((20, 96, 384), BF), ((2304, CH), BF)),
        limit=20,
        flops=2 * 10**9,
    )


def feature_kernel(first3, back_w, out):
    for starts in ([0, 2, 4, 6], [8, 10, 12, 14]):
        value = dot_nt(four_rows(lambda h: first3[h], starts), back_w[...])
        for k, row in enumerate(split_rows(value, starts)):
            out[starts[0] + k] = row.astype(BF)


def feature_step(first3, back_w):
    return call(feature_kernel, "feature_step", (((16, 64, CH), BF),), (first3, back_w), limit=12, flops=10**9)[0]


def scatter_core_kernel(keep_c, keep_f, got_c, got_f, out):
    for k in range(8):
        coarse = keep_c[k].astype(F32) + got_c[k].astype(F32)
        fine = keep_f[k].astype(F32) + got_f[k].astype(F32)
        for j in range(2):
            out[2 * k + j, 0:80, :] = coarse[80 * j : 80 * j + 80].astype(BF)
            out[2 * k + j, 80:152, :] = fine[72 * j : 72 * j + 72].astype(BF)


def scatter_plane_kernel(got, out, total):
    value = got[0].astype(F32)
    for k in range(1, 16):
        value = value + got[k].astype(F32)
    total[0:152, :] = value
    total[152:160, :] = jnp.zeros((8, CH), F32)
    for k in range(8):
        out[k] = total[19 * k : 19 * k + 24, :].astype(BF)


def scatter_column_kernel(got, out):
    value = got[0].astype(F32)
    for k in range(1, 8):
        value = value + got[k].astype(F32)
    value = value.astype(BF)
    for k in range(16):
        out[k] = value


def gather_column_kernel(meta, got, coarse, fine, total):
    for j in range(2):
        for k in range(8):
            total[j, 19 * k : 19 * k + 24, :] = got[8 * j + k].astype(F32)
    coarse[...] = total[:, 0:80, :].astype(BF)
    value = total[meta[5] // 8, 80:152, :].astype(BF)
    for k in range(16):
        fine[k] = value


def finish_kernel(scale, meta, mine, other, first, second):
    core = meta[4] % 2
    for at in range(8):
        out = first if at < 4 else second
        for j in range(2):
            rows = slice(72 * j, 72 * j + 72)
            a = mine[2 * at + j].astype(F32) * scale
            b = other[2 * at + j].astype(F32) * scale
            out[2 * (at % 4), rows, :] = jnp.where(core == 0, a, b)
            out[2 * (at % 4) + 1, rows, :] = jnp.where(core == 0, b, a)


def swap(value, axis, mask):
    count = lax.axis_size(axis)
    return lax.ppermute(value, axis, [(i, i ^ mask) for i in range(count)])


def swap_outer(value, axis):
    count = lax.axis_size(axis)
    pairs = [(i, i + 1 if i % 2 else i - 1) for i in range(1, count - 1)]
    return lax.ppermute(value, axis, pairs)


def exchange_plane(value):
    rows, cols = (lax.axis_size("row"), lax.axis_size("col"))
    groups = []
    for core in range(2):
        for z in range(cols // 2):
            groups.append([r * cols + c for r in range(core, rows, 2) for c in (z, z + cols // 2)])
    return lax.all_to_all(value, ("row", "col"), 0, 0, axis_index_groups=groups, tiled=True)


def exchange_depth(value):
    count = lax.axis_size("col")
    groups = [list(range(k, k + count // 2)) for k in (0, count // 2)]
    return lax.all_to_all(value, "col", 0, 0, axis_index_groups=groups, tiled=True)


def exchange_column(value):
    return lax.all_to_all(value, "col", 0, 0, tiled=True)


def after_all(value, *others):
    return lax.optimization_barrier((value,) + others)[0]


def local(features, conv_first, conv_second, coarse_conv, coarse_proj, cotangent):
    rows, cols = (lax.axis_size("row"), lax.axis_size("col"))
    height, breadth = (features.shape[0] * rows, features.shape[1] * cols)
    fine_scale = 1.0 / (height * breadth * features.shape[2]) ** 0.5
    coarse_scale = 2.0 * fine_scale
    me, mine = (lax.axis_index("row"), lax.axis_index("col"))
    fixed = [jnp.int32(height), jnp.int32(breadth)]
    meta = jnp.stack([me * 16, mine * 16] + fixed + [me, mine]).astype(jnp.int32)
    feat = features.reshape(16, 64, CH)
    cot = cotangent.reshape(16, 64, CH)
    conv = coarse_conv.reshape(9, CH, 16).swapaxes(1, 2)
    slab = ((160, CH), BF)

    side = ((16, 48, CH), BF)
    pair, other, own = call(
        pack_columns_kernel,
        "pack_columns",
        (side, side, slab),
        (meta, feat, cot, conv, coarse_proj),
        (pltpu.SemaphoreType.DMA((14,)),),
        far=(1, 2, 3, 4),
    )
    own = call(copy_kernel, "own_slab", (slab,), (own,), flops=4 * 10**9)[0]
    w1, w2 = (conv_first.reshape(1152, CH), conv_second.reshape(1152, CH))
    big, wide = (((16, 64, CH), BF), ((1536, 256), BF))
    feat_in, cot_in = call(
        bring_kernel,
        "bring",
        (big, big),
        (after_all(feat, own), cot),
        (pltpu.SemaphoreType.DMA((2,)),),
        far=(0, 1),
        flops=0,
    )
    own_far = swap(own, "row", 8)
    weight1, weight2, back1, back2 = call(
        weights_kernel,
        "weights",
        (wide, wide, ((256, 1536), BF), ((256, 1536), BF)),
        (after_all(w1, feat_in), w2),
        (((1152, CH), BF), ((1152, CH), BF), pltpu.SemaphoreType.DMA((2,))),
        far=(0, 1),
        flops=0,
    )
    pair = swap(pair, "col", 1)
    other = swap_outer(other, "col")
    edge = ((EDGE, CH), BF)
    inner, outer, near0 = call(
        pack_rows_kernel,
        "pack_rows",
        (edge, edge, ((2, 160, CH), BF)),
        (meta, feat_in, cot_in, pair, after_all(other, weight1), own, own_far),
    )
    outer = swap_outer(outer, "row")
    inner = swap(inner, "row", 1)
    pair_in = after_all(pair, near0)
    near = [near0] + [swap(near0, "row", 2 * k) for k in range(1, 4)]
    parts = inner_step(meta, feat_in, pair_in, other, weight1, weight2)
    parts, near = lax.optimization_barrier((parts, near))
    far = swap(call(stack_kernel, "stack_eight", (((4, 2, 160, CH), BF),), near)[0], "row", 1)
    pool3, slope1, slope2, act, feat3, act3 = outer_step(meta, inner, outer, parts, weight1, weight2)
    halo = (pair, other, inner, outer)
    own_act, proj, keep_c, send_c, pooled_grad = coarse_step(meta, pool3, cot_in, halo, near, far)
    got_c = swap(send_c, "row", 1)
    keep_f, send_f, first3 = fine_backward(
        meta, pooled_grad, cot_in, halo, slope1, slope2, feat3, act3, back2
    )
    got_f = swap(send_f, "row", 1)
    feature_grad = feature_step(first3, back1)

    got_f = after_all(got_f, feature_grad)
    part = call(scatter_core_kernel, "scatter_core", (((16, 152, CH), BF),), (keep_c, keep_f, got_c, got_f))[0]
    part = call(
        scatter_plane_kernel, "scatter_plane", (((8, 24, CH), BF),), (exchange_plane(part),), (((160, CH), F32),)
    )[0]
    part = call(scatter_column_kernel, "scatter_column", (((16, 24, CH), BF),), (exchange_depth(part),))[0]
    coarse, fine = call(
        gather_column_kernel,
        "gather_column",
        (((2, 80, CH), BF), ((16, 72, CH), BF)),
        (meta, exchange_column(part)),
        (((2, 160, CH), F32),),
    )
    fine = exchange_plane(fine)
    blended, conv_grad, proj_grad = call(
        functools.partial(blend_kernel, coarse_scale),
        "blend",
        (((16, 64, CH), BF), ((9, 16, CH), F32), ((16, CH), F32)),
        (after_all(own_act, fine), proj, act, coarse),
        flops=10**9,
    )
    other = after_all(swap(fine, "row", 1), blended)
    first, second = call(
        functools.partial(finish_kernel, fine_scale),
        "finish",
        (((8, 144, CH), F32), ((8, 144, CH), F32)),
        (meta, fine, other),
    )
    shape = features.shape
    return (
        blended.reshape(shape),
        feature_grad.reshape(shape),
        first.reshape(3, 3, CH, CH),
        second.reshape(3, 3, CH, CH),
        conv_grad.reshape(3, 3, 16, CH).swapaxes(2, 3),
        proj_grad,
    )


def solution(mesh):
    in_specs = (
        P("row", "col", None, None),
        P(),
        P(),
        P(None, None, None, "row"),
        P("row", None),
        P("row", "col", None, None),
    )
    out_specs = (
        P("row", "col", None, None),
        P("row", "col", None, None),
        P(),
        P(),
        P(None, None, None, "row"),
        P("row", None),
    )
    return jax.shard_map(local, mesh=mesh, in_specs=in_specs, out_specs=out_specs, check_vma=False)
```

```python
import functools

import jax
import jax.numpy as jnp
from jax import lax
from jax.experimental import pallas as pl
from jax.experimental.pallas import tpu as pltpu
from jax.sharding import PartitionSpec as P

BF = jnp.bfloat16
F32 = jnp.float32
CH = 128
WIDE = 256
MIB = 1024 * 1024
VM = pl.BlockSpec(memory_space=pltpu.VMEM)
SM = pl.BlockSpec(memory_space=pltpu.SMEM)
HBM = pl.BlockSpec(memory_space=pltpu.HBM)


def call(kernel, name, outs, ins, scratch=(), limit=16, flops=0, moved=0, far=()):
    ins = [pltpu.with_memory_space_constraint(v, pltpu.HBM) if k in far else v for k, v in enumerate(ins)]
    shapes = tuple(jax.ShapeDtypeStruct(shape, dtype) for shape, dtype in outs)
    return pl.pallas_call(
        kernel,
        name=name,
        out_shape=shapes,
        in_specs=[HBM if k in far else SM if v.ndim == 1 else VM for k, v in enumerate(ins)],
        out_specs=tuple(VM for _ in outs),
        scratch_shapes=[pltpu.VMEM(*v) if isinstance(v, tuple) else v for v in scratch],
        compiler_params=pltpu.CompilerParams(vmem_limit_bytes=limit * MIB),
        cost_estimate=pl.CostEstimate(flops=flops, bytes_accessed=moved, transcendentals=0),
    )(*ins)


def dot_nn(a, b):
    return jnp.dot(a, b, preferred_element_type=F32)


def dot_nt(a, b):
    return lax.dot_general(a, b, (((1,), (1,)), ((), ())), preferred_element_type=F32)


def dot_tn(a, b):
    return lax.dot_general(a, b, (((0,), (0,)), ((), ())), preferred_element_type=F32)


def sigmoid(value):
    return 0.5 * jnp.tanh(0.5 * value) + 0.5


def slope_of(value):
    sigma = sigmoid(value)
    return sigma * (1.0 + value * (1.0 - sigma))


def rounded(value):
    return value.astype(BF).astype(F32)


def three(value):
    count = value.shape[0]
    left = pltpu.roll(value, 4, 0)
    right = pltpu.roll(value, count - 4, 0)
    return jnp.concatenate([left.astype(BF), value.astype(BF), right.astype(BF)], axis=1)


def paired(weight, axis):
    pad = jnp.zeros((3 * CH, CH) if axis == 0 else (CH, 3 * CH), BF)
    return jnp.concatenate(
        [jnp.concatenate([weight, pad], axis=axis), jnp.concatenate([pad, weight], axis=axis)], axis=1 - axis
    )


def flipped(weight):
    return jnp.concatenate([weight[(8 - t) * CH : (9 - t) * CH, :] for t in range(9)], axis=1)


def four_rows(row, starts):
    parts = [jnp.concatenate([row(h + k) for h in starts], axis=0) for k in range(4)]
    return jnp.concatenate(parts, axis=1)


def split_rows(value, starts):
    size = value.shape[0] // len(starts)
    out = []
    for k in range(len(starts)):
        out += [value[k * size : (k + 1) * size, e * CH : (e + 1) * CH] for e in range(2)]
    return out


def weight_grad(source, grad):
    gap = jnp.zeros((64, CH), BF)
    parts = []
    for r in range(3):
        parts.append(jnp.concatenate([gap] * r + [grad.reshape(1024, CH)] + [gap] * (2 - r), axis=0))
    whole = dot_tn(source.reshape(1152, 3 * CH), jnp.concatenate(parts, axis=1))
    return [whole[:, r * CH : (r + 1) * CH] for r in range(3)]


def column_mask(first, width, limit):
    place = first + lax.broadcasted_iota(jnp.int32, (width, CH), 0) // 4
    return jnp.where((place >= 0) & (place < limit), 1.0, 0.0).astype(F32)


def row_ok(place, limit):
    return jnp.where((place >= 0) & (place < limit), 1.0, 0.0).astype(F32)


def masked(value, mask, first, limit):
    rows = []
    for k in range(value.shape[0]):
        rows.append((value[k] * (mask * row_ok(first + k, limit)))[None])
    return jnp.concatenate(rows, axis=0)


def pooled_pair(row):
    count = row.shape[0]
    low = (row + pltpu.roll(row, count - 4, 0)).reshape(count // 16, 2, 8, CH)
    high = (row + pltpu.roll(row, 4, 0)).reshape(count // 16, 2, 8, CH)
    first = lax.broadcasted_iota(jnp.int32, (count // 16, 8, CH), 1) < 4
    return jnp.where(first, low[:, 0], high[:, 1]).reshape(count // 2, CH)


def repeated(row):
    count = row.shape[0]
    first = lax.broadcasted_iota(jnp.int32, (count, CH), 0) % 8 < 4
    even = jnp.where(first, row, pltpu.roll(row, 4, 0)).reshape(count // 8, 1, 8, CH)
    odd = jnp.where(first, pltpu.roll(row, count - 4, 0), row).reshape(count // 8, 1, 8, CH)
    return jnp.concatenate([even, odd], axis=1).reshape(count * 2, CH)


def aligned(start, size):
    return pl.ds(pl.multiple_of(start, 16), size)


def sides(meta, pair, other):
    even = meta[5] % 2 == 0
    return lax.select(even, other, pair), lax.select(even, pair, other)


def pack_columns_kernel(meta, feat, cot, conv, proj, pair, other, weights, done):
    odd = meta[5] % 2
    pairs = [
        (feat.at[:, aligned(32 - 32 * odd, 32), :], pair.at[:, 0:32, :]),
        (cot.at[:, aligned(48 - 48 * odd, 16), :], pair.at[:, 32:48, :]),
        (feat.at[:, aligned(32 * odd, 32), :], other.at[:, 0:32, :]),
        (cot.at[:, aligned(48 * odd, 16), :], other.at[:, 32:48, :]),
        (proj, weights.at[144:160, :]),
    ] + [(conv.at[t], weights.at[16 * t : 16 * t + 16, :]) for t in range(9)]
    copies = [pltpu.make_async_copy(a, b, done.at[k]) for k, (a, b) in enumerate(pairs)]
    for copy in copies:
        copy.start()
    for copy in copies:
        copy.wait()


EDGE = 8 * 128 + 2 * 96 + 48


def cot_edge(ref):
    return ref[1024:1216, :].reshape(2, 96, CH)


def copy_kernel(value, out):
    out[...] = value[...]


def bring_kernel(feat_far, cot_far, feat, cot, done):
    pairs = [(feat_far, feat), (cot_far, cot)]
    copies = [pltpu.make_async_copy(a, b, done.at[k]) for k, (a, b) in enumerate(pairs)]
    for copy in copies:
        copy.start()
    for copy in copies:
        copy.wait()


def weights_kernel(w1_far, w2_far, weight1, weight2, back1, back2, w1, w2, done):
    copies = [pltpu.make_async_copy(a, b, done.at[k]) for k, (a, b) in enumerate(((w1_far, w1), (w2_far, w2)))]
    for copy in copies:
        copy.start()
    for copy, w, weight, back in zip(copies, (w1, w2), (weight1, weight2), (back1, back2)):
        copy.wait()
        weight[...] = paired(w[...], 0)
        back[...] = paired(flipped(w), 1)


def pack_rows_kernel(meta, feat, cot, pair, other, own, far, inner, outer, both):
    core = meta[4] % 2

    def cot_row(row):
        before, after = sides(meta, pair[row, 32:48, :], other[row, 32:48, :])
        return jnp.concatenate([before, cot[row], after], axis=0)

    for low, out in ((1 - core, inner), (core, outer)):
        for k in range(8):
            row = 8 * low + k
            before, after = sides(meta, pair[row, 0:32, :], other[row, 0:32, :])
            out[128 * k : 128 * k + 32, :] = before
            out[128 * k + 32 : 128 * k + 96, :] = feat[row]
            out[128 * k + 96 : 128 * k + 128, :] = after
        for k in range(2):
            out[1024 + 96 * k : 1120 + 96 * k, :] = cot_row(14 * low + k)
        away = 2 + 10 * low
        both_rows = cot_row(away).astype(F32) + cot_row(away + 1).astype(F32)
        out[1216:1264, :] = pooled_pair(both_rows).astype(BF)
    both[0] = own[...]
    both[1] = far[...]


def stack_kernel(*refs):
    out = refs[-1]
    for k, ref in enumerate(refs[:-1]):
        out[k] = ref[...]


def first_rows(meta, row, starts, weight):
    top, left, height, breadth = (meta[0], meta[1], meta[2], meta[3])
    mask = column_mask(left - 8, 128, breadth)
    pre = dot_nn(four_rows(row, [h - 1 for h in starts]), weight)
    out = {}
    for k, value in enumerate(split_rows(pre, starts)):
        h = starts[k // 2] + k % 2
        act = rounded(value * sigmoid(value)) * (mask * row_ok(top - 8 + h, height))
        out[h] = (value, three(act))
    return out


def second_rows(meta, row, starts, weight):
    top, left, height, breadth = (meta[0], meta[1], meta[2], meta[3])
    mask = column_mask(left // 2 - 4, 64, breadth // 2)
    rows = split_rows(dot_nn(four_rows(row, [h - 1 for h in starts]), weight), starts)
    out = {}
    for k, h in enumerate(starts):
        pre = rows[2 * k : 2 * k + 2]
        act = [(v * sigmoid(v)).astype(BF) for v in pre]
        small = rounded(0.25 * pooled_pair(act[0].astype(F32) + act[1].astype(F32)))
        small = small * (mask * row_ok(top // 2 - 4 + h // 2, height // 2))
        out[h] = (pre, act, three(small))
    return out


INNER_FIRST = [9, 11, 13, 15, 17, 19, 21]
INNER_SECOND = [10, 12, 14, 16, 18, 20]


def inner_kernel(
    meta, feat, cot, pair, other, weight1, weight2, feat3, act3, slope1, pool3, slope2, act, sums
):
    for k in range(8):
        rows = slice(2 * k, 2 * k + 2)
        before, after = sides(meta, pair[rows, 32:48, :], other[rows, 32:48, :])
        both = jnp.concatenate([before, cot[rows], after], axis=1).astype(F32)
        sums[k] = pooled_pair(both[0] + both[1])
    for k in range(16):
        before, after = sides(meta, pair[k, 0:32, :], other[k, 0:32, :])
        feat3[k] = three(jnp.concatenate([before, feat[k], after], axis=0).astype(F32))
    for h, (pre, wide) in first_rows(meta, lambda h: feat3[h - 8], INNER_FIRST, weight1[...]).items():
        act3[h - 9] = wide
        slope1[h - 9] = slope_of(pre[16:112])
    for h, (pre, value, small) in second_rows(meta, lambda h: act3[h - 9], INNER_SECOND, weight2[...]).items():
        pool3[h // 2 - 5] = small
        for e in range(2):
            slope2[h - 10 + e] = slope_of(pre[e][16:112])
            act[h - 10 + e] = value[e][32:96]


def outer_kernel(
    meta, inner, outer, feat3i, act3i, slope1i, pool3i, slope2i, acti, weight1, weight2,
    pool3, slope1, slope2, act, feat3o, act3o, feat3, act3,
):
    below_at = 8 * (meta[4] % 2)
    for k in range(8):
        feat3[k + below_at] = three(outer[128 * k : 128 * k + 128, :].astype(F32))
        feat3[k + 8 - below_at] = three(inner[128 * k : 128 * k + 128, :].astype(F32))

    def feat_row(h):
        return feat3i[h - 8] if 8 <= h < 24 else feat3[h if h < 8 else h - 16]

    def act_row(h):
        return act3i[h - 9] if 9 <= h < 23 else act3[h - 1 if h < 9 else h - 15]

    for starts in ([1, 3, 5, 7], [23, 25, 27, 29]):
        for h, (pre, wide) in first_rows(meta, feat_row, starts, weight1[...]).items():
            act3[h - 1 if h < 9 else h - 15] = wide
            if 7 <= h <= 24:
                slope1[h - 7] = slope_of(pre[16:112])
    slope1[2:16] = slope1i[...]
    for starts in ([2, 4, 6, 8], [22, 24, 26, 28]):
        for h, (pre, value, small) in second_rows(meta, act_row, starts, weight2[...]).items():
            pool3[h // 2 - 1] = small
            for e in range(2):
                if 6 <= h + e < 26:
                    slope2[h + e - 6] = slope_of(pre[e][16:112])
                if 8 <= h + e < 24:
                    act[h + e - 8] = value[e][32:96]
    pool3[4:10] = pool3i[...]
    slope2[4:16] = slope2i[...]
    act[2:14] = acti[...]
    for k in range(18):
        feat3o[k] = feat_row(k + 7)[32:96]
        act3o[k] = act_row(k + 7)[32:96]


def inner_step(meta, feat, cot, pair, other, weight1, weight2):
    return call(
        inner_kernel,
        "forward_inner",
        (
            ((16, 128, 384), BF),
            ((14, 128, 384), BF),
            ((14, 96, CH), F32),
            ((6, 64, 384), BF),
            ((12, 96, CH), F32),
            ((12, 64, CH), BF),
            ((8, 48, CH), F32),
        ),
        (meta, feat, cot, pair, other, weight1, weight2),
        limit=24,
        flops=0,
    )


def outer_step(meta, inner, outer, parts, weight1, weight2):
    return call(
        outer_kernel,
        "forward_outer",
        (
            ((14, 64, 384), BF),
            ((18, 96, CH), F32),
            ((20, 96, CH), F32),
            ((16, 64, CH), BF),
            ((18, 64, 384), BF),
            ((18, 64, 384), BF),
        ),
        (meta, inner, outer) + tuple(parts) + (weight1, weight2),
        (((16, 128, 384), BF),) * 2,
        limit=24,
        flops=4 * 10**9,
    )


def coarse_kernel(
    meta, pool3, sums, inner, outer, near0, near1, near2, near3, far,
    own, projs_out, keep, send, pooled_grad, wcat, projs, wide3, projin,
):
    top, left, height, breadth, me = (meta[0], meta[1], meta[2], meta[3], meta[4])
    core = me % 2
    near = (near0, near1, near2, near3)
    for rel in range(16):
        c, x, y = (rel % 2, (rel // 2) % 4, rel // 8)
        place = pl.ds(pl.multiple_of((me ^ rel) * 16, 16), 16)
        source = far.at[x, y] if c else near[x].at[y]
        for t in range(9):
            wcat[place, t * CH : (t + 1) * CH] = source[16 * t : 16 * t + 16, :]
        projs[place, :] = source[144:160, :]
    proj_w = projs[...]

    def pair_sum(a, b):
        return pooled_pair(a.astype(F32) + b.astype(F32))

    for ref, far_at, near_at in ((outer, 11 * core, 1 + 9 * core), (inner, 11 - 11 * core, 10 - 9 * core)):
        projin[far_at] = ref[1216:1264, :].astype(F32)
        near_rows = cot_edge(ref)
        projin[near_at] = pair_sum(near_rows[0], near_rows[1])

    projin[2:10] = sums[...]
    proj_in = projin[...].reshape(576, CH)
    proj_in_bf = proj_in.astype(BF)
    lhs = jnp.concatenate([pool3[r : r + 12].reshape(768, 3 * CH) for r in range(3)], axis=1)
    pre = dot_nt(lhs, wcat[...]).reshape(12, 64, WIDE)[:, 8:56].reshape(576, WIDE)
    sigma = sigmoid(pre)
    coarse_act = pre * sigma
    act_grad = dot_nt(proj_in_bf, proj_w)
    grad = rounded(act_grad * (sigma * (1.0 + pre * (1.0 - sigma)))).reshape(12, 48, WIDE)
    mask = column_mask(left // 2 - 2, 48, breadth // 2)
    mask = jnp.concatenate([mask, mask], axis=1)
    grad = masked(grad, mask, top // 2 - 2, height // 2)
    wide3[...] = three(grad.reshape(576, WIDE)).reshape(12, 48, 3 * WIDE)
    own_grad = grad[2:10, 8:40].reshape(256, WIDE).astype(BF)
    own_act = coarse_act.reshape(12, 48, WIDE)[2:10, 8:40].reshape(256, WIDE).astype(BF)
    own_in = proj_in.reshape(12, 48, CH)[2:10, 8:40].reshape(256, CH).astype(BF)

    def emit(first, last, value):
        value = value.reshape(8, 2, 16, CH)
        even, odd = (value[:, 0], value[:, 1])
        keep[:, first:last, :] = jnp.where(core == 0, even, odd).astype(BF)
        send[:, first:last, :] = jnp.where(core == 0, odd, even).astype(BF)

    source = [pool3[2 + r : 10 + r, 16:48, :].reshape(256, 3 * CH) for r in range(3)]
    part = dot_tn(own_grad, jnp.concatenate(source, axis=1))
    for t in range(9):
        emit(16 * t, 16 * t + 16, part[:, t * CH : (t + 1) * CH])
    emit(144, 160, dot_tn(own_act, own_in))
    total = None
    for r in range(3):
        lhs = wide3[r : r + 10].reshape(480, 3 * WIDE)
        first = 3 * (2 - r)
        rhs = jnp.concatenate([wcat[:, (first + 2 - s) * CH : (first + 3 - s) * CH] for s in range(3)], axis=0)
        part = dot_nn(lhs, rhs)
        total = part if total is None else total + part
    pooled_grad[...] = total.reshape(10, 48, CH)
    own[...] = own_act
    projs_out[...] = proj_w


def blend_kernel(scale, own, proj, act, coarse, blended, conv, proj_grad):
    for k in range(9):
        conv[k] = coarse[k // 5, 16 * (k % 5) : 16 * (k % 5) + 16, :].astype(F32) * scale
    proj_grad[...] = coarse[1, 64:80, :].astype(F32) * scale
    projected = dot_nn(own[...], proj[...]).reshape(8, 32, CH)
    for k in range(8):
        row = repeated(projected[k])
        for e in range(2):
            blended[2 * k + e] = (act[2 * k + e].astype(F32) + row).astype(BF)


def coarse_step(meta, pool3, sums, halo, near, far):
    return call(
        coarse_kernel,
        "coarse_step",
        (((256, WIDE), BF), ((WIDE, CH), BF), ((8, 160, CH), BF), ((8, 160, CH), BF), ((10, 48, CH), F32)),
        (meta, pool3, sums) + halo[2:] + tuple(near) + (far,),
        (
            ((WIDE, 9 * CH), BF),
            ((WIDE, CH), BF),
            ((12, 48, 3 * WIDE), BF),
            ((12, 48, CH), F32),
        ),
        limit=20,
        flops=2 * 10**9,
    )


def backward_kernel(
    meta, pooled_grad, cot, pair, other, inner, outer, slope1, slope2, feat3, act3, back_w,
    keep, send, first3, second3, grads,
):
    top, left, height, breadth = (meta[0], meta[1], meta[2], meta[3])
    mask = column_mask(left - 4, 96, breadth)

    def second_pair(k, both):
        wide = 0.25 * repeated(pooled_grad[k])
        for e in range(2):
            value = rounded((both[e].astype(F32) + wide) * slope2[2 * k + e])
            second3[2 * k + e] = three(value * (mask * row_ok(top - 2 + 2 * k + e, height)))

    first_core = meta[4] % 2 == 0
    second_pair(0, lax.select(first_core, cot_edge(outer), cot_edge(inner)))
    second_pair(9, lax.select(first_core, cot_edge(inner), cot_edge(outer)))
    for k in range(8):
        rows = slice(2 * k, 2 * k + 2)
        before, after = sides(meta, pair[rows, 32:48, :], other[rows, 32:48, :])
        second_pair(k + 1, jnp.concatenate([before, cot[rows], after], axis=1))

    def emit(base, parts):
        for r in range(3):
            grads[base + 384 * r : base + 384 * (r + 1), :] = parts[r].astype(BF)

    for starts in ([0, 2, 4, 6], [8, 10, 12, 14, 16]):
        value = dot_nt(four_rows(lambda h: second3[h], starts), back_w[...])
        for k, row in enumerate(split_rows(value, starts)):
            h = starts[k // 2] + k % 2
            row = rounded(row * slope1[h]) * (mask * row_ok(top - 1 + h, height))
            first3[h] = three(row)[16:80]
    emit(1152, weight_grad(act3[...], second3[2:18, 16:80, CH : 2 * CH]))
    emit(0, weight_grad(feat3[...], first3[1:17, :, CH : 2 * CH]))
    core = meta[4] % 2
    for k in range(8):
        keep[k] = grads[pl.ds(pl.multiple_of((2 * k + core) * 144, 16), 144), :]
        send[k] = grads[pl.ds(pl.multiple_of((2 * k + 1 - core) * 144, 16), 144), :]


def fine_backward(meta, pooled_grad, cot, halo, slope1, slope2, feat3, act3, back_w):
    return call(
        backward_kernel,
        "fine_backward",
        (((8, 144, CH), BF), ((8, 144, CH), BF), ((18, 64, 384), BF)),
        (meta, pooled_grad, cot) + halo + (slope1, slope2, feat3, act3, back_w),
        (((20, 96, 384), BF), ((2304, CH), BF)),
        limit=20,
        flops=2 * 10**9,
    )


def feature_kernel(first3, back_w, out):
    for starts in ([0, 2, 4, 6], [8, 10, 12, 14]):
        value = dot_nt(four_rows(lambda h: first3[h], starts), back_w[...])
        for k, row in enumerate(split_rows(value, starts)):
            out[starts[0] + k] = row.astype(BF)


def feature_step(first3, back_w):
    return call(feature_kernel, "feature_step", (((16, 64, CH), BF),), (first3, back_w), limit=12, flops=10**9)[0]


def scatter_core_kernel(keep_c, keep_f, got_c, got_f, out):
    for k in range(8):
        coarse = keep_c[k].astype(F32) + got_c[k].astype(F32)
        fine = keep_f[k].astype(F32) + got_f[k].astype(F32)
        for j in range(2):
            out[2 * k + j, 0:80, :] = coarse[80 * j : 80 * j + 80].astype(BF)
            out[2 * k + j, 80:152, :] = fine[72 * j : 72 * j + 72].astype(BF)


def scatter_plane_kernel(got, out, total):
    value = got[0].astype(F32)
    for k in range(1, 16):
        value = value + got[k].astype(F32)
    total[0:152, :] = value
    total[152:160, :] = jnp.zeros((8, CH), F32)
    for k in range(8):
        out[k] = total[19 * k : 19 * k + 24, :].astype(BF)


def scatter_column_kernel(got, out):
    value = got[0].astype(F32)
    for k in range(1, 8):
        value = value + got[k].astype(F32)
    value = value.astype(BF)
    for k in range(16):
        out[k] = value


def gather_column_kernel(meta, got, coarse, fine, total):
    for j in range(2):
        for k in range(8):
            total[j, 19 * k : 19 * k + 24, :] = got[8 * j + k].astype(F32)
    coarse[...] = total[:, 0:80, :].astype(BF)
    value = total[meta[5] // 8, 80:152, :].astype(BF)
    for k in range(16):
        fine[k] = value


def finish_kernel(scale, meta, mine, other, first, second):
    core = meta[4] % 2
    for at in range(8):
        out = first if at < 4 else second
        for j in range(2):
            rows = slice(72 * j, 72 * j + 72)
            a = mine[2 * at + j].astype(F32) * scale
            b = other[2 * at + j].astype(F32) * scale
            out[2 * (at % 4), rows, :] = jnp.where(core == 0, a, b)
            out[2 * (at % 4) + 1, rows, :] = jnp.where(core == 0, b, a)


def swap(value, axis, mask):
    count = lax.axis_size(axis)
    return lax.ppermute(value, axis, [(i, i ^ mask) for i in range(count)])


def swap_outer(value, axis):
    count = lax.axis_size(axis)
    pairs = [(i, i + 1 if i % 2 else i - 1) for i in range(1, count - 1)]
    return lax.ppermute(value, axis, pairs)


def exchange_plane(value):
    rows, cols = (lax.axis_size("row"), lax.axis_size("col"))
    groups = []
    for core in range(2):
        for z in range(cols // 2):
            groups.append([r * cols + c for r in range(core, rows, 2) for c in (z, z + cols // 2)])
    return lax.all_to_all(value, ("row", "col"), 0, 0, axis_index_groups=groups, tiled=True)


def exchange_depth(value):
    count = lax.axis_size("col")
    groups = [list(range(k, k + count // 2)) for k in (0, count // 2)]
    return lax.all_to_all(value, "col", 0, 0, axis_index_groups=groups, tiled=True)


def exchange_column(value):
    return lax.all_to_all(value, "col", 0, 0, tiled=True)


def after_all(value, *others):
    return lax.optimization_barrier((value,) + others)[0]


def local(features, conv_first, conv_second, coarse_conv, coarse_proj, cotangent):
    rows, cols = (lax.axis_size("row"), lax.axis_size("col"))
    height, breadth = (features.shape[0] * rows, features.shape[1] * cols)
    fine_scale = 1.0 / (height * breadth * features.shape[2]) ** 0.5
    coarse_scale = 2.0 * fine_scale
    me, mine = (lax.axis_index("row"), lax.axis_index("col"))
    fixed = [jnp.int32(height), jnp.int32(breadth)]
    meta = jnp.stack([me * 16, mine * 16] + fixed + [me, mine]).astype(jnp.int32)
    feat = features.reshape(16, 64, CH)
    cot = cotangent.reshape(16, 64, CH)
    conv = coarse_conv.reshape(9, CH, 16).swapaxes(1, 2)
    slab = ((160, CH), BF)

    side = ((16, 48, CH), BF)
    pair, other, own = call(
        pack_columns_kernel,
        "pack_columns",
        (side, side, slab),
        (meta, feat, cot, conv, coarse_proj),
        (pltpu.SemaphoreType.DMA((14,)),),
        far=(1, 2, 3, 4),
    )
    own = call(copy_kernel, "own_slab", (slab,), (own,), flops=4 * 10**9)[0]
    w1, w2 = (conv_first.reshape(1152, CH), conv_second.reshape(1152, CH))
    big, wide = (((16, 64, CH), BF), ((1536, 256), BF))
    feat_in, cot_in = call(
        bring_kernel,
        "bring",
        (big, big),
        (after_all(feat, own), cot),
        (pltpu.SemaphoreType.DMA((2,)),),
        far=(0, 1),
        flops=0,
    )
    own_far = swap(own, "row", 8)
    weight1, weight2, back1, back2 = call(
        weights_kernel,
        "weights",
        (wide, wide, ((256, 1536), BF), ((256, 1536), BF)),
        (after_all(w1, feat_in), w2),
        (((1152, CH), BF), ((1152, CH), BF), pltpu.SemaphoreType.DMA((2,))),
        far=(0, 1),
        flops=0,
    )
    pair = swap(pair, "col", 1)
    other = swap_outer(other, "col")
    edge = ((EDGE, CH), BF)
    inner, outer, near0 = call(
        pack_rows_kernel,
        "pack_rows",
        (edge, edge, ((2, 160, CH), BF)),
        (meta, feat_in, cot_in, pair, after_all(other, weight1), own, own_far),
    )
    outer = swap_outer(outer, "row")
    inner = swap(inner, "row", 1)
    pair_in = after_all(pair, near0)
    near = [near0] + [swap(near0, "row", 2 * k) for k in range(1, 4)]
    *parts, sums = inner_step(meta, feat_in, cot_in, pair_in, other, weight1, weight2)
    parts, near = lax.optimization_barrier((parts, near))
    far = swap(call(stack_kernel, "stack_eight", (((4, 2, 160, CH), BF),), near)[0], "row", 1)
    pool3, slope1, slope2, act, feat3, act3 = outer_step(meta, inner, outer, parts, weight1, weight2)
    halo = (pair, other, inner, outer)
    own_act, proj, keep_c, send_c, pooled_grad = coarse_step(meta, pool3, sums, halo, near, far)
    got_c = swap(send_c, "row", 1)
    keep_f, send_f, first3 = fine_backward(
        meta, pooled_grad, cot_in, halo, slope1, slope2, feat3, act3, back2
    )
    got_f = swap(send_f, "row", 1)
    feature_grad = feature_step(first3, back1)

    got_f = after_all(got_f, feature_grad)
    part = call(scatter_core_kernel, "scatter_core", (((16, 152, CH), BF),), (keep_c, keep_f, got_c, got_f))[0]
    part = call(
        scatter_plane_kernel, "scatter_plane", (((8, 24, CH), BF),), (exchange_plane(part),), (((160, CH), F32),)
    )[0]
    part = call(scatter_column_kernel, "scatter_column", (((16, 24, CH), BF),), (exchange_depth(part),))[0]
    coarse, fine = call(
        gather_column_kernel,
        "gather_column",
        (((2, 80, CH), BF), ((16, 72, CH), BF)),
        (meta, exchange_column(part)),
        (((2, 160, CH), F32),),
    )
    fine = exchange_plane(fine)
    blended, conv_grad, proj_grad = call(
        functools.partial(blend_kernel, coarse_scale),
        "blend",
        (((16, 64, CH), BF), ((9, 16, CH), F32), ((16, CH), F32)),
        (after_all(own_act, fine), proj, act, coarse),
        flops=10**9,
    )
    other = after_all(swap(fine, "row", 1), blended)
    first, second = call(
        functools.partial(finish_kernel, fine_scale),
        "finish",
        (((8, 144, CH), F32), ((8, 144, CH), F32)),
        (meta, fine, other),
    )
    shape = features.shape
    return (
        blended.reshape(shape),
        feature_grad.reshape(shape),
        first.reshape(3, 3, CH, CH),
        second.reshape(3, 3, CH, CH),
        conv_grad.reshape(3, 3, 16, CH).swapaxes(2, 3),
        proj_grad,
    )


def solution(mesh):
    in_specs = (
        P("row", "col", None, None),
        P(),
        P(),
        P(None, None, None, "row"),
        P("row", None),
        P("row", "col", None, None),
    )
    out_specs = (
        P("row", "col", None, None),
        P("row", "col", None, None),
        P(),
        P(),
        P(None, None, None, "row"),
        P("row", None),
    )
    return jax.shard_map(local, mesh=mesh, in_specs=in_specs, out_specs=out_specs, check_vma=False)
```
